32 devices in a mesh: dp: 4 (over z), seq: 8 (over y, x, core).
Axes of the slice: x: 2, y: 2, z: 4, core: 2. Of those that a mesh axis runs over, the one named last changes fastest.
Arguments:
- inputs: bfloat16 [8, 1024, 768], P('dp', 'seq'), may hold values from -6 to 6
- char_ids: int32 [8, 4096], P('dp', 'seq'), may hold values from 0 to 124
- lang_ids: int32 [8], P('dp'), may hold values from 0 to 7
- lengths: int32 [8], P('dp'), may hold values from 256 to 1024, as said below
- char_table: bfloat16 [1000, 256], replicated, may hold values from -6 to 6
- gate_weight: bfloat16 [2, 256, 384], replicated, may hold values from -0.1875 to 0.1875
- gate_bias: float32 [2, 384], replicated, may hold values from -12 to -3
- cand_weight: bfloat16 [2, 256, 384], replicated, may hold values from -0.375 to 0.375
- join_weight: bfloat16 [3, 768, 768], replicated, may hold values from -0.875 to 0.875
- join_bias: float32 [768], replicated, may hold values from -1.8 to 1.8
- query_weight: bfloat16 [768, 768], replicated, may hold values from -0.21875 to 0.21875
- query_bias: float32 [768], replicated, may hold values from -1.8 to 1.8
- key_weight: bfloat16 [768, 768], replicated, may hold values from -0.21875 to 0.21875
- value_weight: bfloat16 [768, 768], replicated, may hold values from -0.21875 to 0.21875
- value_bias: float32 [768], replicated, may hold values from -1.8 to 1.8
- out_weight: bfloat16 [768, 768], replicated, may hold values from -1.25 to 1.25
- out_bias: float32 [768], replicated, may hold values from -1.8 to 1.8
- norm1_gain: float32 [768], replicated, may hold values from 0.5 to 1.5
- norm1_bias: float32 [768], replicated, may hold values from -1.8 to 1.8
- up_weight: bfloat16 [768, 3072], replicated, may hold values from -0.21875 to 0.21875
- up_bias: float32 [3072], replicated, may hold values from -1.8 to 1.8
- down_weight: bfloat16 [3072, 768], replicated, may hold values from -0.109375 to 0.109375
- down_bias: float32 [768], replicated, may hold values from -1.8 to 1.8
- norm2_gain: float32 [768], replicated, may hold values from 0.5 to 1.5
- norm2_bias: float32 [768], replicated, may hold values from -1.8 to 1.8
- cotangent: bfloat16 [8, 1024, 768], P('dp', 'seq'), may hold values from -6 to 6
Outputs:
- output: bfloat16 [8, 1024, 768], P('dp', 'seq')
- input_grad: bfloat16 [8, 1024, 768], P('dp', 'seq')
- grad_char_table: float32 [1000, 256], replicated
- grad_gate_weight: float32 [2, 256, 384], P(None, ('dp', 'seq'))
- grad_gate_bias: float32 [2, 384], replicated
- grad_cand_weight: float32 [2, 256, 384], P(None, ('dp', 'seq'))
- grad_join_weight: float32 [3, 768, 768], P(None, ('dp', 'seq'))
- grad_join_bias: float32 [768], replicated
- grad_query_weight: float32 [768, 768], P(('dp', 'seq'))
- grad_query_bias: float32 [768], replicated
- grad_key_weight: float32 [768, 768], P(('dp', 'seq'))
- grad_value_weight: float32 [768, 768], P(('dp', 'seq'))
- grad_value_bias: float32 [768], replicated
- grad_out_weight: float32 [768, 768], P(('dp', 'seq'))
- grad_out_bias: float32 [768], replicated
- grad_norm1_gain: float32 [768], replicated
- grad_norm1_bias: float32 [768], replicated
- grad_up_weight: float32 [768, 3072], P(('dp', 'seq'))
- grad_up_bias: float32 [3072], replicated
- grad_down_weight: float32 [3072, 768], P(('dp', 'seq'))
- grad_down_bias: float32 [768], replicated
- grad_norm2_gain: float32 [768], replicated
- grad_norm2_bias: float32 [768], replicated
The draws below stay inside these ranges and needn't reach their ends.
Inputs may be any that keep to these rules, and one draw needn't show every extreme that they name: `lengths`: at least one of the 2 sequences of each index of dp has all 1024 tokens.
All inputs are finite; a program needn't handle non-finite values.
Results may differ from the reference program's by a relative error of at most 0.02.
Values may be sent and summed in bfloat16 or wider, within the bound.
No kernel may reach another device: no remote copies, remote signals or barrier semaphores. Data moves between devices by JAX's collectives and lax.ppermute only.
A program may use at most 320 MiB of HBM per device.

```python
import math
import jax
import jax.numpy as jnp
from jax import lax

HEADS = 12
HEAD_DIM = 64
D = 768
FF = 3072
H = 384
CE = 256
VOC = 1000
GROUPS = 8
CHAR_PER = 4
SEQ_DP = 2
SUBV = 125
SEQ_LEN = 1024
SEQS = 8
CHARS_SEQ = 4096


def draw_lengths(key, part):
    key = jax.random.fold_in(key, 11)
    span_key, pick_key = jax.random.split(key)
    drawn = jax.random.randint(span_key, (SEQS,), SEQ_LEN // 4, SEQ_LEN + 1)
    picked = jax.random.randint(pick_key, (SEQS // SEQ_DP,), 0, SEQ_DP)
    position = jnp.arange(SEQS) % SEQ_DP
    full_one = position == jnp.repeat(picked, SEQ_DP)
    return jnp.where(full_one, SEQ_LEN, drawn).astype(jnp.int32)


def draw_gate_bias(key, part):
    key = jax.random.fold_in(key, 7)
    slow_key, fast_key, pick_key = jax.random.split(key, 3)
    slow_rate = jnp.exp(jax.random.uniform(slow_key, (2, H), jnp.float32, math.log(0.5 / CHARS_SEQ), math.log(2.0 / CHARS_SEQ)))
    fast_rate = jnp.exp(jax.random.uniform(fast_key, (2, H), jnp.float32, math.log(1.0 / 50), math.log(1.0 / 30)))
    slow_share = 0.5
    chosen = jax.random.uniform(pick_key, (2, H), jnp.float32) < slow_share
    gate_rate = jnp.where(chosen, slow_rate, fast_rate)
    return jnp.log(gate_rate) - jnp.log(1.0 - gate_rate)


def plant(array, stream_key, low, top_value):
    place = [jax.random.randint(jax.random.fold_in(stream_key, axis), (), 0, length) for axis, length in enumerate(array.shape)]
    widest = array.shape.index(max(array.shape))
    next_to = place[:widest] + [(place[widest] + 1) % array.shape[widest]] + place[widest + 1:]
    return array.at[tuple(place)].set(low).at[tuple(next_to)].set(top_value)


def steps_of(stream_key, dims, pieces, low, largest):
    level = 1.0
    for dim, shards_of in pieces:
        heights = jax.random.uniform(jax.random.fold_in(jax.random.fold_in(stream_key, 6), dim), (shards_of,), jnp.float32, low / len(pieces), largest / len(pieces))
        level = level * jnp.repeat(jnp.exp(heights), dims[dim] // shards_of).reshape((-1,) + (1,) * (len(dims) - 1 - dim))
    return level


def noise(rng, extent, scale, most, cuts=(), kind=jnp.bfloat16):
    values = jax.random.normal(rng, extent, jnp.float32) * scale
    if len(cuts) > 0:
        values = steps_of(rng, extent, cuts, -0.22, 0.18) * values
    return jnp.clip(values, min=-most, max=most).astype(kind)


def setup_inputs(seed: int = 0) -> dict:
    key_list = jax.random.split(jax.random.key(seed), 27)
    inputs = noise(key_list[0], (SEQS, SEQ_LEN, D), 1.0, 6.0, ((0, 4), (1, 8)))
    char_ids = plant(jax.random.randint(key_list[1], (SEQS, CHARS_SEQ), 0, SUBV), jax.random.fold_in(key_list[1], 1), 0, SUBV - 1).astype(jnp.int32)
    lang_ids = plant(jax.random.randint(key_list[2], (SEQS,), 0, GROUPS), jax.random.fold_in(key_list[2], 1), 0, GROUPS - 1).astype(jnp.int32)
    lengths = draw_lengths(jax.random.fold_in(key_list[26], 71), 0)
    char_table = noise(key_list[4], (VOC, CE), 1.0, 6.0)
    gate_weight = noise(key_list[5], (2, CE, H), (4 * CE) ** -0.5, 0.1875)
    gate_bias = draw_gate_bias(jax.random.fold_in(key_list[26], 71), 0)
    cand_weight = noise(key_list[7], (2, CE, H), CE ** -0.5, 0.375)
    join_weight = noise(key_list[8], (3, D, D), (H // 8) ** -0.5, 0.875)
    join_bias = noise(key_list[9], (D,), 0.3, 1.8, (), jnp.float32)
    query_weight = noise(key_list[10], (D, D), D ** -0.5, 0.21875)
    query_bias = noise(key_list[11], (D,), 0.3, 1.8, (), jnp.float32)
    key_weight = noise(key_list[12], (D, D), D ** -0.5, 0.21875)
    value_weight = noise(key_list[13], (D, D), D ** -0.5, 0.21875)
    value_bias = noise(key_list[14], (D,), 0.3, 1.8, (), jnp.float32)
    out_weight = noise(key_list[15], (D, D), (D // 32) ** -0.5, 1.25)
    out_bias = noise(key_list[16], (D,), 0.3, 1.8, (), jnp.float32)
    norm1_gain = jnp.clip(1.0 + 0.1 * jax.random.normal(key_list[17], (D,), jnp.float32), 0.5, 1.5)
    norm1_bias = noise(key_list[18], (D,), 0.3, 1.8, (), jnp.float32)
    up_weight = noise(key_list[19], (D, FF), D ** -0.5, 0.21875)
    up_bias = noise(key_list[20], (FF,), 0.3, 1.8, (), jnp.float32)
    down_weight = noise(key_list[21], (FF, D), FF ** -0.5, 0.109375)
    down_bias = noise(key_list[22], (D,), 0.3, 1.8, (), jnp.float32)
    norm2_gain = jnp.clip(1.0 + 0.1 * jax.random.normal(key_list[23], (D,), jnp.float32), 0.5, 1.5)
    norm2_bias = noise(key_list[24], (D,), 0.3, 1.8, (), jnp.float32)
    cotangent = noise(key_list[25], (SEQS, SEQ_LEN, D), 1.0, 6.0, ((0, 4), (1, 8)))
    return {"inputs": inputs, "char_ids": char_ids, "lang_ids": lang_ids, "lengths": lengths, "char_table": char_table, "gate_weight": gate_weight, "gate_bias": gate_bias, "cand_weight": cand_weight, "join_weight": join_weight, "join_bias": join_bias, "query_weight": query_weight, "query_bias": query_bias, "key_weight": key_weight, "value_weight": value_weight, "value_bias": value_bias, "out_weight": out_weight, "out_bias": out_bias, "norm1_gain": norm1_gain, "norm1_bias": norm1_bias, "up_weight": up_weight, "up_bias": up_bias, "down_weight": down_weight, "down_bias": down_bias, "norm2_gain": norm2_gain, "norm2_bias": norm2_bias, "cotangent": cotangent}


@jax.custom_vjp
def low(v):
    return lax.optimization_barrier(v.astype(jnp.bfloat16)).astype(jnp.float32)

@jax.custom_vjp
def low_back(v):
    return v

def low_keep(v):
    return (low(v), None)

def low_pass(kept, grad):
    return (grad,)

def back_keep(v):
    return (v, None)

def back_low(kept, grad):
    return (low(grad),)
low.defvjp(low_keep, low_pass)
low_back.defvjp(back_keep, back_low)
norm_eps = 1e-05

def matmul(left, right):
    return jnp.dot(left, right, precision=lax.Precision.HIGHEST)

def compose(earlier_map, later_map):
    return (later_map[0] * earlier_map[0], later_map[0] * earlier_map[1] + later_map[1])

def layer_norm(values, gain, shift):
    center = values - lax.optimization_barrier(jnp.mean(values, axis=-1, keepdims=True))
    spread = lax.optimization_barrier(jnp.mean(center * center, axis=-1, keepdims=True))
    return center * lax.rsqrt(spread + norm_eps) * gain + shift

def sequence_forward(params, tokens_in, chars_in, lang_id, seq_length):
    char_table, gate_weight, gate_bias, cand_weight, join_weight, join_bias, query_weight, query_bias, key_weight, value_weight, value_bias, out_weight, out_bias, norm1_gain, norm1_bias, up_weight, up_bias, down_weight, down_bias, norm2_gain, norm2_bias = params
    table_rows = (lang_id * SUBV + chars_in).astype(jnp.int32)
    embedded = low_back(char_table[table_rows])
    states = []
    for direction in range(2):
        gate_pre = low_back(matmul(embedded, gate_weight[direction]) + gate_bias[direction])
        candidate = low_back(matmul(embedded, cand_weight[direction]))
        update = jax.nn.sigmoid(gate_pre)
        scanned = lax.associative_scan(compose, (1.0 - update, update * candidate), reverse=direction == 1, axis=0)
        states.append(scanned[1])
    forward_last = states[0].reshape(SEQ_LEN, CHAR_PER, H)[:, CHAR_PER - 1]
    backward_first = states[1].reshape(SEQ_LEN, CHAR_PER, H)[:, 0]
    char_repr = low(jnp.concatenate([forward_last, backward_first], axis=1))
    padded = jnp.pad(char_repr, ((1, 1), (0, 0)))
    joining = matmul(padded[:-2], join_weight[0]) + matmul(padded[1:-1], join_weight[1])
    joining = joining + matmul(padded[2:], join_weight[2]) + join_bias
    resid = tokens_in + low_back(joining)
    resid_low = low(resid)
    query = low(low_back(matmul(resid_low, query_weight) + query_bias)).reshape(SEQ_LEN, HEADS, HEAD_DIM)
    key_low = low(low_back(matmul(resid_low, key_weight))).reshape(SEQ_LEN, HEADS, HEAD_DIM)
    value = low(low_back(matmul(resid_low, value_weight) + value_bias)).reshape(SEQ_LEN, HEADS, HEAD_DIM)
    scores = low_back(jnp.einsum('qhd,khd->hqk', query, key_low, precision=lax.Precision.HIGHEST) * 0.125)
    key_valid = jnp.arange(SEQ_LEN) < seq_length
    scores = jnp.where(key_valid[None, None, :], scores, -1000000000.0)
    probs = low(jax.nn.softmax(scores, axis=-1))
    mixed = jnp.einsum('hqk,khd->qhd', probs, value, precision=lax.Precision.HIGHEST)
    mixed = low(low_back(mixed)).reshape(SEQ_LEN, D)
    attended = low_back(matmul(mixed, out_weight) + out_bias)
    first = layer_norm(resid + attended, norm1_gain, norm1_bias)
    hidden = low_back(matmul(low(first), up_weight) + up_bias)
    act = low(jax.nn.gelu(hidden))
    second = low_back(matmul(act, down_weight) + down_bias)
    return layer_norm(first + second, norm2_gain, norm2_bias)

def reference(inputs, char_ids, lang_ids, lengths, char_table, gate_weight, gate_bias, cand_weight, join_weight, join_bias, query_weight, query_bias, key_weight, value_weight, value_bias, out_weight, out_bias, norm1_gain, norm1_bias, up_weight, up_bias, down_weight, down_bias, norm2_gain, norm2_bias, cotangent):
    params = tuple((weight.astype(jnp.float32) for weight in (char_table, gate_weight, gate_bias, cand_weight, join_weight, join_bias, query_weight, query_bias, key_weight, value_weight, value_bias, out_weight, out_bias, norm1_gain, norm1_bias, up_weight, up_bias, down_weight, down_bias, norm2_gain, norm2_bias)))
    activations = inputs.astype(jnp.float32)
    checked_forward = jax.checkpoint(sequence_forward)

    def forward(weights, tokens_all):

        def per_sequence(sequence_items):
            return checked_forward(weights, sequence_items[0], sequence_items[1], sequence_items[2], sequence_items[3])
        return lax.map(per_sequence, (tokens_all, char_ids, lang_ids, lengths))
    result, pull_back = jax.vjp(forward, params, activations)
    weight_grads, input_grad = pull_back(cotangent.astype(jnp.float32))
    g_table, g_gate, g_gate_bias, g_cand, g_join, g_join_bias, g_query, g_query_bias, g_key, g_value, g_value_bias, g_out, g_out_bias, g_norm1_gain, g_norm1_bias, g_up, g_up_bias, g_down, g_down_bias, g_norm2_gain, g_norm2_bias = weight_grads
    return (result.astype(jnp.bfloat16), input_grad.astype(jnp.bfloat16), g_table, g_gate, g_gate_bias, g_cand, g_join, g_join_bias, g_query, g_query_bias, g_key, g_value, g_value_bias, g_out, g_out_bias, g_norm1_gain, g_norm1_bias, g_up, g_up_bias, g_down, g_down_bias, g_norm2_gain, g_norm2_bias)
```

```python
import functools

import jax
import jax.numpy as jnp
from jax import lax
from jax.experimental import pallas as pl
from jax.experimental.pallas import tpu as pltpu
from jax.sharding import PartitionSpec as P

HEADS = 12
GROUPS = 8
SEGS = 8
LANES = 128
NORM_EPS = 1e-05
MASKED = -1000000000.0
MIB = 1 << 20
F32 = jnp.float32
BF16 = jnp.bfloat16


def dot(left, right):
    return jnp.dot(left, right, preferred_element_type=F32)


def dot_nt(left, right):
    return lax.dot_general(left, right, (((1,), (1,)), ((), ())), preferred_element_type=F32)


def dot_tn(left, right):
    return lax.dot_general(left, right, (((0,), (0,)), ((), ())), preferred_element_type=F32)


def column_sum(values):
    return jnp.sum(values.astype(F32), axis=0, keepdims=True)


VMEM = pl.BlockSpec(memory_space=pltpu.VMEM)
SMEM = pl.BlockSpec(memory_space=pltpu.SMEM)
HBM = pl.BlockSpec(memory_space=pl.ANY)


def call(body, ins, outs, scratch=(), limit=48, flops=0, moved=0, name=None):
    return pl.pallas_call(
        body,
        in_specs=ins,
        out_specs=[VMEM] * len(outs),
        out_shape=[jax.ShapeDtypeStruct(shape, kind) for shape, kind in outs],
        scratch_shapes=list(scratch),
        compiler_params=pltpu.CompilerParams(vmem_limit_bytes=limit * MIB),
        cost_estimate=pl.CostEstimate(flops=flops, bytes_accessed=moved, transcendentals=0),
        name=name,
    )


def gates(embedded, gate_w, gate_b, cand_w, upd, cand):
    for r in range(2):
        upd[r] = jax.nn.sigmoid(dot(embedded, gate_w[r]) + gate_b[r : r + 1])
        cand[r] = dot(embedded, cand_w[r])


def chars_forward_body(
    seqs, steps, per, sub,
    lang, ids, table, gate_w, gate_b, cand_w,
    embedded_out, htok, ptok, pre, pseg, payload,
    upd, cand, hseg, padded_table,
):
    rows = seqs * SEGS
    vocab = table.shape[0]
    padded_table[...] = jnp.zeros_like(padded_table)
    padded_table[0:vocab] = table[...]
    wide = padded_table.shape[0]
    local = lax.broadcasted_iota(jnp.int32, (LANES, wide), 0)
    place = lax.broadcasted_iota(jnp.int32, (LANES, wide), 1)
    mine = []
    for s in range(seqs):
        pick = (place == lang[s] * sub + local) & (local < sub)
        mine.append(dot(pick.astype(BF16), padded_table[...]).astype(BF16))
    own_table = jnp.concatenate(mine, axis=0)
    chars = ids.shape[0]
    one_hot = (lax.broadcasted_iota(jnp.int32, (chars, seqs * LANES), 1) == ids[...]).astype(BF16)
    embedded = dot(one_hot, own_table).astype(BF16)
    embedded_out[...] = embedded
    gates(embedded, gate_w, gate_b[...], cand_w, upd, cand)

    def token(q, carry):
        h0, p0, h1, p1 = carry
        for j in range(per):
            at = pl.ds(pl.multiple_of((q * per + j) * rows, rows), rows)
            u = upd[0, at, :]
            h0 = h0 + u * (cand[0, at, :] - h0)
            p0 = p0 * (1.0 - u)
            at = pl.ds(pl.multiple_of((steps - 1 - q * per - j) * rows, rows), rows)
            u = upd[1, at, :]
            h1 = h1 + u * (cand[1, at, :] - h1)
            p1 = p1 * (1.0 - u)
        htok[0, q] = h0
        ptok[0, q] = p0
        back = steps // per - 1 - q
        htok[1, back] = h1
        ptok[1, back] = p1
        return h0, p0, h1, p1

    zero = jnp.zeros((rows, upd.shape[2]), F32)
    h0, p0, h1, p1 = lax.fori_loop(0, steps // per, token, (zero, zero + 1.0, zero, zero + 1.0))
    pseg[0], pseg[1], hseg[0], hseg[1] = p0, p1, h0, h1
    last = steps // per - 1
    for s in range(seqs):
        for r in range(2):
            total_a = jnp.ones((1, upd.shape[2]), F32)
            total_b = jnp.zeros((1, upd.shape[2]), F32)
            order = range(SEGS) if r == 0 else range(SEGS - 1, -1, -1)
            for g in order:
                row = s * SEGS + g
                pre[0, r, row : row + 1] = total_a
                pre[1, r, row : row + 1] = total_b
                p_row = pseg[r, row : row + 1]
                total_b = p_row * total_b + hseg[r, row : row + 1]
                total_a = p_row * total_a
            payload[4 * r, s : s + 1] = total_a
            payload[4 * r + 1, s : s + 1] = total_b
            edge = s * SEGS if r == 0 else s * SEGS + SEGS - 1
            q = 0 if r == 0 else last
            payload[4 * r + 2, s : s + 1] = ptok[r, q, edge : edge + 1]
            payload[4 * r + 3, s : s + 1] = htok[r, q, edge : edge + 1]


def spread(values, seqs):
    wide = values.shape[1]
    return jnp.concatenate(
        [jnp.broadcast_to(values[s : s + 1], (SEGS, wide)) for s in range(seqs)], axis=0
    )


def token_row(token, tokens, per_seg, seqs):
    s = token // tokens
    t = token % tokens
    return (t % per_seg) * (seqs * SEGS) + s * SEGS + t // per_seg


def join_query_body(
    count, seqs, tokens, pairs,
    me_ref, gathered, htok, ptok, pre, inputs, join_b, query_b, value_b,
    join_w, query_w, key_w, value_w,
    *rest,
):
    taps, resid_out, low_out, enter = rest[:4]
    chunks = rest[4 : 4 + count]
    join_v, query_v, key_v, value_v, sems, stage = rest[4 + count :]
    copies = [pltpu.make_async_copy(join_w.at[k], join_v.at[k], sems.at[k]) for k in range(3)]
    for k, (far, near) in enumerate(((query_w, query_v), (key_w, key_v), (value_w, value_v))):
        copies.append(pltpu.make_async_copy(far, near, sems.at[3 + k]))
    for copy in copies:
        copy.start()
    me = me_ref[0]
    half = htok.shape[3]
    per_seg = htok.shape[1]
    total = seqs * tokens
    x0 = jnp.zeros((seqs, half), F32)
    x1 = jnp.zeros((seqs, half), F32)
    for j in range(count):
        x0 = jnp.where(j < me, gathered[j, 0] * x0 + gathered[j, 1], x0)
        i = count - 1 - j
        x1 = jnp.where(i > me, gathered[i, 4] * x1 + gathered[i, 5], x1)
    carry0 = pre[0, 0] * spread(x0, seqs) + pre[1, 0]
    carry1 = pre[0, 1] * spread(x1, seqs) + pre[1, 1]
    enter[0] = carry0
    enter[1] = carry1
    forward = htok[0] + ptok[0] * carry0[None]
    backward = htok[1] + ptok[1] * carry1[None]
    rows = seqs * SEGS
    last = per_seg - 1
    f_last = jnp.concatenate(
        [forward[last, s * SEGS + SEGS - 1 : s * SEGS + SEGS] for s in range(seqs)], axis=0
    )
    b_first = jnp.concatenate(
        [backward[0, s * SEGS : s * SEGS + 1] for s in range(seqs)], axis=0
    )
    left = jnp.maximum(me - 1, 0)
    right = jnp.minimum(me + 1, count - 1)
    left_b = gathered[left, 6] * b_first + gathered[left, 7]
    right_f = gathered[right, 2] * f_last + gathered[right, 3]
    left_row = jnp.where(me > 0, jnp.concatenate([x0, left_b], axis=1), 0.0)
    right_row = jnp.where(me < count - 1, jnp.concatenate([right_f, x1], axis=1), 0.0)
    rim = jnp.concatenate(
        [left_row, right_row, jnp.zeros((16 - 2 * seqs, 2 * half), F32)], axis=0
    ).astype(BF16)
    tokens_perm = jnp.concatenate(
        [forward.reshape(total, half), backward.reshape(total, half)], axis=1
    ).astype(BF16)
    source = jnp.concatenate([tokens_perm, rim], axis=0)
    token = lax.broadcasted_iota(jnp.int32, (total, total + 16), 0)
    place = lax.broadcasted_iota(jnp.int32, (total, total + 16), 1)
    joining = jnp.broadcast_to(join_b[...], (total, 2 * half))
    for k in range(3):
        moved = token + (k - 1)
        want = token_row(moved, tokens, per_seg, seqs)
        if k == 0:
            want = jnp.where(token % tokens == 0, total + token // tokens, want)
        if k == 2:
            want = jnp.where(token % tokens == tokens - 1, total + seqs + token // tokens, want)
        tap = dot((place == want).astype(BF16), source).astype(BF16)
        taps[k] = tap
        copies[k].wait()
        joining = joining + dot(tap, join_v[k])
    resid = inputs[...].astype(F32) + joining
    resid_out[...] = resid
    low = resid.astype(BF16)
    low_out[...] = low
    size = 2 * half // HEADS
    wide = pairs * size
    copies[3].wait()
    query = (dot(low, query_v[...]) + query_b[...]).astype(BF16)
    copies[4].wait()
    key = dot(low, key_v[...]).astype(BF16)
    copies[5].wait()
    value = (dot(low, value_v[...]) + value_b[...]).astype(BF16)
    send_pairs((query, key, value), stage, chunks, me, count, seqs, tokens, pairs, size, wide)


def send_pairs(arrays, stage, chunks, me, count, seqs, tokens, pairs, size, wide):
    for d in range(count):
        for a, array in enumerate(arrays):
            first = d * pairs
            if first >= seqs * HEADS:
                stage[d, :, a * wide : (a + 1) * wide] = jnp.zeros((tokens, wide), BF16)
                continue
            s, head = first // HEADS, first % HEADS
            stage[d, :, a * wide : (a + 1) * wide] = array[
                s * tokens : (s + 1) * tokens, head * size : head * size + wide
            ]
    for k in range(count):
        chunks[k][...] = stage[lax.rem(me + k, count)]


def receive_pairs(chunks, stage, place, me, count, seqs, tokens, pairs, size, parts):
    wide = pairs * size
    for k in range(count):
        stage[lax.rem(me + count - k, count)] = chunks[k][...]
    for d in range(count):
        first = d * pairs
        if first >= seqs * HEADS:
            continue
        s, head = first // HEADS, first % HEADS
        for a in range(parts):
            place(a, s, head * size, stage[d, :, a * wide : (a + 1) * wide])


def load_heads(chunks, me, count, tokens, pairs, size, part, target, scale=None):
    wide = pairs * size
    for k in range(count):
        at = pl.ds(pl.multiple_of(lax.rem(me + count - k, count) * tokens, tokens), tokens)
        for h in range(pairs):
            lane = part * wide + h * size
            block = chunks[k][:, lane : lane + size]
            target[h, at, :] = block if scale is None else block * scale


def pair_length(lengths, me, pairs, h, seqs):
    return lengths[jnp.minimum((me * pairs + h) // HEADS, seqs - 1)]


def transposed(values):
    return jnp.transpose(values.astype(F32))


def attend_body(count, seqs, tokens, pairs, size, block, me_ref, lengths, *rest):
    chunks, rest = rest[:count], rest[count:]
    outs, lse = rest[:count], rest[count]
    q, k, v, vt, mixed_t, mixed = rest[count + 1 :]
    me = me_ref[0]
    full = count * tokens
    load_heads(chunks, me, count, tokens, pairs, size, 0, q, jnp.asarray(0.125, BF16))
    load_heads(chunks, me, count, tokens, pairs, size, 1, k)
    load_heads(chunks, me, count, tokens, pairs, size, 2, v)
    for h in range(pairs):
        vt[h] = transposed(v[h]).astype(BF16)
        valid = pair_length(lengths, me, pairs, h, seqs)

        def rows(i, _, h=h, valid=valid):
            at = pl.ds(pl.multiple_of(i * block, block), block)
            scores = dot_nt(k[h], q[h, at, :])
            key_at = lax.broadcasted_iota(jnp.int32, (full, block), 0)
            scores = jnp.where(key_at < valid, scores, MASKED)
            top = jnp.max(scores, axis=0, keepdims=True)
            probs = jnp.exp(scores - top)
            total = jnp.sum(probs, axis=0, keepdims=True)
            lse[h, :, at] = top + jnp.log(total)
            mixed_t[h * size : (h + 1) * size, at] = dot(vt[h], probs.astype(BF16)) / total
            return 0

        lax.fori_loop(0, full // block, rows, 0)
    mixed[...] = transposed(mixed_t[...]).astype(BF16)
    for j in range(count):
        at = pl.ds(pl.multiple_of(lax.rem(me + j, count) * tokens, tokens), tokens)
        outs[j][...] = mixed[at, :]


def attend_back_body(count, seqs, tokens, pairs, size, block, me_ref, lengths, lse, *rest):
    chunks, d_chunks, rest = rest[:count], rest[count : 2 * count], rest[2 * count :]
    outs = rest[:count]
    q, k, v, kt, d_o, dq_t, dk, dv, stage = rest[count:]
    me = me_ref[0]
    full = count * tokens
    wide = pairs * size
    load_heads(chunks, me, count, tokens, pairs, size, 0, q, jnp.asarray(0.125, BF16))
    load_heads(chunks, me, count, tokens, pairs, size, 1, k)
    load_heads(chunks, me, count, tokens, pairs, size, 2, v)
    load_heads(d_chunks, me, count, tokens, pairs, size, 0, d_o)
    for h in range(pairs):
        kt[h] = transposed(k[h]).astype(BF16)
        valid = pair_length(lengths, me, pairs, h, seqs)
        dk[h] = jnp.zeros_like(dk[h])
        dv[h] = jnp.zeros_like(dv[h])

        def rows(i, _, h=h, valid=valid):
            at = pl.ds(pl.multiple_of(i * block, block), block)
            scores = dot_nt(k[h], q[h, at, :])
            key_at = lax.broadcasted_iota(jnp.int32, (full, block), 0)
            scores = jnp.where(key_at < valid, scores, MASKED)
            probs = jnp.exp(scores - lse[h, :, at])
            d_probs = dot_nt(v[h], d_o[h, at, :])
            row_dot = jnp.sum(d_probs * probs, axis=0, keepdims=True)
            d_scores = (probs * (d_probs - row_dot)).astype(BF16)
            dv[h] += dot(probs.astype(BF16), d_o[h, at, :])
            dk[h] += dot(d_scores, q[h, at, :])
            dq_t[h * size : (h + 1) * size, at] = dot(kt[h], d_scores) * 0.125
            return 0

        lax.fori_loop(0, full // block, rows, 0)
        for part, grad in ((1, dk), (2, dv)):
            lane = part * wide + h * size
            stage[:, lane : lane + size] = grad[h].astype(BF16)
    stage[:, 0:wide] = transposed(dq_t[...]).astype(BF16)
    for j in range(count):
        at = pl.ds(pl.multiple_of(lax.rem(me + j, count) * tokens, tokens), tokens)
        outs[j][...] = stage[at, :]


def normed(values):
    center = values - jnp.mean(values, axis=-1, keepdims=True)
    scale = lax.rsqrt(jnp.mean(center * center, axis=-1, keepdims=True) + NORM_EPS)
    return center * scale, scale


def norm_back(cotangent, unit, scale, gain):
    d_unit = cotangent * gain
    mean = jnp.mean(d_unit, axis=-1, keepdims=True)
    lean = jnp.mean(d_unit * unit, axis=-1, keepdims=True)
    return scale * (d_unit - mean - unit * lean)


GELU_A = 0.7978845608028654
GELU_B = 0.044715


def feed_body(
    count, seqs, tokens, pairs, size, block,
    me_ref, resid, cotangent, out_b, gain1, shift1, up_b, down_b, gain2, shift2,
    out_w, up_w, down_w,
    *rest,
):
    chunks, rest = rest[:count], rest[count:]
    output, mixed_out, first_low_out, act_out, d_second_out, d_hidden_out = rest[:6]
    d_attn_out, d_first_in_out, vec, up_vec = rest[6:10]
    outs = rest[10 : 10 + count]
    out_v, up_v, down_v, sems, stage, mixed, slope, acc = rest[10 + count :]
    me = me_ref[0]
    ff = up_v.shape[1]
    parts = ff // block
    out_copy = pltpu.make_async_copy(out_w, out_v, sems.at[0])
    out_copy.start()

    def lanes(j):
        return pl.ds(pl.multiple_of(j * block, block), block)

    def up_copy(j):
        return pltpu.make_async_copy(up_w.at[:, lanes(j)], up_v.at[:, lanes(j)], sems.at[1 + j])

    def down_copy(j):
        return pltpu.make_async_copy(down_w.at[lanes(j)], down_v.at[lanes(j)], sems.at[1 + parts + j])

    for j in range(parts):
        up_copy(j).start()
        down_copy(j).start()

    def place(part, s, lane, values):
        mixed[s * tokens : (s + 1) * tokens, lane : lane + values.shape[1]] = values

    receive_pairs(chunks, stage, place, me, count, seqs, tokens, pairs, size, 1)
    mixed_out[...] = mixed[...]
    out_copy.wait()
    first_in = resid[...] + dot(mixed[...], out_v[...]) + out_b[...]
    unit1, scale1 = normed(first_in)
    first = unit1 * gain1[...] + shift1[...]
    first_low = first.astype(BF16)
    first_low_out[...] = first_low
    acc[...] = first + down_b[...]

    def ahead(j, _):
        up_copy(j).wait()
        hidden = dot(first_low_out[...], up_v[:, lanes(j)]) + up_b[:, lanes(j)]
        square = hidden * hidden
        bend = jnp.tanh(GELU_A * (hidden + GELU_B * (square * hidden)))
        act = (0.5 * hidden * (1.0 + bend)).astype(BF16)
        act_out[:, lanes(j)] = act
        slope[:, lanes(j)] = 0.5 * (1.0 + bend) + 0.5 * hidden * (1.0 - bend * bend) * (
            GELU_A * (1.0 + 3.0 * GELU_B * square)
        )
        down_copy(j).wait()
        acc[...] += dot(act, down_v[lanes(j), :])
        return 0

    lax.fori_loop(0, parts, ahead, 0)
    unit2, scale2 = normed(acc[...])
    output[...] = (unit2 * gain2[...] + shift2[...]).astype(BF16)
    cot = cotangent[...].astype(F32)
    vec[0:1] = column_sum(cot * unit2)
    vec[1:2] = column_sum(cot)
    d_second_in = norm_back(cot, unit2, scale2, gain2[...])
    d_second = d_second_in.astype(BF16)
    d_second_out[...] = d_second
    vec[2:3] = column_sum(d_second)
    acc[...] = d_second_in

    def astern(j, _):
        d_act = dot_nt(d_second_out[...], down_v[lanes(j), :])
        d_hidden = (d_act * slope[:, lanes(j)]).astype(BF16)
        d_hidden_out[:, lanes(j)] = d_hidden
        up_vec[:, lanes(j)] = column_sum(d_hidden)
        acc[...] += dot_nt(d_hidden, up_v[:, lanes(j)])
        return 0

    lax.fori_loop(0, parts, astern, 0)
    d_first = acc[...]
    vec[3:4] = column_sum(d_first * unit1)
    vec[4:5] = column_sum(d_first)
    d_first_in = norm_back(d_first, unit1, scale1, gain1[...])
    d_first_in_out[...] = d_first_in
    d_attn = d_first_in.astype(BF16)
    d_attn_out[...] = d_attn
    vec[5:6] = column_sum(d_attn)
    vec[6:8] = jnp.zeros((2, vec.shape[1]), F32)
    d_mixed = dot_nt(d_attn, out_v[...]).astype(BF16)
    send_pairs((d_mixed,), stage, outs, me, count, seqs, tokens, pairs, size, pairs * size)


def up_down_body(first_low, d_hidden, act, d_second, up_out, down_out):
    up_out[...] = dot_tn(first_low[...], d_hidden[...]).astype(BF16)
    down_out[...] = dot_tn(act[...], d_second[...]).astype(BF16)


def up_down_grads(first_low, d_hidden, act, d_second, block=384):
    rows, width = first_low.shape
    ff = act.shape[1]
    return pl.pallas_call(
        up_down_body,
        grid=(ff // block,),
        in_specs=[
            pl.BlockSpec((rows, width), lambda j: (0, 0)),
            pl.BlockSpec((rows, block), lambda j: (0, j)),
            pl.BlockSpec((rows, block), lambda j: (0, j)),
            pl.BlockSpec((rows, width), lambda j: (0, 0)),
        ],
        out_specs=[
            pl.BlockSpec((width, block), lambda j: (0, j)),
            pl.BlockSpec((block, width), lambda j: (j, 0)),
        ],
        out_shape=[
            jax.ShapeDtypeStruct((width, ff), BF16),
            jax.ShapeDtypeStruct((ff, width), BF16),
        ],
        compiler_params=pltpu.CompilerParams(vmem_limit_bytes=32 * MIB),
        cost_estimate=pl.CostEstimate(
            flops=4 * rows * width * ff, bytes_accessed=4 * width * ff, transcendentals=0
        ),
        name="grad_up_down",
    )(first_low, d_hidden, act, d_second)


def outer_body(pairs, *refs):
    ins, out = refs[:-1], refs[-1]
    at = 0
    for left, right in pairs:
        grad = dot_tn(ins[left][...], ins[right][...])
        out[:, at : at + grad.shape[1]] = grad.astype(BF16)
        at += grad.shape[1]


def outer_grads(arrays, pairs, name):
    rows, height = arrays[pairs[0][0]].shape
    width = sum(arrays[right].shape[1] for _, right in pairs)
    (out,) = call(
        functools.partial(outer_body, pairs),
        [VMEM] * len(arrays),
        [((height, width), BF16)],
        limit=40,
        flops=2 * rows * height * width,
        moved=2 * height * width,
        name=name,
    )(*arrays)
    return out


def project_back_body(
    count, seqs, tokens, pairs, size, per_seg,
    me_ref, d_first_in, ptok, pre, query_w, key_w, value_w, join_w,
    *rest,
):
    chunks, rest = rest[:count], rest[count:]
    d_query, d_key, d_value, grad_out, d_perm, payload, vec = rest[:7]
    query_v, key_v, value_v, join_v, sems, stage = rest[7:]
    copies = []
    for k, (far, near) in enumerate(((query_w, query_v), (key_w, key_v), (value_w, value_v))):
        copies.append(pltpu.make_async_copy(far, near, sems.at[k]))
    for k in range(3):
        copies.append(pltpu.make_async_copy(join_w.at[k], join_v.at[k], sems.at[3 + k]))
    for copy in copies:
        copy.start()
    me = me_ref[0]
    targets = (d_query, d_key, d_value)

    def place(part, s, lane, values):
        targets[part][s * tokens : (s + 1) * tokens, lane : lane + values.shape[1]] = values

    receive_pairs(chunks, stage, place, me, count, seqs, tokens, pairs, size, 3)
    d_resid = d_first_in[...]
    for k, near in enumerate((query_v, key_v, value_v)):
        copies[k].wait()
        d_resid = d_resid + dot_nt(targets[k][...], near[...])
    grad = d_resid.astype(BF16)
    grad_out[...] = grad
    vec[0:1] = column_sum(d_query[...])
    vec[1:2] = column_sum(d_value[...])
    vec[2:3] = column_sum(grad)
    vec[3:8] = jnp.zeros((5, vec.shape[1]), F32)
    total = seqs * tokens
    half = vec.shape[1] // 2
    row = lax.broadcasted_iota(jnp.int32, (total + 16, total), 0)
    place_at = lax.broadcasted_iota(jnp.int32, (total + 16, total), 1)
    rows = seqs * SEGS
    step, rest_row = row // rows, row % rows
    seq = rest_row // SEGS
    tok = (rest_row % SEGS) * per_seg + step
    extra = row - total
    seq = jnp.where(extra >= 0, extra % seqs, seq)
    tok = jnp.where(extra >= 0, jnp.where(extra < seqs, -1, tokens), tok)
    known = extra < 2 * seqs
    d_char = jnp.zeros((total + 16, 2 * half), F32)
    for k in range(3):
        moved = tok + 1 - k
        pick = (place_at == seq * tokens + moved) & (moved >= 0) & (moved < tokens) & known
        shifted = dot(pick.astype(BF16), grad).astype(BF16)
        copies[3 + k].wait()
        d_char = d_char + dot_nt(shifted, join_v[k])
    for r in range(2):
        grads = d_char[0:total, r * half : (r + 1) * half].reshape(per_seg, rows, half)
        d_perm[r] = grads
        weighted = jnp.sum(grads * ptok[r], axis=0) * pre[0, r]
        payload[r] = jnp.concatenate(
            [column_sum(weighted[s * SEGS : (s + 1) * SEGS]) for s in range(seqs)], axis=0
        )
        payload[2 + r] = d_char[total : total + seqs, r * half : (r + 1) * half]
        payload[4 + r] = d_char[total + seqs : total + 2 * seqs, r * half : (r + 1) * half]


def chars_back_body(
    count, seqs, steps, per,
    me_ref, embedded, ids, gate_w, gate_b, cand_w, enter, ptok, pseg, gathered, gathered_back, d_perm,
    grad_w, grad_table, grad_b,
    upd, work, d_all, d_tok, gseg, gin,
):
    me = me_ref[0]
    rows = seqs * SEGS
    half = upd.shape[2]
    gates(embedded[...], gate_w, gate_b[...], cand_w, upd, work)

    def ahead(q, carry):
        h0, h1 = carry
        for j in range(per):
            at = pl.ds(pl.multiple_of((q * per + j) * rows, rows), rows)
            u = upd[0, at, :]
            gap = work[0, at, :] - h0
            work[0, at, :] = gap * (u * (1.0 - u))
            h0 = h0 + u * gap
            at = pl.ds(pl.multiple_of((steps - 1 - q * per - j) * rows, rows), rows)
            u = upd[1, at, :]
            gap = work[1, at, :] - h1
            work[1, at, :] = gap * (u * (1.0 - u))
            h1 = h1 + u * gap
        return h0, h1

    lax.fori_loop(0, steps // per, ahead, (enter[0], enter[1]))

    left = jnp.maximum(me - 1, 0)
    right = jnp.minimum(me + 1, count - 1)
    last = steps // per - 1
    d_tok[...] = d_perm[...]
    for r in range(2):
        from_left = jnp.where(me > 0, gathered_back[left, 4 + r], 0.0)
        from_right = jnp.where(me < count - 1, gathered_back[right, 2 + r], 0.0)
        for s in range(seqs):
            low, high = s * SEGS, s * SEGS + SEGS - 1
            d_tok[r, 0, low : low + 1] += from_left[s : s + 1]
            d_tok[r, last, high : high + 1] += from_right[s : s + 1]
        gseg[r] = jnp.sum(d_tok[r] * ptok[r], axis=0)

    def block_sum(j, r):
        total = gathered_back[j, r]
        near, far = gathered[j, 4 * r + 2], gathered[j, 4 * r]
        if r == 1:
            near, far = far, near
        if j > 0:
            total = total + near * gathered_back[j - 1, 4 + r]
        if j < count - 1:
            total = total + far * gathered_back[j + 1, 2 + r]
        return total

    g0 = jnp.zeros((seqs, half), F32)
    g1 = jnp.zeros((seqs, half), F32)
    for j in range(count):
        i = count - 1 - j
        g0 = jnp.where(i > me, gathered[i, 0] * g0 + block_sum(i, 0), g0)
        g1 = jnp.where(j < me, gathered[j, 4] * g1 + block_sum(j, 1), g1)
    for s in range(seqs):
        flow = g0[s : s + 1]
        for g in range(SEGS - 1, -1, -1):
            row = s * SEGS + g
            gin[0, row : row + 1] = flow
            flow = pseg[0, row : row + 1] * flow + gseg[0, row : row + 1]
        flow = g1[s : s + 1]
        for g in range(SEGS):
            row = s * SEGS + g
            gin[1, row : row + 1] = flow
            flow = pseg[1, row : row + 1] * flow + gseg[1, row : row + 1]

    def astern(q, carry):
        flow0, flow1 = carry
        for j in range(per):
            at = pl.ds(pl.multiple_of((steps - 1 - q * per - j) * rows, rows), rows)
            if j == 0:
                flow0 = flow0 + d_tok[0, steps // per - 1 - q]
            u = upd[0, at, :]
            d_all[at, 0:half] = (flow0 * work[0, at, :]).astype(BF16)
            d_cand = flow0 * u
            d_all[at, half : 2 * half] = d_cand.astype(BF16)
            flow0 = flow0 - d_cand
            at = pl.ds(pl.multiple_of((q * per + j) * rows, rows), rows)
            if j == 0:
                flow1 = flow1 + d_tok[1, q]
            u = upd[1, at, :]
            d_all[at, 2 * half : 3 * half] = (flow1 * work[1, at, :]).astype(BF16)
            d_cand = flow1 * u
            d_all[at, 3 * half : 4 * half] = d_cand.astype(BF16)
            flow1 = flow1 - d_cand
        return flow0, flow1

    lax.fori_loop(0, steps // per, astern, (gin[0], gin[1]))
    grad_w[...] = dot_tn(embedded[...], d_all[...]).astype(BF16)
    d_emb = jnp.zeros(embedded.shape, F32)
    for r in range(2):
        grad_b[:, r * half : (r + 1) * half] = column_sum(d_all[:, 2 * r * half : (2 * r + 1) * half])
        d_emb = d_emb + dot_nt(d_all[:, 2 * r * half : (2 * r + 1) * half], gate_w[r])
        d_emb = d_emb + dot_nt(d_all[:, (2 * r + 1) * half : (2 * r + 2) * half], cand_w[r])
    chars = embedded.shape[0]
    pick = (lax.broadcasted_iota(jnp.int32, (seqs * LANES, chars), 0) == ids[...]).astype(BF16)
    grad_table[...] = dot(pick, d_emb.astype(BF16))


def shift(array, by):
    count = lax.axis_size("seq")
    return lax.ppermute(array, "seq", [(i, (i + by) % count) for i in range(count)])


def swap(array, axis, bit):
    return lax.ppermute(array, axis, [(i, i ^ bit) for i in range(lax.axis_size(axis))])


def exchange(chunks):
    return [chunks[0]] + [shift(chunk, k) for k, chunk in enumerate(chunks) if k > 0]


def bits_of(count):
    return [1 << b for b in range(count.bit_length() - 1)]


def all_sum(vector):
    for axis in ("seq", "dp"):
        for bit in bits_of(lax.axis_size(axis)):
            vector = vector + swap(vector, axis, bit)
    return vector


def take(array, dim, index):
    return lax.dynamic_index_in_dim(array, index, dim, keepdims=False)


def scatter_sum(grad, high_first):
    count, groups = lax.axis_size("seq"), lax.axis_size("dp")
    places = bits_of(count)
    width = grad.shape[1]
    rows = grad.shape[0] // (count * groups)
    part = grad.reshape((groups,) + (2,) * len(places) + (rows, width))
    seq, dp = lax.axis_index("seq"), lax.axis_index("dp")
    order = [places[0]] + (places[:0:-1] if high_first else places[1:])
    left = list(reversed(places))
    parts = [part]
    for bit in order:
        dim = 1 + left.index(bit)
        left.remove(bit)
        mine = (seq // bit) % 2

        def half(which, parts=parts, dim=dim):
            total = take(parts[0], dim, which).astype(F32)
            for other in parts[1:]:
                total = total + take(other, dim, which).astype(F32)
            return total.astype(BF16)

        got = swap(half(1 - mine), "seq", bit)
        parts = [half(mine), got]
    total = parts[0].astype(F32) + parts[1].astype(F32)
    low = total.astype(BF16)
    out = take(total, 0, dp)
    for k in range(1, groups):
        out = out + swap(take(low, 0, dp ^ k), "dp", k).astype(F32)
    return out


def table_sum(partial, langs, sub):
    seqs, _, width = partial.shape
    seq = lax.axis_index("seq")
    mine = seq % 2
    halves = partial.astype(BF16).reshape(seqs, LANES, 2, width // 2)
    kept = take(halves, 2, mine).astype(F32)
    part = (kept + swap(take(halves, 2, 1 - mine), "seq", 1).astype(F32)).astype(BF16)
    for bit in bits_of(lax.axis_size("seq"))[1:]:
        part = (part.astype(F32) + swap(part, "seq", bit).astype(F32)).astype(BF16)
    every = lax.all_gather(part, "dp")
    other = swap(every, "seq", 1)
    whole = jnp.where(
        mine == 0,
        jnp.concatenate([every, other], axis=-1),
        jnp.concatenate([other, every], axis=-1),
    )
    whole = whole.reshape(-1, LANES * width)
    pick = (lax.broadcasted_iota(jnp.int32, (GROUPS, whole.shape[0]), 0) == langs[None, :]).astype(
        BF16
    )
    spread_out = dot(pick, whole).reshape(GROUPS, LANES, width)
    return spread_out[:, :sub].reshape(GROUPS * sub, width)


def shards(
    inputs, char_ids, lang_ids, lengths, char_table, gate_weight, gate_bias, cand_weight,
    join_weight, join_bias, query_weight, query_bias, key_weight, value_weight, value_bias,
    out_weight, out_bias, norm1_gain, norm1_bias, up_weight, up_bias, down_weight, down_bias,
    norm2_gain, norm2_bias, cotangent,
):
    seqs, tokens, width = inputs.shape
    chars = char_ids.shape[1]
    per = chars // tokens
    steps = chars // SEGS
    per_seg = steps // per
    vocab, embed = char_table.shape
    sub = vocab // GROUPS
    half = width // 2
    size = width // HEADS
    ff = up_weight.shape[1]
    count = lax.axis_size("seq")
    pairs = -(-seqs * HEADS // count)
    while HEADS % pairs:
        pairs += 1
    full = count * tokens
    total = seqs * tokens
    rows = seqs * SEGS
    wide = pairs * size
    me = lax.axis_index("seq").astype(jnp.int32).reshape(1)
    flat = inputs.reshape(total, width)
    cot = cotangent.reshape(total, width)
    line = lambda vector: vector.reshape(1, -1)

    ids = char_ids.reshape(seqs, SEGS, steps) + LANES * lax.broadcasted_iota(
        jnp.int32, (seqs, 1, 1), 0
    )
    ids = ids.transpose(2, 0, 1).reshape(-1)
    langs = lax.all_gather(lang_ids, "dp", tiled=True)

    embedded, htok, ptok, pre, pseg, payload = call(
        functools.partial(chars_forward_body, seqs, steps, per, sub),
        [SMEM] + [VMEM] * 5,
        [
            ((seqs * chars, embed), BF16),
            ((2, per_seg, rows, half), F32),
            ((2, per_seg, rows, half), F32),
            ((2, 2, rows, half), F32),
            ((2, rows, half), F32),
            ((8, seqs, half), F32),
        ],
        [
            pltpu.VMEM((2, seqs * chars, half), F32),
            pltpu.VMEM((2, seqs * chars, half), F32),
            pltpu.VMEM((2, rows, half), F32),
            pltpu.VMEM((-(-vocab // LANES) * LANES, embed), BF16),
        ],
        flops=8 * seqs * chars * embed * half,
        name="chars_forward",
    )(lang_ids, ids.reshape(-1, 1), char_table, gate_weight, gate_bias, cand_weight)
    gathered = lax.all_gather(payload, "seq")

    taps, resid, resid_low, enter, *sent = call(
        functools.partial(join_query_body, count, seqs, tokens, pairs),
        [SMEM] + [VMEM] * 8 + [HBM] * 4,
        [
            ((3, total, width), BF16),
            ((total, width), F32),
            ((total, width), BF16),
            ((2, rows, half), F32),
        ]
        + [((tokens, 3 * wide), BF16)] * count,
        [
            pltpu.VMEM((3, width, width), BF16),
            pltpu.VMEM((width, width), BF16),
            pltpu.VMEM((width, width), BF16),
            pltpu.VMEM((width, width), BF16),
            pltpu.SemaphoreType.DMA((6,)),
            pltpu.VMEM((count, tokens, 3 * wide), BF16),
        ],
        flops=12 * total * width * width,
        moved=12 * width * width,
        name="join_query",
    )(
        me, gathered, htok, ptok, pre, flat, line(join_bias), line(query_bias), line(value_bias),
        join_weight, query_weight, key_weight, value_weight,
    )
    heads = exchange(sent)

    block = min(256, full)
    *sent, lse = call(
        functools.partial(attend_body, count, seqs, tokens, pairs, size, block),
        [SMEM, SMEM] + [VMEM] * count,
        [((tokens, wide), BF16)] * count + [((pairs, 1, full), F32)],
        [pltpu.VMEM((pairs, full, size), BF16)] * 3
        + [
            pltpu.VMEM((pairs, size, full), BF16),
            pltpu.VMEM((wide, full), F32),
            pltpu.VMEM((full, wide), BF16),
        ],
        flops=4 * pairs * full * full * size,
        name="attend",
    )(me, lengths, *heads)
    mixed_chunks = exchange(sent)

    ff_block = 512
    (
        output, mixed, first_low, act, d_second, d_hidden, d_attn, d_first_in, vec1, up_vec, *sent
    ) = call(
        functools.partial(feed_body, count, seqs, tokens, pairs, size, ff_block),
        [SMEM] + [VMEM] * 9 + [HBM] * 3 + [VMEM] * count,
        [
            ((total, width), BF16),
            ((total, width), BF16),
            ((total, width), BF16),
            ((total, ff), BF16),
            ((total, width), BF16),
            ((total, ff), BF16),
            ((total, width), BF16),
            ((total, width), F32),
            ((8, width), F32),
            ((1, ff), F32),
        ]
        + [((tokens, wide), BF16)] * count,
        [
            pltpu.VMEM((width, width), BF16),
            pltpu.VMEM((width, ff), BF16),
            pltpu.VMEM((ff, width), BF16),
            pltpu.SemaphoreType.DMA((1 + 2 * (ff // ff_block),)),
            pltpu.VMEM((count, tokens, wide), BF16),
            pltpu.VMEM((total, width), BF16),
            pltpu.VMEM((total, ff), F32),
            pltpu.VMEM((total, width), F32),
        ],
        flops=8 * total * width * ff + 4 * total * width * width,
        moved=4 * width * ff,
        name="feed_forward",
    )(
        me, resid, cot, line(out_bias), line(norm1_gain), line(norm1_bias), line(up_bias),
        line(down_bias), line(norm2_gain), line(norm2_bias), out_weight, up_weight, down_weight,
        *mixed_chunks,
    )
    d_mixed_chunks = exchange(sent)

    grad_up, grad_down = up_down_grads(first_low, d_hidden, act, d_second)
    grad_out = outer_grads([mixed, d_attn], [(0, 1)], "grad_out")
    grad_up = scatter_sum(grad_up, False)
    grad_down = scatter_sum(grad_down, True)
    grad_out = scatter_sum(grad_out, False)
    early = all_sum(jnp.concatenate([vec1[:6].reshape(-1), up_vec.reshape(-1)]))

    sent = call(
        functools.partial(attend_back_body, count, seqs, tokens, pairs, size, block),
        [SMEM, SMEM] + [VMEM] * (1 + 2 * count),
        [((tokens, 3 * wide), BF16)] * count,
        [pltpu.VMEM((pairs, full, size), BF16)] * 3
        + [
            pltpu.VMEM((pairs, size, full), BF16),
            pltpu.VMEM((pairs, full, size), BF16),
            pltpu.VMEM((wide, full), F32),
            pltpu.VMEM((pairs, full, size), F32),
            pltpu.VMEM((pairs, full, size), F32),
            pltpu.VMEM((full, 3 * wide), BF16),
        ],
        flops=10 * pairs * full * full * size,
        name="attend_back",
    )(me, lengths, lse, *heads, *d_mixed_chunks)
    d_chunks = exchange(sent)

    d_query, d_key, d_value, input_grad, d_perm, payload_back, vec2 = call(
        functools.partial(project_back_body, count, seqs, tokens, pairs, size, per_seg),
        [SMEM] + [VMEM] * 3 + [HBM] * 4 + [VMEM] * count,
        [
            ((total, width), BF16),
            ((total, width), BF16),
            ((total, width), BF16),
            ((total, width), BF16),
            ((2, per_seg, rows, half), F32),
            ((6, seqs, half), F32),
            ((8, width), F32),
        ],
        [
            pltpu.VMEM((width, width), BF16),
            pltpu.VMEM((width, width), BF16),
            pltpu.VMEM((width, width), BF16),
            pltpu.VMEM((3, width, width), BF16),
            pltpu.SemaphoreType.DMA((6,)),
            pltpu.VMEM((count, tokens, 3 * wide), BF16),
        ],
        flops=12 * total * width * width,
        moved=12 * width * width,
        name="project_back",
    )(me, d_first_in, ptok, pre, query_weight, key_weight, value_weight, join_weight, *d_chunks)
    gathered_back = lax.all_gather(payload_back, "seq")

    grad_qkv = outer_grads(
        [resid_low, d_query, d_key, d_value], [(0, 1), (0, 2), (0, 3)], "grad_query"
    )
    grad_join = outer_grads(
        [taps[0], taps[1], taps[2], input_grad], [(0, 3), (1, 3), (2, 3)], "grad_join"
    )
    grad_qkv = scatter_sum(grad_qkv, False)
    grad_join = scatter_sum(grad_join, True)

    grad_chars, grad_table, gate_vec = call(
        functools.partial(chars_back_body, count, seqs, steps, per),
        [SMEM] + [VMEM] * 11,
        [
            ((embed, 4 * half), BF16),
            ((seqs * LANES, embed), F32),
            ((1, 2 * half), F32),
        ],
        [
            pltpu.VMEM((2, seqs * chars, half), F32),
            pltpu.VMEM((2, seqs * chars, half), F32),
            pltpu.VMEM((seqs * chars, 4 * half), BF16),
            pltpu.VMEM((2, per_seg, rows, half), F32),
            pltpu.VMEM((2, rows, half), F32),
            pltpu.VMEM((2, rows, half), F32),
        ],
        flops=24 * seqs * chars * embed * half,
        name="chars_back",
    )(
        me, embedded, ids.reshape(1, -1), gate_weight, gate_bias, cand_weight, enter, ptok, pseg,
        gathered, gathered_back, d_perm,
    )
    grad_chars = scatter_sum(grad_chars, False)
    grad_table = table_sum(grad_table.reshape(seqs, LANES, embed), langs, sub)
    late = all_sum(jnp.concatenate([vec2[:3].reshape(-1), gate_vec.reshape(-1)]))

    def columns(array, k, wide):
        return array[:, k * wide : (k + 1) * wide]

    early_row = lambda k: early[k * width : (k + 1) * width]
    late_row = lambda k: late[k * width : (k + 1) * width]
    return (
        output.reshape(inputs.shape),
        input_grad.reshape(inputs.shape),
        grad_table,
        jnp.stack([columns(grad_chars, 0, half), columns(grad_chars, 2, half)]),
        late[3 * width :].reshape(2, half),
        jnp.stack([columns(grad_chars, 1, half), columns(grad_chars, 3, half)]),
        jnp.stack([columns(grad_join, k, width) for k in range(3)]),
        late_row(2),
        columns(grad_qkv, 0, width),
        late_row(0),
        columns(grad_qkv, 1, width),
        columns(grad_qkv, 2, width),
        late_row(1),
        grad_out,
        early_row(5),
        early_row(3),
        early_row(4),
        grad_up,
        early[6 * width :],
        grad_down,
        early_row(2),
        early_row(0),
        early_row(1),
    )


def solution(mesh):
    spread_rows = P("dp", "seq", None)
    placed = (
        (spread_rows, P("dp", "seq"), P("dp"), P("dp")) + (P(),) * 21 + (spread_rows,)
    )
    owned = P(("dp", "seq"), None)
    owned_mid = P(None, ("dp", "seq"), None)
    return jax.shard_map(
        shards,
        mesh=mesh,
        in_specs=placed,
        out_specs=(
            spread_rows, spread_rows, P(), owned_mid, P(), owned_mid, owned_mid, P(),
            owned, P(), owned, owned, P(), owned, P(), P(), P(), owned, P(), owned, P(), P(), P(),
        ),
        check_vma=False,
    )
```

```python
import functools

import jax
import jax.numpy as jnp
from jax import lax
from jax.experimental import pallas as pl
from jax.experimental.pallas import tpu as pltpu
from jax.sharding import PartitionSpec as P

HEADS = 12
GROUPS = 8
SEGS = 8
LANES = 128
NORM_EPS = 1e-05
MASKED = -1000000000.0
MIB = 1 << 20
F32 = jnp.float32
BF16 = jnp.bfloat16


def dot(left, right):
    return jnp.dot(left, right, preferred_element_type=F32)


def dot_nt(left, right):
    return lax.dot_general(left, right, (((1,), (1,)), ((), ())), preferred_element_type=F32)


def dot_tn(left, right):
    return lax.dot_general(left, right, (((0,), (0,)), ((), ())), preferred_element_type=F32)


def column_sum(values):
    return jnp.sum(values.astype(F32), axis=0, keepdims=True)


VMEM = pl.BlockSpec(memory_space=pltpu.VMEM)
SMEM = pl.BlockSpec(memory_space=pltpu.SMEM)
HBM = pl.BlockSpec(memory_space=pltpu.HBM)


def call(body, ins, outs, scratch=(), limit=60, name=None):
    return pl.pallas_call(
        body,
        in_specs=ins,
        out_specs=[HBM if len(out) > 2 else VMEM for out in outs],
        out_shape=[jax.ShapeDtypeStruct(out[0], out[1]) for out in outs],
        scratch_shapes=list(scratch),
        compiler_params=pltpu.CompilerParams(vmem_limit_bytes=limit * MIB),
        cost_estimate=pl.CostEstimate(flops=1, bytes_accessed=1, transcendentals=0),
        name=name,
    )


def pull(pairs, sems):
    copies = [pltpu.make_async_copy(far, near, sems.at[k]) for k, (far, near) in enumerate(pairs)]
    for copy in copies:
        copy.start()
    return copies


def arrivals(chunks, stage, me, count):
    return [(chunk, stage.at[lax.rem(me + count - k, count)]) for k, chunk in enumerate(chunks)]


def summaries(groups, gathered, me):
    pairs = []
    for j, group in enumerate(groups):
        for i in range(2):
            pairs.append((group.at[i], gathered.at[jnp.bitwise_xor(me, 2 * j + i)]))
    return pairs


def gates(embedded, gate_w, gate_b, cand_w, upd, cand):
    for r in range(2):
        upd[r] = jax.nn.sigmoid(dot(embedded, gate_w[r]) + gate_b[r : r + 1])
        cand[r] = dot(embedded, cand_w[r])


def one_hot_rows(ids, seqs, steps):
    rows = []
    for s in range(seqs):
        for g in range(SEGS):
            rows.append(ids[s : s + 1, g * steps : (g + 1) * steps] + s * LANES)
    held = jnp.concatenate(rows, axis=0)
    place = lax.broadcasted_iota(jnp.int32, (seqs * SEGS, seqs * LANES), 1)
    return jnp.concatenate(
        [(place == held[:, t : t + 1]).astype(F32).astype(BF16) for t in range(steps)], axis=0
    )


def chars_forward_body(
    seqs, steps, per, sub,
    lang, ids, gate_b, table, gate_w_far, cand_w_far,
    embedded_out, htok, ptok, pre, pseg, payload,
    upd, cand, hseg, padded_table, gate_w, cand_w, sems,
):
    rows = seqs * SEGS
    vocab = table.shape[0]
    wide = padded_table.shape[0]
    copies = pull(
        [(table, padded_table.at[0:vocab]), (gate_w_far, gate_w), (cand_w_far, cand_w)], sems
    )
    padded_table[vocab:wide] = jnp.zeros((wide - vocab, padded_table.shape[1]), BF16)
    copies[0].wait()
    local = lax.broadcasted_iota(jnp.int32, (LANES, wide), 0)
    place = lax.broadcasted_iota(jnp.int32, (LANES, wide), 1)
    mine = []
    for s in range(seqs):
        pick = (place == lang[s] * sub + local) & (local < sub)
        mine.append(dot(pick.astype(BF16), padded_table[...]).astype(BF16))
    own_table = jnp.concatenate(mine, axis=0)
    embedded = dot(one_hot_rows(ids, seqs, steps), own_table).astype(BF16)
    embedded_out[...] = embedded
    copies[1].wait()
    copies[2].wait()
    gates(embedded, gate_w, gate_b[...], cand_w, upd, cand)

    def token(q, carry):
        h0, p0, h1, p1 = carry
        for j in range(per):
            at = pl.ds(pl.multiple_of((q * per + j) * rows, rows), rows)
            u = upd[0, at, :]
            h0 = h0 + u * (cand[0, at, :] - h0)
            p0 = p0 * (1.0 - u)
            at = pl.ds(pl.multiple_of((steps - 1 - q * per - j) * rows, rows), rows)
            u = upd[1, at, :]
            h1 = h1 + u * (cand[1, at, :] - h1)
            p1 = p1 * (1.0 - u)
        htok[0, q] = h0
        ptok[0, q] = p0
        back = steps // per - 1 - q
        htok[1, back] = h1
        ptok[1, back] = p1
        return h0, p0, h1, p1

    zero = jnp.zeros((rows, upd.shape[2]), F32)
    h0, p0, h1, p1 = lax.fori_loop(0, steps // per, token, (zero, zero + 1.0, zero, zero + 1.0))
    pseg[0], pseg[1], hseg[0], hseg[1] = p0, p1, h0, h1
    last = steps // per - 1
    for s in range(seqs):
        for r in range(2):
            total_a = jnp.ones((1, upd.shape[2]), F32)
            total_b = jnp.zeros((1, upd.shape[2]), F32)
            order = range(SEGS) if r == 0 else range(SEGS - 1, -1, -1)
            for g in order:
                row = s * SEGS + g
                pre[0, r, row : row + 1] = total_a
                pre[1, r, row : row + 1] = total_b
                p_row = pseg[r, row : row + 1]
                total_b = p_row * total_b + hseg[r, row : row + 1]
                total_a = p_row * total_a
            edge = s * SEGS if r == 0 else s * SEGS + SEGS - 1
            q = 0 if r == 0 else last
            near_a, near_b = ptok[r, q, edge : edge + 1], htok[r, q, edge : edge + 1]
            for k, value in enumerate((total_a, total_b, near_a, near_b)):
                row = (4 * r + k) * seqs + s
                payload[row : row + 1] = value


def spread(values, seqs):
    wide = values.shape[1]
    return jnp.concatenate(
        [jnp.broadcast_to(values[s : s + 1], (SEGS, wide)) for s in range(seqs)], axis=0
    )


def token_row(token, tokens, per_seg, seqs):
    s = token // tokens
    t = token % tokens
    return (t % per_seg) * (seqs * SEGS) + s * SEGS + t // per_seg


def join_query_body(
    count, seqs, tokens, pairs,
    me_ref, htok, ptok, pre, inputs, join_b, query_b, value_b,
    join_w, query_w, key_w, value_w,
    *rest,
):
    groups, rest = rest[: count // 2], rest[count // 2 :]
    resid_out, enter, left_out = rest[:3]
    chunks = rest[3 : 3 + count]
    join_v, query_v, key_v, value_v, held, sems, stage, lefts, left_sems = rest[3 + count :]
    me = me_ref[0]
    width = join_v.shape[1]
    outgoing = []

    def emit(k, values):
        lanes = slice(k * width, (k + 1) * width)
        lefts[:, lanes] = values
        copy = pltpu.make_async_copy(lefts.at[:, lanes], left_out.at[:, lanes], left_sems.at[k])
        copy.start()
        outgoing.append(copy)

    wanted = [(join_w.at[k], join_v.at[k]) for k in range(3)]
    wanted += [(query_w, query_v), (key_w, key_v), (value_w, value_v)]
    copies = pull(summaries(groups, held, me) + wanted, sems)
    for copy in copies[:count]:
        copy.wait()
    copies = copies[count:]
    half = htok.shape[3]

    def gathered(j, k):
        return held[j, k * seqs : (k + 1) * seqs]

    per_seg = htok.shape[1]
    total = seqs * tokens
    x0 = jnp.zeros((seqs, half), F32)
    x1 = jnp.zeros((seqs, half), F32)
    for j in range(count):
        x0 = jnp.where(j < me, gathered(j, 0) * x0 + gathered(j, 1), x0)
        i = count - 1 - j
        x1 = jnp.where(i > me, gathered(i, 4) * x1 + gathered(i, 5), x1)
    carry0 = pre[0, 0] * spread(x0, seqs) + pre[1, 0]
    carry1 = pre[0, 1] * spread(x1, seqs) + pre[1, 1]
    enter[0] = carry0
    enter[1] = carry1
    forward = htok[0] + ptok[0] * carry0[None]
    backward = htok[1] + ptok[1] * carry1[None]
    rows = seqs * SEGS
    last = per_seg - 1
    f_last = jnp.concatenate(
        [forward[last, s * SEGS + SEGS - 1 : s * SEGS + SEGS] for s in range(seqs)], axis=0
    )
    b_first = jnp.concatenate(
        [backward[0, s * SEGS : s * SEGS + 1] for s in range(seqs)], axis=0
    )
    left = jnp.maximum(me - 1, 0)
    right = jnp.minimum(me + 1, count - 1)
    left_b = gathered(left, 6) * b_first + gathered(left, 7)
    right_f = gathered(right, 2) * f_last + gathered(right, 3)
    left_row = jnp.where(me > 0, jnp.concatenate([x0, left_b], axis=1), 0.0)
    right_row = jnp.where(me < count - 1, jnp.concatenate([right_f, x1], axis=1), 0.0)
    rim = jnp.concatenate(
        [left_row, right_row, jnp.zeros((16 - 2 * seqs, 2 * half), F32)], axis=0
    ).astype(BF16)
    tokens_perm = jnp.concatenate(
        [forward.reshape(total, half), backward.reshape(total, half)], axis=1
    ).astype(BF16)
    source = jnp.concatenate([tokens_perm, rim], axis=0)
    token = lax.broadcasted_iota(jnp.int32, (total, total + 16), 0)
    place = lax.broadcasted_iota(jnp.int32, (total, total + 16), 1)
    joining = jnp.broadcast_to(join_b[...][None], (total, 2 * half))
    for k in range(3):
        moved = token + (k - 1)
        want = token_row(moved, tokens, per_seg, seqs)
        if k == 0:
            want = jnp.where(token % tokens == 0, total + token // tokens, want)
        if k == 2:
            want = jnp.where(token % tokens == tokens - 1, total + seqs + token // tokens, want)
        tap = dot((place == want).astype(BF16), source).astype(BF16)
        emit(1 + k, tap)
        copies[k].wait()
        joining = joining + dot(tap, join_v[k])
    resid = inputs[...].astype(F32) + joining
    resid_out[...] = resid
    low = resid.astype(BF16)
    emit(0, low)
    size = 2 * half // HEADS
    wide = pairs * size
    copies[3].wait()
    query = (dot(low, query_v[...]) + query_b[...][None]).astype(BF16)
    copies[4].wait()
    key = dot(low, key_v[...]).astype(BF16)
    copies[5].wait()
    value = (dot(low, value_v[...]) + value_b[...][None]).astype(BF16)
    send_pairs((query, key, value), stage, chunks, me, count, seqs, tokens, pairs, size, wide)
    for copy in outgoing:
        copy.wait()


def send_pairs(arrays, stage, chunks, me, count, seqs, tokens, pairs, size, wide):
    for d in range(count):
        for a, array in enumerate(arrays):
            first = d * pairs
            if first >= seqs * HEADS:
                stage[d, :, a * wide : (a + 1) * wide] = jnp.zeros((tokens, wide), BF16)
                continue
            s, head = first // HEADS, first % HEADS
            stage[d, :, a * wide : (a + 1) * wide] = array[
                s * tokens : (s + 1) * tokens, head * size : head * size + wide
            ]
    for k in range(count):
        chunks[k][...] = stage[lax.rem(me + k, count)]


def receive_pairs(stage, place, count, seqs, pairs, size, parts):
    wide = pairs * size
    for d in range(count):
        first = d * pairs
        if first >= seqs * HEADS:
            continue
        s, head = first // HEADS, first % HEADS
        for a in range(parts):
            place(a, s, head * size, stage[d, :, a * wide : (a + 1) * wide])


def load_heads(stage, count, tokens, pairs, size, part, target, scale=None):
    wide = pairs * size
    for d in range(count):
        for h in range(pairs):
            lane = part * wide + h * size
            block = stage[d, :, lane : lane + size]
            target[h, d * tokens : (d + 1) * tokens, :] = block if scale is None else block * scale


def pair_length(lengths, me, pairs, h, seqs):
    return lengths[jnp.minimum((me * pairs + h) // HEADS, seqs - 1)]


def transposed(values):
    return jnp.transpose(values.astype(F32))


def attend_body(count, seqs, tokens, pairs, size, block, me_ref, lengths, *rest):
    chunks, rest = rest[:count], rest[count:]
    outs, lse = rest[:count], rest[count]
    q, k, v, vt, mixed_t, mixed, held, sems = rest[count + 1 :]
    me = me_ref[0]
    full = count * tokens
    for copy in pull(arrivals(chunks, held, me, count), sems):
        copy.wait()
    load_heads(held, count, tokens, pairs, size, 0, q, jnp.asarray(0.125, BF16))
    load_heads(held, count, tokens, pairs, size, 1, k)
    load_heads(held, count, tokens, pairs, size, 2, v)
    for h in range(pairs):
        vt[h] = transposed(v[h]).astype(BF16)
        valid = pair_length(lengths, me, pairs, h, seqs)

        def rows(i, _, h=h, valid=valid):
            at = pl.ds(pl.multiple_of(i * block, block), block)
            scores = dot_nt(k[h], q[h, at, :])
            key_at = lax.broadcasted_iota(jnp.int32, (full, block), 0)
            scores = jnp.where(key_at < valid, scores, MASKED)
            top = jnp.max(scores, axis=0, keepdims=True)
            probs = jnp.exp(scores - top)
            total = jnp.sum(probs, axis=0, keepdims=True)
            lse[h, :, at] = top + jnp.log(total)
            mixed_t[h * size : (h + 1) * size, at] = dot(vt[h], probs.astype(BF16)) / total
            return 0

        lax.fori_loop(0, full // block, rows, 0)
    mixed[...] = transposed(mixed_t[...]).astype(BF16)
    for j in range(count):
        at = pl.ds(pl.multiple_of(lax.rem(me + j, count) * tokens, tokens), tokens)
        outs[j][...] = mixed[at, :]


def attend_back_body(count, seqs, tokens, pairs, size, block, me_ref, lengths, lse, *rest):
    chunks, d_chunks, rest = rest[:count], rest[count : 2 * count], rest[2 * count :]
    outs = rest[:count]
    q, k, v, kt, d_o, dq_t, dk, dv, stage, held, d_held, sems = rest[count:]
    me = me_ref[0]
    full = count * tokens
    wide = pairs * size
    wanted = arrivals(chunks, held, me, count) + arrivals(d_chunks, d_held, me, count)
    for copy in pull(wanted, sems):
        copy.wait()
    load_heads(held, count, tokens, pairs, size, 0, q, jnp.asarray(0.125, BF16))
    load_heads(held, count, tokens, pairs, size, 1, k)
    load_heads(held, count, tokens, pairs, size, 2, v)
    load_heads(d_held, count, tokens, pairs, size, 0, d_o)
    for h in range(pairs):
        kt[h] = transposed(k[h]).astype(BF16)
        valid = pair_length(lengths, me, pairs, h, seqs)
        dk[h] = jnp.zeros_like(dk[h])
        dv[h] = jnp.zeros_like(dv[h])

        def rows(i, _, h=h, valid=valid):
            at = pl.ds(pl.multiple_of(i * block, block), block)
            scores = dot_nt(k[h], q[h, at, :])
            key_at = lax.broadcasted_iota(jnp.int32, (full, block), 0)
            scores = jnp.where(key_at < valid, scores, MASKED)
            probs = jnp.exp(scores - lse[h, :, at])
            d_probs = dot_nt(v[h], d_o[h, at, :])
            row_dot = jnp.sum(d_probs * probs, axis=0, keepdims=True)
            d_scores = (probs * (d_probs - row_dot)).astype(BF16)
            dv[h] += dot(probs.astype(BF16), d_o[h, at, :])
            dk[h] += dot(d_scores, q[h, at, :])
            dq_t[h * size : (h + 1) * size, at] = dot(kt[h], d_scores) * 0.125
            return 0

        lax.fori_loop(0, full // block, rows, 0)
        for part, grad in ((1, dk), (2, dv)):
            lane = part * wide + h * size
            stage[:, lane : lane + size] = grad[h].astype(BF16)
    stage[:, 0:wide] = transposed(dq_t[...]).astype(BF16)
    for j in range(count):
        at = pl.ds(pl.multiple_of(lax.rem(me + j, count) * tokens, tokens), tokens)
        outs[j][...] = stage[at, :]


def normed(values):
    center = values - jnp.mean(values, axis=-1, keepdims=True)
    scale = lax.rsqrt(jnp.mean(center * center, axis=-1, keepdims=True) + NORM_EPS)
    return center * scale, scale


def norm_back(cotangent, unit, scale, gain):
    d_unit = cotangent * gain
    mean = jnp.mean(d_unit, axis=-1, keepdims=True)
    lean = jnp.mean(d_unit * unit, axis=-1, keepdims=True)
    return scale * (d_unit - mean - unit * lean)


GELU_A = 0.7978845608028654
GELU_B = 0.044715


def feed_body(
    count, seqs, tokens, pairs, size, block,
    me_ref, out_b, gain1, shift1, up_b, down_b, gain2, shift2,
    resid_far, cotangent_far, out_w, up_w, down_w,
    *rest,
):
    chunks, rest = rest[:count], rest[count:]
    output, d_first_in_out, vec, up_vec, left_out, keep_out, send_out = rest[:7]
    outs = rest[7 : 7 + count]
    (
        out_v, up_v, down_v, sems, first_sems, stage, slope, acc, resid, cotangent,
        lefts, d_hidden_v, d_second_v, d_attn_v, out_sems,
    ) = rest[7 + count :]
    me, core = me_ref[0], me_ref[1]
    width = out_v.shape[0]
    ff = up_v.shape[1]
    parts = ff // block
    mixed = lefts.at[:, ff + width : ff + 2 * width]
    first_low_v = lefts.at[:, ff : ff + width]
    outgoing = []

    def emit(source, target):
        copy = pltpu.make_async_copy(source, target, out_sems.at[len(outgoing)])
        copy.start()
        outgoing.append(copy)

    def emit_halves(source, lane, wide):
        for out, part in ((keep_out, core), (send_out, 1 - core)):
            at = pl.ds(pl.multiple_of(part * wide, LANES), wide)
            emit(source.at[:, at], out.at[:, lane : lane + wide])

    wanted = arrivals(chunks, stage, me, count)
    wanted += [(out_w, out_v), (resid_far, resid), (cotangent_far, cotangent)]
    first_copies = pull(wanted, first_sems)

    def lanes(j):
        return pl.ds(pl.multiple_of(j * block, block), block)

    def up_copy(j):
        return pltpu.make_async_copy(up_w.at[:, lanes(j)], up_v.at[:, lanes(j)], sems.at[j])

    def down_copy(j):
        return pltpu.make_async_copy(down_w.at[lanes(j)], down_v.at[lanes(j)], sems.at[parts + j])

    for j in range(parts):
        up_copy(j).start()
        down_copy(j).start()

    def place(part, s, lane, values):
        mixed[s * tokens : (s + 1) * tokens, lane : lane + values.shape[1]] = values

    for copy in first_copies:
        copy.wait()
    receive_pairs(stage, place, count, seqs, pairs, size, 1)
    first_in = resid[...] + dot(mixed[...], out_v[...]) + out_b[...][None]
    unit1, scale1 = normed(first_in)
    first = unit1 * gain1[...][None] + shift1[...][None]
    first_low = first.astype(BF16)
    first_low_v[...] = first_low
    emit(lefts.at[:, ff : ff + 2 * width], left_out.at[:, ff : ff + 2 * width])
    acc[...] = first + down_b[...][None]

    def ahead(j, _):
        up_copy(j).wait()
        hidden = dot(first_low_v[...], up_v[:, lanes(j)]) + up_b[lanes(j)][None]
        square = hidden * hidden
        bend = jnp.tanh(GELU_A * (hidden + GELU_B * (square * hidden)))
        act = (0.5 * hidden * (1.0 + bend)).astype(BF16)
        lefts[:, lanes(j)] = act
        slope[:, lanes(j)] = 0.5 * (1.0 + bend) + 0.5 * hidden * (1.0 - bend * bend) * (
            GELU_A * (1.0 + 3.0 * GELU_B * square)
        )
        down_copy(j).wait()
        acc[...] += dot(act, down_v[lanes(j), :])
        return 0

    lax.fori_loop(0, parts, ahead, 0)
    emit(lefts.at[:, 0:ff], left_out.at[:, 0:ff])
    unit2, scale2 = normed(acc[...])
    output[...] = (unit2 * gain2[...][None] + shift2[...][None]).astype(BF16)
    cot = cotangent[...].astype(F32)
    vec[0:1] = column_sum(cot * unit2)
    vec[1:2] = column_sum(cot)
    d_second_in = norm_back(cot, unit2, scale2, gain2[...][None])
    d_second = d_second_in.astype(BF16)
    d_second_v[...] = d_second
    emit_halves(d_second_v, ff // 2, width // 2)
    vec[2:3] = column_sum(d_second)
    acc[...] = d_second_in

    def astern(j, _):
        d_act = dot_nt(d_second_v[...], down_v[lanes(j), :])
        d_hidden = (d_act * slope[:, lanes(j)]).astype(BF16)
        d_hidden_v[:, lanes(j)] = d_hidden
        up_vec[:, lanes(j)] = column_sum(d_hidden)
        acc[...] += dot_nt(d_hidden, up_v[:, lanes(j)])
        return 0

    lax.fori_loop(0, parts, astern, 0)
    emit_halves(d_hidden_v, 0, ff // 2)
    d_first = acc[...]
    vec[3:4] = column_sum(d_first * unit1)
    vec[4:5] = column_sum(d_first)
    d_first_in = norm_back(d_first, unit1, scale1, gain1[...][None])
    d_first_in_out[...] = d_first_in
    d_attn = d_first_in.astype(BF16)
    d_attn_v[...] = d_attn
    emit_halves(d_attn_v, ff // 2 + width // 2, width // 2)
    vec[5:6] = column_sum(d_attn)
    vec[6:8] = jnp.zeros((2, vec.shape[1]), F32)
    d_mixed = dot_nt(d_attn, out_v[...]).astype(BF16)
    send_pairs((d_mixed,), stage, outs, me, count, seqs, tokens, pairs, size, pairs * size)
    for copy in outgoing:
        copy.wait()


def fetch_columns(arrays, lanes, sems, at):
    copies = []
    for far, near in arrays:
        copy = pltpu.make_async_copy(far.at[:, lanes], near.at[:, lanes], sems.at[at + len(copies)])
        copy.start()
        copies.append(copy)
    return copies


def feed_grads_body(ff, left, left_got, right, right_got, out, lefts, lefts_got, rights, rights_got, res, sems):
    half = out.shape[-1]
    width = 2 * half
    blocks = out.shape[0]
    step = ff // blocks
    lane = lambda far, near, at, size: (far.at[:, at : at + size], near.at[:, at : at + size])
    first = ff // 2
    waves = [
        lane(right, rights, first, half), lane(right_got, rights_got, first, half),
    ]
    for j in range(blocks):
        waves += [lane(left, lefts, j * step, step), lane(left_got, lefts_got, j * step, step)]
    for at, size in ((ff, width),):
        waves += [lane(left, lefts, at, size), lane(left_got, lefts_got, at, size)]
    waves += [lane(right, rights, 0, first), lane(right_got, rights_got, 0, first)]
    waves += [lane(left, lefts, ff + width, width), lane(left_got, lefts_got, ff + width, width)]
    waves += [lane(right, rights, first + half, half), lane(right_got, rights_got, first + half, half)]
    copies = [pltpu.make_async_copy(far, near, sems.at[k]) for k, (far, near) in enumerate(waves)]
    for copy in copies:
        copy.start()
    waited = [0]

    def wait(count):
        for copy in copies[waited[0] : waited[0] + count]:
            copy.wait()
        waited[0] += count

    outgoing = []

    def emit(place):
        at = sems.at[len(copies) + len(outgoing)]
        copy = pltpu.make_async_copy(res.at[place], out.at[place], at)
        copy.start()
        outgoing.append(copy)

    def grad(at, size, begin):
        rows, lanes = slice(at, at + size), slice(begin, begin + half)
        return dot_tn(lefts[:, rows], rights[:, lanes]) + dot_tn(lefts_got[:, rows], rights_got[:, lanes])

    whole = slice(None)
    owners = 1
    for size in out.shape[:-2]:
        owners *= size
    pieces = (ff + width) // width
    up_rows = width // owners
    down_rows = ff // owners
    start = pieces * up_rows
    mids = (whole,) * (len(out.shape) - 3)
    by_piece = up_rows % 16 == 0 and down_rows % 16 == 0
    wait(2)
    for j in range(blocks):
        wait(2)
        part = grad(j * step, step, first)
        spread_rows(res, (j,), slice(start, start + down_rows), part)
        if by_piece:
            emit((j,) + mids + (slice(start, start + down_rows), whole))
    wait(4)
    for k in range(pieces):
        if k == pieces - 1:
            wait(4)
            part = grad(ff + width, width, first + half)
        else:
            part = grad(ff, width, k * half)
        rows = slice(k * up_rows, (k + 1) * up_rows)
        spread_rows(res, (), rows, part)
        if by_piece:
            emit((whole,) + mids + (rows, whole))
    if not by_piece:
        emit((whole,) * len(out.shape))
    for copy in outgoing:
        copy.wait()


def spread_rows(res, head, rows, grad):
    size = rows.stop - rows.start
    wide = res.shape[len(head) : -2]
    if size % 16 == 0:
        at = head + (slice(None),) * len(wide) + (rows, slice(None))
        res[at] = grad.astype(BF16).reshape(wide + (size, grad.shape[1]))
        return
    places = [()]
    for count in wide:
        places = [place + (k,) for place in places for k in range(count)]
    for k, place in enumerate(places):
        res[head + place + (rows, slice(None))] = grad[k * size : (k + 1) * size].astype(BF16)


def feed_grads(left, left_got, right, right_got, ff, width):
    tokens = left.shape[0]
    count, groups = lax.axis_size("seq"), lax.axis_size("dp")
    places = bits_of(count)[1:]
    owners = count * groups // 2
    rows = (ff + width) // width * (width // owners) + ff // owners
    shape = (groups,) + (2,) * len(places) + (rows, width // 2)
    (out,) = call(
        functools.partial(feed_grads_body, ff),
        [HBM] * 4,
        [(shape, BF16, HBM)],
        [
            pltpu.VMEM((tokens, ff + 2 * width), BF16),
            pltpu.VMEM((tokens, ff + 2 * width), BF16),
            pltpu.VMEM((tokens, ff // 2 + width), BF16),
            pltpu.VMEM((tokens, ff // 2 + width), BF16),
            pltpu.VMEM(shape, BF16),
            pltpu.SemaphoreType.DMA((10 + 3 * groups + (ff + width) // width,)),
        ],
        name="grad_feed",
    )(left, left_got, right, right_got)
    return out


def store_rows(res, lanes, grad):
    rows = res.shape[-2]
    if rows % 16 == 0:
        res[..., lanes] = grad.astype(BF16).reshape(res.shape[:-1] + (grad.shape[1],))
        return
    places = [()]
    for wide in res.shape[:-2]:
        places = [place + (k,) for place in places for k in range(wide)]
    for k, place in enumerate(places):
        res[place + (slice(None), lanes)] = grad[k * rows : (k + 1) * rows].astype(BF16)


def outer_body(plan, cut, bits_ref, left, left_got, right, right_got, *rest):
    low_send, low_keep, high_send, high_keep = rest[:4]
    lefts, lefts_got, rights, rights_got, res, sems = rest[4:]
    height = lefts.shape[1] // len({lane for lane, _, _ in plan})
    homes, waits, lane_at = {}, {}, 0
    used = 0
    for number, (lane, first, wide) in enumerate(plan):
        if lane not in homes:
            homes[lane] = len(homes) * height
            at = homes[lane]
            waits[number] = [
                pltpu.make_async_copy(
                    far.at[:, lane : lane + height], near.at[:, at : at + height], sems.at[used + k]
                )
                for k, (far, near) in enumerate(((left, lefts), (left_got, lefts_got)))
            ]
            used += 2
        else:
            waits[number] = []
        if all(first != other[1] for other in plan[:number]):
            waits[number] += [
                pltpu.make_async_copy(
                    far.at[:, first : first + wide],
                    near.at[:, lane_at : lane_at + wide],
                    sems.at[used + k],
                )
                for k, (far, near) in enumerate(((right, rights), (right_got, rights_got)))
            ]
            used += 2
        for copy in waits[number]:
            copy.start()
        lane_at += wide
    low, high = bits_ref[0], bits_ref[1]
    outgoing = []
    whole = slice(None)
    mids = len(res.shape) - 4

    def emit(low_half):
        if low_half:
            place = lambda which: (whole,) * (1 + mids) + (which, whole, slice(0, cut))
            pairs = ((low_send, 1 - low), (low_keep, low))
        else:
            place = lambda which: (whole, which) + (whole,) * (1 + mids) + (slice(cut, res.shape[-1]),)
            pairs = ((high_send, 1 - high), (high_keep, high))
        for out, which in pairs:
            copy = pltpu.make_async_copy(res.at[place(which)], out, sems.at[used + len(outgoing)])
            copy.start()
            outgoing.append(copy)

    lane_at = 0
    places = {}
    for number, (lane, first, wide) in enumerate(plan):
        for copy in waits[number]:
            copy.wait()
        places.setdefault(first, lane_at)
        home, near = homes[lane], places[first]
        for k in range(0, wide, 512):
            size = min(512, wide - k)
            lanes = slice(near + k, near + k + size)
            grad = dot_tn(lefts[:, home : home + height], rights[:, lanes])
            grad = grad + dot_tn(lefts_got[:, home : home + height], rights_got[:, lanes])
            lanes = slice(lane_at + k, lane_at + k + size)
            store_rows(res, lanes, grad)
            if lane_at + k + size == cut:
                emit(True)
        lane_at += wide
    emit(False)
    for copy in outgoing:
        copy.wait()


def outer_grads(arrays, plan, cut, height, name):
    count, groups = lax.axis_size("seq"), lax.axis_size("dp")
    places = bits_of(count)[1:]
    rows = 2 * height // (count * groups)
    tokens = arrays[0].shape[0]
    wide = sum(piece[2] for piece in plan)
    lefts = len({piece[0] for piece in plan})
    shape = (groups,) + (2,) * len(places) + (rows,)
    less = (groups,) + (2,) * (len(places) - 1) + (rows,)
    seq = lax.axis_index("seq")
    bits = jnp.stack([(seq // places[0]) % 2, (seq // places[-1]) % 2]).astype(jnp.int32)
    return call(
        functools.partial(outer_body, plan, cut),
        [SMEM] + [HBM] * 4,
        [(less + (cut,), BF16, HBM)] * 2 + [(less + (wide - cut,), BF16, HBM)] * 2,
        [
            pltpu.VMEM((tokens, lefts * height), BF16),
            pltpu.VMEM((tokens, lefts * height), BF16),
            pltpu.VMEM((tokens, wide), BF16),
            pltpu.VMEM((tokens, wide), BF16),
            pltpu.VMEM(shape + (wide,), BF16),
            pltpu.SemaphoreType.DMA((4 * len(plan) + 4,)),
        ],
        name=name,
    )(bits, *arrays)


def project_back_body(
    count, seqs, tokens, pairs, size, per_seg,
    me_ref, pre, d_first_in_far, ptok_far, query_w, key_w, value_w, join_w,
    *rest,
):
    chunks, rest = rest[:count], rest[count:]
    grad_out, d_perm, payload, vec, keep_out, send_out = rest[:6]
    query_v, key_v, value_v, join_v, d_first_in, ptok, sems, stage, rights, out_sems = rest[6:]
    me, core = me_ref[0], me_ref[1]
    width = query_v.shape[0]
    outgoing = []

    def emit_halves(part):
        wide = width // 2
        for out, which in ((keep_out, core), (send_out, 1 - core)):
            at = pl.ds(pl.multiple_of(part * width + which * wide, LANES), wide)
            copy = pltpu.make_async_copy(
                rights.at[:, at],
                out.at[:, part * wide : (part + 1) * wide],
                out_sems.at[len(outgoing)],
            )
            copy.start()
            outgoing.append(copy)

    wanted = arrivals(chunks, stage, me, count)
    wanted += [(d_first_in_far, d_first_in)]
    wanted += [(query_w, query_v), (key_w, key_v), (value_w, value_v)]
    wanted += [(join_w.at[k], join_v.at[k]) for k in range(3)]
    wanted += [(ptok_far, ptok)]
    copies = pull(wanted, sems)
    for copy in copies[: count + 1]:
        copy.wait()
    copies = copies[count + 1 :]
    targets = [rights.at[:, k * width : (k + 1) * width] for k in range(4)]

    def place(part, s, lane, values):
        at = part * width + lane
        rights[s * tokens : (s + 1) * tokens, at : at + values.shape[1]] = values

    receive_pairs(stage, place, count, seqs, pairs, size, 3)
    for part in range(3):
        emit_halves(part)
    d_resid = d_first_in[...]
    for k, near in enumerate((query_v, key_v, value_v)):
        copies[k].wait()
        d_resid = d_resid + dot_nt(targets[k][...], near[...])
    grad = d_resid.astype(BF16)
    grad_out[...] = grad
    targets[3][...] = grad
    emit_halves(3)
    vec[0:1] = column_sum(targets[0][...])
    vec[1:2] = column_sum(targets[2][...])
    vec[2:3] = column_sum(grad)
    vec[3:8] = jnp.zeros((5, vec.shape[1]), F32)
    total = seqs * tokens
    half = vec.shape[1] // 2
    row = lax.broadcasted_iota(jnp.int32, (total + 16, total), 0)
    place_at = lax.broadcasted_iota(jnp.int32, (total + 16, total), 1)
    rows = seqs * SEGS
    step, rest_row = row // rows, row % rows
    seq = rest_row // SEGS
    tok = (rest_row % SEGS) * per_seg + step
    extra = row - total
    seq = jnp.where(extra >= 0, extra % seqs, seq)
    tok = jnp.where(extra >= 0, jnp.where(extra < seqs, -1, tokens), tok)
    known = extra < 2 * seqs
    d_char = jnp.zeros((total + 16, 2 * half), F32)
    for k in range(3):
        moved = tok + 1 - k
        pick = (place_at == seq * tokens + moved) & (moved >= 0) & (moved < tokens) & known
        shifted = dot(pick.astype(BF16), grad).astype(BF16)
        copies[3 + k].wait()
        d_char = d_char + dot_nt(shifted, join_v[k])
    copies[6].wait()
    payload[6 * seqs :] = jnp.zeros((payload.shape[0] - 6 * seqs, half), F32)
    for r in range(2):
        grads = d_char[0:total, r * half : (r + 1) * half].reshape(per_seg, rows, half)
        d_perm[r] = grads
        weighted = jnp.sum(grads * ptok[r], axis=0) * pre[0, r]
        for s in range(seqs):
            row = r * seqs + s
            payload[row : row + 1] = column_sum(weighted[s * SEGS : (s + 1) * SEGS])
        edges = d_char[total : total + 2 * seqs, r * half : (r + 1) * half]
        payload[(2 + r) * seqs : (3 + r) * seqs] = edges[0:seqs]
        payload[(4 + r) * seqs : (5 + r) * seqs] = edges[seqs : 2 * seqs]
    for copy in outgoing:
        copy.wait()


def chars_back_body(
    count, seqs, steps, per,
    lang, me_ref, ids, gate_b, enter, pseg, vec1, up_vec, vec2, embedded_far, gate_w_far, cand_w_far, ptok_far, d_perm,
    *rest,
):
    groups, back_groups, rest = rest[: count // 2], rest[count // 2 : count], rest[count:]
    (
        keep_out, send_out,
        upd, work, d_all, d_tok, gseg, gin, embedded, gate_w, cand_w, ptok, held, back, sems, vector, owned,
    ) = rest
    me = me_ref[0]
    wanted = [(embedded_far, embedded), (gate_w_far, gate_w), (cand_w_far, cand_w)]
    wanted += [(d_perm, d_tok), (ptok_far, ptok)]
    wanted += summaries(groups, held, me) + summaries(back_groups, back, me)
    copies = pull(wanted, sems)
    for copy in copies[:3]:
        copy.wait()

    def gathered(j, k):
        return held[j, k * seqs : (k + 1) * seqs]

    def gathered_back(j, k):
        return back[j, k * seqs : (k + 1) * seqs]

    rows = seqs * SEGS
    half = upd.shape[2]
    gates(embedded[...], gate_w, gate_b[...], cand_w, upd, work)

    def ahead(q, carry):
        h0, h1 = carry
        for j in range(per):
            at = pl.ds(pl.multiple_of((q * per + j) * rows, rows), rows)
            u = upd[0, at, :]
            gap = work[0, at, :] - h0
            work[0, at, :] = gap * (u * (1.0 - u))
            h0 = h0 + u * gap
            at = pl.ds(pl.multiple_of((steps - 1 - q * per - j) * rows, rows), rows)
            u = upd[1, at, :]
            gap = work[1, at, :] - h1
            work[1, at, :] = gap * (u * (1.0 - u))
            h1 = h1 + u * gap
        return h0, h1

    lax.fori_loop(0, steps // per, ahead, (enter[0], enter[1]))

    left = jnp.maximum(me - 1, 0)
    right = jnp.minimum(me + 1, count - 1)
    last = steps // per - 1
    for copy in copies[3:]:
        copy.wait()
    for r in range(2):
        from_left = jnp.where(me > 0, gathered_back(left, 4 + r), 0.0)
        from_right = jnp.where(me < count - 1, gathered_back(right, 2 + r), 0.0)
        for s in range(seqs):
            low, high = s * SEGS, s * SEGS + SEGS - 1
            d_tok[r, 0, low : low + 1] += from_left[s : s + 1]
            d_tok[r, last, high : high + 1] += from_right[s : s + 1]
        gseg[r] = jnp.sum(d_tok[r] * ptok[r], axis=0)

    def block_sum(j, r):
        total = gathered_back(j, r)
        near, far = gathered(j, 4 * r + 2), gathered(j, 4 * r)
        if r == 1:
            near, far = far, near
        if j > 0:
            total = total + near * gathered_back(j - 1, 4 + r)
        if j < count - 1:
            total = total + far * gathered_back(j + 1, 2 + r)
        return total

    g0 = jnp.zeros((seqs, half), F32)
    g1 = jnp.zeros((seqs, half), F32)
    for j in range(count):
        i = count - 1 - j
        g0 = jnp.where(i > me, gathered(i, 0) * g0 + block_sum(i, 0), g0)
        g1 = jnp.where(j < me, gathered(j, 4) * g1 + block_sum(j, 1), g1)
    for s in range(seqs):
        flow = g0[s : s + 1]
        for g in range(SEGS - 1, -1, -1):
            row = s * SEGS + g
            gin[0, row : row + 1] = flow
            flow = pseg[0, row : row + 1] * flow + gseg[0, row : row + 1]
        flow = g1[s : s + 1]
        for g in range(SEGS):
            row = s * SEGS + g
            gin[1, row : row + 1] = flow
            flow = pseg[1, row : row + 1] * flow + gseg[1, row : row + 1]

    def astern(q, carry):
        flow0, flow1 = carry
        for j in range(per):
            at = pl.ds(pl.multiple_of((steps - 1 - q * per - j) * rows, rows), rows)
            if j == 0:
                flow0 = flow0 + d_tok[0, steps // per - 1 - q]
            u = upd[0, at, :]
            d_all[at, 0:half] = (flow0 * work[0, at, :]).astype(BF16)
            d_cand = flow0 * u
            d_all[at, half : 2 * half] = d_cand.astype(BF16)
            flow0 = flow0 - d_cand
            at = pl.ds(pl.multiple_of((q * per + j) * rows, rows), rows)
            if j == 0:
                flow1 = flow1 + d_tok[1, q]
            u = upd[1, at, :]
            d_all[at, 2 * half : 3 * half] = (flow1 * work[1, at, :]).astype(BF16)
            d_cand = flow1 * u
            d_all[at, 3 * half : 4 * half] = d_cand.astype(BF16)
            flow1 = flow1 - d_cand
        return flow0, flow1

    lax.fori_loop(0, steps // per, astern, (gin[0], gin[1]))
    grad_w = dot_tn(embedded[...], d_all[...])
    place_owned(owned, grad_w)
    d_emb = jnp.zeros(embedded.shape, F32)
    gate_sums = []
    for r in range(2):
        gate_sums.append(column_sum(d_all[:, 2 * r * half : (2 * r + 1) * half]))
        d_emb = d_emb + dot_nt(d_all[:, 2 * r * half : (2 * r + 1) * half], gate_w[r])
        d_emb = d_emb + dot_nt(d_all[:, (2 * r + 1) * half : (2 * r + 2) * half], cand_w[r])
    partial = dot_tn(one_hot_rows(ids, seqs, steps), d_emb.astype(BF16))
    local = lax.broadcasted_iota(jnp.int32, partial.shape, 0)
    for s in range(seqs):
        tag = lang[s].astype(F32)
        partial = jnp.where(local == s * LANES + LANES - 1, tag, partial)
    core = me_ref[1]
    wide = partial.shape[1] // 2
    low, high = partial[:, :wide].astype(BF16), partial[:, wide:].astype(BF16)
    rows = partial.shape[0]
    keep_out[0:rows] = jnp.where(core == 0, low, high)
    send_out[0:rows] = jnp.where(core == 0, high, low)
    sums = [vec1[k : k + 1] for k in range(6)] + [up_vec[...]]
    sums += [vec2[k : k + 1] for k in range(3)] + gate_sums
    vector[...] = jnp.zeros_like(vector)
    at = 0
    for values in sums:
        for k in range(values.shape[1] // LANES):
            vector[at : at + 1] = values[:, k * LANES : (k + 1) * LANES]
            at += 1
    put_low(send_out, rows, vector[...])
    keep_out[rows:] = owned[core].astype(BF16)
    send_out[rows + 2 * vector.shape[0] :] = owned[1 - core].astype(BF16)


def place_owned(owned, grad):
    count, groups = lax.axis_size("seq"), lax.axis_size("dp")
    rows = grad.shape[0] // (count * groups)
    tiles = grad.shape[1] // LANES
    bits = count.bit_length() - 1
    for d in range(groups):
        for s in range(count):
            mirrored = 0
            for b in range(1, bits):
                mirrored = mirrored * 2 + (s >> b) % 2
            at = (mirrored * groups + d) * rows * tiles
            first = (d * count + s) * rows
            for t in range(tiles):
                value = grad[first : first + rows, t * LANES : (t + 1) * LANES]
                owned[s % 2, at + t * rows : at + (t + 1) * rows] = value


def put_low(packed, at, vector):
    rows = vector.shape[0]
    high = vector.astype(BF16)
    packed[at : at + rows] = high
    packed[at + rows : at + 2 * rows] = (vector - high.astype(F32)).astype(BF16)


def get_low(packed, at, rows):
    return packed[at : at + rows].astype(F32) + packed[at + rows : at + 2 * rows].astype(F32)


def mix_body(rows, vector_rows, first, last, bits_ref, keep, sent, got, *outs):
    fixed = rows + 2 * vector_rows
    table = (keep if first else sent)[0:rows].astype(F32) + got[0:rows].astype(F32)
    vector = get_low(sent, rows, vector_rows) + get_low(got, rows, vector_rows)
    start = rows if first else 0
    size = keep.shape[0] - start
    if last:
        piece = size // len(outs)
        for k, out in enumerate(outs):
            which = jnp.bitwise_xor(bits_ref[0], k) * piece
            at = pl.ds(pl.multiple_of(start + which, 8), piece)
            from_got = pl.ds(pl.multiple_of(fixed + which, 8), piece)
            out[fixed:] = (keep[at].astype(F32) + got[from_got].astype(F32)).astype(BF16)
    else:
        piece = size // 2
        for out, bit in ((outs[0], 1 - bits_ref[0]), (outs[1], bits_ref[0])):
            at = pl.ds(pl.multiple_of(start + bit * piece, 16), piece)
            from_got = pl.ds(pl.multiple_of(fixed + bit * piece, 16), piece)
            total = (keep[at].astype(F32) + got[from_got].astype(F32)).astype(BF16)
            if out is outs[0]:
                out[fixed:] = total
            else:
                out[...] = total
    for out in outs if last else outs[:1]:
        out[0:rows] = table.astype(BF16)
        put_low(out, rows, vector)


def table_body(groups, seqs, sub, count, place_ref, *refs):
    own, other, rest = refs[:groups], refs[groups : 2 * groups], refs[2 * groups :]
    table, vector, gate_out, cand_out, low, high, vec, held = rest
    dp, core = place_ref[0], place_ref[1]
    vocab, width = table.shape
    half = width // 2
    rows = low.shape[1]
    for k in range(groups):
        at = jnp.bitwise_xor(dp, k)
        mine, their = own[k][0:rows], other[k][0:rows]
        low[at] = jnp.where(core == 0, mine, their)
        high[at] = jnp.where(core == 0, their, mine)
        vec[at] = get_low(own[k], rows, vector.shape[0])
    fixed = rows + 2 * vector.shape[0]
    mine = own[0][fixed:].astype(F32)
    for part in own[1:]:
        mine = mine + part[fixed:].astype(F32)
    held[...] = mine
    owned = gate_out.shape[1]
    tiles = held.shape[0] // owned // 4
    for k in range(4):
        home = (gate_out, cand_out)[k % 2]
        for t in range(tiles):
            at = (k * tiles + t) * owned
            home[k // 2, :, t * LANES : (t + 1) * LANES] = held[at : at + owned]
    wide = -(-vocab // 16) * 16
    row = lax.broadcasted_iota(jnp.int32, (wide, LANES), 0)
    local = lax.broadcasted_iota(jnp.int32, (wide, LANES), 1)
    left = jnp.zeros((wide, half), F32)
    right = jnp.zeros((wide, half), F32)
    total = jnp.zeros(vector.shape, F32)
    for g in range(groups):
        for s in range(seqs):
            tag = low[g, (s + 1) * LANES - 16 : (s + 1) * LANES, 0:1].astype(F32)[15:16]
            lang = (tag * (1.0 / count) + 0.5).astype(jnp.int32)
            pick = ((row - lang * sub == local) & (local < sub)).astype(BF16)
            left = left + dot(pick, low[g, s * LANES : (s + 1) * LANES])
            right = right + dot(pick, high[g, s * LANES : (s + 1) * LANES])
        total = total + vec[g]
    table[:, 0:half] = left[0:vocab]
    table[:, half:width] = right[0:vocab]
    vector[...] = total


def fold_body(bits_ref, *refs):
    ins, outs = refs[:4], refs[4:]
    for k in range(2):
        keep, got, bit = ins[2 * k], ins[2 * k + 1], bits_ref[k]
        for out, which in ((outs[2 * k], 1 - bit), (outs[2 * k + 1], bit)):
            out[...] = (keep[:, which].astype(F32) + got[:, which].astype(F32)).astype(BF16)


def halve_body(sizes, alone, bits_ref, *refs):
    ins, outs = refs[:-4], refs[-4:]
    owners = ins[0].shape[0]
    at = 0
    for k, size in enumerate(sizes):
        rows = slice(at, at + size) if alone else slice(0, size)
        parts = ins if alone else ins[2 * k : 2 * k + 2]
        for out, which in ((outs[2 * k], 1 - bits_ref[k]), (outs[2 * k + 1], bits_ref[k])):
            for i in range(owners // 2):
                place = which * (owners // 2) + i if k == 0 else 2 * i + which
                total = parts[0][place, rows].astype(F32)
                for part in parts[1:]:
                    total = total + part[place, rows].astype(F32)
                out[i] = total.astype(BF16)
        at += size if alone else 0


def part_rows_body(sizes, core_ref, kept, got, kept_on, got_on, send, keep):
    core = core_ref[0]
    total = jnp.concatenate(
        [a[...].astype(F32) + b[...].astype(F32) for a, b in ((kept, got), (kept_on, got_on))], axis=0
    )
    at = 0
    for size in sizes:
        first, second = total[2 * at : 2 * at + size], total[2 * at + size : 2 * at + 2 * size]
        send[at : at + size] = jnp.where(core == 0, second, first)
        keep[at : at + size] = jnp.where(core == 0, first, second)
        at += size


def beside_body(pieces, core_ref, keep, got, up, out, down):
    core = core_ref[0]
    wide = keep.shape[1]
    rows = up.shape[0]
    low = jnp.where(core == 0, keep[...], got[...])
    high = jnp.where(core == 0, got[...], keep[...])
    for k in range(pieces + 1):
        home, lane = (up, k * wide) if k < pieces else (out, 0)
        gap = up.shape[1] // 2 if k < pieces else wide
        home[:, lane : lane + wide] = low[k * rows : (k + 1) * rows]
        home[:, lane + gap : lane + gap + wide] = high[k * rows : (k + 1) * rows]
    down[:, 0:wide] = low[(pieces + 1) * rows :]
    down[:, wide : 2 * wide] = high[(pieces + 1) * rows :]


def part_cores_body(core_ref, low_keep, low_got, high_keep, high_got, send, keep):
    core = core_ref[0]
    rows = keep.shape[1]
    lane = 0
    for mine, got in ((low_keep, low_got), (high_keep, high_got)):
        wide = mine.shape[2]
        total = mine[...].astype(F32) + got[...].astype(F32)
        first, second = total[:, 0:rows], total[:, rows : 2 * rows]
        send[:, :, lane : lane + wide] = jnp.where(core == 0, second, first).astype(BF16)
        keep[:, :, lane : lane + wide] = jnp.where(core == 0, first, second).astype(BF16)
        lane += wide


def part_groups_body(widths, groups, place_ref, keep, got, own, *sends):
    dp, core = place_ref[0], place_ref[1]
    for k in range(groups):
        at = jnp.bitwise_xor(dp, k)
        mine, their = keep[at], got[at]
        out = own if k == 0 else sends[k - 1]
        lane = 0
        for wide in widths:
            a, b = mine[:, lane : lane + wide], their[:, lane : lane + wide]
            out[:, 2 * lane : 2 * lane + wide] = jnp.where(core == 0, a, b)
            out[:, 2 * lane + wide : 2 * lane + 2 * wide] = jnp.where(core == 0, b, a)
            lane += wide


def total_body(widths, groups, *refs):
    ins, outs = refs[:groups], refs[groups:]
    total = ins[0][...].astype(F32)
    for part in ins[1:]:
        total = total + part[...].astype(F32)
    lane = 0
    for out, wide in zip(outs, widths):
        out[...] = total[:, lane : lane + 2 * wide]
        lane += 2 * wide


def shift(array, by):
    count = lax.axis_size("seq")
    return lax.ppermute(array, "seq", [(i, (i + by) % count) for i in range(count)])


def swap(array, axis, bit):
    return lax.ppermute(array, axis, [(i, i ^ bit) for i in range(lax.axis_size(axis))])


def exchange(chunks):
    return [chunks[0]] + [shift(chunk, k) for k, chunk in enumerate(chunks) if k > 0]


def bits_of(count):
    return [1 << b for b in range(count.bit_length() - 1)]


def tie(arrays, *after):
    held = lax.optimization_barrier((tuple(arrays), after))
    return list(held[0])


def gather_summaries(rows):
    pair = jnp.stack([rows, swap(rows, "seq", 1)])
    return [pair] + [swap(pair, "seq", 2 * j) for j in range(1, lax.axis_size("seq") // 2)]


class Columns:
    def __init__(self, sends_and_keeps, widths):
        self.places = bits_of(lax.axis_size("seq"))[1:]
        self.seq = lax.axis_index("seq")
        self.widths = widths
        self.done = 0
        low_send, low_keep, high_send, high_keep = sends_and_keeps
        self.sends, self.keeps = (low_send, high_send), (low_keep, high_keep)
        self.hold_swap()

    def hold_swap(self):
        bits = self.places[self.done], self.places[-1 - self.done]
        self.gots = tuple(swap(send, "seq", bit) for send, bit in zip(self.sends, bits))
        self.done += 1

    def fold(self, *after):
        keeps, gots = self.keeps, self.gots
        if after:
            keeps = tie(keeps, *after)
        bits = self.places[self.done], self.places[-1 - self.done]
        chosen = jnp.stack([(self.seq // bit) % 2 for bit in bits]).astype(jnp.int32)
        flat, shapes = [], []
        for k, (keep, got) in enumerate(zip(keeps, gots)):
            dims = keep.shape
            if k == 0:
                flat += [x.reshape((-1, 2) + dims[-2:]) for x in (keep, got)]
                shapes.append(dims[:-3] + dims[-2:])
            else:
                flat += [x.reshape(dims[:2] + (-1, dims[-1])) for x in (keep, got)]
                shapes.append(dims[:1] + dims[2:])
        outs = []
        for k in range(2):
            dims = flat[2 * k].shape
            outs += [((dims[0],) + dims[2:], BF16)] * 2
        got = call(fold_body, [SMEM] + [VMEM] * 4, outs, limit=24, name="fold")(chosen, *flat)
        self.sends = (got[0].reshape(shapes[0]), got[2].reshape(shapes[1]))
        self.keeps = (got[1].reshape(shapes[0]), got[3].reshape(shapes[1]))
        self.hold_swap()

    def part_cores(self, *after):
        while self.done < len(self.places):
            self.fold()
        keeps = self.keeps
        if after:
            keeps = tie(keeps, *after)
        groups, rows, _ = keeps[0].shape
        wide = sum(self.widths)
        core = (self.seq % 2).astype(jnp.int32).reshape(1)
        self.send, self.keep = call(
            part_cores_body,
            [SMEM] + [VMEM] * 4,
            [((groups, rows // 2, wide), BF16)] * 2,
            limit=24,
            name="part_cores",
        )(core, keeps[0], self.gots[0], keeps[1], self.gots[1])
        self.got = swap(self.send, "seq", 1)

    def part_groups(self, *after):
        keep = self.keep
        if after:
            (keep,) = tie([keep], *after)
        groups, rows, wide = keep.shape
        place = jnp.stack([lax.axis_index("dp"), self.seq % 2]).astype(jnp.int32)
        self.own, *self.sends = call(
            functools.partial(part_groups_body, self.widths, groups),
            [SMEM] + [VMEM] * 2,
            [((rows, 2 * wide), BF16)] * groups,
            limit=24,
            name="part_groups",
        )(place, keep, self.got)
        self.gots = [swap(send, "dp", k + 1) for k, send in enumerate(self.sends)]

    def finish(self):
        groups = len(self.gots) + 1
        return call(
            functools.partial(total_body, self.widths, groups),
            [VMEM] * groups,
            [((self.own.shape[0], 2 * wide), F32) for wide in self.widths],
            limit=24,
            name="total",
        )(self.own, *self.gots)


class FeedRows:
    def __init__(self, grad, first):
        self.places = bits_of(lax.axis_size("seq"))[1:]
        self.seq = lax.axis_index("seq")
        self.first = first
        flat = grad.reshape(-1, grad.shape[-1])
        got = lax.psum_scatter(flat, "dp", scatter_dimension=0, tiled=True)
        self.parts = [got.reshape(grad.shape[1:])]
        self.done = 0

    def step(self, *after):
        parts = self.parts
        if after:
            parts = tie(parts, *after)
        bits = self.places[-1 - self.done], self.places[self.done]
        chosen = jnp.stack([(self.seq // bit) % 2 for bit in bits]).astype(jnp.int32)
        if self.done == 0:
            rows, wide = parts[0].shape[-2:]
            sizes = (self.first, rows - self.first)
            ins = [parts[0].reshape((-1, rows, wide))]
        else:
            wide = parts[0].shape[-1]
            sizes = (self.first, parts[2].shape[-2])
            ins = parts
        owners = 2 ** (len(self.places) - self.done - 1)
        outs = [((owners, size, wide), BF16) for size in sizes for _ in range(2)]
        got = call(
            functools.partial(halve_body, sizes, len(ins) == 1),
            [SMEM] + [VMEM] * len(ins),
            outs,
            limit=24,
            name="halve",
        )(chosen, *ins)
        self.sends = (got[0], got[2])
        gots = [swap(send, "seq", bit) for send, bit in zip(self.sends, bits)]
        self.parts = [got[1], gots[0], got[3], gots[1]]
        self.done += 1

    def finish(self, ff, width):
        while self.done < len(self.places):
            self.step()
        parts = [part[0] for part in self.parts]
        rows, wide = sum(part.shape[0] for part in parts[::2]), parts[0].shape[1]
        core = (self.seq % 2).astype(jnp.int32).reshape(1)
        pieces = (ff + width) // width
        owned = width // (lax.axis_size("seq") * lax.axis_size("dp"))
        send, keep = call(
            functools.partial(part_rows_body, (owned,) * pieces + (rows // 2 - pieces * owned,)),
            [SMEM] + [VMEM] * 4,
            [((rows // 2, wide), F32)] * 2,
            limit=24,
            name="part_rows",
        )(core, *parts)
        got = swap(send, "seq", 1)
        return call(
            functools.partial(beside_body, pieces - 1),
            [SMEM] + [VMEM] * 2,
            [((owned, ff), F32), ((owned, width), F32), ((rows // 2 - pieces * owned, width), F32)],
            limit=24,
            name="beside",
        )(core, keep, got)


class CharsSums:
    def __init__(self, keep, send, rows, vector_rows):
        self.keep, self.send, self.rows, self.vector_rows = keep, send, rows, vector_rows
        self.seq = lax.axis_index("seq")
        self.bits = bits_of(lax.axis_size("seq"))
        self.first = True

    def step(self, *after):
        bit = self.bits.pop(0)
        groups = lax.axis_size("dp")
        send, keep = self.send, self.keep
        if after:
            send, keep = tie([send, keep], *after)
        got = swap(send, "seq", bit)
        last = not self.bits
        start = self.rows if self.first else 0
        size = keep.shape[0] - start
        fixed = self.rows + 2 * self.vector_rows
        if last:
            which = lax.axis_index("dp")
            outs = [((fixed + size // groups, LANES), BF16)] * groups
        else:
            which = (self.seq // self.bits[0]) % 2
            outs = [((fixed + size // 2, LANES), BF16), ((size // 2, LANES), BF16)]
        outs = call(
            functools.partial(mix_body, self.rows, self.vector_rows, self.first, last),
            [SMEM] + [VMEM] * 3,
            outs,
            limit=12,
            name="mix",
        )(which.astype(jnp.int32).reshape(1), keep, send, got)
        self.first = False
        if last:
            self.own, self.sends = outs[0], outs[1:]
        else:
            self.send, self.keep = outs

    def across(self):
        self.own = [self.own] + [swap(part, "dp", k + 1) for k, part in enumerate(self.sends)]

    def finish(self, seqs, vocab, sub, gate_shape):
        own = self.own
        other = [swap(part, "seq", 1) for part in own]
        groups = len(own)
        rows, vector_rows = self.rows, self.vector_rows
        place = jnp.stack([lax.axis_index("dp"), self.seq % 2]).astype(jnp.int32)
        return call(
            functools.partial(table_body, groups, seqs, sub, lax.axis_size("seq")),
            [SMEM] + [VMEM] * (2 * groups),
            [((vocab, 2 * LANES), F32), ((vector_rows, LANES), F32)] + [(gate_shape, F32)] * 2,
            [
                pltpu.VMEM((groups, rows, LANES), BF16),
                pltpu.VMEM((groups, rows, LANES), BF16),
                pltpu.VMEM((groups, vector_rows, LANES), F32),
                pltpu.VMEM((own[0].shape[0] - rows - 2 * vector_rows, LANES), F32),
            ],
            limit=24,
            name="table_rows",
        )(place, *own, *other)


def shards(
    inputs, char_ids, lang_ids, lengths, char_table, gate_weight, gate_bias, cand_weight,
    join_weight, join_bias, query_weight, query_bias, key_weight, value_weight, value_bias,
    out_weight, out_bias, norm1_gain, norm1_bias, up_weight, up_bias, down_weight, down_bias,
    norm2_gain, norm2_bias, cotangent,
):
    seqs, tokens, width = inputs.shape
    chars = char_ids.shape[1]
    per = chars // tokens
    steps = chars // SEGS
    per_seg = steps // per
    vocab, embed = char_table.shape
    sub = vocab // GROUPS
    half = width // 2
    size = width // HEADS
    ff = up_weight.shape[1]
    count = lax.axis_size("seq")
    pairs = -(-seqs * HEADS // count)
    while HEADS % pairs:
        pairs += 1
    full = count * tokens
    total = seqs * tokens
    rows = seqs * SEGS
    wide = pairs * size
    seq = lax.axis_index("seq")
    me = jnp.stack([seq, seq % 2]).astype(jnp.int32)
    flat = inputs.reshape(total, width)
    cot = cotangent.reshape(total, width)
    line = lambda vector: vector

    embedded, htok, ptok, pre, pseg, payload = call(
        functools.partial(chars_forward_body, seqs, steps, per, sub),
        [SMEM] + [VMEM] * 2 + [HBM] * 3,
        [
            ((seqs * chars, embed), BF16),
            ((2, per_seg, rows, half), F32),
            ((2, per_seg, rows, half), F32),
            ((2, 2, rows, half), F32),
            ((2, rows, half), F32),
            ((8 * seqs, half), F32),
        ],
        [
            pltpu.VMEM((2, seqs * chars, half), F32),
            pltpu.VMEM((2, seqs * chars, half), F32),
            pltpu.VMEM((2, rows, half), F32),
            pltpu.VMEM((-(-vocab // LANES) * LANES, embed), BF16),
            pltpu.VMEM(gate_weight.shape, BF16),
            pltpu.VMEM(cand_weight.shape, BF16),
            pltpu.SemaphoreType.DMA((3,)),
        ],
        name="chars_forward",
    )(lang_ids, char_ids, gate_bias, char_table, gate_weight, cand_weight)
    groups = gather_summaries(payload)

    resid, enter, joined, *sent = call(
        functools.partial(join_query_body, count, seqs, tokens, pairs),
        [SMEM] + [VMEM] * 7 + [HBM] * (4 + count // 2),
        [
            ((total, width), F32),
            ((2, rows, half), F32),
            ((total, 4 * width), BF16, HBM),
        ]
        + [((tokens, 3 * wide), BF16)] * count,
        [
            pltpu.VMEM((3, width, width), BF16),
            pltpu.VMEM((width, width), BF16),
            pltpu.VMEM((width, width), BF16),
            pltpu.VMEM((width, width), BF16),
            pltpu.VMEM((count, 8 * seqs, half), F32),
            pltpu.SemaphoreType.DMA((count + 6,)),
            pltpu.VMEM((count, tokens, 3 * wide), BF16),
            pltpu.VMEM((total, 4 * width), BF16),
            pltpu.SemaphoreType.DMA((4,)),
        ],
        name="join_query",
    )(
        me, htok, ptok, pre, flat, line(join_bias), line(query_bias), line(value_bias),
        join_weight, query_weight, key_weight, value_weight, *groups,
    )
    heads = exchange(sent)
    (joined_far,) = tie([joined], *heads)
    joined_got = swap(joined_far, "seq", 1)

    block = min(256, full)
    *sent, lse = call(
        functools.partial(attend_body, count, seqs, tokens, pairs, size, block),
        [SMEM, SMEM] + [HBM] * count,
        [((tokens, wide), BF16)] * count + [((pairs, 1, full), F32)],
        [pltpu.VMEM((pairs, full, size), BF16)] * 3
        + [
            pltpu.VMEM((pairs, size, full), BF16),
            pltpu.VMEM((wide, full), F32),
            pltpu.VMEM((full, wide), BF16),
            pltpu.VMEM((count, tokens, 3 * wide), BF16),
            pltpu.SemaphoreType.DMA((count,)),
        ],
        name="attend",
    )(me, lengths, *heads)
    mixed_chunks = exchange(sent)

    ff_block = 512
    output, d_first_in, vec1, up_vec, fed, fed_keep, fed_send, *sent = call(
        functools.partial(feed_body, count, seqs, tokens, pairs, size, ff_block),
        [SMEM] + [VMEM] * 7 + [HBM] * (5 + count),
        [
            ((total, width), BF16),
            ((total, width), F32),
            ((8, width), F32),
            ((1, ff), F32),
            ((total, ff + 2 * width), BF16, HBM),
            ((total, ff // 2 + width), BF16, HBM),
            ((total, ff // 2 + width), BF16, HBM),
        ]
        + [((tokens, wide), BF16)] * count,
        [
            pltpu.VMEM((width, width), BF16),
            pltpu.VMEM((width, ff), BF16),
            pltpu.VMEM((ff, width), BF16),
            pltpu.SemaphoreType.DMA((2 * (ff // ff_block),)),
            pltpu.SemaphoreType.DMA((count + 3,)),
            pltpu.VMEM((count, tokens, wide), BF16),
            pltpu.VMEM((total, ff), F32),
            pltpu.VMEM((total, width), F32),
            pltpu.VMEM((total, width), F32),
            pltpu.VMEM((total, width), BF16),
            pltpu.VMEM((total, ff + 2 * width), BF16),
            pltpu.VMEM((total, ff), BF16),
            pltpu.VMEM((total, width), BF16),
            pltpu.VMEM((total, width), BF16),
            pltpu.SemaphoreType.DMA((8,)),
        ],
        name="feed_forward",
    )(
        me, line(out_bias), line(norm1_gain), line(norm1_bias), line(up_bias), line(down_bias),
        line(norm2_gain), line(norm2_bias), resid, cot, out_weight, up_weight, down_weight,
        *mixed_chunks,
    )
    d_mixed_chunks = exchange(sent)

    fed_got, fed_keep_got = swap(fed, "seq", 1), swap(fed_send, "seq", 1)
    fed, fed_got, fed_keep, fed_keep_got = tie(
        [fed, fed_got, fed_keep, fed_keep_got], *d_mixed_chunks
    )
    grad_feed = feed_grads(fed, fed_got, fed_keep, fed_keep_got, ff, width)
    feed = FeedRows(grad_feed, (ff + width) * 2 // (count * lax.axis_size("dp")))
    d_mixed_chunks = tie(d_mixed_chunks, grad_feed)

    sent = call(
        functools.partial(attend_back_body, count, seqs, tokens, pairs, size, block),
        [SMEM, SMEM, VMEM] + [HBM] * (2 * count),
        [((tokens, 3 * wide), BF16)] * count,
        [pltpu.VMEM((pairs, full, size), BF16)] * 3
        + [
            pltpu.VMEM((pairs, size, full), BF16),
            pltpu.VMEM((pairs, full, size), BF16),
            pltpu.VMEM((wide, full), F32),
            pltpu.VMEM((pairs, full, size), F32),
            pltpu.VMEM((pairs, full, size), F32),
            pltpu.VMEM((full, 3 * wide), BF16),
            pltpu.VMEM((count, tokens, 3 * wide), BF16),
            pltpu.VMEM((count, tokens, wide), BF16),
            pltpu.SemaphoreType.DMA((2 * count,)),
        ],
        name="attend_back",
    )(me, lengths, lse, *heads, *d_mixed_chunks)
    d_chunks = exchange(sent)
    input_grad, d_perm, payload_back, vec2, back_keep, back_send = call(
        functools.partial(project_back_body, count, seqs, tokens, pairs, size, per_seg),
        [SMEM, VMEM] + [HBM] * (6 + count),
        [
            ((total, width), BF16),
            ((2, per_seg, rows, half), F32),
            ((8 * seqs, half), F32),
            ((8, width), F32),
            ((total, 2 * width), BF16, HBM),
            ((total, 2 * width), BF16, HBM),
        ],
        [
            pltpu.VMEM((width, width), BF16),
            pltpu.VMEM((width, width), BF16),
            pltpu.VMEM((width, width), BF16),
            pltpu.VMEM((3, width, width), BF16),
            pltpu.VMEM((total, width), F32),
            pltpu.VMEM((2, per_seg, rows, half), F32),
            pltpu.SemaphoreType.DMA((count + 8,)),
            pltpu.VMEM((count, tokens, 3 * wide), BF16),
            pltpu.VMEM((total, 4 * width), BF16),
            pltpu.SemaphoreType.DMA((8,)),
        ],
        name="project_back",
    )(me, pre, d_first_in, ptok, query_weight, key_weight, value_weight, join_weight, *d_chunks)
    back_groups = gather_summaries(payload_back)
    vector_rows = -(-(10 * width + ff) // (16 * LANES)) * 16

    back_got = swap(back_send, "seq", 1)
    back_all = tie([joined, joined_got, back_keep, back_got], *back_groups)
    back_plan = tuple((0, k * half, half) for k in range(3))
    back_plan += tuple(((1 + k) * width, 3 * half, half) for k in range(3))
    back_parts = outer_grads(back_all, back_plan, 3 * half, width, "grad_back")
    back = Columns(back_parts, (half,) * 6)
    back_groups = tie(back_groups, *back_parts)

    own_rows = 4 * half * embed // (2 * LANES)
    table_rows = seqs * LANES
    chars_keep, chars_send = call(
        functools.partial(chars_back_body, count, seqs, steps, per),
        [SMEM, SMEM] + [VMEM] * 7 + [HBM] * (5 + count),
        [
            ((table_rows + own_rows, LANES), BF16),
            ((table_rows + 2 * vector_rows + own_rows, LANES), BF16),
        ],
        [
            pltpu.VMEM((2, seqs * chars, half), F32),
            pltpu.VMEM((2, seqs * chars, half), F32),
            pltpu.VMEM((seqs * chars, 4 * half), BF16),
            pltpu.VMEM((2, per_seg, rows, half), F32),
            pltpu.VMEM((2, rows, half), F32),
            pltpu.VMEM((2, rows, half), F32),
            pltpu.VMEM(embedded.shape, BF16),
            pltpu.VMEM(gate_weight.shape, BF16),
            pltpu.VMEM(cand_weight.shape, BF16),
            pltpu.VMEM((2, per_seg, rows, half), F32),
            pltpu.VMEM((count, 8 * seqs, half), F32),
            pltpu.VMEM((count, 8 * seqs, half), F32),
            pltpu.SemaphoreType.DMA((5 + 2 * count,)),
            pltpu.VMEM((vector_rows, LANES), F32),
            pltpu.VMEM((2, own_rows, LANES), F32),
        ],
        name="chars_back",
    )(
        lang_ids, me, char_ids, gate_bias, enter, pseg, vec1, up_vec, vec2, embedded, gate_weight, cand_weight,
        ptok, d_perm, *groups, *back_groups,
    )
    chars_sums = CharsSums(chars_keep, chars_send, table_rows, vector_rows)
    chars_sums.step()
    back.fold(chars_sums.send)
    chars_sums.step(*back.sends)
    back.part_cores()
    chars_sums.step(back.send)
    back.part_groups()
    while chars_sums.bits:
        chars_sums.step()
    feed.step(*back.sends, *chars_sums.sends)
    chars_sums.across()
    feed.step()
    gate_shape = (2, embed // (count * lax.axis_size("dp")), half)
    grad_table, sums, grad_gate, grad_cand = chars_sums.finish(seqs, vocab, sub, gate_shape)
    sums = sums.reshape(-1)
    early, late = sums[: 6 * width + ff], sums[6 * width + ff : 10 * width + ff]
    grad_up, grad_out, grad_down = feed.finish(ff, width)
    grad_query, grad_key, grad_value, *grad_join = back.finish()

    early_row = lambda k: early[k * width : (k + 1) * width]
    late_row = lambda k: late[k * width : (k + 1) * width]
    return (
        output.reshape(inputs.shape),
        input_grad.reshape(inputs.shape),
        grad_table,
        grad_gate,
        late[3 * width :].reshape(2, half),
        grad_cand,
        jnp.stack(grad_join),
        late_row(2),
        grad_query,
        late_row(0),
        grad_key,
        grad_value,
        late_row(1),
        grad_out,
        early_row(5),
        early_row(3),
        early_row(4),
        grad_up,
        early[6 * width :],
        grad_down,
        early_row(2),
        early_row(0),
        early_row(1),
    )


def solution(mesh):
    spread_rows = P("dp", "seq", None)
    placed = (
        (spread_rows, P("dp", "seq"), P("dp"), P("dp")) + (P(),) * 21 + (spread_rows,)
    )
    owned = P(("dp", "seq"), None)
    owned_mid = P(None, ("dp", "seq"), None)
    return jax.shard_map(
        shards,
        mesh=mesh,
        in_specs=placed,
        out_specs=(
            spread_rows, spread_rows, P(), owned_mid, P(), owned_mid, owned_mid, P(),
            owned, P(), owned, owned, P(), owned, P(), P(), P(), owned, P(), owned, P(), P(), P(),
        ),
        check_vma=False,
    )
```

```python
import functools

import jax
import jax.numpy as jnp
from jax import lax
from jax.experimental import pallas as pl
from jax.experimental.pallas import tpu as pltpu
from jax.sharding import PartitionSpec as P

HEADS = 12
GROUPS = 8
SEGS = 8
LANES = 128
NORM_EPS = 1e-05
MASKED = -1000000000.0
MIB = 1 << 20
F32 = jnp.float32
BF16 = jnp.bfloat16


def dot(left, right):
    return jnp.dot(left, right, preferred_element_type=F32)


def dot_nt(left, right):
    return lax.dot_general(left, right, (((1,), (1,)), ((), ())), preferred_element_type=F32)


def dot_tn(left, right):
    return lax.dot_general(left, right, (((0,), (0,)), ((), ())), preferred_element_type=F32)


def column_sum(values):
    return jnp.sum(values.astype(F32), axis=0, keepdims=True)


VMEM = pl.BlockSpec(memory_space=pltpu.VMEM)
SMEM = pl.BlockSpec(memory_space=pltpu.SMEM)
HBM, PIN, COPY = "hbm", "pin", "copy"


def call(body, ins, outs, scratch=(), limit=40, name=None, fetch=()):
    spaces = {PIN: pltpu.VMEM, HBM: pltpu.HBM, COPY: pltpu.HBM}
    specs = {PIN: VMEM, HBM: pl.BlockSpec(memory_space=pltpu.HBM), COPY: VMEM}
    space_of = lambda spec: spaces[spec] if isinstance(spec, str) else None
    spec_of = lambda spec: specs[spec] if isinstance(spec, str) else spec
    all_ins = list(ins) + [HBM] * len(fetch)
    all_outs = [out if len(out) > 2 else out + (VMEM,) for out in outs]
    homes = {}
    for array in fetch:
        homes.setdefault(array.shape[-2:], []).append(array)
    homes = list(homes.items())
    fetch = [array for _, arrays in homes for array in arrays]
    for shape, arrays in homes:
        count = sum(array.size for array in arrays) // (shape[0] * shape[1])
        all_outs.append(((count,) + shape, arrays[0].dtype, PIN))
    scratch = list(scratch)
    inner = body
    if fetch:
        parts = 4
        scratch.append(pltpu.SemaphoreType.DMA((len(fetch) * parts,)))

        def inner(*refs):
            sems, n_in = refs[-1], len(ins)
            far, rest = refs[n_in : n_in + len(fetch)], refs[n_in + len(fetch) :]
            near, last = rest[len(outs) : len(outs) + len(homes)], len(outs) + len(homes)
            rest = rest[: len(outs)] + rest[last:-1]
            far = list(far)
            copies = []
            for b, (shape, arrays) in zip(near, homes):
                at = 0
                for _ in arrays:
                    a = far.pop(0)
                    wide = a.shape[0] if len(a.shape) > 2 else 1
                    rows = shape[0] // parts
                    for k in range(parts):
                        piece = slice(k * rows, (k + 1) * rows)
                        if len(a.shape) > 2:
                            pair = a.at[:, piece], b.at[slice(at, at + wide), piece]
                        else:
                            pair = a.at[piece], b.at[at, piece]
                        copies.append(pltpu.make_async_copy(*pair, sems.at[len(copies)]))
                    at += wide

            def begin():
                for copy in copies:
                    copy.start()

            body(begin, *refs[:n_in], *rest)
            for copy in copies:
                copy.wait()

    kernel = pl.pallas_call(
        inner,
        in_specs=[spec_of(spec) for spec in all_ins],
        out_specs=[spec_of(out[2]) for out in all_outs],
        out_shape=[
            space_of(out[2])(out[0], out[1]) if space_of(out[2]) else jax.ShapeDtypeStruct(out[0], out[1])
            for out in all_outs
        ],
        scratch_shapes=scratch,
        compiler_params=pltpu.CompilerParams(vmem_limit_bytes=limit * MIB),
        cost_estimate=pl.CostEstimate(flops=1, bytes_accessed=1, transcendentals=0),
        name=name,
    )

    def run(*args):
        args = list(args) + list(fetch)
        held = [
            pltpu.with_memory_space_constraint(arg, space_of(spec)) if space_of(spec) else arg
            for arg, spec in zip(args, all_ins)
        ]
        return kernel(*held)

    return run


def pull(pairs, sems):
    copies = [pltpu.make_async_copy(far, near, sems.at[k]) for k, (far, near) in enumerate(pairs)]
    for copy in copies:
        copy.start()
    return copies


def collect(chunks, stage, me, count):
    for k, chunk in enumerate(chunks):
        stage[lax.rem(me + count - k, count)] = chunk[...]


def summaries(groups, gathered, me):
    pairs = []
    for j, group in enumerate(groups):
        for i in range(2):
            pairs.append((group.at[i], gathered.at[jnp.bitwise_xor(me, 2 * j + i)]))
    return pairs


def gates(embedded, gate_w, gate_b, cand_w, upd, cand):
    for r in range(2):
        upd[r] = jax.nn.sigmoid(dot(embedded, gate_w[r]) + gate_b[r : r + 1])
        cand[r] = dot(embedded, cand_w[r])


def one_hot_rows(ids, seqs, steps):
    rows = []
    for s in range(seqs):
        for g in range(SEGS):
            rows.append(ids[s : s + 1, g * steps : (g + 1) * steps] + s * LANES)
    held = jnp.concatenate(rows, axis=0)
    place = lax.broadcasted_iota(jnp.int32, (seqs * SEGS, seqs * LANES), 1)
    return jnp.concatenate(
        [(place == held[:, t : t + 1]).astype(F32).astype(BF16) for t in range(steps)], axis=0
    )


def chars_forward_body(
    seqs, steps, per, sub,
    lang, ids, gate_b, table, gate_w_far, cand_w_far,
    embedded_out, htok, ptok, pre, pseg, payload,
    upd, cand, hseg, padded_table, gate_w, cand_w, sems,
):
    rows = seqs * SEGS
    vocab = table.shape[0]
    wide = padded_table.shape[0]
    copies = pull(
        [(table, padded_table.at[0:vocab]), (gate_w_far, gate_w), (cand_w_far, cand_w)], sems
    )
    padded_table[vocab:wide] = jnp.zeros((wide - vocab, padded_table.shape[1]), BF16)
    copies[0].wait()
    local = lax.broadcasted_iota(jnp.int32, (LANES, wide), 0)
    place = lax.broadcasted_iota(jnp.int32, (LANES, wide), 1)
    mine = []
    for s in range(seqs):
        pick = (place == lang[s] * sub + local) & (local < sub)
        mine.append(dot(pick.astype(BF16), padded_table[...]).astype(BF16))
    own_table = jnp.concatenate(mine, axis=0)
    embedded = dot(one_hot_rows(ids, seqs, steps), own_table).astype(BF16)
    embedded_out[...] = embedded
    copies[1].wait()
    copies[2].wait()
    gates(embedded, gate_w, gate_b[...], cand_w, upd, cand)

    def token(q, carry):
        h0, p0, h1, p1 = carry
        for j in range(per):
            at = pl.ds(pl.multiple_of((q * per + j) * rows, rows), rows)
            u = upd[0, at, :]
            h0 = h0 + u * (cand[0, at, :] - h0)
            p0 = p0 * (1.0 - u)
            at = pl.ds(pl.multiple_of((steps - 1 - q * per - j) * rows, rows), rows)
            u = upd[1, at, :]
            h1 = h1 + u * (cand[1, at, :] - h1)
            p1 = p1 * (1.0 - u)
        htok[0, q] = h0
        ptok[0, q] = p0
        back = steps // per - 1 - q
        htok[1, back] = h1
        ptok[1, back] = p1
        return h0, p0, h1, p1

    zero = jnp.zeros((rows, upd.shape[2]), F32)
    h0, p0, h1, p1 = lax.fori_loop(0, steps // per, token, (zero, zero + 1.0, zero, zero + 1.0))
    pseg[0], pseg[1], hseg[0], hseg[1] = p0, p1, h0, h1
    last = steps // per - 1
    for s in range(seqs):
        for r in range(2):
            total_a = jnp.ones((1, upd.shape[2]), F32)
            total_b = jnp.zeros((1, upd.shape[2]), F32)
            order = range(SEGS) if r == 0 else range(SEGS - 1, -1, -1)
            for g in order:
                row = s * SEGS + g
                pre[0, r, row : row + 1] = total_a
                pre[1, r, row : row + 1] = total_b
                p_row = pseg[r, row : row + 1]
                total_b = p_row * total_b + hseg[r, row : row + 1]
                total_a = p_row * total_a
            edge = s * SEGS if r == 0 else s * SEGS + SEGS - 1
            q = 0 if r == 0 else last
            near_a, near_b = ptok[r, q, edge : edge + 1], htok[r, q, edge : edge + 1]
            for k, value in enumerate((total_a, total_b, near_a, near_b)):
                row = (4 * r + k) * seqs + s
                payload[row : row + 1] = value


def spread(values, seqs):
    wide = values.shape[1]
    return jnp.concatenate(
        [jnp.broadcast_to(values[s : s + 1], (SEGS, wide)) for s in range(seqs)], axis=0
    )


def token_row(token, tokens, per_seg, seqs):
    s = token // tokens
    t = token % tokens
    return (t % per_seg) * (seqs * SEGS) + s * SEGS + t // per_seg


def join_query_body(
    count, seqs, tokens, pairs,
    me_ref, htok, ptok, pre, join_b, query_b, value_b, join_w, query_w, key_w, value_w, inputs_far,
    *rest,
):
    groups, rest = rest[: count // 2], rest[count // 2 :]
    resid_out, enter, left_out = rest[:3]
    chunks = rest[3 : 3 + count]
    held, near_w, inputs, sems, stage = rest[3 + count :]
    me = me_ref[0]
    width = near_w.shape[1]

    def emit(k, values):
        left_out[:, k * width : (k + 1) * width] = values

    wanted = [(join_w.at[k], near_w.at[k]) for k in range(3)] + [(inputs_far, inputs)]
    wanted += [(far, near_w.at[3 + k]) for k, far in enumerate((query_w, key_w, value_w))]
    copies = pull(summaries(groups, held, me) + wanted, sems)
    for copy in copies[:count]:
        copy.wait()
    copies = copies[count:]
    half = htok.shape[3]

    def gathered(j, k):
        return held[j, k * seqs : (k + 1) * seqs]

    per_seg = htok.shape[1]
    total = seqs * tokens
    x0 = jnp.zeros((seqs, half), F32)
    x1 = jnp.zeros((seqs, half), F32)
    for j in range(count):
        x0 = jnp.where(j < me, gathered(j, 0) * x0 + gathered(j, 1), x0)
        i = count - 1 - j
        x1 = jnp.where(i > me, gathered(i, 4) * x1 + gathered(i, 5), x1)
    carry0 = pre[0, 0] * spread(x0, seqs) + pre[1, 0]
    carry1 = pre[0, 1] * spread(x1, seqs) + pre[1, 1]
    enter[0] = carry0
    enter[1] = carry1
    forward = htok[0] + ptok[0] * carry0[None]
    backward = htok[1] + ptok[1] * carry1[None]
    rows = seqs * SEGS
    last = per_seg - 1
    f_last = jnp.concatenate(
        [forward[last, s * SEGS + SEGS - 1 : s * SEGS + SEGS] for s in range(seqs)], axis=0
    )
    b_first = jnp.concatenate(
        [backward[0, s * SEGS : s * SEGS + 1] for s in range(seqs)], axis=0
    )
    left = jnp.maximum(me - 1, 0)
    right = jnp.minimum(me + 1, count - 1)
    left_b = gathered(left, 6) * b_first + gathered(left, 7)
    right_f = gathered(right, 2) * f_last + gathered(right, 3)
    left_row = jnp.where(me > 0, jnp.concatenate([x0, left_b], axis=1), 0.0)
    right_row = jnp.where(me < count - 1, jnp.concatenate([right_f, x1], axis=1), 0.0)
    rim = jnp.concatenate(
        [left_row, right_row, jnp.zeros((16 - 2 * seqs, 2 * half), F32)], axis=0
    ).astype(BF16)
    tokens_perm = jnp.concatenate(
        [forward.reshape(total, half), backward.reshape(total, half)], axis=1
    ).astype(BF16)
    source = jnp.concatenate([tokens_perm, rim], axis=0)
    token = lax.broadcasted_iota(jnp.int32, (total, total + 16), 0)
    place = lax.broadcasted_iota(jnp.int32, (total, total + 16), 1)
    joining = jnp.broadcast_to(join_b[...][None], (total, 2 * half))
    for k in range(3):
        moved = token + (k - 1)
        want = token_row(moved, tokens, per_seg, seqs)
        if k == 0:
            want = jnp.where(token % tokens == 0, total + token // tokens, want)
        if k == 2:
            want = jnp.where(token % tokens == tokens - 1, total + seqs + token // tokens, want)
        tap = dot((place == want).astype(BF16), source).astype(BF16)
        emit(1 + k, tap)
        copies[k].wait()
        joining = joining + dot(tap, near_w[k])
    copies[3].wait()
    resid = inputs[...].astype(F32) + joining
    resid_out[...] = resid
    low = resid.astype(BF16)
    emit(0, low)
    size = 2 * half // HEADS
    wide = pairs * size
    copies[4].wait()
    query = (dot(low, near_w[3]) + query_b[...][None]).astype(BF16)
    copies[5].wait()
    key = dot(low, near_w[4]).astype(BF16)
    copies[6].wait()
    value = (dot(low, near_w[5]) + value_b[...][None]).astype(BF16)
    send_pairs((query, key, value), stage, chunks, me, count, seqs, tokens, pairs, size, wide)


def send_pairs(arrays, stage, chunks, me, count, seqs, tokens, pairs, size, wide):
    for d in range(count):
        for a, array in enumerate(arrays):
            first = d * pairs
            if first >= seqs * HEADS:
                stage[d, :, a * wide : (a + 1) * wide] = jnp.zeros((tokens, wide), BF16)
                continue
            s, head = first // HEADS, first % HEADS
            stage[d, :, a * wide : (a + 1) * wide] = array[
                s * tokens : (s + 1) * tokens, head * size : head * size + wide
            ]
    for k in range(count):
        chunks[k][...] = stage[lax.rem(me + k, count)]


def receive_pairs(stage, place, count, seqs, pairs, size, parts):
    wide = pairs * size
    for d in range(count):
        first = d * pairs
        if first >= seqs * HEADS:
            continue
        s, head = first // HEADS, first % HEADS
        for a in range(parts):
            place(a, s, head * size, stage[d, :, a * wide : (a + 1) * wide])


def load_heads(chunks, me, count, tokens, pairs, size, part, target, scale=None):
    wide = pairs * size
    for k in range(count):
        at = block_of(me, count - k, count, tokens)
        for h in range(pairs):
            lane = part * wide + h * size
            block = chunks[k][:, lane : lane + size]
            target[h, at, 0:size] = block if scale is None else block * scale


def pair_length(lengths, me, pairs, h, seqs):
    return lengths[jnp.minimum((me * pairs + h) // HEADS, seqs - 1)]


def transposed(values):
    return jnp.transpose(values.astype(F32))


def mask_lanes(q, k, full, valid, size):
    shape = (full, k.shape[2] - size)
    lane = lax.broadcasted_iota(jnp.int32, shape, 1)
    key_at = lax.broadcasted_iota(jnp.int32, shape, 0)
    ones = jnp.where(lane == 0, 1.0, 0.0).astype(BF16)
    mask = jnp.where((lane == 0) & (key_at >= valid), MASKED, 0.0).astype(BF16)
    for h in range(k.shape[0]):
        q[h, :, size:] = ones
        k[h, :, size:] = mask


def attend_body(count, seqs, tokens, pairs, size, block, begin, me_ref, lengths, *rest):
    chunks, rest = rest[:count], rest[count:]
    outs, lse, far = rest[:count], rest[count], rest[count + 1 : count + 4]
    q, k, v, vt, mixed_t, mixed, sems = rest[count + 4 :]
    me = me_ref[0]
    full = count * tokens
    begin()
    load_heads(chunks, me, count, tokens, pairs, size, 0, q, jnp.asarray(0.125, BF16))
    load_heads(chunks, me, count, tokens, pairs, size, 1, k)
    load_heads(chunks, me, count, tokens, pairs, size, 2, v)
    lse[...] = jnp.zeros_like(lse)
    mask_lanes(q, k, full, pair_length(lengths, me, pairs, 0, seqs), size)
    copies = pull(list(zip((q, k, v), far)), sems)
    for h in range(pairs):
        vt[h, 0:size] = transposed(v[h, :, 0:size]).astype(BF16)
        row = lax.broadcasted_iota(jnp.int32, (vt.shape[1] - size, full), 0)
        vt[h, size:] = jnp.where(row == 0, 1.0, 0.0).astype(BF16)

        def rows(i, _, h=h):
            at = pl.ds(pl.multiple_of(i * block, block), block)
            scores = dot_nt(k[h], q[h, at, :])
            top = jnp.max(scores, axis=0, keepdims=True)
            sums = dot(vt[h], jnp.exp(scores - top).astype(BF16))
            total = sums[size : size + 1]
            lse[h : h + 1, at] = top + jnp.log(total)
            mixed_t[h * size : (h + 1) * size, at] = sums[0:size] / total
            return 0

        lax.fori_loop(0, full // block, rows, 0, unroll=2)
    mixed[...] = transposed(mixed_t[...]).astype(BF16)
    for j in range(count):
        outs[j][...] = mixed[block_of(me, j, count, tokens), :]
    for copy in copies:
        copy.wait()


def block_of(me, j, count, tokens):
    return pl.ds(pl.multiple_of(lax.rem(me + j, count) * tokens, tokens), tokens)


def attend_back_body(count, seqs, tokens, pairs, size, block, begin, me_ref, lse, *rest):
    far, d_chunks, rest = rest[:3], rest[3 : 3 + count], rest[3 + count :]
    outs = rest[:count]
    q, k, v, kt, d_o, dq_t, probs_all, d_scores_all, stage, sems = rest[count:]
    me = me_ref[0]
    full = count * tokens
    wide = pairs * size
    copies = pull(list(zip(far, (q, k, v))), sems)
    load_heads(d_chunks, me, count, tokens, pairs, size, 0, d_o)
    for copy in copies:
        copy.wait()
    begin()
    for h in range(pairs):
        kt[...] = transposed(k[h, :, 0:size]).astype(BF16)

        def rows(i, _, h=h):
            at = pl.ds(pl.multiple_of(i * block, block), block)
            probs = jnp.exp(dot_nt(k[h], q[h, at, :]) - lse[h : h + 1, at])
            d_probs = dot_nt(v[h, :, 0:size], d_o[h, at, :])
            probs_all[:, at] = probs.astype(BF16)
            row_dot = jnp.sum(probs * d_probs, axis=0, keepdims=True)
            d_scores_all[:, at] = (probs * (d_probs - row_dot)).astype(BF16)
            return 0

        lax.fori_loop(0, full // block, rows, 0, unroll=2)
        dq_t[h * size : (h + 1) * size, :] = dot(kt[...], d_scores_all[...]) * 0.125
        for part, grad in (
            (1, dot(d_scores_all[...], q[h])), (2, dot(probs_all[...], d_o[h])),
        ):
            lane = part * wide + h * size
            stage[:, lane : lane + size] = grad[:, 0:size].astype(BF16)
    stage[:, 0:wide] = transposed(dq_t[...]).astype(BF16)
    for j in range(count):
        outs[j][...] = stage[block_of(me, j, count, tokens), :]


def normed(values):
    center = values - jnp.mean(values, axis=-1, keepdims=True)
    scale = lax.rsqrt(jnp.mean(center * center, axis=-1, keepdims=True) + NORM_EPS)
    return center * scale, scale


def norm_back(cotangent, unit, scale, gain):
    d_unit = cotangent * gain
    mean = jnp.mean(d_unit, axis=-1, keepdims=True)
    lean = jnp.mean(d_unit * unit, axis=-1, keepdims=True)
    return scale * (d_unit - mean - unit * lean)


GELU_A = 0.7978845608028654
GELU_B = 0.044715


def feed_body(
    count, seqs, tokens, pairs, size, block,
    me_ref, out_b, gain1, shift1, up_b, down_b, gain2, shift2,
    resid, out_v, up_v, cotangent_far, down_far,
    *rest,
):
    chunks, rest = rest[:count], rest[count:]
    output_far, d_first_in_out, vec, up_vec, lefts, keep_out, send_out = rest[:7]
    outs = rest[7 : 7 + count]
    out_v, up_v = out_v.at[0], up_v.at[0]
    stage, slope, acc, cotangent, output, d_hidden_v, d_second_v, down_v, sems = rest[7 + count :]
    me, core = me_ref[0], me_ref[1]
    width = out_v.shape[0]
    ff = up_v.shape[1]
    parts = ff // block
    mixed = lefts.at[:, ff + width : ff + 2 * width]
    first_low_v = lefts.at[:, ff : ff + width]

    def emit_halves(source, lane, wide):
        for out, part in ((keep_out, core), (send_out, 1 - core)):
            at = pl.ds(pl.multiple_of(part * wide, LANES), wide)
            out[:, lane : lane + wide] = source[:, at]

    pieces = [slice(j * block, (j + 1) * block) for j in range(parts)]
    first_copies = pull(
        [(cotangent_far, cotangent)]
        + [(down_far.at[piece], down_v.at[piece]) for piece in pieces],
        sems,
    )
    collect(chunks, stage, me, count)

    def lanes(j):
        return pl.ds(pl.multiple_of(j * block, block), block)

    def place(part, s, lane, values):
        mixed[s * tokens : (s + 1) * tokens, lane : lane + values.shape[1]] = values

    receive_pairs(stage, place, count, seqs, pairs, size, 1)
    first_in = resid[...] + dot(mixed[...], out_v[...]) + out_b[...][None]
    unit1, scale1 = normed(first_in)
    first = unit1 * gain1[...][None] + shift1[...][None]
    first_low = first.astype(BF16)
    first_low_v[...] = first_low
    acc[...] = first + down_b[...][None]

    def ahead(j, _):
        hidden = dot(first_low_v[...], up_v[:, lanes(j)]) + up_b[lanes(j)][None]
        square = hidden * hidden
        bend = jnp.tanh(GELU_A * (hidden + GELU_B * (square * hidden)))
        act = (0.5 * hidden * (1.0 + bend)).astype(BF16)
        lefts[:, lanes(j)] = act
        slope[:, lanes(j)] = 0.5 * (1.0 + bend) + 0.5 * hidden * (1.0 - bend * bend) * (
            GELU_A * (1.0 + 3.0 * GELU_B * square)
        )
        first_copies[1 + j].wait()
        acc[...] += dot(act, down_v[lanes(j), :])

    for j in range(parts):
        ahead(j, 0)
    unit2, scale2 = normed(acc[...])
    first_copies[0].wait()
    output[...] = (unit2 * gain2[...][None] + shift2[...][None]).astype(BF16)
    done = pltpu.make_async_copy(output, output_far, sems.at[1 + parts])
    done.start()
    cot = cotangent[...].astype(F32)
    vec[0:1] = column_sum(cot * unit2)
    vec[1:2] = column_sum(cot)
    d_second_in = norm_back(cot, unit2, scale2, gain2[...][None])
    d_second = d_second_in.astype(BF16)
    d_second_v[...] = d_second
    emit_halves(d_second_v, ff // 2, width // 2)
    vec[2:3] = column_sum(d_second)
    acc[...] = d_second_in

    def astern(j, _):
        d_act = dot_nt(d_second_v[...], down_v[lanes(j), :])
        d_hidden = (d_act * slope[:, lanes(j)]).astype(BF16)
        d_hidden_v[:, lanes(j)] = d_hidden
        up_vec[:, lanes(j)] = column_sum(d_hidden)
        acc[...] += dot_nt(d_hidden, up_v[:, lanes(j)])
        return 0

    lax.fori_loop(0, parts, astern, 0, unroll=True)
    emit_halves(d_hidden_v, 0, ff // 2)
    d_first = acc[...]
    vec[3:4] = column_sum(d_first * unit1)
    vec[4:5] = column_sum(d_first)
    d_first_in = norm_back(d_first, unit1, scale1, gain1[...][None])
    d_first_in_out[...] = d_first_in
    d_attn = d_first_in.astype(BF16)
    d_second_v[...] = d_attn
    emit_halves(d_second_v, ff // 2 + width // 2, width // 2)
    vec[5:6] = column_sum(d_attn)
    vec[6:8] = jnp.zeros((2, vec.shape[1]), F32)
    d_mixed = dot_nt(d_attn, out_v[...]).astype(BF16)
    send_pairs((d_mixed,), stage, outs, me, count, seqs, tokens, pairs, size, pairs * size)
    done.wait()


def fetch_columns(arrays, lanes, sems, at):
    copies = []
    for far, near in arrays:
        copy = pltpu.make_async_copy(far.at[:, lanes], near.at[:, lanes], sems.at[at + len(copies)])
        copy.start()
        copies.append(copy)
    return copies


def feed_grads_body(ff, lefts, left_got, rights, right_got, out, lefts_got, rights_got, res, sems):
    half = out.shape[-1]
    width = 2 * half
    blocks = out.shape[0]
    step = ff // blocks
    lane = lambda far, near, at, size: (far.at[:, at : at + size], near.at[:, at : at + size])
    first = ff // 2
    waves = [lane(right_got, rights_got, first, half)]
    for j in range(blocks):
        waves.append(lane(left_got, lefts_got, j * step, step))
    waves += [lane(left_got, lefts_got, ff, width), lane(right_got, rights_got, 0, first)]
    waves += [lane(left_got, lefts_got, ff + width, width)]
    waves += [lane(right_got, rights_got, first + half, half)]
    copies = [pltpu.make_async_copy(far, near, sems.at[k]) for k, (far, near) in enumerate(waves)]
    for copy in copies:
        copy.start()
    waited = [0]

    def wait(count):
        for copy in copies[waited[0] : waited[0] + count]:
            copy.wait()
        waited[0] += count

    outgoing = []

    def emit(place):
        at = sems.at[len(copies) + len(outgoing)]
        copy = pltpu.make_async_copy(res.at[place], out.at[place], at)
        copy.start()
        outgoing.append(copy)

    def grad(at, size, begin):
        rows, lanes = slice(at, at + size), slice(begin, begin + half)
        return dot_tn(lefts[:, rows], rights[:, lanes]) + dot_tn(lefts_got[:, rows], rights_got[:, lanes])

    whole = slice(None)
    owners = 1
    for size in out.shape[:-2]:
        owners *= size
    pieces = (ff + width) // width
    up_rows = width // owners
    down_rows = ff // owners
    start = pieces * up_rows
    mids = (whole,) * (len(out.shape) - 3)
    by_piece = up_rows % 16 == 0 and down_rows % 16 == 0
    wait(1)
    for j in range(blocks):
        wait(1)
        part = grad(j * step, step, first)
        spread_rows(res, (j,), slice(start, start + down_rows), part)
        if by_piece:
            emit((j,) + mids + (slice(start, start + down_rows), whole))
    wait(2)
    for k in range(pieces):
        if k == pieces - 1:
            wait(2)
            part = grad(ff + width, width, first + half)
        else:
            part = grad(ff, width, k * half)
        rows = slice(k * up_rows, (k + 1) * up_rows)
        spread_rows(res, (), rows, part)
        if by_piece:
            emit((whole,) + mids + (rows, whole))
    if not by_piece:
        emit((whole,) * len(out.shape))
    for copy in outgoing:
        copy.wait()


def spread_rows(res, head, rows, grad):
    size = rows.stop - rows.start
    wide = res.shape[len(head) : -2]
    if size % 16 == 0:
        at = head + (slice(None),) * len(wide) + (rows, slice(None))
        res[at] = grad.astype(BF16).reshape(wide + (size, grad.shape[1]))
        return
    places = [()]
    for count in wide:
        places = [place + (k,) for place in places for k in range(count)]
    for k, place in enumerate(places):
        res[head + place + (rows, slice(None))] = grad[k * size : (k + 1) * size].astype(BF16)


def feed_grads(left, left_got, right, right_got, ff, width):
    tokens = left.shape[0]
    count, groups = lax.axis_size("seq"), lax.axis_size("dp")
    places = bits_of(count)[1:]
    owners = count * groups // 2
    rows = (ff + width) // width * (width // owners) + ff // owners
    shape = (groups,) + (2,) * len(places) + (rows, width // 2)
    (out,) = call(
        functools.partial(feed_grads_body, ff),
        [PIN, HBM, PIN, HBM],
        [(shape, BF16, HBM)],
        [
            pltpu.VMEM((tokens, ff + 2 * width), BF16),
            pltpu.VMEM((tokens, ff // 2 + width), BF16),
            pltpu.VMEM(shape, BF16),
            pltpu.SemaphoreType.DMA((10 + 3 * groups + (ff + width) // width,)),
        ],
        name="grad_feed",
    )(left, left_got, right, right_got)
    return out


def store_rows(res, lanes, grad):
    rows = res.shape[-2]
    if rows % 16 == 0:
        res[..., lanes] = grad.astype(BF16).reshape(res.shape[:-1] + (grad.shape[1],))
        return
    places = [()]
    for wide in res.shape[:-2]:
        places = [place + (k,) for place in places for k in range(wide)]
    for k, place in enumerate(places):
        res[place + (slice(None), lanes)] = grad[k * rows : (k + 1) * rows].astype(BF16)


def outer_body(plan, cut, bits_ref, lefts, left_got, rights, right_got, *rest):
    low_send, low_keep, high_send, high_keep = rest[:4]
    lefts_got, rights_got, res, sems = rest[4:]
    height = lefts.shape[1] // len({lane for lane, _, _ in plan})
    waits = []
    for number, (lane, first, wide) in enumerate(plan):
        copies = []
        for far, near, at, size, seen in (
            (left_got, lefts_got, lane, height, [other[0] for other in plan[:number]]),
            (right_got, rights_got, first, wide, [other[1] for other in plan[:number]]),
        ):
            if at not in seen:
                lanes = slice(at, at + size)
                sem = sems.at[sum(map(len, waits)) + len(copies)]
                copies.append(pltpu.make_async_copy(far.at[:, lanes], near.at[:, lanes], sem))
        waits.append(copies)
        for copy in copies:
            copy.start()
    used = sum(map(len, waits))
    low, high = bits_ref[0], bits_ref[1]
    outgoing = []
    whole = slice(None)
    mids = len(res.shape) - 4

    def emit(low_half):
        if low_half:
            place = lambda which: (whole,) * (1 + mids) + (which, whole, slice(0, cut))
            pairs = ((low_send, 1 - low), (low_keep, low))
        else:
            place = lambda which: (whole, which) + (whole,) * (1 + mids) + (slice(cut, res.shape[-1]),)
            pairs = ((high_send, 1 - high), (high_keep, high))
        for out, which in pairs:
            copy = pltpu.make_async_copy(res.at[place(which)], out, sems.at[used + len(outgoing)])
            copy.start()
            outgoing.append(copy)

    lane_at = 0
    for number, (lane, first, wide) in enumerate(plan):
        for copy in waits[number]:
            copy.wait()
        for k in range(0, wide, 512):
            size = min(512, wide - k)
            lanes = slice(first + k, first + k + size)
            grad = dot_tn(lefts[:, lane : lane + height], rights[:, lanes])
            grad = grad + dot_tn(lefts_got[:, lane : lane + height], rights_got[:, lanes])
            lanes = slice(lane_at + k, lane_at + k + size)
            store_rows(res, lanes, grad)
            if lane_at + k + size == cut:
                emit(True)
        lane_at += wide
    emit(False)
    for copy in outgoing:
        copy.wait()


def outer_grads(arrays, plan, cut, height, name):
    count, groups = lax.axis_size("seq"), lax.axis_size("dp")
    places = bits_of(count)[1:]
    rows = 2 * height // (count * groups)
    tokens = arrays[0].shape[0]
    wide = sum(piece[2] for piece in plan)
    lefts = len({piece[0] for piece in plan})
    shape = (groups,) + (2,) * len(places) + (rows,)
    less = (groups,) + (2,) * (len(places) - 1) + (rows,)
    seq = lax.axis_index("seq")
    bits = jnp.stack([(seq // places[0]) % 2, (seq // places[-1]) % 2]).astype(jnp.int32)
    return call(
        functools.partial(outer_body, plan, cut),
        [SMEM, COPY, HBM, PIN, HBM],
        [(less + (cut,), BF16, HBM)] * 2 + [(less + (wide - cut,), BF16, HBM)] * 2,
        [
            pltpu.VMEM((tokens, lefts * height), BF16),
            pltpu.VMEM((tokens, arrays[2].shape[1]), BF16),
            pltpu.VMEM(shape + (wide,), BF16),
            pltpu.SemaphoreType.DMA((4 * len(plan) + 4,)),
        ],
        name=name,
    )(bits, *arrays)


def project_back_body(
    count, seqs, tokens, pairs, size, per_seg,
    me_ref, pre, d_first_in, ptok, near_w,
    *rest,
):
    chunks, rest = rest[:count], rest[count:]
    grad_out, d_perm, payload, vec, keep_out, send_out = rest[:6]
    stage, rights = rest[6:]
    me, core = me_ref[0], me_ref[1]
    width = near_w.shape[1]

    def emit_halves(part):
        wide = width // 2
        for out, which in ((keep_out, core), (send_out, 1 - core)):
            at = pl.ds(pl.multiple_of(part * width + which * wide, LANES), wide)
            out[:, part * wide : (part + 1) * wide] = rights[:, at]

    collect(chunks, stage, me, count)
    targets = [rights.at[:, k * width : (k + 1) * width] for k in range(4)]

    def place(part, s, lane, values):
        at = part * width + lane
        rights[s * tokens : (s + 1) * tokens, at : at + values.shape[1]] = values

    receive_pairs(stage, place, count, seqs, pairs, size, 3)
    for part in range(3):
        emit_halves(part)
    d_resid = d_first_in[...]
    for k in range(3):
        d_resid = d_resid + dot_nt(targets[k][...], near_w[3 + k])
    grad = d_resid.astype(BF16)
    grad_out[...] = grad
    targets[3][...] = grad
    emit_halves(3)
    vec[0:1] = column_sum(targets[0][...])
    vec[1:2] = column_sum(targets[2][...])
    vec[2:3] = column_sum(grad)
    vec[3:8] = jnp.zeros((5, vec.shape[1]), F32)
    total = seqs * tokens
    half = vec.shape[1] // 2
    row = lax.broadcasted_iota(jnp.int32, (total + 16, total), 0)
    place_at = lax.broadcasted_iota(jnp.int32, (total + 16, total), 1)
    rows = seqs * SEGS
    step, rest_row = row // rows, row % rows
    seq = rest_row // SEGS
    tok = (rest_row % SEGS) * per_seg + step
    extra = row - total
    seq = jnp.where(extra >= 0, extra % seqs, seq)
    tok = jnp.where(extra >= 0, jnp.where(extra < seqs, -1, tokens), tok)
    known = extra < 2 * seqs
    d_char = jnp.zeros((total + 16, 2 * half), F32)
    for k in range(3):
        moved = tok + 1 - k
        pick = (place_at == seq * tokens + moved) & (moved >= 0) & (moved < tokens) & known
        shifted = dot(pick.astype(BF16), grad).astype(BF16)
        d_char = d_char + dot_nt(shifted, near_w[k])
    payload[6 * seqs :] = jnp.zeros((payload.shape[0] - 6 * seqs, half), F32)
    for r in range(2):
        grads = d_char[0:total, r * half : (r + 1) * half].reshape(per_seg, rows, half)
        d_perm[r] = grads
        weighted = jnp.sum(grads * ptok[r], axis=0) * pre[0, r]
        for s in range(seqs):
            row = r * seqs + s
            payload[row : row + 1] = column_sum(weighted[s * SEGS : (s + 1) * SEGS])
        edges = d_char[total : total + 2 * seqs, r * half : (r + 1) * half]
        payload[(2 + r) * seqs : (3 + r) * seqs] = edges[0:seqs]
        payload[(4 + r) * seqs : (5 + r) * seqs] = edges[seqs : 2 * seqs]


def chars_back_body(
    count, seqs, steps, per,
    lang, me_ref, ids, gate_b, enter, pseg, vec1, up_vec, vec2, embedded, ptok, d_perm, gate_w_far, cand_w_far,
    *rest,
):
    groups, back_groups, rest = rest[: count // 2], rest[count // 2 : count], rest[count:]
    (
        keep_out, send_out,
        upd, work, d_all, d_tok, gseg, gin, gate_w, cand_w, held, back, sems, vector, owned,
    ) = rest
    me = me_ref[0]
    wanted = [(gate_w_far, gate_w), (cand_w_far, cand_w)]
    wanted += summaries(groups, held, me) + summaries(back_groups, back, me)
    copies = pull(wanted, sems)
    for copy in copies[:2]:
        copy.wait()

    def gathered(j, k):
        return held[j, k * seqs : (k + 1) * seqs]

    def gathered_back(j, k):
        return back[j, k * seqs : (k + 1) * seqs]

    rows = seqs * SEGS
    half = upd.shape[2]
    gates(embedded[...], gate_w, gate_b[...], cand_w, upd, work)

    def ahead(q, carry):
        h0, h1 = carry
        for j in range(per):
            at = pl.ds(pl.multiple_of((q * per + j) * rows, rows), rows)
            u = upd[0, at, :]
            gap = work[0, at, :] - h0
            work[0, at, :] = gap * (u * (1.0 - u))
            h0 = h0 + u * gap
            at = pl.ds(pl.multiple_of((steps - 1 - q * per - j) * rows, rows), rows)
            u = upd[1, at, :]
            gap = work[1, at, :] - h1
            work[1, at, :] = gap * (u * (1.0 - u))
            h1 = h1 + u * gap
        return h0, h1

    lax.fori_loop(0, steps // per, ahead, (enter[0], enter[1]))

    left = jnp.maximum(me - 1, 0)
    right = jnp.minimum(me + 1, count - 1)
    last = steps // per - 1
    for copy in copies[2:]:
        copy.wait()
    d_tok[...] = d_perm[...]
    for r in range(2):
        from_left = jnp.where(me > 0, gathered_back(left, 4 + r), 0.0)
        from_right = jnp.where(me < count - 1, gathered_back(right, 2 + r), 0.0)
        for s in range(seqs):
            low, high = s * SEGS, s * SEGS + SEGS - 1
            d_tok[r, 0, low : low + 1] += from_left[s : s + 1]
            d_tok[r, last, high : high + 1] += from_right[s : s + 1]
        gseg[r] = jnp.sum(d_tok[r] * ptok[r], axis=0)

    def block_sum(j, r):
        total = gathered_back(j, r)
        near, far = gathered(j, 4 * r + 2), gathered(j, 4 * r)
        if r == 1:
            near, far = far, near
        if j > 0:
            total = total + near * gathered_back(j - 1, 4 + r)
        if j < count - 1:
            total = total + far * gathered_back(j + 1, 2 + r)
        return total

    g0 = jnp.zeros((seqs, half), F32)
    g1 = jnp.zeros((seqs, half), F32)
    for j in range(count):
        i = count - 1 - j
        g0 = jnp.where(i > me, gathered(i, 0) * g0 + block_sum(i, 0), g0)
        g1 = jnp.where(j < me, gathered(j, 4) * g1 + block_sum(j, 1), g1)
    for s in range(seqs):
        flow = g0[s : s + 1]
        for g in range(SEGS - 1, -1, -1):
            row = s * SEGS + g
            gin[0, row : row + 1] = flow
            flow = pseg[0, row : row + 1] * flow + gseg[0, row : row + 1]
        flow = g1[s : s + 1]
        for g in range(SEGS):
            row = s * SEGS + g
            gin[1, row : row + 1] = flow
            flow = pseg[1, row : row + 1] * flow + gseg[1, row : row + 1]

    def astern(q, carry):
        flow0, flow1 = carry
        for j in range(per):
            at = pl.ds(pl.multiple_of((steps - 1 - q * per - j) * rows, rows), rows)
            if j == 0:
                flow0 = flow0 + d_tok[0, steps // per - 1 - q]
            u = upd[0, at, :]
            d_all[at, 0:half] = (flow0 * work[0, at, :]).astype(BF16)
            d_cand = flow0 * u
            d_all[at, half : 2 * half] = d_cand.astype(BF16)
            flow0 = flow0 - d_cand
            at = pl.ds(pl.multiple_of((q * per + j) * rows, rows), rows)
            if j == 0:
                flow1 = flow1 + d_tok[1, q]
            u = upd[1, at, :]
            d_all[at, 2 * half : 3 * half] = (flow1 * work[1, at, :]).astype(BF16)
            d_cand = flow1 * u
            d_all[at, 3 * half : 4 * half] = d_cand.astype(BF16)
            flow1 = flow1 - d_cand
        return flow0, flow1

    lax.fori_loop(0, steps // per, astern, (gin[0], gin[1]))
    grad_w = dot_tn(embedded[...], d_all[...])
    place_owned(owned, grad_w)
    d_emb = jnp.zeros(embedded.shape, F32)
    gate_sums = []
    for r in range(2):
        gate_sums.append(column_sum(d_all[:, 2 * r * half : (2 * r + 1) * half]))
        d_emb = d_emb + dot_nt(d_all[:, 2 * r * half : (2 * r + 1) * half], gate_w[r])
        d_emb = d_emb + dot_nt(d_all[:, (2 * r + 1) * half : (2 * r + 2) * half], cand_w[r])
    partial = dot_tn(one_hot_rows(ids, seqs, steps), d_emb.astype(BF16))
    local = lax.broadcasted_iota(jnp.int32, partial.shape, 0)
    for s in range(seqs):
        tag = lang[s].astype(F32)
        partial = jnp.where(local == s * LANES + LANES - 1, tag, partial)
    core = me_ref[1]
    wide = partial.shape[1] // 2
    low, high = partial[:, :wide].astype(BF16), partial[:, wide:].astype(BF16)
    rows = partial.shape[0]
    keep_out[0:rows] = jnp.where(core == 0, low, high)
    send_out[0:rows] = jnp.where(core == 0, high, low)
    sums = [vec1[k : k + 1] for k in range(6)] + [up_vec[...]]
    sums += [vec2[k : k + 1] for k in range(3)] + gate_sums
    vector[...] = jnp.zeros_like(vector)
    at = 0
    for values in sums:
        for k in range(values.shape[1] // LANES):
            vector[at : at + 1] = values[:, k * LANES : (k + 1) * LANES]
            at += 1
    put_low(send_out, rows, vector[...])
    keep_out[rows:] = owned[core].astype(BF16)
    send_out[rows + 2 * vector.shape[0] :] = owned[1 - core].astype(BF16)


def place_owned(owned, grad):
    count, groups = lax.axis_size("seq"), lax.axis_size("dp")
    rows = grad.shape[0] // (count * groups)
    tiles = grad.shape[1] // LANES
    bits = count.bit_length() - 1
    for d in range(groups):
        for s in range(count):
            mirrored = 0
            for b in range(1, bits):
                mirrored = mirrored * 2 + (s >> b) % 2
            at = (mirrored * groups + d) * rows * tiles
            first = (d * count + s) * rows
            for t in range(tiles):
                value = grad[first : first + rows, t * LANES : (t + 1) * LANES]
                owned[s % 2, at + t * rows : at + (t + 1) * rows] = value


def put_low(packed, at, vector):
    rows = vector.shape[0]
    high = vector.astype(BF16)
    packed[at : at + rows] = high
    packed[at + rows : at + 2 * rows] = (vector - high.astype(F32)).astype(BF16)


def get_low(packed, at, rows):
    return packed[at : at + rows].astype(F32) + packed[at + rows : at + 2 * rows].astype(F32)


def mix_body(rows, vector_rows, first, last, bits_ref, keep, sent, got, *outs):
    fixed = rows + 2 * vector_rows
    table = (keep if first else sent)[0:rows].astype(F32) + got[0:rows].astype(F32)
    vector = get_low(sent, rows, vector_rows) + get_low(got, rows, vector_rows)
    start = rows if first else 0
    size = keep.shape[0] - start
    if last:
        piece = size // len(outs)
        for k, out in enumerate(outs):
            which = jnp.bitwise_xor(bits_ref[0], k) * piece
            at = pl.ds(pl.multiple_of(start + which, 8), piece)
            from_got = pl.ds(pl.multiple_of(fixed + which, 8), piece)
            out[fixed:] = (keep[at].astype(F32) + got[from_got].astype(F32)).astype(BF16)
    else:
        piece = size // 2
        for out, bit in ((outs[0], 1 - bits_ref[0]), (outs[1], bits_ref[0])):
            at = pl.ds(pl.multiple_of(start + bit * piece, 16), piece)
            from_got = pl.ds(pl.multiple_of(fixed + bit * piece, 16), piece)
            total = (keep[at].astype(F32) + got[from_got].astype(F32)).astype(BF16)
            if out is outs[0]:
                out[fixed:] = total
            else:
                out[...] = total
    for out in outs if last else outs[:1]:
        out[0:rows] = table.astype(BF16)
        put_low(out, rows, vector)


def table_body(groups, seqs, sub, count, place_ref, *refs):
    own, other, rest = refs[:groups], refs[groups : 2 * groups], refs[2 * groups :]
    table, vector, gate_out, cand_out, low, high, vec, held = rest
    dp, core = place_ref[0], place_ref[1]
    vocab, width = table.shape
    half = width // 2
    rows = low.shape[1]
    for k in range(groups):
        at = jnp.bitwise_xor(dp, k)
        mine, their = own[k][0:rows], other[k][0:rows]
        low[at] = jnp.where(core == 0, mine, their)
        high[at] = jnp.where(core == 0, their, mine)
        vec[at] = get_low(own[k], rows, vector.shape[0])
    fixed = rows + 2 * vector.shape[0]
    mine = own[0][fixed:].astype(F32)
    for part in own[1:]:
        mine = mine + part[fixed:].astype(F32)
    held[...] = mine
    owned = gate_out.shape[1]
    tiles = held.shape[0] // owned // 4
    for k in range(4):
        home = (gate_out, cand_out)[k % 2]
        for t in range(tiles):
            at = (k * tiles + t) * owned
            home[k // 2, :, t * LANES : (t + 1) * LANES] = held[at : at + owned]
    wide = -(-vocab // 16) * 16
    row = lax.broadcasted_iota(jnp.int32, (wide, LANES), 0)
    local = lax.broadcasted_iota(jnp.int32, (wide, LANES), 1)
    left = jnp.zeros((wide, half), F32)
    right = jnp.zeros((wide, half), F32)
    total = jnp.zeros(vector.shape, F32)
    for g in range(groups):
        for s in range(seqs):
            tag = low[g, (s + 1) * LANES - 16 : (s + 1) * LANES, 0:1].astype(F32)[15:16]
            lang = (tag * (1.0 / count) + 0.5).astype(jnp.int32)
            pick = ((row - lang * sub == local) & (local < sub)).astype(BF16)
            left = left + dot(pick, low[g, s * LANES : (s + 1) * LANES])
            right = right + dot(pick, high[g, s * LANES : (s + 1) * LANES])
        total = total + vec[g]
    table[:, 0:half] = left[0:vocab]
    table[:, half:width] = right[0:vocab]
    vector[...] = total


def fold_body(bits_ref, *refs):
    ins, outs = refs[:4], refs[4:]
    for k in range(2):
        keep, got, bit = ins[2 * k], ins[2 * k + 1], bits_ref[k]
        for out, which in ((outs[2 * k], 1 - bit), (outs[2 * k + 1], bit)):
            out[...] = (keep[:, which].astype(F32) + got[:, which].astype(F32)).astype(BF16)


def halve_body(sizes, alone, bits_ref, *refs):
    ins, outs = refs[:-4], refs[-4:]
    owners = ins[0].shape[0]
    at = 0
    for k, size in enumerate(sizes):
        rows = slice(at, at + size) if alone else slice(0, size)
        parts = ins if alone else ins[2 * k : 2 * k + 2]
        for out, which in ((outs[2 * k], 1 - bits_ref[k]), (outs[2 * k + 1], bits_ref[k])):
            for i in range(owners // 2):
                place = which * (owners // 2) + i if k == 0 else 2 * i + which
                total = parts[0][place, rows].astype(F32)
                for part in parts[1:]:
                    total = total + part[place, rows].astype(F32)
                out[i] = total.astype(BF16)
        at += size if alone else 0


def part_rows_body(sizes, core_ref, kept, got, kept_on, got_on, send, keep):
    core = core_ref[0]
    total = jnp.concatenate(
        [a[...].astype(F32) + b[...].astype(F32) for a, b in ((kept, got), (kept_on, got_on))], axis=0
    )
    at = 0
    for size in sizes:
        first, second = total[2 * at : 2 * at + size], total[2 * at + size : 2 * at + 2 * size]
        send[at : at + size] = jnp.where(core == 0, second, first)
        keep[at : at + size] = jnp.where(core == 0, first, second)
        at += size


def beside_body(pieces, core_ref, keep, got, up, out, down):
    core = core_ref[0]
    wide = keep.shape[1]
    rows = up.shape[0]
    low = jnp.where(core == 0, keep[...], got[...])
    high = jnp.where(core == 0, got[...], keep[...])
    for k in range(pieces + 1):
        home, lane = (up, k * wide) if k < pieces else (out, 0)
        gap = up.shape[1] // 2 if k < pieces else wide
        home[:, lane : lane + wide] = low[k * rows : (k + 1) * rows]
        home[:, lane + gap : lane + gap + wide] = high[k * rows : (k + 1) * rows]
    down[:, 0:wide] = low[(pieces + 1) * rows :]
    down[:, wide : 2 * wide] = high[(pieces + 1) * rows :]


def part_cores_body(core_ref, low_keep, low_got, high_keep, high_got, send, keep):
    core = core_ref[0]
    rows = keep.shape[1]
    lane = 0
    for mine, got in ((low_keep, low_got), (high_keep, high_got)):
        wide = mine.shape[2]
        total = mine[...].astype(F32) + got[...].astype(F32)
        first, second = total[:, 0:rows], total[:, rows : 2 * rows]
        send[:, :, lane : lane + wide] = jnp.where(core == 0, second, first).astype(BF16)
        keep[:, :, lane : lane + wide] = jnp.where(core == 0, first, second).astype(BF16)
        lane += wide


def part_groups_body(widths, groups, place_ref, keep, got, own, *sends):
    dp, core = place_ref[0], place_ref[1]
    for k in range(groups):
        at = jnp.bitwise_xor(dp, k)
        mine, their = keep[at], got[at]
        out = own if k == 0 else sends[k - 1]
        lane = 0
        for wide in widths:
            a, b = mine[:, lane : lane + wide], their[:, lane : lane + wide]
            out[:, 2 * lane : 2 * lane + wide] = jnp.where(core == 0, a, b)
            out[:, 2 * lane + wide : 2 * lane + 2 * wide] = jnp.where(core == 0, b, a)
            lane += wide


def total_body(widths, groups, *refs):
    ins, outs = refs[:groups], refs[groups:]
    total = ins[0][...].astype(F32)
    for part in ins[1:]:
        total = total + part[...].astype(F32)
    lane = 0
    for out, wide in zip(outs, widths):
        out[...] = total[:, lane : lane + 2 * wide]
        lane += 2 * wide


def shift(array, by):
    count = lax.axis_size("seq")
    return lax.ppermute(array, "seq", [(i, (i + by) % count) for i in range(count)])


def swap(array, axis, bit):
    return lax.ppermute(array, axis, [(i, i ^ bit) for i in range(lax.axis_size(axis))])


def exchange(chunks):
    return [chunks[0]] + [shift(chunk, k) for k, chunk in enumerate(chunks) if k > 0]


def bits_of(count):
    return [1 << b for b in range(count.bit_length() - 1)]


def tie(arrays, *after):
    held = lax.optimization_barrier((tuple(arrays), after))
    return list(held[0])


def gather_summaries(rows):
    pair = jnp.stack([rows, swap(rows, "seq", 1)])
    return [pair] + [swap(pair, "seq", 2 * j) for j in range(1, lax.axis_size("seq") // 2)]


class Columns:
    def __init__(self, sends_and_keeps, widths):
        self.places = bits_of(lax.axis_size("seq"))[1:]
        self.seq = lax.axis_index("seq")
        self.widths = widths
        self.done = 0
        low_send, low_keep, high_send, high_keep = sends_and_keeps
        self.sends, self.keeps = (low_send, high_send), (low_keep, high_keep)
        self.hold_swap()

    def hold_swap(self):
        bits = self.places[self.done], self.places[-1 - self.done]
        self.gots = tuple(swap(send, "seq", bit) for send, bit in zip(self.sends, bits))
        self.done += 1

    def fold(self, *after):
        keeps, gots = self.keeps, self.gots
        if after:
            keeps = tie(keeps, *after)
        bits = self.places[self.done], self.places[-1 - self.done]
        chosen = jnp.stack([(self.seq // bit) % 2 for bit in bits]).astype(jnp.int32)
        flat, shapes = [], []
        for k, (keep, got) in enumerate(zip(keeps, gots)):
            dims = keep.shape
            if k == 0:
                flat += [x.reshape((-1, 2) + dims[-2:]) for x in (keep, got)]
                shapes.append(dims[:-3] + dims[-2:])
            else:
                flat += [x.reshape(dims[:2] + (-1, dims[-1])) for x in (keep, got)]
                shapes.append(dims[:1] + dims[2:])
        outs = []
        for k in range(2):
            dims = flat[2 * k].shape
            outs += [((dims[0],) + dims[2:], BF16)] * 2
        got = call(fold_body, [SMEM] + [VMEM] * 4, outs, limit=24, name="fold")(chosen, *flat)
        self.sends = (got[0].reshape(shapes[0]), got[2].reshape(shapes[1]))
        self.keeps = (got[1].reshape(shapes[0]), got[3].reshape(shapes[1]))
        self.hold_swap()

    def part_cores(self, *after):
        while self.done < len(self.places):
            self.fold()
        keeps = self.keeps
        if after:
            keeps = tie(keeps, *after)
        groups, rows, _ = keeps[0].shape
        wide = sum(self.widths)
        core = (self.seq % 2).astype(jnp.int32).reshape(1)
        self.send, self.keep = call(
            part_cores_body,
            [SMEM] + [VMEM] * 4,
            [((groups, rows // 2, wide), BF16)] * 2,
            limit=24,
            name="part_cores",
        )(core, keeps[0], self.gots[0], keeps[1], self.gots[1])
        self.got = swap(self.send, "seq", 1)

    def part_groups(self, *after):
        keep = self.keep
        if after:
            (keep,) = tie([keep], *after)
        groups, rows, wide = keep.shape
        place = jnp.stack([lax.axis_index("dp"), self.seq % 2]).astype(jnp.int32)
        self.own, *self.sends = call(
            functools.partial(part_groups_body, self.widths, groups),
            [SMEM] + [VMEM] * 2,
            [((rows, 2 * wide), BF16)] * groups,
            limit=24,
            name="part_groups",
        )(place, keep, self.got)
        self.gots = [swap(send, "dp", k + 1) for k, send in enumerate(self.sends)]

    def finish(self):
        groups = len(self.gots) + 1
        return call(
            functools.partial(total_body, self.widths, groups),
            [VMEM] * groups,
            [((self.own.shape[0], 2 * wide), F32) for wide in self.widths],
            limit=24,
            name="total",
        )(self.own, *self.gots)


class FeedRows:
    def __init__(self, grad, first):
        self.places = bits_of(lax.axis_size("seq"))[1:]
        self.seq = lax.axis_index("seq")
        self.first = first
        flat = grad.reshape(-1, grad.shape[-1])
        got = lax.psum_scatter(flat, "dp", scatter_dimension=0, tiled=True)
        self.parts = [got.reshape(grad.shape[1:])]
        self.done = 0

    def step(self, *after):
        parts = self.parts
        if after:
            parts = tie(parts, *after)
        bits = self.places[-1 - self.done], self.places[self.done]
        chosen = jnp.stack([(self.seq // bit) % 2 for bit in bits]).astype(jnp.int32)
        if self.done == 0:
            rows, wide = parts[0].shape[-2:]
            sizes = (self.first, rows - self.first)
            ins = [parts[0].reshape((-1, rows, wide))]
        else:
            wide = parts[0].shape[-1]
            sizes = (self.first, parts[2].shape[-2])
            ins = parts
        owners = 2 ** (len(self.places) - self.done - 1)
        outs = [((owners, size, wide), BF16) for size in sizes for _ in range(2)]
        got = call(
            functools.partial(halve_body, sizes, len(ins) == 1),
            [SMEM] + [VMEM] * len(ins),
            outs,
            limit=24,
            name="halve",
        )(chosen, *ins)
        self.sends = (got[0], got[2])
        gots = [swap(send, "seq", bit) for send, bit in zip(self.sends, bits)]
        self.parts = [got[1], gots[0], got[3], gots[1]]
        self.done += 1

    def finish(self, ff, width):
        while self.done < len(self.places):
            self.step()
        parts = [part[0] for part in self.parts]
        rows, wide = sum(part.shape[0] for part in parts[::2]), parts[0].shape[1]
        core = (self.seq % 2).astype(jnp.int32).reshape(1)
        pieces = (ff + width) // width
        owned = width // (lax.axis_size("seq") * lax.axis_size("dp"))
        send, keep = call(
            functools.partial(part_rows_body, (owned,) * pieces + (rows // 2 - pieces * owned,)),
            [SMEM] + [VMEM] * 4,
            [((rows // 2, wide), F32)] * 2,
            limit=24,
            name="part_rows",
        )(core, *parts)
        got = swap(send, "seq", 1)
        return call(
            functools.partial(beside_body, pieces - 1),
            [SMEM] + [VMEM] * 2,
            [((owned, ff), F32), ((owned, width), F32), ((rows // 2 - pieces * owned, width), F32)],
            limit=24,
            name="beside",
        )(core, keep, got)


class CharsSums:
    def __init__(self, keep, send, rows, vector_rows):
        self.keep, self.send, self.rows, self.vector_rows = keep, send, rows, vector_rows
        self.seq = lax.axis_index("seq")
        self.bits = bits_of(lax.axis_size("seq"))
        self.first = True

    def step(self, *after):
        bit = self.bits.pop(0)
        groups = lax.axis_size("dp")
        send, keep = self.send, self.keep
        if after:
            send, keep = tie([send, keep], *after)
        got = swap(send, "seq", bit)
        last = not self.bits
        start = self.rows if self.first else 0
        size = keep.shape[0] - start
        fixed = self.rows + 2 * self.vector_rows
        if last:
            which = lax.axis_index("dp")
            outs = [((fixed + size // groups, LANES), BF16)] * groups
        else:
            which = (self.seq // self.bits[0]) % 2
            outs = [((fixed + size // 2, LANES), BF16), ((size // 2, LANES), BF16)]
        outs = call(
            functools.partial(mix_body, self.rows, self.vector_rows, self.first, last),
            [SMEM] + [VMEM] * 3,
            outs,
            limit=12,
            name="mix",
        )(which.astype(jnp.int32).reshape(1), keep, send, got)
        self.first = False
        if last:
            self.own, self.sends = outs[0], outs[1:]
        else:
            self.send, self.keep = outs

    def across(self, *after):
        self.sends = tie(self.sends, *after)
        self.own = [self.own] + [swap(part, "dp", k + 1) for k, part in enumerate(self.sends)]

    def finish(self, seqs, vocab, sub, gate_shape, *after):
        own = tie(self.own, *after)
        other = [swap(part, "seq", 1) for part in own]
        groups = len(own)
        rows, vector_rows = self.rows, self.vector_rows
        place = jnp.stack([lax.axis_index("dp"), self.seq % 2]).astype(jnp.int32)
        return call(
            functools.partial(table_body, groups, seqs, sub, lax.axis_size("seq")),
            [SMEM] + [VMEM] * (2 * groups),
            [((vocab, 2 * LANES), F32), ((vector_rows, LANES), F32)] + [(gate_shape, F32)] * 2,
            [
                pltpu.VMEM((groups, rows, LANES), BF16),
                pltpu.VMEM((groups, rows, LANES), BF16),
                pltpu.VMEM((groups, vector_rows, LANES), F32),
                pltpu.VMEM((own[0].shape[0] - rows - 2 * vector_rows, LANES), F32),
            ],
            limit=24,
            name="table_rows",
        )(place, *own, *other)


def shards(
    inputs, char_ids, lang_ids, lengths, char_table, gate_weight, gate_bias, cand_weight,
    join_weight, join_bias, query_weight, query_bias, key_weight, value_weight, value_bias,
    out_weight, out_bias, norm1_gain, norm1_bias, up_weight, up_bias, down_weight, down_bias,
    norm2_gain, norm2_bias, cotangent,
):
    seqs, tokens, width = inputs.shape
    chars = char_ids.shape[1]
    per = chars // tokens
    steps = chars // SEGS
    per_seg = steps // per
    vocab, embed = char_table.shape
    sub = vocab // GROUPS
    half = width // 2
    size = width // HEADS
    ff = up_weight.shape[1]
    count = lax.axis_size("seq")
    pairs = -(-seqs * HEADS // count)
    while HEADS % pairs:
        pairs += 1
    full = count * tokens
    total = seqs * tokens
    rows = seqs * SEGS
    wide = pairs * size
    seq = lax.axis_index("seq")
    me = jnp.stack([seq, seq % 2]).astype(jnp.int32)
    flat = inputs.reshape(total, width)
    cot = cotangent.reshape(total, width)

    embedded, htok, ptok, pre, pseg, payload = call(
        functools.partial(chars_forward_body, seqs, steps, per, sub),
        [SMEM] + [COPY] * 2 + [HBM] * 3,
        [
            ((seqs * chars, embed), BF16, COPY),
            ((2, per_seg, rows, half), F32, COPY),
            ((2, per_seg, rows, half), F32, COPY),
            ((2, 2, rows, half), F32, COPY),
            ((2, rows, half), F32),
            ((8 * seqs, half), F32),
        ],
        [
            pltpu.VMEM((2, seqs * chars, half), F32),
            pltpu.VMEM((2, seqs * chars, half), F32),
            pltpu.VMEM((2, rows, half), F32),
            pltpu.VMEM((-(-vocab // LANES) * LANES, embed), BF16),
            pltpu.VMEM(gate_weight.shape, BF16),
            pltpu.VMEM(cand_weight.shape, BF16),
            pltpu.SemaphoreType.DMA((3,)),
        ],
        name="chars_forward",
    )(lang_ids, char_ids, gate_bias, char_table, gate_weight, cand_weight)
    groups = gather_summaries(payload)

    resid, enter, joined, *sent = call(
        functools.partial(join_query_body, count, seqs, tokens, pairs),
        [SMEM] + [COPY] * 6 + [HBM] * (5 + count // 2),
        [
            ((total, width), F32, PIN),
            ((2, rows, half), F32),
            ((total, 4 * width), BF16, COPY),
        ]
        + [((tokens, 3 * wide), BF16, PIN)] * count,
        [
            pltpu.VMEM((count, 8 * seqs, half), F32),
            pltpu.VMEM((6, width, width), BF16),
            pltpu.VMEM((total, width), BF16),
            pltpu.SemaphoreType.DMA((count + 7,)),
            pltpu.VMEM((count, tokens, 3 * wide), BF16),
        ],
        name="join_query",
    )(
        me, htok, ptok, pre, join_bias, query_bias, value_bias, join_weight, query_weight, key_weight,
        value_weight,        flat, *groups,
    )
    heads = exchange(sent)

    block = min(1024, full)
    *sent, lse, heads_q, heads_k, heads_v, out_v, up_v = call(
        functools.partial(attend_body, count, seqs, tokens, pairs, size, block),
        [SMEM, SMEM] + [PIN] * count,
        [((tokens, wide), BF16, PIN)] * count
        + [((8, full), F32)]
        + [((pairs, full, LANES), BF16, HBM)] * 3,
        [pltpu.VMEM((pairs, full, LANES), BF16)] * 3
        + [
            pltpu.VMEM((pairs, size + 16, full), BF16),
            pltpu.VMEM((wide, full), F32),
            pltpu.VMEM((full, wide), BF16),
            pltpu.SemaphoreType.DMA((3,)),
        ],
        name="attend",
        fetch=(out_weight, up_weight),
    )(me, lengths, *heads)
    mixed_chunks = exchange(sent)
    (joined_far,) = tie([joined], *mixed_chunks)
    joined_got = swap(joined_far, "seq", 1)

    ff_block = 768
    output, d_first_in, vec1, up_vec, fed, fed_keep, fed_send, *sent = call(
        functools.partial(feed_body, count, seqs, tokens, pairs, size, ff_block),
        [SMEM] + [VMEM] * 7 + [PIN] * 3 + [HBM] * 2 + [PIN] * count,
        [
            ((total, width), BF16, HBM),
            ((total, width), F32, COPY),
            ((8, width), F32),
            ((1, ff), F32),
            ((total, ff + 2 * width), BF16, PIN),
            ((total, ff // 2 + width), BF16, PIN),
            ((total, ff // 2 + width), BF16),
        ]
        + [((tokens, wide), BF16, PIN)] * count,
        [
            pltpu.VMEM((count, tokens, wide), BF16),
            pltpu.VMEM((total, ff), F32),
            pltpu.VMEM((total, width), F32),
            pltpu.VMEM((total, width), BF16),
            pltpu.VMEM((total, width), BF16),
            pltpu.VMEM((total, ff), BF16),
            pltpu.VMEM((total, width), BF16),
            pltpu.VMEM((ff, width), BF16),
            pltpu.SemaphoreType.DMA((2 + ff // ff_block,)),
        ],
        limit=32,
        name="feed_forward",
    )(
        me, out_bias, norm1_gain, norm1_bias, up_bias, down_bias, norm2_gain, norm2_bias, resid,
        out_v, up_v, cot, down_weight, *mixed_chunks,
    )
    d_mixed_chunks = exchange(sent)

    fed_got, fed_keep_got = swap(fed, "seq", 1), swap(fed_send, "seq", 1)
    fed, fed_got, fed_keep, fed_keep_got = tie(
        [fed, fed_got, fed_keep, fed_keep_got], *d_mixed_chunks
    )
    grad_feed = feed_grads(fed, fed_got, fed_keep, fed_keep_got, ff, width)
    feed = FeedRows(grad_feed, (ff + width) * 2 // (count * lax.axis_size("dp")))
    d_mixed_chunks = tie(d_mixed_chunks, grad_feed)

    back_block = min(512, full)
    *sent, near_w = call(
        functools.partial(attend_back_body, count, seqs, tokens, pairs, size, back_block),
        [SMEM, VMEM] + [HBM] * 3 + [PIN] * count,
        [((tokens, 3 * wide), BF16, PIN)] * count,
        [pltpu.VMEM((pairs, full, LANES), BF16)] * 3
        + [
            pltpu.VMEM((size, full), BF16),
            pltpu.VMEM((pairs, full, size), BF16),
            pltpu.VMEM((wide, full), F32),
            pltpu.VMEM((full, full), BF16),
            pltpu.VMEM((full, full), BF16),
            pltpu.VMEM((full, 3 * wide), BF16),
            pltpu.SemaphoreType.DMA((3,)),
        ],
        name="attend_back",
        fetch=(join_weight, query_weight, key_weight, value_weight),
    )(me, lse, heads_q, heads_k, heads_v, *d_mixed_chunks)
    d_chunks = exchange(sent)
    input_grad, d_perm, payload_back, vec2, back_keep, back_send = call(
        functools.partial(project_back_body, count, seqs, tokens, pairs, size, per_seg),
        [SMEM, COPY, COPY, COPY, PIN] + [PIN] * count,
        [
            ((total, width), BF16, COPY),
            ((2, per_seg, rows, half), F32, COPY),
            ((8 * seqs, half), F32),
            ((8, width), F32),
            ((total, 2 * width), BF16, PIN),
            ((total, 2 * width), BF16),
        ],
        [
            pltpu.VMEM((count, tokens, 3 * wide), BF16),
            pltpu.VMEM((total, 4 * width), BF16),
        ],
        name="project_back",
    )(me, pre, d_first_in, ptok, near_w, *d_chunks)
    back_groups = gather_summaries(payload_back)
    vector_rows = -(-(10 * width + ff) // (16 * LANES)) * 16

    back_got = swap(back_send, "seq", 1)
    back_all = tie([joined, joined_got, back_keep, back_got], back_groups[0])
    back_plan = tuple((0, k * half, half) for k in range(3))
    back_plan += tuple(((1 + k) * width, 3 * half, half) for k in range(3))
    back_parts = outer_grads(back_all, back_plan, 3 * half, width, "grad_back")
    back_parts = tie(back_parts, *back_groups)
    back = Columns(back_parts, (half,) * 6)
    back_groups = tie(back_groups, *back_parts)

    own_rows = 4 * half * embed // (2 * LANES)
    table_rows = seqs * LANES
    chars_keep, chars_send = call(
        functools.partial(chars_back_body, count, seqs, steps, per),
        [SMEM, SMEM] + [VMEM] * 7 + [COPY] * 3 + [HBM] * (2 + count),
        [
            ((table_rows + own_rows, LANES), BF16),
            ((table_rows + 2 * vector_rows + own_rows, LANES), BF16),
        ],
        [
            pltpu.VMEM((2, seqs * chars, half), F32),
            pltpu.VMEM((2, seqs * chars, half), F32),
            pltpu.VMEM((seqs * chars, 4 * half), BF16),
            pltpu.VMEM((2, per_seg, rows, half), F32),
            pltpu.VMEM((2, rows, half), F32),
            pltpu.VMEM((2, rows, half), F32),
            pltpu.VMEM(gate_weight.shape, BF16),
            pltpu.VMEM(cand_weight.shape, BF16),
            pltpu.VMEM((count, 8 * seqs, half), F32),
            pltpu.VMEM((count, 8 * seqs, half), F32),
            pltpu.SemaphoreType.DMA((2 + 2 * count,)),
            pltpu.VMEM((vector_rows, LANES), F32),
            pltpu.VMEM((2, own_rows, LANES), F32),
        ],
        name="chars_back",
    )(
        lang_ids, me, char_ids, gate_bias, enter, pseg, vec1, up_vec, vec2, embedded, ptok, d_perm,
        gate_weight, cand_weight, *groups, *back_groups,
    )
    chars_sums = CharsSums(chars_keep, chars_send, table_rows, vector_rows)
    chars_sums.step()
    back.fold(chars_sums.send)
    chars_sums.step()
    back.part_cores()
    back.part_groups()
    while chars_sums.bits:
        chars_sums.step()
    feed.step(*back.sends, *chars_sums.sends)
    chars_sums.across(*back.sends)
    feed.step()
    gate_shape = (2, embed // (count * lax.axis_size("dp")), half)
    grad_table, sums, grad_gate, grad_cand = chars_sums.finish(seqs, vocab, sub, gate_shape)
    sums = sums.reshape(-1)
    early, late = sums[: 6 * width + ff], sums[6 * width + ff : 10 * width + ff]
    grad_up, grad_out, grad_down = feed.finish(ff, width)
    grad_query, grad_key, grad_value, *grad_join = back.finish()

    early_row = lambda k: early[k * width : (k + 1) * width]
    late_row = lambda k: late[k * width : (k + 1) * width]
    return (
        output.reshape(inputs.shape),
        input_grad.reshape(inputs.shape),
        grad_table,
        grad_gate,
        late[3 * width :].reshape(2, half),
        grad_cand,
        jnp.stack(grad_join),
        late_row(2),
        grad_query,
        late_row(0),
        grad_key,
        grad_value,
        late_row(1),
        grad_out,
        early_row(5),
        early_row(3),
        early_row(4),
        grad_up,
        early[6 * width :],
        grad_down,
        early_row(2),
        early_row(0),
        early_row(1),
    )


def solution(mesh):
    spread_rows = P("dp", "seq", None)
    placed = (
        (spread_rows, P("dp", "seq"), P("dp"), P("dp")) + (P(),) * 21 + (spread_rows,)
    )
    owned = P(("dp", "seq"), None)
    owned_mid = P(None, ("dp", "seq"), None)
    return jax.shard_map(
        shards,
        mesh=mesh,
        in_specs=placed,
        out_specs=(
            spread_rows, spread_rows, P(), owned_mid, P(), owned_mid, owned_mid, P(),
            owned, P(), owned, owned, P(), owned, P(), P(), P(), owned, P(), owned, P(), P(), P(),
        ),
        check_vma=False,
    )
```

```python
import functools

import jax
import jax.numpy as jnp
from jax import lax
from jax.experimental import pallas as pl
from jax.experimental.pallas import tpu as pltpu
from jax.sharding import PartitionSpec as P

HEADS = 12
GROUPS = 8
SEGS = 8
LANES = 128
NORM_EPS = 1e-05
MASKED = -1000000000.0
MIB = 1 << 20
F32 = jnp.float32
BF16 = jnp.bfloat16


def dot(left, right):
    return jnp.dot(left, right, preferred_element_type=F32)


def dot_nt(left, right):
    return lax.dot_general(left, right, (((1,), (1,)), ((), ())), preferred_element_type=F32)


def dot_tn(left, right):
    return lax.dot_general(left, right, (((0,), (0,)), ((), ())), preferred_element_type=F32)


def column_sum(values):
    return jnp.sum(values.astype(F32), axis=0, keepdims=True)


VMEM = pl.BlockSpec(memory_space=pltpu.VMEM)
SMEM = pl.BlockSpec(memory_space=pltpu.SMEM)
HBM, PIN, COPY = "hbm", "pin", "copy"


def call(body, ins, outs, scratch=(), limit=40, name=None, fetch=()):
    spaces = {PIN: pltpu.VMEM, HBM: pltpu.HBM, COPY: pltpu.HBM}
    specs = {PIN: VMEM, HBM: pl.BlockSpec(memory_space=pltpu.HBM), COPY: VMEM}
    space_of = lambda spec: spaces[spec] if isinstance(spec, str) else None
    spec_of = lambda spec: specs[spec] if isinstance(spec, str) else spec
    all_ins = list(ins) + [HBM] * len(fetch)
    all_outs = [out if len(out) > 2 else out + (VMEM,) for out in outs]
    homes = {}
    for array in fetch:
        homes.setdefault(array.shape[-2:], []).append(array)
    homes = list(homes.items())
    fetch = [array for _, arrays in homes for array in arrays]
    for shape, arrays in homes:
        count = sum(array.size for array in arrays) // (shape[0] * shape[1])
        all_outs.append(((count,) + shape, arrays[0].dtype, PIN))
    scratch = list(scratch)
    inner = body
    if fetch:
        parts = 4
        scratch.append(pltpu.SemaphoreType.DMA((len(fetch) * parts,)))

        def inner(*refs):
            sems, n_in = refs[-1], len(ins)
            far, rest = refs[n_in : n_in + len(fetch)], refs[n_in + len(fetch) :]
            near, last = rest[len(outs) : len(outs) + len(homes)], len(outs) + len(homes)
            rest = rest[: len(outs)] + rest[last:-1]
            far = list(far)
            copies = []
            for b, (shape, arrays) in zip(near, homes):
                at = 0
                for _ in arrays:
                    a = far.pop(0)
                    wide = a.shape[0] if len(a.shape) > 2 else 1
                    rows = shape[0] // parts
                    for k in range(parts):
                        piece = slice(k * rows, (k + 1) * rows)
                        if len(a.shape) > 2:
                            pair = a.at[:, piece], b.at[slice(at, at + wide), piece]
                        else:
                            pair = a.at[piece], b.at[at, piece]
                        copies.append(pltpu.make_async_copy(*pair, sems.at[len(copies)]))
                    at += wide

            def begin():
                for copy in copies:
                    copy.start()

            body(begin, *refs[:n_in], *rest)
            for copy in copies:
                copy.wait()

    kernel = pl.pallas_call(
        inner,
        in_specs=[spec_of(spec) for spec in all_ins],
        out_specs=[spec_of(out[2]) for out in all_outs],
        out_shape=[
            space_of(out[2])(out[0], out[1]) if space_of(out[2]) else jax.ShapeDtypeStruct(out[0], out[1])
            for out in all_outs
        ],
        scratch_shapes=scratch,
        compiler_params=pltpu.CompilerParams(vmem_limit_bytes=limit * MIB),
        cost_estimate=pl.CostEstimate(flops=1, bytes_accessed=1, transcendentals=0),
        name=name,
    )

    def run(*args):
        args = list(args) + list(fetch)
        held = [
            pltpu.with_memory_space_constraint(arg, space_of(spec)) if space_of(spec) else arg
            for arg, spec in zip(args, all_ins)
        ]
        return kernel(*held)

    return run


def ahead_of(arrays, *after):
    def body(begin, *refs):
        begin()

    arrays = tie(arrays, *after)
    return call(body, [], [], fetch=tuple(arrays), limit=8, name="weights")()


def pull(pairs, sems):
    copies = [pltpu.make_async_copy(far, near, sems.at[k]) for k, (far, near) in enumerate(pairs)]
    for copy in copies:
        copy.start()
    return copies


def collect(chunks, stage, me, count):
    for k, chunk in enumerate(chunks):
        stage[lax.rem(me + count - k, count)] = chunk[...]


def summaries(groups, gathered, me):
    pairs = []
    for j, group in enumerate(groups):
        for i in range(2):
            pairs.append((group.at[i], gathered.at[jnp.bitwise_xor(me, 2 * j + i)]))
    return pairs


def gates(embedded, gate_w, gate_b, cand_w, upd, cand):
    for r in range(2):
        upd[r] = jax.nn.sigmoid(dot(embedded, gate_w[r]) + gate_b[r : r + 1])
        cand[r] = dot(embedded, cand_w[r])


def one_hot_rows(ids, seqs, steps):
    rows = []
    for s in range(seqs):
        for g in range(SEGS):
            rows.append(ids[s : s + 1, g * steps : (g + 1) * steps] + s * LANES)
    held = jnp.concatenate(rows, axis=0)
    place = lax.broadcasted_iota(jnp.int32, (seqs * SEGS, seqs * LANES), 1)
    return jnp.concatenate(
        [(place == held[:, t : t + 1]).astype(F32).astype(BF16) for t in range(steps)], axis=0
    )


def chars_forward_body(
    seqs, steps, per, sub,
    lang, ids, gate_b, table, gate_w_far, cand_w_far,
    embedded_out, htok, ptok, pre, pseg, payload,
    upd, cand, hseg, padded_table, gate_w, cand_w, sems,
):
    rows = seqs * SEGS
    vocab = table.shape[0]
    wide = padded_table.shape[0]
    copies = pull(
        [(table, padded_table.at[0:vocab]), (gate_w_far, gate_w), (cand_w_far, cand_w)], sems
    )
    padded_table[vocab:wide] = jnp.zeros((wide - vocab, padded_table.shape[1]), BF16)
    copies[0].wait()
    local = lax.broadcasted_iota(jnp.int32, (LANES, wide), 0)
    place = lax.broadcasted_iota(jnp.int32, (LANES, wide), 1)
    mine = []
    for s in range(seqs):
        pick = (place == lang[s] * sub + local) & (local < sub)
        mine.append(dot(pick.astype(BF16), padded_table[...]).astype(BF16))
    own_table = jnp.concatenate(mine, axis=0)
    embedded = dot(one_hot_rows(ids, seqs, steps), own_table).astype(BF16)
    embedded_out[...] = embedded
    copies[1].wait()
    copies[2].wait()
    gates(embedded, gate_w, gate_b[...], cand_w, upd, cand)

    def token(q, carry):
        h0, p0, h1, p1 = carry
        for j in range(per):
            at = pl.ds(pl.multiple_of((q * per + j) * rows, rows), rows)
            u = upd[0, at, :]
            h0 = h0 + u * (cand[0, at, :] - h0)
            p0 = p0 * (1.0 - u)
            at = pl.ds(pl.multiple_of((steps - 1 - q * per - j) * rows, rows), rows)
            u = upd[1, at, :]
            h1 = h1 + u * (cand[1, at, :] - h1)
            p1 = p1 * (1.0 - u)
        htok[0, q] = h0
        ptok[0, q] = p0
        back = steps // per - 1 - q
        htok[1, back] = h1
        ptok[1, back] = p1
        return h0, p0, h1, p1

    zero = jnp.zeros((rows, upd.shape[2]), F32)
    h0, p0, h1, p1 = lax.fori_loop(0, steps // per, token, (zero, zero + 1.0, zero, zero + 1.0))
    pseg[0], pseg[1], hseg[0], hseg[1] = p0, p1, h0, h1
    last = steps // per - 1
    for s in range(seqs):
        for r in range(2):
            total_a = jnp.ones((1, upd.shape[2]), F32)
            total_b = jnp.zeros((1, upd.shape[2]), F32)
            order = range(SEGS) if r == 0 else range(SEGS - 1, -1, -1)
            for g in order:
                row = s * SEGS + g
                pre[0, r, row : row + 1] = total_a
                pre[1, r, row : row + 1] = total_b
                p_row = pseg[r, row : row + 1]
                total_b = p_row * total_b + hseg[r, row : row + 1]
                total_a = p_row * total_a
            edge = s * SEGS if r == 0 else s * SEGS + SEGS - 1
            q = 0 if r == 0 else last
            near_a, near_b = ptok[r, q, edge : edge + 1], htok[r, q, edge : edge + 1]
            for k, value in enumerate((total_a, total_b, near_a, near_b)):
                row = (4 * r + k) * seqs + s
                payload[row : row + 1] = value


def spread(values, seqs):
    wide = values.shape[1]
    return jnp.concatenate(
        [jnp.broadcast_to(values[s : s + 1], (SEGS, wide)) for s in range(seqs)], axis=0
    )


def token_row(token, tokens, per_seg, seqs):
    s = token // tokens
    t = token % tokens
    return (t % per_seg) * (seqs * SEGS) + s * SEGS + t // per_seg


def join_query_body(
    count, seqs, tokens, pairs,
    me_ref, htok, ptok, pre, join_b, query_b, value_b, near_w, inputs_far,
    *rest,
):
    groups, rest = rest[: count // 2], rest[count // 2 :]
    resid_out, enter, left_out = rest[:3]
    chunks = rest[3 : 3 + count]
    held, inputs, sems, stage = rest[3 + count :]
    me = me_ref[0]
    width = near_w.shape[1]

    def emit(k, values):
        left_out[:, k * width : (k + 1) * width] = values

    copies = pull(summaries(groups, held, me) + [(inputs_far, inputs)], sems)
    for copy in copies[:count]:
        copy.wait()
    copies = copies[count:]
    half = htok.shape[3]

    def gathered(j, k):
        return held[j, k * seqs : (k + 1) * seqs]

    per_seg = htok.shape[1]
    total = seqs * tokens
    x0 = jnp.zeros((seqs, half), F32)
    x1 = jnp.zeros((seqs, half), F32)
    for j in range(count):
        x0 = jnp.where(j < me, gathered(j, 0) * x0 + gathered(j, 1), x0)
        i = count - 1 - j
        x1 = jnp.where(i > me, gathered(i, 4) * x1 + gathered(i, 5), x1)
    carry0 = pre[0, 0] * spread(x0, seqs) + pre[1, 0]
    carry1 = pre[0, 1] * spread(x1, seqs) + pre[1, 1]
    enter[0] = carry0
    enter[1] = carry1
    forward = htok[0] + ptok[0] * carry0[None]
    backward = htok[1] + ptok[1] * carry1[None]
    rows = seqs * SEGS
    last = per_seg - 1
    f_last = jnp.concatenate(
        [forward[last, s * SEGS + SEGS - 1 : s * SEGS + SEGS] for s in range(seqs)], axis=0
    )
    b_first = jnp.concatenate(
        [backward[0, s * SEGS : s * SEGS + 1] for s in range(seqs)], axis=0
    )
    left = jnp.maximum(me - 1, 0)
    right = jnp.minimum(me + 1, count - 1)
    left_b = gathered(left, 6) * b_first + gathered(left, 7)
    right_f = gathered(right, 2) * f_last + gathered(right, 3)
    left_row = jnp.where(me > 0, jnp.concatenate([x0, left_b], axis=1), 0.0)
    right_row = jnp.where(me < count - 1, jnp.concatenate([right_f, x1], axis=1), 0.0)
    rim = jnp.concatenate(
        [left_row, right_row, jnp.zeros((16 - 2 * seqs, 2 * half), F32)], axis=0
    ).astype(BF16)
    tokens_perm = jnp.concatenate(
        [forward.reshape(total, half), backward.reshape(total, half)], axis=1
    ).astype(BF16)
    source = jnp.concatenate([tokens_perm, rim], axis=0)
    token = lax.broadcasted_iota(jnp.int32, (total, total + 16), 0)
    place = lax.broadcasted_iota(jnp.int32, (total, total + 16), 1)
    joining = jnp.broadcast_to(join_b[...][None], (total, 2 * half))
    for k in range(3):
        moved = token + (k - 1)
        want = token_row(moved, tokens, per_seg, seqs)
        if k == 0:
            want = jnp.where(token % tokens == 0, total + token // tokens, want)
        if k == 2:
            want = jnp.where(token % tokens == tokens - 1, total + seqs + token // tokens, want)
        tap = dot((place == want).astype(BF16), source).astype(BF16)
        emit(1 + k, tap)
        joining = joining + dot(tap, near_w[k])
    copies[0].wait()
    resid = inputs[...].astype(F32) + joining
    resid_out[...] = resid
    low = resid.astype(BF16)
    emit(0, low)
    size = 2 * half // HEADS
    wide = pairs * size
    query = (dot(low, near_w[3]) + query_b[...][None]).astype(BF16)
    key = dot(low, near_w[4]).astype(BF16)
    value = (dot(low, near_w[5]) + value_b[...][None]).astype(BF16)
    send_pairs((query, key, value), stage, chunks, me, count, seqs, tokens, pairs, size, wide)


def send_pairs(arrays, stage, chunks, me, count, seqs, tokens, pairs, size, wide):
    for d in range(count):
        for a, array in enumerate(arrays):
            first = d * pairs
            if first >= seqs * HEADS:
                stage[d, :, a * wide : (a + 1) * wide] = jnp.zeros((tokens, wide), BF16)
                continue
            s, head = first // HEADS, first % HEADS
            stage[d, :, a * wide : (a + 1) * wide] = array[
                s * tokens : (s + 1) * tokens, head * size : head * size + wide
            ]
    for k in range(count):
        chunks[k][...] = stage[lax.rem(me + k, count)]


def receive_pairs(stage, place, count, seqs, pairs, size, parts):
    wide = pairs * size
    for d in range(count):
        first = d * pairs
        if first >= seqs * HEADS:
            continue
        s, head = first // HEADS, first % HEADS
        for a in range(parts):
            place(a, s, head * size, stage[d, :, a * wide : (a + 1) * wide])


def load_heads(chunks, me, count, tokens, pairs, size, part, target, scale=None):
    wide = pairs * size
    for k in range(count):
        at = block_of(me, count - k, count, tokens)
        for h in range(pairs):
            lane = part * wide + h * size
            block = chunks[k][:, lane : lane + size]
            target[h, at, 0:size] = block if scale is None else block * scale


def pair_length(lengths, me, pairs, h, seqs):
    return lengths[jnp.minimum((me * pairs + h) // HEADS, seqs - 1)]


def transposed(values):
    return jnp.transpose(values.astype(F32))


def mask_lanes(q, k, full, valid, size):
    shape = (full, k.shape[2] - size)
    lane = lax.broadcasted_iota(jnp.int32, shape, 1)
    key_at = lax.broadcasted_iota(jnp.int32, shape, 0)
    ones = jnp.where(lane == 0, 1.0, 0.0).astype(BF16)
    mask = jnp.where((lane == 0) & (key_at >= valid), MASKED, 0.0).astype(BF16)
    for h in range(k.shape[0]):
        q[h, :, size:] = ones
        k[h, :, size:] = mask


def attend_body(count, seqs, tokens, pairs, size, block, begin, me_ref, lengths, *rest):
    chunks, rest = rest[:count], rest[count:]
    outs, lse, far = rest[:count], rest[count], rest[count + 1 : count + 4]
    q, k, v, vt, mixed_t, mixed, sems = rest[count + 4 :]
    me = me_ref[0]
    full = count * tokens
    begin()
    load_heads(chunks, me, count, tokens, pairs, size, 0, q, jnp.asarray(0.125, BF16))
    load_heads(chunks, me, count, tokens, pairs, size, 1, k)
    load_heads(chunks, me, count, tokens, pairs, size, 2, v)
    lse[...] = jnp.zeros_like(lse)
    mask_lanes(q, k, full, pair_length(lengths, me, pairs, 0, seqs), size)
    copies = pull(list(zip((q, k, v), far)), sems)
    for h in range(pairs):
        vt[h, 0:size] = transposed(v[h, :, 0:size]).astype(BF16)
        row = lax.broadcasted_iota(jnp.int32, (vt.shape[1] - size, full), 0)
        vt[h, size:] = jnp.where(row == 0, 1.0, 0.0).astype(BF16)

        def rows(i, _, h=h):
            at = pl.ds(pl.multiple_of(i * block, block), block)
            scores = dot_nt(k[h], q[h, at, :])
            top = jnp.max(scores, axis=0, keepdims=True)
            sums = dot(vt[h], jnp.exp(scores - top).astype(BF16))
            total = sums[size : size + 1]
            lse[h : h + 1, at] = top + jnp.log(total)
            mixed_t[h * size : (h + 1) * size, at] = sums[0:size] / total
            return 0

        lax.fori_loop(0, full // block, rows, 0, unroll=2)
    mixed[...] = transposed(mixed_t[...]).astype(BF16)
    for j in range(count):
        outs[j][...] = mixed[block_of(me, j, count, tokens), :]
    for copy in copies:
        copy.wait()


def block_of(me, j, count, tokens):
    return pl.ds(pl.multiple_of(lax.rem(me + j, count) * tokens, tokens), tokens)


def attend_back_body(count, seqs, tokens, pairs, size, block, me_ref, lse, *rest):
    far, d_chunks, rest = rest[:3], rest[3 : 3 + count], rest[3 + count :]
    outs = rest[:count]
    q, k, v, kt, d_o, dq_t, probs_all, d_scores_all, stage, sems = rest[count:]
    me = me_ref[0]
    full = count * tokens
    wide = pairs * size
    copies = pull(list(zip(far, (q, k, v))), sems)
    load_heads(d_chunks, me, count, tokens, pairs, size, 0, d_o)
    for copy in copies:
        copy.wait()
    for h in range(pairs):
        kt[...] = transposed(k[h, :, 0:size]).astype(BF16)

        def rows(i, _, h=h):
            at = pl.ds(pl.multiple_of(i * block, block), block)
            probs = jnp.exp(dot_nt(k[h], q[h, at, :]) - lse[h : h + 1, at])
            d_probs = dot_nt(v[h, :, 0:size], d_o[h, at, :])
            probs_all[:, at] = probs.astype(BF16)
            row_dot = jnp.sum(probs * d_probs, axis=0, keepdims=True)
            d_scores_all[:, at] = (probs * (d_probs - row_dot)).astype(BF16)
            return 0

        lax.fori_loop(0, full // block, rows, 0, unroll=2)
        dq_t[h * size : (h + 1) * size, :] = dot(kt[...], d_scores_all[...]) * 0.125
        for part, grad in (
            (1, dot(d_scores_all[...], q[h])), (2, dot(probs_all[...], d_o[h])),
        ):
            lane = part * wide + h * size
            stage[:, lane : lane + size] = grad[:, 0:size].astype(BF16)
    stage[:, 0:wide] = transposed(dq_t[...]).astype(BF16)
    for j in range(count):
        outs[j][...] = stage[block_of(me, j, count, tokens), :]


def normed(values):
    center = values - jnp.mean(values, axis=-1, keepdims=True)
    scale = lax.rsqrt(jnp.mean(center * center, axis=-1, keepdims=True) + NORM_EPS)
    return center * scale, scale


def norm_back(cotangent, unit, scale, gain):
    d_unit = cotangent * gain
    mean = jnp.mean(d_unit, axis=-1, keepdims=True)
    lean = jnp.mean(d_unit * unit, axis=-1, keepdims=True)
    return scale * (d_unit - mean - unit * lean)


GELU_A = 0.7978845608028654
GELU_B = 0.044715


def feed_body(
    count, seqs, tokens, pairs, size, block,
    me_ref, out_b, gain1, shift1, up_b, down_b, gain2, shift2,
    resid, out_v, up_v, cotangent_far, down_far,
    *rest,
):
    chunks, rest = rest[:count], rest[count:]
    output_far, d_first_in_out, vec, up_vec, lefts, keep_out, send_out = rest[:7]
    outs = rest[7 : 7 + count]
    out_v, up_v = out_v.at[0], up_v.at[0]
    stage, slope, acc, cotangent, output, d_hidden_v, d_second_v, down_v, sems = rest[7 + count :]
    me, core = me_ref[0], me_ref[1]
    width = out_v.shape[0]
    ff = up_v.shape[1]
    parts = ff // block
    mixed = lefts.at[:, ff + width : ff + 2 * width]
    first_low_v = lefts.at[:, ff : ff + width]

    def emit_halves(source, lane, wide):
        for out, part in ((keep_out, core), (send_out, 1 - core)):
            at = pl.ds(pl.multiple_of(part * wide, LANES), wide)
            out[:, lane : lane + wide] = source[:, at]

    pieces = [slice(j * block, (j + 1) * block) for j in range(parts)]
    first_copies = pull(
        [(cotangent_far, cotangent)]
        + [(down_far.at[piece], down_v.at[piece]) for piece in pieces],
        sems,
    )
    collect(chunks, stage, me, count)

    def lanes(j):
        return pl.ds(pl.multiple_of(j * block, block), block)

    def place(part, s, lane, values):
        mixed[s * tokens : (s + 1) * tokens, lane : lane + values.shape[1]] = values

    receive_pairs(stage, place, count, seqs, pairs, size, 1)
    first_in = resid[...] + dot(mixed[...], out_v[...]) + out_b[...][None]
    unit1, scale1 = normed(first_in)
    first = unit1 * gain1[...][None] + shift1[...][None]
    first_low = first.astype(BF16)
    first_low_v[...] = first_low
    acc[...] = first + down_b[...][None]

    def ahead(j, _):
        hidden = dot(first_low_v[...], up_v[:, lanes(j)]) + up_b[lanes(j)][None]
        square = hidden * hidden
        bend = jnp.tanh(GELU_A * (hidden + GELU_B * (square * hidden)))
        act = (0.5 * hidden * (1.0 + bend)).astype(BF16)
        lefts[:, lanes(j)] = act
        slope[:, lanes(j)] = 0.5 * (1.0 + bend) + 0.5 * hidden * (1.0 - bend * bend) * (
            GELU_A * (1.0 + 3.0 * GELU_B * square)
        )
        first_copies[1 + j].wait()
        acc[...] += dot(act, down_v[lanes(j), :])

    for j in range(parts):
        ahead(j, 0)
    unit2, scale2 = normed(acc[...])
    first_copies[0].wait()
    output[...] = (unit2 * gain2[...][None] + shift2[...][None]).astype(BF16)
    done = pltpu.make_async_copy(output, output_far, sems.at[1 + parts])
    done.start()
    cot = cotangent[...].astype(F32)
    vec[0:1] = column_sum(cot * unit2)
    vec[1:2] = column_sum(cot)
    d_second_in = norm_back(cot, unit2, scale2, gain2[...][None])
    d_second = d_second_in.astype(BF16)
    d_second_v[...] = d_second
    emit_halves(d_second_v, ff // 2, width // 2)
    vec[2:3] = column_sum(d_second)
    acc[...] = d_second_in

    def astern(j, _):
        d_act = dot_nt(d_second_v[...], down_v[lanes(j), :])
        d_hidden = (d_act * slope[:, lanes(j)]).astype(BF16)
        d_hidden_v[:, lanes(j)] = d_hidden
        up_vec[:, lanes(j)] = column_sum(d_hidden)
        acc[...] += dot_nt(d_hidden, up_v[:, lanes(j)])
        return 0

    lax.fori_loop(0, parts, astern, 0, unroll=True)
    emit_halves(d_hidden_v, 0, ff // 2)
    d_first = acc[...]
    vec[3:4] = column_sum(d_first * unit1)
    vec[4:5] = column_sum(d_first)
    d_first_in = norm_back(d_first, unit1, scale1, gain1[...][None])
    d_first_in_out[...] = d_first_in
    d_attn = d_first_in.astype(BF16)
    d_second_v[...] = d_attn
    emit_halves(d_second_v, ff // 2 + width // 2, width // 2)
    vec[5:6] = column_sum(d_attn)
    vec[6:8] = jnp.zeros((2, vec.shape[1]), F32)
    d_mixed = dot_nt(d_attn, out_v[...]).astype(BF16)
    send_pairs((d_mixed,), stage, outs, me, count, seqs, tokens, pairs, size, pairs * size)
    done.wait()


def fetch_columns(arrays, lanes, sems, at):
    copies = []
    for far, near in arrays:
        copy = pltpu.make_async_copy(far.at[:, lanes], near.at[:, lanes], sems.at[at + len(copies)])
        copy.start()
        copies.append(copy)
    return copies


def feed_grads_body(ff, lefts, lefts_got, rights, rights_got, out, res, sems):
    half = out.shape[-1]
    width = 2 * half
    blocks = out.shape[0]
    step = ff // blocks
    first = ff // 2
    outgoing = []

    def emit(place):
        at = sems.at[len(outgoing)]
        copy = pltpu.make_async_copy(res.at[place], out.at[place], at)
        copy.start()
        outgoing.append(copy)

    def grad(at, size, begin):
        rows, lanes = slice(at, at + size), slice(begin, begin + half)
        return dot_tn(lefts[:, rows], rights[:, lanes]) + dot_tn(lefts_got[:, rows], rights_got[:, lanes])

    whole = slice(None)
    owners = 1
    for size in out.shape[:-2]:
        owners *= size
    pieces = (ff + width) // width
    up_rows = width // owners
    down_rows = ff // owners
    start = pieces * up_rows
    mids = (whole,) * (len(out.shape) - 3)
    by_piece = up_rows % 16 == 0 and down_rows % 16 == 0
    for j in range(blocks):
        part = grad(j * step, step, first)
        spread_rows(res, (j,), slice(start, start + down_rows), part)
        if by_piece:
            emit((j,) + mids + (slice(start, start + down_rows), whole))
    for k in range(pieces):
        if k == pieces - 1:
            part = grad(ff + width, width, first + half)
        else:
            part = grad(ff, width, k * half)
        rows = slice(k * up_rows, (k + 1) * up_rows)
        spread_rows(res, (), rows, part)
        if by_piece:
            emit((whole,) + mids + (rows, whole))
    if not by_piece:
        emit((whole,) * len(out.shape))
    for copy in outgoing:
        copy.wait()


def spread_rows(res, head, rows, grad):
    size = rows.stop - rows.start
    wide = res.shape[len(head) : -2]
    if size % 16 == 0:
        at = head + (slice(None),) * len(wide) + (rows, slice(None))
        res[at] = grad.astype(BF16).reshape(wide + (size, grad.shape[1]))
        return
    places = [()]
    for count in wide:
        places = [place + (k,) for place in places for k in range(count)]
    for k, place in enumerate(places):
        res[head + place + (rows, slice(None))] = grad[k * size : (k + 1) * size].astype(BF16)


def feed_grads(left, left_got, right, right_got, ff, width):
    count, groups = lax.axis_size("seq"), lax.axis_size("dp")
    places = bits_of(count)[1:]
    owners = count * groups // 2
    rows = (ff + width) // width * (width // owners) + ff // owners
    shape = (groups,) + (2,) * len(places) + (rows, width // 2)
    (out,) = call(
        functools.partial(feed_grads_body, ff),
        [PIN] * 4,
        [(shape, BF16, HBM)],
        [
            pltpu.VMEM(shape, BF16),
            pltpu.SemaphoreType.DMA((groups + (ff + width) // width,)),
        ],
        name="grad_feed",
    )(left, left_got, right, right_got)
    return out


def store_rows(res, lanes, grad):
    rows = res.shape[-2]
    if rows % 16 == 0:
        res[..., lanes] = grad.astype(BF16).reshape(res.shape[:-1] + (grad.shape[1],))
        return
    places = [()]
    for wide in res.shape[:-2]:
        places = [place + (k,) for place in places for k in range(wide)]
    for k, place in enumerate(places):
        res[place + (slice(None), lanes)] = grad[k * rows : (k + 1) * rows].astype(BF16)


def outer_body(plan, cut, bits_ref, left, left_got, rights, rights_got, *rest):
    low_send, low_keep, high_send, high_keep = rest[:4]
    lefts, lefts_got, res, sems = rest[4:]
    height = lefts.shape[1] // len({lane for lane, _, _ in plan})
    waits = []
    for number, (lane, first, wide) in enumerate(plan):
        copies = []
        for far, near, at, size, seen in (
            (left, lefts, lane, height, [other[0] for other in plan[:number]]),
            (left_got, lefts_got, lane, height, [other[0] for other in plan[:number]]),
        ):
            if at not in seen:
                lanes = slice(at, at + size)
                sem = sems.at[sum(map(len, waits)) + len(copies)]
                copies.append(pltpu.make_async_copy(far.at[:, lanes], near.at[:, lanes], sem))
        waits.append(copies)
        for copy in copies:
            copy.start()
    used = sum(map(len, waits))
    low, high = bits_ref[0], bits_ref[1]
    outgoing = []
    whole = slice(None)
    mids = len(res.shape) - 4

    def emit(low_half):
        if low_half:
            place = lambda which: (whole,) * (1 + mids) + (which, whole, slice(0, cut))
            pairs = ((low_send, 1 - low), (low_keep, low))
        else:
            place = lambda which: (whole, which) + (whole,) * (1 + mids) + (slice(cut, res.shape[-1]),)
            pairs = ((high_send, 1 - high), (high_keep, high))
        for out, which in pairs:
            copy = pltpu.make_async_copy(res.at[place(which)], out, sems.at[used + len(outgoing)])
            copy.start()
            outgoing.append(copy)

    lane_at = 0
    for number, (lane, first, wide) in enumerate(plan):
        for copy in waits[number]:
            copy.wait()
        for k in range(0, wide, 512):
            size = min(512, wide - k)
            lanes = slice(first + k, first + k + size)
            grad = dot_tn(lefts[:, lane : lane + height], rights[:, lanes])
            grad = grad + dot_tn(lefts_got[:, lane : lane + height], rights_got[:, lanes])
            lanes = slice(lane_at + k, lane_at + k + size)
            store_rows(res, lanes, grad)
            if lane_at + k + size == cut:
                emit(True)
        lane_at += wide
    emit(False)
    for copy in outgoing:
        copy.wait()


def outer_grads(arrays, plan, cut, height, name):
    count, groups = lax.axis_size("seq"), lax.axis_size("dp")
    places = bits_of(count)[1:]
    rows = 2 * height // (count * groups)
    tokens = arrays[0].shape[0]
    wide = sum(piece[2] for piece in plan)
    lefts = len({piece[0] for piece in plan})
    shape = (groups,) + (2,) * len(places) + (rows,)
    less = (groups,) + (2,) * (len(places) - 1) + (rows,)
    seq = lax.axis_index("seq")
    bits = jnp.stack([(seq // places[0]) % 2, (seq // places[-1]) % 2]).astype(jnp.int32)
    return call(
        functools.partial(outer_body, plan, cut),
        [SMEM, HBM, HBM, PIN, PIN],
        [(less + (cut,), BF16, HBM)] * 2 + [(less + (wide - cut,), BF16, HBM)] * 2,
        [
            pltpu.VMEM((tokens, lefts * height), BF16),
            pltpu.VMEM((tokens, lefts * height), BF16),
            pltpu.VMEM(shape + (wide,), BF16),
            pltpu.SemaphoreType.DMA((4 * len(plan) + 4,)),
        ],
        name=name,
    )(bits, *arrays)


def project_back_body(
    count, seqs, tokens, pairs, size, per_seg,
    me_ref, pre, d_first_in, ptok, near_w,
    *rest,
):
    chunks, rest = rest[:count], rest[count:]
    grad_out, d_perm, payload, vec, keep_out, send_out = rest[:6]
    stage, rights = rest[6:]
    me, core = me_ref[0], me_ref[1]
    width = near_w.shape[1]

    def emit_halves(part):
        wide = width // 2
        for out, which in ((keep_out, core), (send_out, 1 - core)):
            at = pl.ds(pl.multiple_of(part * width + which * wide, LANES), wide)
            out[:, part * wide : (part + 1) * wide] = rights[:, at]

    collect(chunks, stage, me, count)
    targets = [rights.at[:, k * width : (k + 1) * width] for k in range(4)]

    def place(part, s, lane, values):
        at = part * width + lane
        rights[s * tokens : (s + 1) * tokens, at : at + values.shape[1]] = values

    receive_pairs(stage, place, count, seqs, pairs, size, 3)
    for part in range(3):
        emit_halves(part)
    d_resid = d_first_in[...]
    for k in range(3):
        d_resid = d_resid + dot_nt(targets[k][...], near_w[3 + k])
    grad = d_resid.astype(BF16)
    grad_out[...] = grad
    targets[3][...] = grad
    emit_halves(3)
    vec[0:1] = column_sum(targets[0][...])
    vec[1:2] = column_sum(targets[2][...])
    vec[2:3] = column_sum(grad)
    vec[3:8] = jnp.zeros((5, vec.shape[1]), F32)
    total = seqs * tokens
    half = vec.shape[1] // 2
    row = lax.broadcasted_iota(jnp.int32, (total + 16, total), 0)
    place_at = lax.broadcasted_iota(jnp.int32, (total + 16, total), 1)
    rows = seqs * SEGS
    step, rest_row = row // rows, row % rows
    seq = rest_row // SEGS
    tok = (rest_row % SEGS) * per_seg + step
    extra = row - total
    seq = jnp.where(extra >= 0, extra % seqs, seq)
    tok = jnp.where(extra >= 0, jnp.where(extra < seqs, -1, tokens), tok)
    known = extra < 2 * seqs
    d_char = jnp.zeros((total + 16, 2 * half), F32)
    for k in range(3):
        moved = tok + 1 - k
        pick = (place_at == seq * tokens + moved) & (moved >= 0) & (moved < tokens) & known
        shifted = dot(pick.astype(BF16), grad).astype(BF16)
        d_char = d_char + dot_nt(shifted, near_w[k])
    payload[6 * seqs :] = jnp.zeros((payload.shape[0] - 6 * seqs, half), F32)
    for r in range(2):
        grads = d_char[0:total, r * half : (r + 1) * half].reshape(per_seg, rows, half)
        d_perm[r] = grads
        weighted = jnp.sum(grads * ptok[r], axis=0) * pre[0, r]
        for s in range(seqs):
            row = r * seqs + s
            payload[row : row + 1] = column_sum(weighted[s * SEGS : (s + 1) * SEGS])
        edges = d_char[total : total + 2 * seqs, r * half : (r + 1) * half]
        payload[(2 + r) * seqs : (3 + r) * seqs] = edges[0:seqs]
        payload[(4 + r) * seqs : (5 + r) * seqs] = edges[seqs : 2 * seqs]


def chars_back_body(
    count, seqs, steps, per,
    lang, me_ref, ids, gate_b, enter, pseg, vec1, up_vec, vec2, embedded, ptok, d_perm, gate_w_far, cand_w_far,
    *rest,
):
    groups, back_groups, rest = rest[: count // 2], rest[count // 2 : count], rest[count:]
    (
        keep_out, send_out,
        upd, work, d_all, d_tok, gseg, gin, gate_w, cand_w, held, back, sems, vector, owned,
    ) = rest
    me = me_ref[0]
    wanted = [(gate_w_far, gate_w), (cand_w_far, cand_w)]
    wanted += summaries(groups, held, me) + summaries(back_groups, back, me)
    copies = pull(wanted, sems)
    for copy in copies[:2]:
        copy.wait()

    def gathered(j, k):
        return held[j, k * seqs : (k + 1) * seqs]

    def gathered_back(j, k):
        return back[j, k * seqs : (k + 1) * seqs]

    rows = seqs * SEGS
    half = upd.shape[2]
    gates(embedded[...], gate_w, gate_b[...], cand_w, upd, work)

    def ahead(q, carry):
        h0, h1 = carry
        for j in range(per):
            at = pl.ds(pl.multiple_of((q * per + j) * rows, rows), rows)
            u = upd[0, at, :]
            gap = work[0, at, :] - h0
            work[0, at, :] = gap * (u * (1.0 - u))
            h0 = h0 + u * gap
            at = pl.ds(pl.multiple_of((steps - 1 - q * per - j) * rows, rows), rows)
            u = upd[1, at, :]
            gap = work[1, at, :] - h1
            work[1, at, :] = gap * (u * (1.0 - u))
            h1 = h1 + u * gap
        return h0, h1

    lax.fori_loop(0, steps // per, ahead, (enter[0], enter[1]))

    left = jnp.maximum(me - 1, 0)
    right = jnp.minimum(me + 1, count - 1)
    last = steps // per - 1
    for copy in copies[2:]:
        copy.wait()
    d_tok[...] = d_perm[...]
    for r in range(2):
        from_left = jnp.where(me > 0, gathered_back(left, 4 + r), 0.0)
        from_right = jnp.where(me < count - 1, gathered_back(right, 2 + r), 0.0)
        for s in range(seqs):
            low, high = s * SEGS, s * SEGS + SEGS - 1
            d_tok[r, 0, low : low + 1] += from_left[s : s + 1]
            d_tok[r, last, high : high + 1] += from_right[s : s + 1]
        gseg[r] = jnp.sum(d_tok[r] * ptok[r], axis=0)

    def block_sum(j, r):
        total = gathered_back(j, r)
        near, far = gathered(j, 4 * r + 2), gathered(j, 4 * r)
        if r == 1:
            near, far = far, near
        if j > 0:
            total = total + near * gathered_back(j - 1, 4 + r)
        if j < count - 1:
            total = total + far * gathered_back(j + 1, 2 + r)
        return total

    g0 = jnp.zeros((seqs, half), F32)
    g1 = jnp.zeros((seqs, half), F32)
    for j in range(count):
        i = count - 1 - j
        g0 = jnp.where(i > me, gathered(i, 0) * g0 + block_sum(i, 0), g0)
        g1 = jnp.where(j < me, gathered(j, 4) * g1 + block_sum(j, 1), g1)
    for s in range(seqs):
        flow = g0[s : s + 1]
        for g in range(SEGS - 1, -1, -1):
            row = s * SEGS + g
            gin[0, row : row + 1] = flow
            flow = pseg[0, row : row + 1] * flow + gseg[0, row : row + 1]
        flow = g1[s : s + 1]
        for g in range(SEGS):
            row = s * SEGS + g
            gin[1, row : row + 1] = flow
            flow = pseg[1, row : row + 1] * flow + gseg[1, row : row + 1]

    def astern(q, carry):
        flow0, flow1 = carry
        for j in range(per):
            at = pl.ds(pl.multiple_of((steps - 1 - q * per - j) * rows, rows), rows)
            if j == 0:
                flow0 = flow0 + d_tok[0, steps // per - 1 - q]
            u = upd[0, at, :]
            d_all[at, 0:half] = (flow0 * work[0, at, :]).astype(BF16)
            d_cand = flow0 * u
            d_all[at, half : 2 * half] = d_cand.astype(BF16)
            flow0 = flow0 - d_cand
            at = pl.ds(pl.multiple_of((q * per + j) * rows, rows), rows)
            if j == 0:
                flow1 = flow1 + d_tok[1, q]
            u = upd[1, at, :]
            d_all[at, 2 * half : 3 * half] = (flow1 * work[1, at, :]).astype(BF16)
            d_cand = flow1 * u
            d_all[at, 3 * half : 4 * half] = d_cand.astype(BF16)
            flow1 = flow1 - d_cand
        return flow0, flow1

    lax.fori_loop(0, steps // per, astern, (gin[0], gin[1]))
    grad_w = dot_tn(embedded[...], d_all[...])
    place_owned(owned, grad_w)
    d_emb = jnp.zeros(embedded.shape, F32)
    gate_sums = []
    for r in range(2):
        gate_sums.append(column_sum(d_all[:, 2 * r * half : (2 * r + 1) * half]))
        d_emb = d_emb + dot_nt(d_all[:, 2 * r * half : (2 * r + 1) * half], gate_w[r])
        d_emb = d_emb + dot_nt(d_all[:, (2 * r + 1) * half : (2 * r + 2) * half], cand_w[r])
    partial = dot_tn(one_hot_rows(ids, seqs, steps), d_emb.astype(BF16))
    local = lax.broadcasted_iota(jnp.int32, partial.shape, 0)
    for s in range(seqs):
        tag = lang[s].astype(F32)
        partial = jnp.where(local == s * LANES + LANES - 1, tag, partial)
    core = me_ref[1]
    wide = partial.shape[1] // 2
    low, high = partial[:, :wide].astype(BF16), partial[:, wide:].astype(BF16)
    rows = partial.shape[0]
    keep_out[0:rows] = jnp.where(core == 0, low, high)
    send_out[0:rows] = jnp.where(core == 0, high, low)
    sums = [vec1[k : k + 1] for k in range(6)] + [up_vec[...]]
    sums += [vec2[k : k + 1] for k in range(3)] + gate_sums
    vector[...] = jnp.zeros_like(vector)
    at = 0
    for values in sums:
        for k in range(values.shape[1] // LANES):
            vector[at : at + 1] = values[:, k * LANES : (k + 1) * LANES]
            at += 1
    send_out[rows : rows + vector.shape[0]] = vector[...].astype(BF16)
    keep_out[rows:] = owned[core].astype(BF16)
    send_out[rows + vector.shape[0] :] = owned[1 - core].astype(BF16)


def place_owned(owned, grad):
    count, groups = lax.axis_size("seq"), lax.axis_size("dp")
    rows = grad.shape[0] // (count * groups)
    tiles = grad.shape[1] // LANES
    bits = count.bit_length() - 1
    for d in range(groups):
        for s in range(count):
            mirrored = 0
            for b in range(1, bits):
                mirrored = mirrored * 2 + (s >> b) % 2
            at = (mirrored * groups + d) * rows * tiles
            first = (d * count + s) * rows
            for t in range(tiles):
                value = grad[first : first + rows, t * LANES : (t + 1) * LANES]
                owned[s % 2, at + t * rows : at + (t + 1) * rows] = value


def mix_body(rows, vector_rows, first, last, bits_ref, keep, sent, got, *outs):
    fixed = rows + vector_rows
    table = (keep if first else sent)[0:rows].astype(F32) + got[0:rows].astype(F32)
    vector = sent[rows:fixed].astype(F32) + got[rows:fixed].astype(F32)
    start = rows if first else 0
    size = keep.shape[0] - start
    if last:
        piece = size // len(outs)
        for k, out in enumerate(outs):
            which = jnp.bitwise_xor(bits_ref[0], k) * piece
            at = pl.ds(pl.multiple_of(start + which, 8), piece)
            from_got = pl.ds(pl.multiple_of(fixed + which, 8), piece)
            out[fixed:] = (keep[at].astype(F32) + got[from_got].astype(F32)).astype(BF16)
    else:
        piece = size // 2
        for out, bit in ((outs[0], 1 - bits_ref[0]), (outs[1], bits_ref[0])):
            at = pl.ds(pl.multiple_of(start + bit * piece, 16), piece)
            from_got = pl.ds(pl.multiple_of(fixed + bit * piece, 16), piece)
            total = (keep[at].astype(F32) + got[from_got].astype(F32)).astype(BF16)
            if out is outs[0]:
                out[fixed:] = total
            else:
                out[...] = total
    for out in outs if last else outs[:1]:
        out[0:rows] = table.astype(BF16)
        out[rows:fixed] = vector.astype(BF16)


def table_body(groups, seqs, sub, count, place_ref, *refs):
    own, other, rest = refs[:groups], refs[groups : 2 * groups], refs[2 * groups :]
    table, gate_out, cand_out, *vectors, vector, low, high, vec, held = rest
    dp, core = place_ref[0], place_ref[1]
    vocab, width = table.shape
    half = width // 2
    rows = low.shape[1]
    for k in range(groups):
        at = jnp.bitwise_xor(dp, k)
        mine, their = own[k][0:rows], other[k][0:rows]
        low[at] = jnp.where(core == 0, mine, their)
        high[at] = jnp.where(core == 0, their, mine)
        vec[at] = own[k][rows : rows + vector.shape[0]].astype(F32)
    fixed = rows + vector.shape[0]
    mine = own[0][fixed:].astype(F32)
    for part in own[1:]:
        mine = mine + part[fixed:].astype(F32)
    held[...] = mine
    owned = gate_out.shape[1]
    tiles = held.shape[0] // owned // 4
    for k in range(4):
        home = (gate_out, cand_out)[k % 2]
        for t in range(tiles):
            at = (k * tiles + t) * owned
            home[k // 2, :, t * LANES : (t + 1) * LANES] = held[at : at + owned]
    wide = -(-vocab // 16) * 16
    row = lax.broadcasted_iota(jnp.int32, (wide, LANES), 0)
    local = lax.broadcasted_iota(jnp.int32, (wide, LANES), 1)
    sums = jnp.zeros((wide, width), F32)
    total = jnp.zeros(vector.shape, F32)
    for g in range(groups):
        picks = []
        for s in range(seqs):
            tag = low[g, (s + 1) * LANES - 16 : (s + 1) * LANES, 0:1].astype(F32)[15:16]
            lang = (tag * (1.0 / count) + 0.5).astype(jnp.int32)
            picks.append(jnp.where((row - lang * sub == local) & (local < sub), 1.0, 0.0).astype(BF16))
        both = jnp.concatenate([low[g], high[g]], axis=1)
        sums = sums + dot(jnp.concatenate(picks, axis=1), both)
        total = total + vec[g]
    table[...] = sums[0:vocab]
    vector[...] = total
    at = 0
    for out in vectors:
        for k in range(out.shape[-1] // LANES * (out.shape[0] if len(out.shape) > 1 else 1)):
            if len(out.shape) > 1:
                per_row = out.shape[1] // LANES
                lanes = slice(k % per_row * LANES, (k % per_row + 1) * LANES)
                out[k // per_row : k // per_row + 1, lanes] = vector[at : at + 1]
            else:
                out[k * LANES : (k + 1) * LANES] = vector[at]
            at += 1


def fold_body(bits_ref, *refs):
    ins, outs = refs[:4], refs[4:]
    for k in range(2):
        keep, got, bit = ins[2 * k], ins[2 * k + 1], bits_ref[k]
        for out, which in ((outs[2 * k], 1 - bit), (outs[2 * k + 1], bit)):
            out[...] = (keep[:, which].astype(F32) + got[:, which].astype(F32)).astype(BF16)


def halve_body(sizes, alone, bits_ref, *refs):
    ins, outs = refs[:-4], refs[-4:]
    owners = ins[0].shape[0]
    at = 0
    for k, size in enumerate(sizes):
        rows = slice(at, at + size) if alone else slice(0, size)
        parts = ins if alone else ins[2 * k : 2 * k + 2]
        for out, which in ((outs[2 * k], 1 - bits_ref[k]), (outs[2 * k + 1], bits_ref[k])):
            for i in range(owners // 2):
                place = which * (owners // 2) + i if k == 0 else 2 * i + which
                total = parts[0][place, rows].astype(F32)
                for part in parts[1:]:
                    total = total + part[place, rows].astype(F32)
                out[i] = total.astype(BF16)
        at += size if alone else 0


def part_rows_body(sizes, core_ref, kept, got, kept_on, got_on, send, keep):
    core = core_ref[0]
    total = jnp.concatenate(
        [a[...].astype(F32) + b[...].astype(F32) for a, b in ((kept, got), (kept_on, got_on))], axis=0
    )
    at = 0
    for size in sizes:
        first, second = total[2 * at : 2 * at + size], total[2 * at + size : 2 * at + 2 * size]
        send[at : at + size] = jnp.where(core == 0, second, first)
        keep[at : at + size] = jnp.where(core == 0, first, second)
        at += size


def beside_body(pieces, core_ref, keep, got, up, out, down):
    core = core_ref[0]
    wide = keep.shape[1]
    rows = up.shape[0]
    low = jnp.where(core == 0, keep[...], got[...])
    high = jnp.where(core == 0, got[...], keep[...])
    for k in range(pieces + 1):
        home, lane = (up, k * wide) if k < pieces else (out, 0)
        gap = up.shape[1] // 2 if k < pieces else wide
        home[:, lane : lane + wide] = low[k * rows : (k + 1) * rows]
        home[:, lane + gap : lane + gap + wide] = high[k * rows : (k + 1) * rows]
    down[:, 0:wide] = low[(pieces + 1) * rows :]
    down[:, wide : 2 * wide] = high[(pieces + 1) * rows :]


def part_cores_body(core_ref, low_keep, low_got, high_keep, high_got, send, keep):
    core = core_ref[0]
    rows = keep.shape[1]
    lane = 0
    for mine, got in ((low_keep, low_got), (high_keep, high_got)):
        wide = mine.shape[2]
        total = mine[...].astype(F32) + got[...].astype(F32)
        first, second = total[:, 0:rows], total[:, rows : 2 * rows]
        send[:, :, lane : lane + wide] = jnp.where(core == 0, second, first).astype(BF16)
        keep[:, :, lane : lane + wide] = jnp.where(core == 0, first, second).astype(BF16)
        lane += wide


def both_body(widths, core_ref, keep, got, out):
    core = core_ref[0]
    lane = 0
    for wide in widths:
        a, b = keep[:, :, lane : lane + wide], got[:, :, lane : lane + wide]
        out[:, :, 2 * lane : 2 * lane + wide] = jnp.where(core == 0, a, b)
        out[:, :, 2 * lane + wide : 2 * lane + 2 * wide] = jnp.where(core == 0, b, a)
        lane += wide


def total_body(widths, both, *outs):
    outs = list(outs[:-1]) + [outs[-1].at[k] for k in range(outs[-1].shape[0])]
    lane = 0
    for out, wide in zip(outs, widths):
        out[...] = both[:, lane : lane + 2 * wide].astype(F32)
        lane += 2 * wide


def shift(array, by):
    count = lax.axis_size("seq")
    return lax.ppermute(array, "seq", [(i, (i + by) % count) for i in range(count)])


def swap(array, axis, bit):
    return lax.ppermute(array, axis, [(i, i ^ bit) for i in range(lax.axis_size(axis))])


def exchange(chunks):
    return [chunks[0]] + [shift(chunk, k) for k, chunk in enumerate(chunks) if k > 0]


def bits_of(count):
    return [1 << b for b in range(count.bit_length() - 1)]


def tie(arrays, *after):
    held = lax.optimization_barrier((tuple(arrays), after))
    return list(held[0])


def gather_summaries(rows):
    pair = jnp.stack([rows, swap(rows, "seq", 1)])
    return [pair] + [swap(pair, "seq", 2 * j) for j in range(1, lax.axis_size("seq") // 2)]


class Columns:
    def __init__(self, sends_and_keeps, widths):
        self.places = bits_of(lax.axis_size("seq"))[1:]
        self.seq = lax.axis_index("seq")
        self.widths = widths
        self.done = 0
        low_send, low_keep, high_send, high_keep = sends_and_keeps
        self.sends, self.keeps = (low_send, high_send), (low_keep, high_keep)
        self.hold_swap()

    def hold_swap(self):
        bits = self.places[self.done], self.places[-1 - self.done]
        self.gots = tuple(swap(send, "seq", bit) for send, bit in zip(self.sends, bits))
        self.done += 1

    def fold(self, *after):
        keeps, gots = self.keeps, self.gots
        if after:
            keeps = tie(keeps, *after)
        bits = self.places[self.done], self.places[-1 - self.done]
        chosen = jnp.stack([(self.seq // bit) % 2 for bit in bits]).astype(jnp.int32)
        flat, shapes = [], []
        for k, (keep, got) in enumerate(zip(keeps, gots)):
            dims = keep.shape
            if k == 0:
                flat += [x.reshape((-1, 2) + dims[-2:]) for x in (keep, got)]
                shapes.append(dims[:-3] + dims[-2:])
            else:
                flat += [x.reshape(dims[:2] + (-1, dims[-1])) for x in (keep, got)]
                shapes.append(dims[:1] + dims[2:])
        outs = []
        for k in range(2):
            dims = flat[2 * k].shape
            outs += [((dims[0],) + dims[2:], BF16)] * 2
        got = call(fold_body, [SMEM] + [VMEM] * 4, outs, limit=24, name="fold")(chosen, *flat)
        self.sends = (got[0].reshape(shapes[0]), got[2].reshape(shapes[1]))
        self.keeps = (got[1].reshape(shapes[0]), got[3].reshape(shapes[1]))
        self.hold_swap()

    def part_cores(self, *after):
        while self.done < len(self.places):
            self.fold()
        keeps = self.keeps
        if after:
            keeps = tie(keeps, *after)
        groups, rows, _ = keeps[0].shape
        wide = sum(self.widths)
        core = (self.seq % 2).astype(jnp.int32).reshape(1)
        self.send, self.keep = call(
            part_cores_body,
            [SMEM] + [VMEM] * 4,
            [((groups, rows // 2, wide), BF16)] * 2,
            limit=24,
            name="part_cores",
        )(core, keeps[0], self.gots[0], keeps[1], self.gots[1])
        self.got = swap(self.send, "seq", 1)

    def scatter_groups(self, *after):
        groups, rows, wide = self.keep.shape
        (keep,) = tie([self.keep], *after)
        core = (self.seq % 2).astype(jnp.int32).reshape(1)
        (self.both,) = call(
            functools.partial(both_body, self.widths),
            [SMEM] + [VMEM] * 2,
            [((groups, rows, 2 * wide), BF16)],
            limit=24,
            name="both_cores",
        )(core, keep, self.got)
        both = self.both.reshape(groups * rows, 2 * wide)
        self.own = lax.psum_scatter(both, "dp", scatter_dimension=0, tiled=True)

    def finish(self, last):
        return call(
            functools.partial(total_body, self.widths),
            [VMEM],
            [((self.own.shape[0], 2 * wide), F32) for wide in self.widths[:-last]]
            + [((last, self.own.shape[0], 2 * self.widths[-1]), F32)],
            limit=24,
            name="total",
        )(self.own)


class FeedRows:
    def __init__(self, grad, first):
        self.places = bits_of(lax.axis_size("seq"))[1:]
        self.seq = lax.axis_index("seq")
        self.first = first
        flat = grad.reshape(-1, grad.shape[-1])
        got = lax.psum_scatter(flat, "dp", scatter_dimension=0, tiled=True)
        self.parts = [got.reshape(grad.shape[1:])]
        self.done = 0

    def step(self, *after):
        parts = self.parts
        if after:
            parts = tie(parts, *after)
        bits = self.places[-1 - self.done], self.places[self.done]
        chosen = jnp.stack([(self.seq // bit) % 2 for bit in bits]).astype(jnp.int32)
        if self.done == 0:
            rows, wide = parts[0].shape[-2:]
            sizes = (self.first, rows - self.first)
            ins = [parts[0].reshape((-1, rows, wide))]
        else:
            wide = parts[0].shape[-1]
            sizes = (self.first, parts[2].shape[-2])
            ins = parts
        owners = 2 ** (len(self.places) - self.done - 1)
        outs = [((owners, size, wide), BF16) for size in sizes for _ in range(2)]
        got = call(
            functools.partial(halve_body, sizes, len(ins) == 1),
            [SMEM] + [VMEM] * len(ins),
            outs,
            limit=24,
            name="halve",
        )(chosen, *ins)
        self.sends = (got[0], got[2])
        gots = [swap(send, "seq", bit) for send, bit in zip(self.sends, bits)]
        self.parts = [got[1], gots[0], got[3], gots[1]]
        self.done += 1

    def finish(self, ff, width, *after):
        while self.done < len(self.places):
            self.step()
        parts = tie([part[0] for part in self.parts], *after)
        rows, wide = sum(part.shape[0] for part in parts[::2]), parts[0].shape[1]
        core = (self.seq % 2).astype(jnp.int32).reshape(1)
        pieces = (ff + width) // width
        owned = width // (lax.axis_size("seq") * lax.axis_size("dp"))
        send, keep = call(
            functools.partial(part_rows_body, (owned,) * pieces + (rows // 2 - pieces * owned,)),
            [SMEM] + [VMEM] * 4,
            [((rows // 2, wide), F32)] * 2,
            limit=24,
            name="part_rows",
        )(core, *parts)
        got = swap(send, "seq", 1)
        return call(
            functools.partial(beside_body, pieces - 1),
            [SMEM] + [VMEM] * 2,
            [((owned, ff), F32), ((owned, width), F32), ((rows // 2 - pieces * owned, width), F32)],
            limit=24,
            name="beside",
        )(core, keep, got)


class CharsSums:
    def __init__(self, keep, send, rows, vector_rows):
        self.keep, self.send, self.rows, self.vector_rows = keep, send, rows, vector_rows
        self.seq = lax.axis_index("seq")
        self.bits = bits_of(lax.axis_size("seq"))
        self.first = True

    def step(self, *after):
        bit = self.bits.pop(0)
        groups = lax.axis_size("dp")
        send, keep = self.send, self.keep
        got = swap(send, "seq", bit)
        if after:
            (keep,) = tie([keep], *after)
        last = not self.bits
        start = self.rows if self.first else 0
        size = keep.shape[0] - start
        fixed = self.rows + self.vector_rows
        if last:
            which = lax.axis_index("dp")
            outs = [((fixed + size // groups, LANES), BF16)] * groups
        else:
            which = (self.seq // self.bits[0]) % 2
            outs = [((fixed + size // 2, LANES), BF16), ((size // 2, LANES), BF16)]
        outs = call(
            functools.partial(mix_body, self.rows, self.vector_rows, self.first, last),
            [SMEM] + [VMEM] * 3,
            outs,
            limit=12,
            name="mix",
        )(which.astype(jnp.int32).reshape(1), keep, send, got)
        self.first = False
        if last:
            self.own, self.sends = outs[0], outs[1:]
        else:
            self.send, self.keep = outs

    def across(self, *after):
        self.sends = tie(self.sends, *after)
        self.own = [self.own] + [swap(part, "dp", k + 1) for k, part in enumerate(self.sends)]

    def finish(self, seqs, vocab, sub, gate_shape, sizes, *after):
        own = self.own
        other = tie([swap(part, "seq", 1) for part in own], *after)
        groups = len(own)
        rows, vector_rows = self.rows, self.vector_rows
        place = jnp.stack([lax.axis_index("dp"), self.seq % 2]).astype(jnp.int32)
        return call(
            functools.partial(table_body, groups, seqs, sub, lax.axis_size("seq")),
            [SMEM] + [VMEM] * (2 * groups),
            [((vocab, 2 * LANES), F32)] + [(gate_shape, F32)] * 2 + [(size, F32) for size in sizes],
            [
                pltpu.VMEM((vector_rows, LANES), F32),
                pltpu.VMEM((groups, rows, LANES), BF16),
                pltpu.VMEM((groups, rows, LANES), BF16),
                pltpu.VMEM((groups, vector_rows, LANES), F32),
                pltpu.VMEM((own[0].shape[0] - rows - vector_rows, LANES), F32),
            ],
            limit=24,
            name="table_rows",
        )(place, *own, *other)


def shards(
    inputs, char_ids, lang_ids, lengths, char_table, gate_weight, gate_bias, cand_weight,
    join_weight, join_bias, query_weight, query_bias, key_weight, value_weight, value_bias,
    out_weight, out_bias, norm1_gain, norm1_bias, up_weight, up_bias, down_weight, down_bias,
    norm2_gain, norm2_bias, cotangent,
):
    seqs, tokens, width = inputs.shape
    chars = char_ids.shape[1]
    per = chars // tokens
    steps = chars // SEGS
    per_seg = steps // per
    vocab, embed = char_table.shape
    sub = vocab // GROUPS
    half = width // 2
    size = width // HEADS
    ff = up_weight.shape[1]
    count = lax.axis_size("seq")
    pairs = -(-seqs * HEADS // count)
    while HEADS % pairs:
        pairs += 1
    full = count * tokens
    total = seqs * tokens
    rows = seqs * SEGS
    wide = pairs * size
    seq = lax.axis_index("seq")
    me = jnp.stack([seq, seq % 2]).astype(jnp.int32)
    flat = inputs.reshape(total, width)
    cot = cotangent.reshape(total, width)

    embedded, htok, ptok, pre, pseg, payload = call(
        functools.partial(chars_forward_body, seqs, steps, per, sub),
        [SMEM] + [COPY] * 2 + [HBM] * 3,
        [
            ((seqs * chars, embed), BF16, COPY),
            ((2, per_seg, rows, half), F32, COPY),
            ((2, per_seg, rows, half), F32, COPY),
            ((2, 2, rows, half), F32, COPY),
            ((2, rows, half), F32),
            ((8 * seqs, half), F32),
        ],
        [
            pltpu.VMEM((2, seqs * chars, half), F32),
            pltpu.VMEM((2, seqs * chars, half), F32),
            pltpu.VMEM((2, rows, half), F32),
            pltpu.VMEM((-(-vocab // LANES) * LANES, embed), BF16),
            pltpu.VMEM(gate_weight.shape, BF16),
            pltpu.VMEM(cand_weight.shape, BF16),
            pltpu.SemaphoreType.DMA((3,)),
        ],
        name="chars_forward",
    )(lang_ids, char_ids, gate_bias, char_table, gate_weight, cand_weight)
    groups = gather_summaries(payload)
    projections = (join_weight, query_weight, key_weight, value_weight)
    (near_w,) = ahead_of(projections, groups[0])

    resid, enter, joined, *sent = call(
        functools.partial(join_query_body, count, seqs, tokens, pairs),
        [SMEM] + [COPY] * 6 + [PIN] + [HBM] * (1 + count // 2),
        [
            ((total, width), F32, PIN),
            ((2, rows, half), F32),
            ((total, 4 * width), BF16, COPY),
        ]
        + [((tokens, 3 * wide), BF16, PIN)] * count,
        [
            pltpu.VMEM((count, 8 * seqs, half), F32),
            pltpu.VMEM((total, width), BF16),
            pltpu.SemaphoreType.DMA((count + 1,)),
            pltpu.VMEM((count, tokens, 3 * wide), BF16),
        ],
        name="join_query",
    )(
        me, htok, ptok, pre, join_bias, query_bias, value_bias, near_w,
               flat, *groups,
    )
    heads = exchange(sent)

    block = min(1024, full)
    *sent, lse, heads_q, heads_k, heads_v, out_v, up_v = call(
        functools.partial(attend_body, count, seqs, tokens, pairs, size, block),
        [SMEM, SMEM] + [PIN] * count,
        [((tokens, wide), BF16, PIN)] * count
        + [((8, full), F32)]
        + [((pairs, full, LANES), BF16, HBM)] * 3,
        [pltpu.VMEM((pairs, full, LANES), BF16)] * 3
        + [
            pltpu.VMEM((pairs, size + 16, full), BF16),
            pltpu.VMEM((wide, full), F32),
            pltpu.VMEM((full, wide), BF16),
            pltpu.SemaphoreType.DMA((3,)),
        ],
        name="attend",
        fetch=(out_weight, up_weight),
    )(me, lengths, *heads)
    mixed_chunks = exchange(sent)
    (joined_far,) = tie([joined], *mixed_chunks)
    joined_got = swap(joined_far, "seq", 1)

    ff_block = 768
    output, d_first_in, vec1, up_vec, fed, fed_keep, fed_send, *sent = call(
        functools.partial(feed_body, count, seqs, tokens, pairs, size, ff_block),
        [SMEM] + [VMEM] * 7 + [PIN] * 3 + [HBM] * 2 + [PIN] * count,
        [
            ((total, width), BF16, HBM),
            ((total, width), F32, COPY),
            ((8, width), F32),
            ((1, ff), F32),
            ((total, ff + 2 * width), BF16, PIN),
            ((total, ff // 2 + width), BF16, PIN),
            ((total, ff // 2 + width), BF16),
        ]
        + [((tokens, wide), BF16, PIN)] * count,
        [
            pltpu.VMEM((count, tokens, wide), BF16),
            pltpu.VMEM((total, ff), F32),
            pltpu.VMEM((total, width), F32),
            pltpu.VMEM((total, width), BF16),
            pltpu.VMEM((total, width), BF16),
            pltpu.VMEM((total, ff), BF16),
            pltpu.VMEM((total, width), BF16),
            pltpu.VMEM((ff, width), BF16),
            pltpu.SemaphoreType.DMA((2 + ff // ff_block,)),
        ],
        limit=32,
        name="feed_forward",
    )(
        me, out_bias, norm1_gain, norm1_bias, up_bias, down_bias, norm2_gain, norm2_bias, resid,
        out_v, up_v, cot, down_weight, *mixed_chunks,
    )
    d_mixed_chunks = exchange(sent)

    fed_got, fed_keep_got = swap(fed, "seq", 1), swap(fed_send, "seq", 1)
    fed, fed_got, fed_keep, fed_keep_got = tie(
        [fed, fed_got, fed_keep, fed_keep_got], *d_mixed_chunks
    )
    grad_feed = feed_grads(fed, fed_got, fed_keep, fed_keep_got, ff, width)
    feed = FeedRows(grad_feed, (ff + width) * 2 // (count * lax.axis_size("dp")))
    d_mixed_chunks = tie(d_mixed_chunks, grad_feed)

    back_block = min(512, full)
    sent = call(
        functools.partial(attend_back_body, count, seqs, tokens, pairs, size, back_block),
        [SMEM, VMEM] + [HBM] * 3 + [PIN] * count,
        [((tokens, 3 * wide), BF16, PIN)] * count,
        [pltpu.VMEM((pairs, full, LANES), BF16)] * 3
        + [
            pltpu.VMEM((size, full), BF16),
            pltpu.VMEM((pairs, full, size), BF16),
            pltpu.VMEM((wide, full), F32),
            pltpu.VMEM((full, full), BF16),
            pltpu.VMEM((full, full), BF16),
            pltpu.VMEM((full, 3 * wide), BF16),
            pltpu.SemaphoreType.DMA((3,)),
        ],
        name="attend_back",
    )(me, lse, heads_q, heads_k, heads_v, *d_mixed_chunks)
    d_chunks = exchange(sent)
    (near_w,) = ahead_of(projections, sent[0])
    input_grad, d_perm, payload_back, vec2, back_keep, back_send = call(
        functools.partial(project_back_body, count, seqs, tokens, pairs, size, per_seg),
        [SMEM, COPY, COPY, COPY, PIN] + [PIN] * count,
        [
            ((total, width), BF16, COPY),
            ((2, per_seg, rows, half), F32, COPY),
            ((8 * seqs, half), F32),
            ((8, width), F32),
            ((total, 2 * width), BF16, PIN),
            ((total, 2 * width), BF16),
        ],
        [
            pltpu.VMEM((count, tokens, 3 * wide), BF16),
            pltpu.VMEM((total, 4 * width), BF16),
        ],
        name="project_back",
    )(me, pre, d_first_in, ptok, near_w, *d_chunks)
    back_groups = gather_summaries(payload_back)
    vector_rows = -(-(10 * width + ff) // (16 * LANES)) * 16

    back_got = swap(back_send, "seq", 1)
    back_all = tie([joined, joined_got, back_keep, back_got], back_groups[0])
    back_plan = tuple((0, k * half, half) for k in range(3))
    back_plan += tuple(((1 + k) * width, 3 * half, half) for k in range(3))
    back_parts = outer_grads(back_all, back_plan, 3 * half, width, "grad_back")
    back_parts = tie(back_parts, *back_groups)
    back = Columns(back_parts, (half,) * 6)
    back_groups = tie(back_groups, *back_parts)

    own_rows = 4 * half * embed // (2 * LANES)
    table_rows = seqs * LANES
    chars_keep, chars_send = call(
        functools.partial(chars_back_body, count, seqs, steps, per),
        [SMEM, SMEM] + [VMEM] * 7 + [COPY] * 3 + [HBM] * (2 + count),
        [
            ((table_rows + own_rows, LANES), BF16),
            ((table_rows + vector_rows + own_rows, LANES), BF16),
        ],
        [
            pltpu.VMEM((2, seqs * chars, half), F32),
            pltpu.VMEM((2, seqs * chars, half), F32),
            pltpu.VMEM((seqs * chars, 4 * half), BF16),
            pltpu.VMEM((2, per_seg, rows, half), F32),
            pltpu.VMEM((2, rows, half), F32),
            pltpu.VMEM((2, rows, half), F32),
            pltpu.VMEM(gate_weight.shape, BF16),
            pltpu.VMEM(cand_weight.shape, BF16),
            pltpu.VMEM((count, 8 * seqs, half), F32),
            pltpu.VMEM((count, 8 * seqs, half), F32),
            pltpu.SemaphoreType.DMA((2 + 2 * count,)),
            pltpu.VMEM((vector_rows, LANES), F32),
            pltpu.VMEM((2, own_rows, LANES), F32),
        ],
        name="chars_back",
    )(
        lang_ids, me, char_ids, gate_bias, enter, pseg, vec1, up_vec, vec2, embedded, ptok, d_perm,
        gate_weight, cand_weight, *groups, *back_groups,
    )
    chars_sums = CharsSums(chars_keep, chars_send, table_rows, vector_rows)
    chars_sums.step()
    back.fold(chars_sums.send)
    chars_sums.step()
    back.part_cores()
    back.scatter_groups(chars_sums.send)
    while chars_sums.bits:
        chars_sums.step()
    chars_sums.across()
    feed.step(back.both, *chars_sums.sends)
    feed.step(*chars_sums.own[1:3])
    grad_up, grad_out, grad_down = feed.finish(ff, width, *chars_sums.own)
    grad_query, grad_key, grad_value, grad_join = back.finish(3)
    gate_shape = (2, embed // (count * lax.axis_size("dp")), half)
    sizes = [(width,)] * 6 + [(ff,)] + [(width,)] * 3 + [(2, half)]
    grad_table, grad_gate, grad_cand, *sums = chars_sums.finish(
        seqs, vocab, sub, gate_shape, sizes, grad_up, grad_query
    )

    return (
        output.reshape(inputs.shape),
        input_grad.reshape(inputs.shape),
        grad_table,
        grad_gate,
        sums[10],
        grad_cand,
        grad_join,
        sums[9],
        grad_query,
        sums[7],
        grad_key,
        grad_value,
        sums[8],
        grad_out,
        sums[5],
        sums[3],
        sums[4],
        grad_up,
        sums[6],
        grad_down,
        sums[2],
        sums[0],
        sums[1],
    )


def solution(mesh):
    spread_rows = P("dp", "seq", None)
    placed = (
        (spread_rows, P("dp", "seq"), P("dp"), P("dp")) + (P(),) * 21 + (spread_rows,)
    )
    owned = P(("dp", "seq"), None)
    owned_mid = P(None, ("dp", "seq"), None)
    return jax.shard_map(
        shards,
        mesh=mesh,
        in_specs=placed,
        out_specs=(
            spread_rows, spread_rows, P(), owned_mid, P(), owned_mid, owned_mid, P(),
            owned, P(), owned, owned, P(), owned, P(), P(), P(), owned, P(), owned, P(), P(), P(),
        ),
        check_vma=False,
    )
```

```python
import functools

import jax
import jax.numpy as jnp
from jax import lax
from jax.experimental import pallas as pl
from jax.experimental.pallas import tpu as pltpu
from jax.sharding import PartitionSpec as P

HEADS = 12
GROUPS = 8
SEGS = 8
LANES = 128
NORM_EPS = 1e-05
MASKED = (-998244352.0, -1753088.0, -2560.0)
MIB = 1 << 20
F32 = jnp.float32
BF16 = jnp.bfloat16


def dot(left, right):
    return jnp.dot(left, right, preferred_element_type=F32)


def dot_nt(left, right):
    return lax.dot_general(left, right, (((1,), (1,)), ((), ())), preferred_element_type=F32)


def dot_tn(left, right):
    return lax.dot_general(left, right, (((0,), (0,)), ((), ())), preferred_element_type=F32)


def column_sum(values):
    return jnp.sum(values.astype(F32), axis=0, keepdims=True)


VMEM = pl.BlockSpec(memory_space=pltpu.VMEM)
SMEM = pl.BlockSpec(memory_space=pltpu.SMEM)
HBM, PIN, COPY = "hbm", "pin", "copy"


def call(body, ins, outs, scratch=(), limit=40, name=None, fetch=()):
    spaces = {PIN: pltpu.VMEM, HBM: pltpu.HBM, COPY: pltpu.HBM}
    specs = {PIN: VMEM, HBM: pl.BlockSpec(memory_space=pltpu.HBM), COPY: VMEM}
    space_of = lambda spec: spaces[spec] if isinstance(spec, str) else None
    spec_of = lambda spec: specs[spec] if isinstance(spec, str) else spec
    all_ins = list(ins) + [HBM] * len(fetch)
    all_outs = [out if len(out) > 2 else out + (VMEM,) for out in outs]
    homes = {}
    for array in fetch:
        homes.setdefault(array.shape[-2:], []).append(array)
    homes = list(homes.items())
    fetch = [array for _, arrays in homes for array in arrays]
    for shape, arrays in homes:
        count = sum(array.size for array in arrays) // (shape[0] * shape[1])
        all_outs.append(((count,) + shape, arrays[0].dtype, PIN))
    scratch = list(scratch)
    inner = body
    if fetch:
        parts = 4
        scratch.append(pltpu.SemaphoreType.DMA((len(fetch) * parts,)))

        def inner(*refs):
            sems, n_in = refs[-1], len(ins)
            far, rest = refs[n_in : n_in + len(fetch)], refs[n_in + len(fetch) :]
            near, last = rest[len(outs) : len(outs) + len(homes)], len(outs) + len(homes)
            rest = rest[: len(outs)] + rest[last:-1]
            far = list(far)
            copies = []
            for b, (shape, arrays) in zip(near, homes):
                at = 0
                for _ in arrays:
                    a = far.pop(0)
                    wide = a.shape[0] if len(a.shape) > 2 else 1
                    rows = shape[0] // parts
                    for k in range(parts):
                        piece = slice(k * rows, (k + 1) * rows)
                        if len(a.shape) > 2:
                            pair = a.at[:, piece], b.at[slice(at, at + wide), piece]
                        else:
                            pair = a.at[piece], b.at[at, piece]
                        copies.append(pltpu.make_async_copy(*pair, sems.at[len(copies)]))
                    at += wide

            def begin():
                for copy in copies:
                    copy.start()

            body(begin, *refs[:n_in], *rest)
            for copy in copies:
                copy.wait()

    kernel = pl.pallas_call(
        inner,
        in_specs=[spec_of(spec) for spec in all_ins],
        out_specs=[spec_of(out[2]) for out in all_outs],
        out_shape=[
            space_of(out[2])(out[0], out[1]) if space_of(out[2]) else jax.ShapeDtypeStruct(out[0], out[1])
            for out in all_outs
        ],
        scratch_shapes=scratch,
        compiler_params=pltpu.CompilerParams(vmem_limit_bytes=limit * MIB),
        cost_estimate=pl.CostEstimate(flops=1, bytes_accessed=1, transcendentals=0),
        name=name,
    )

    def run(*args):
        args = list(args) + list(fetch)
        held = [
            pltpu.with_memory_space_constraint(arg, space_of(spec)) if space_of(spec) else arg
            for arg, spec in zip(args, all_ins)
        ]
        return kernel(*held)

    return run


def ahead_of(arrays, *after):
    def body(begin, *refs):
        begin()

    arrays = tie(arrays, *after)
    return call(body, [], [], fetch=tuple(arrays), limit=8, name="weights")()


def pull(pairs, sems):
    copies = [pltpu.make_async_copy(far, near, sems.at[k]) for k, (far, near) in enumerate(pairs)]
    for copy in copies:
        copy.start()
    return copies


def collect(chunks, stage, me, count):
    for k, chunk in enumerate(chunks):
        stage[lax.rem(me + count - k, count)] = chunk[...]


def summaries(groups, gathered, me):
    pairs = []
    for j, group in enumerate(groups):
        for i in range(2):
            pairs.append((group.at[i], gathered.at[jnp.bitwise_xor(me, 2 * j + i)]))
    return pairs


def gates(embedded, gate_w, gate_b, cand_w, upd, cand):
    for r in range(2):
        upd[r] = jax.nn.sigmoid(dot(embedded, gate_w[r]) + gate_b[r : r + 1])
        cand[r] = dot(embedded, cand_w[r])


def one_hot_rows(ids, seqs, steps):
    rows = []
    for s in range(seqs):
        for g in range(SEGS):
            rows.append(ids[s : s + 1, g * steps : (g + 1) * steps] + s * LANES)
    held = jnp.concatenate(rows, axis=0)
    place = lax.broadcasted_iota(jnp.int32, (seqs * SEGS, seqs * LANES), 1)
    return jnp.concatenate(
        [(place == held[:, t : t + 1]).astype(F32).astype(BF16) for t in range(steps)], axis=0
    )


def chars_forward_body(
    seqs, steps, per, sub,
    lang, ids, gate_b, table, gate_w_far, cand_w_far,
    embedded_out, htok, ptok, pre, pseg, payload,
    upd, cand, hseg, padded_table, gate_w, cand_w, sems,
):
    rows = seqs * SEGS
    vocab = table.shape[0]
    wide = padded_table.shape[0]
    copies = pull(
        [(table, padded_table.at[0:vocab]), (gate_w_far, gate_w), (cand_w_far, cand_w)], sems
    )
    padded_table[vocab:wide] = jnp.zeros((wide - vocab, padded_table.shape[1]), BF16)
    copies[0].wait()
    local = lax.broadcasted_iota(jnp.int32, (LANES, wide), 0)
    place = lax.broadcasted_iota(jnp.int32, (LANES, wide), 1)
    mine = []
    for s in range(seqs):
        pick = (place == lang[s] * sub + local) & (local < sub)
        mine.append(dot(pick.astype(BF16), padded_table[...]).astype(BF16))
    own_table = jnp.concatenate(mine, axis=0)
    embedded = dot(one_hot_rows(ids, seqs, steps), own_table).astype(BF16)
    embedded_out[...] = embedded
    copies[1].wait()
    copies[2].wait()
    gates(embedded, gate_w, gate_b[...], cand_w, upd, cand)

    def token(q, carry):
        h0, p0, h1, p1 = carry
        for j in range(per):
            at = pl.ds(pl.multiple_of((q * per + j) * rows, rows), rows)
            u = upd[0, at, :]
            h0 = h0 + u * (cand[0, at, :] - h0)
            p0 = p0 * (1.0 - u)
            at = pl.ds(pl.multiple_of((steps - 1 - q * per - j) * rows, rows), rows)
            u = upd[1, at, :]
            h1 = h1 + u * (cand[1, at, :] - h1)
            p1 = p1 * (1.0 - u)
        htok[0, q] = h0
        ptok[0, q] = p0
        back = steps // per - 1 - q
        htok[1, back] = h1
        ptok[1, back] = p1
        return h0, p0, h1, p1

    zero = jnp.zeros((rows, upd.shape[2]), F32)
    h0, p0, h1, p1 = lax.fori_loop(0, steps // per, token, (zero, zero + 1.0, zero, zero + 1.0))
    pseg[0], pseg[1], hseg[0], hseg[1] = p0, p1, h0, h1
    last = steps // per - 1
    for s in range(seqs):
        for r in range(2):
            total_a = jnp.ones((1, upd.shape[2]), F32)
            total_b = jnp.zeros((1, upd.shape[2]), F32)
            order = range(SEGS) if r == 0 else range(SEGS - 1, -1, -1)
            for g in order:
                row = s * SEGS + g
                pre[0, r, row : row + 1] = total_a
                pre[1, r, row : row + 1] = total_b
                p_row = pseg[r, row : row + 1]
                total_b = p_row * total_b + hseg[r, row : row + 1]
                total_a = p_row * total_a
            edge = s * SEGS if r == 0 else s * SEGS + SEGS - 1
            q = 0 if r == 0 else last
            near_a, near_b = ptok[r, q, edge : edge + 1], htok[r, q, edge : edge + 1]
            for k, value in enumerate((total_a, total_b, near_a, near_b)):
                row = (4 * r + k) * seqs + s
                payload[row : row + 1] = value


def spread(values, seqs):
    wide = values.shape[1]
    return jnp.concatenate(
        [jnp.broadcast_to(values[s : s + 1], (SEGS, wide)) for s in range(seqs)], axis=0
    )


def token_row(token, tokens, per_seg, seqs):
    s = token // tokens
    t = token % tokens
    return (t % per_seg) * (seqs * SEGS) + s * SEGS + t // per_seg


def join_query_body(
    count, seqs, tokens, pairs,
    me_ref, htok, ptok, pre, join_b, query_b, value_b, near_w, inputs_far,
    *rest,
):
    groups, rest = rest[: count // 2], rest[count // 2 :]
    resid_out, enter, left_out = rest[:3]
    chunks = rest[3 : 3 + count]
    held, inputs, sems, stage, lefts, left_sems = rest[3 + count :]
    me = me_ref[0]
    width = near_w.shape[1]
    outgoing = []

    def emit(k, values):
        lanes = slice(k * width, (k + 1) * width)
        lefts[:, lanes] = values
        copy = pltpu.make_async_copy(lefts.at[:, lanes], left_out.at[:, lanes], left_sems.at[k])
        copy.start()
        outgoing.append(copy)

    copies = pull(summaries(groups, held, me) + [(inputs_far, inputs)], sems)
    for copy in copies[:count]:
        copy.wait()
    copies = copies[count:]
    half = htok.shape[3]

    def gathered(j, k):
        return held[j, k * seqs : (k + 1) * seqs]

    per_seg = htok.shape[1]
    total = seqs * tokens
    x0 = jnp.zeros((seqs, half), F32)
    x1 = jnp.zeros((seqs, half), F32)
    for j in range(count):
        x0 = jnp.where(j < me, gathered(j, 0) * x0 + gathered(j, 1), x0)
        i = count - 1 - j
        x1 = jnp.where(i > me, gathered(i, 4) * x1 + gathered(i, 5), x1)
    carry0 = pre[0, 0] * spread(x0, seqs) + pre[1, 0]
    carry1 = pre[0, 1] * spread(x1, seqs) + pre[1, 1]
    enter[0] = carry0
    enter[1] = carry1
    forward = htok[0] + ptok[0] * carry0[None]
    backward = htok[1] + ptok[1] * carry1[None]
    rows = seqs * SEGS
    last = per_seg - 1
    f_last = jnp.concatenate(
        [forward[last, s * SEGS + SEGS - 1 : s * SEGS + SEGS] for s in range(seqs)], axis=0
    )
    b_first = jnp.concatenate(
        [backward[0, s * SEGS : s * SEGS + 1] for s in range(seqs)], axis=0
    )
    left = jnp.maximum(me - 1, 0)
    right = jnp.minimum(me + 1, count - 1)
    left_b = gathered(left, 6) * b_first + gathered(left, 7)
    right_f = gathered(right, 2) * f_last + gathered(right, 3)
    left_row = jnp.where(me > 0, jnp.concatenate([x0, left_b], axis=1), 0.0)
    right_row = jnp.where(me < count - 1, jnp.concatenate([right_f, x1], axis=1), 0.0)
    rim = jnp.concatenate(
        [left_row, right_row, jnp.zeros((16 - 2 * seqs, 2 * half), F32)], axis=0
    ).astype(BF16)
    tokens_perm = jnp.concatenate(
        [forward.reshape(total, half), backward.reshape(total, half)], axis=1
    ).astype(BF16)
    source = jnp.concatenate([tokens_perm, rim], axis=0)
    token = lax.broadcasted_iota(jnp.int32, (total, total + 16), 0)
    place = lax.broadcasted_iota(jnp.int32, (total, total + 16), 1)
    joining = jnp.broadcast_to(join_b[...][None], (total, 2 * half))
    for k in range(3):
        moved = token + (k - 1)
        want = token_row(moved, tokens, per_seg, seqs)
        if k == 0:
            want = jnp.where(token % tokens == 0, total + token // tokens, want)
        if k == 2:
            want = jnp.where(token % tokens == tokens - 1, total + seqs + token // tokens, want)
        tap = dot((place == want).astype(BF16), source).astype(BF16)
        emit(1 + k, tap)
        joining = joining + dot(tap, near_w[k])
    copies[0].wait()
    resid = inputs[...].astype(F32) + joining
    resid_out[...] = resid
    low = resid.astype(BF16)
    emit(0, low)
    size = 2 * half // HEADS
    wide = pairs * size
    query = (dot(low, near_w[3]) + query_b[...][None]).astype(BF16)
    key = dot(low, near_w[4]).astype(BF16)
    value = (dot(low, near_w[5]) + value_b[...][None]).astype(BF16)
    send_pairs((query, key, value), stage, chunks, me, count, seqs, tokens, pairs, size, wide)
    for copy in outgoing:
        copy.wait()


def send_pairs(arrays, stage, chunks, me, count, seqs, tokens, pairs, size, wide):
    half = tokens // 2
    for d in range(count):
        for a, array in enumerate(arrays):
            first = d * pairs
            for part in range(2):
                lane = (part * len(arrays) + a) * wide
                if first >= seqs * HEADS:
                    stage[d, :, lane : lane + wide] = jnp.zeros((half, wide), BF16)
                    continue
                s, head = first // HEADS, first % HEADS
                row = s * tokens + part * half
                stage[d, :, lane : lane + wide] = array[row : row + half, head * size : head * size + wide]
    for k in range(count):
        chunks[k][...] = stage[lax.rem(me + k, count)]


def split_tokens(source, me, chunks, tokens):
    half, wide = tokens // 2, source.shape[1]
    for k, chunk in enumerate(chunks):
        start = lax.rem(me + k, len(chunks)) * tokens
        for part in range(2):
            at = pl.ds(pl.multiple_of(start + part * half, half), half)
            chunk[:, part * wide : (part + 1) * wide] = source[at, :]


def receive_pairs(stage, place, count, seqs, tokens, pairs, size, parts):
    wide = pairs * size
    for d in range(count):
        first = d * pairs
        if first >= seqs * HEADS:
            continue
        s, head = first // HEADS, first % HEADS
        for part in range(2):
            for a in range(parts):
                lane = (part * parts + a) * wide
                row = s * tokens + part * (tokens // 2)
                place(a, row, head * size, stage[d, :, lane : lane + wide])


def load_heads(chunks, me, count, tokens, pairs, size, parts, part, target, scale=None):
    wide, half = pairs * size, tokens // 2
    for k in range(count):
        start = lax.rem(me + count - k, count) * tokens
        for second in range(2):
            at = pl.ds(pl.multiple_of(start + second * half, half), half)
            for h in range(pairs):
                lane = (second * parts + part) * wide + h * size
                block = chunks[k][:, lane : lane + size]
                target[h, at, 0:size] = block if scale is None else block * scale


def pair_length(lengths, me, pairs, h, seqs):
    return lengths[jnp.minimum((me * pairs + h) // HEADS, seqs - 1)]


def transposed(values):
    return jnp.transpose(values.astype(F32))


def mask_lanes(q, k, full, valid, size):
    shape = (full, k.shape[2] - size)
    lane = lax.broadcasted_iota(jnp.int32, shape, 1)
    padded = lax.broadcasted_iota(jnp.int32, shape, 0) >= valid
    ones = jnp.where(lane < 3, 1.0, 0.0).astype(BF16)
    parts = jnp.where(lane == 0, MASKED[0], jnp.where(lane == 1, MASKED[1], MASKED[2]))
    mask = jnp.where((lane < 3) & padded, parts, 0.0).astype(BF16)
    keep = (lax.broadcasted_iota(jnp.int32, (full, size), 0) < valid).astype(F32).astype(BF16)
    for h in range(k.shape[0]):
        q[h, :, size:] = ones
        k[h, :, size:] = mask
        k[h, :, 0:size] = k[h, :, 0:size] * keep


def attend_body(count, seqs, tokens, pairs, size, block, begin, me_ref, lengths, *rest):
    chunks, rest = rest[:count], rest[count:]
    outs, lse, far = rest[:count], rest[count], rest[count + 1 : count + 4]
    q, k, v, vt, mixed_t, mixed, sems = rest[count + 4 :]
    me = me_ref[0]
    full = count * tokens
    begin()
    load_heads(chunks, me, count, tokens, pairs, size, 3, 0, q, jnp.asarray(0.125, BF16))
    load_heads(chunks, me, count, tokens, pairs, size, 3, 1, k)
    load_heads(chunks, me, count, tokens, pairs, size, 3, 2, v)
    lse[...] = jnp.zeros_like(lse)
    mask_lanes(q, k, full, pair_length(lengths, me, pairs, 0, seqs), size)
    copies = pull(list(zip((q, k, v), far)), sems)
    for h in range(pairs):
        vt[h, 0:size] = transposed(v[h, :, 0:size]).astype(BF16)
        row = lax.broadcasted_iota(jnp.int32, (vt.shape[1] - size, full), 0)
        vt[h, size:] = jnp.where(row == 0, 1.0, 0.0).astype(BF16)

        def rows(i, _, h=h):
            at = pl.ds(pl.multiple_of(i * block, block), block)
            scores = dot_nt(k[h], q[h, at, :])
            top = jnp.max(scores, axis=0, keepdims=True)
            sums = dot(vt[h], jnp.exp(scores - top).astype(BF16))
            total = sums[size : size + 1]
            lse[h : h + 1, at] = top + jnp.log(total)
            mixed_t[h * size : (h + 1) * size, at] = sums[0:size] / total
            return 0

        lax.fori_loop(0, full // block, rows, 0, unroll=2)
    mixed[...] = transposed(mixed_t[...]).astype(BF16)
    split_tokens(mixed, me, outs, tokens)
    for copy in copies:
        copy.wait()


def attend_back_body(count, seqs, tokens, pairs, size, block, me_ref, lse, *rest):
    far, d_chunks, rest = rest[:3], rest[3 : 3 + count], rest[3 + count :]
    outs = rest[:count]
    q, k, v, kt, d_o, dq_t, probs_all, d_scores_all, stage, sems = rest[count:]
    me = me_ref[0]
    full = count * tokens
    wide = pairs * size
    copies = pull(list(zip(far, (q, k, v))), sems)
    load_heads(d_chunks, me, count, tokens, pairs, size, 1, 0, d_o)
    for copy in copies:
        copy.wait()
    for h in range(pairs):
        kt[...] = transposed(k[h, :, 0:size]).astype(BF16)

        def rows(i, _, h=h):
            at = pl.ds(pl.multiple_of(i * block, block), block)
            probs = jnp.exp(dot_nt(k[h], q[h, at, :]) - lse[h : h + 1, at])
            d_probs = dot_nt(v[h, :, 0:size], d_o[h, at, :])
            probs_all[:, at] = probs.astype(BF16)
            row_dot = jnp.sum(probs * d_probs, axis=0, keepdims=True)
            d_scores_all[:, at] = (probs * (d_probs - row_dot)).astype(BF16)
            return 0

        lax.fori_loop(0, full // block, rows, 0, unroll=2)
        dq_t[h * size : (h + 1) * size, :] = dot(kt[...], d_scores_all[...]) * 0.125
        for part, grad in (
            (1, dot(d_scores_all[...], q[h])), (2, dot(probs_all[...], d_o[h])),
        ):
            lane = part * wide + h * size
            stage[:, lane : lane + size] = grad[:, 0:size].astype(BF16)
    stage[:, 0:wide] = transposed(dq_t[...]).astype(BF16)
    split_tokens(stage, me, outs, tokens)


def normed(values):
    center = values - jnp.mean(values, axis=-1, keepdims=True)
    scale = lax.rsqrt(jnp.mean(center * center, axis=-1, keepdims=True) + NORM_EPS)
    return center * scale, scale


def norm_back(cotangent, unit, scale, gain):
    d_unit = cotangent * gain
    mean = jnp.mean(d_unit, axis=-1, keepdims=True)
    lean = jnp.mean(d_unit * unit, axis=-1, keepdims=True)
    return scale * (d_unit - mean - unit * lean)


GELU_A = 0.7978845608028654
GELU_B = 0.044715


def feed_body(
    count, seqs, tokens, pairs, size, block,
    me_ref, out_b, gain1, shift1, up_b, down_b, gain2, shift2,
    resid, out_v, up_v, cotangent_far, down_far,
    *rest,
):
    chunks, rest = rest[:count], rest[count:]
    output_far, d_first_in_out, vec, up_vec, lefts, keep_out, send_out = rest[:7]
    outs = rest[7 : 7 + count]
    out_v, up_v = out_v.at[0], up_v.at[0]
    stage, slope, acc, cotangent, output, d_hidden_v, d_second_v, down_v, sems = rest[7 + count :]
    me, core = me_ref[0], me_ref[1]
    width = out_v.shape[0]
    ff = up_v.shape[1]
    parts = ff // block
    mixed = lefts.at[:, ff + width : ff + 2 * width]
    first_low_v = lefts.at[:, ff : ff + width]

    def emit_halves(source, lane, wide):
        for out, part in ((keep_out, core), (send_out, 1 - core)):
            at = pl.ds(pl.multiple_of(part * wide, LANES), wide)
            out[:, lane : lane + wide] = source[:, at]

    pieces = [slice(j * block, (j + 1) * block) for j in range(parts)]
    first_copies = pull(
        [(cotangent_far, cotangent)]
        + [(down_far.at[piece], down_v.at[piece]) for piece in pieces],
        sems,
    )
    collect(chunks, stage, me, count)

    def lanes(j):
        return pl.ds(pl.multiple_of(j * block, block), block)

    def place(part, row, lane, values):
        mixed[row : row + values.shape[0], lane : lane + values.shape[1]] = values

    receive_pairs(stage, place, count, seqs, tokens, pairs, size, 1)
    first_in = resid[...] + dot(mixed[...], out_v[...]) + out_b[...][None]
    unit1, scale1 = normed(first_in)
    first = unit1 * gain1[...][None] + shift1[...][None]
    first_low = first.astype(BF16)
    first_low_v[...] = first_low
    acc[...] = first + down_b[...][None]

    def ahead(j, _):
        hidden = dot(first_low_v[...], up_v[:, lanes(j)]) + up_b[lanes(j)][None]
        square = hidden * hidden
        bend = jnp.tanh(GELU_A * (hidden + GELU_B * (square * hidden)))
        act = (0.5 * hidden * (1.0 + bend)).astype(BF16)
        lefts[:, lanes(j)] = act
        slope[:, lanes(j)] = 0.5 * (1.0 + bend) + 0.5 * hidden * (1.0 - bend * bend) * (
            GELU_A * (1.0 + 3.0 * GELU_B * square)
        )
        first_copies[1 + j].wait()
        acc[...] += dot(act, down_v[lanes(j), :])

    for j in range(parts):
        ahead(j, 0)
    unit2, scale2 = normed(acc[...])
    first_copies[0].wait()
    output[...] = (unit2 * gain2[...][None] + shift2[...][None]).astype(BF16)
    done = pltpu.make_async_copy(output, output_far, sems.at[1 + parts])
    done.start()
    cot = cotangent[...].astype(F32)
    vec[0:1] = column_sum(cot * unit2)
    vec[1:2] = column_sum(cot)
    d_second_in = norm_back(cot, unit2, scale2, gain2[...][None])
    d_second = d_second_in.astype(BF16)
    d_second_v[...] = d_second
    emit_halves(d_second_v, ff // 2, width // 2)
    vec[2:3] = column_sum(d_second)
    acc[...] = d_second_in

    def astern(j, _):
        d_act = dot_nt(d_second_v[...], down_v[lanes(j), :])
        d_hidden = (d_act * slope[:, lanes(j)]).astype(BF16)
        d_hidden_v[:, lanes(j)] = d_hidden
        up_vec[:, lanes(j)] = column_sum(d_hidden)
        acc[...] += dot_nt(d_hidden, up_v[:, lanes(j)])
        return 0

    lax.fori_loop(0, parts, astern, 0, unroll=True)
    emit_halves(d_hidden_v, 0, ff // 2)
    d_first = acc[...]
    vec[3:4] = column_sum(d_first * unit1)
    vec[4:5] = column_sum(d_first)
    d_first_in = norm_back(d_first, unit1, scale1, gain1[...][None])
    d_first_in_out[...] = d_first_in
    d_attn = d_first_in.astype(BF16)
    d_second_v[...] = d_attn
    emit_halves(d_second_v, ff // 2 + width // 2, width // 2)
    vec[5:6] = column_sum(d_attn)
    vec[6:8] = jnp.zeros((2, vec.shape[1]), F32)
    d_mixed = dot_nt(d_attn, out_v[...]).astype(BF16)
    send_pairs((d_mixed,), stage, outs, me, count, seqs, tokens, pairs, size, pairs * size)
    done.wait()


def fetch_columns(arrays, lanes, sems, at):
    copies = []
    for far, near in arrays:
        copy = pltpu.make_async_copy(far.at[:, lanes], near.at[:, lanes], sems.at[at + len(copies)])
        copy.start()
        copies.append(copy)
    return copies


def feed_grads_body(ff, lefts, lefts_got, rights, rights_got, out, res, sems):
    half = out.shape[-1]
    width = 2 * half
    blocks = out.shape[0]
    step = ff // blocks
    first = ff // 2
    outgoing = []

    def emit(place):
        at = sems.at[len(outgoing)]
        copy = pltpu.make_async_copy(res.at[place], out.at[place], at)
        copy.start()
        outgoing.append(copy)

    def grad(at, size, begin):
        rows, lanes = slice(at, at + size), slice(begin, begin + half)
        return dot_tn(lefts[:, rows], rights[:, lanes]) + dot_tn(lefts_got[:, rows], rights_got[:, lanes])

    whole = slice(None)
    owners = 1
    for size in out.shape[:-2]:
        owners *= size
    pieces = (ff + width) // width
    up_rows = width // owners
    down_rows = ff // owners
    start = pieces * up_rows
    mids = (whole,) * (len(out.shape) - 3)
    by_piece = up_rows % 16 == 0 and down_rows % 16 == 0
    for j in range(blocks):
        part = grad(j * step, step, first)
        spread_rows(res, (j,), slice(start, start + down_rows), part)
        if by_piece:
            emit((j,) + mids + (slice(start, start + down_rows), whole))
    for k in range(pieces):
        if k == pieces - 1:
            part = grad(ff + width, width, first + half)
        else:
            part = grad(ff, width, k * half)
        rows = slice(k * up_rows, (k + 1) * up_rows)
        spread_rows(res, (), rows, part)
        if by_piece:
            emit((whole,) + mids + (rows, whole))
    if not by_piece:
        emit((whole,) * len(out.shape))
    for copy in outgoing:
        copy.wait()


def spread_rows(res, head, rows, grad):
    size = rows.stop - rows.start
    wide = res.shape[len(head) : -2]
    if size % 16 == 0:
        at = head + (slice(None),) * len(wide) + (rows, slice(None))
        res[at] = grad.astype(BF16).reshape(wide + (size, grad.shape[1]))
        return
    places = [()]
    for count in wide:
        places = [place + (k,) for place in places for k in range(count)]
    for k, place in enumerate(places):
        res[head + place + (rows, slice(None))] = grad[k * size : (k + 1) * size].astype(BF16)


def feed_grads(left, left_got, right, right_got, ff, width):
    count, groups = lax.axis_size("seq"), lax.axis_size("dp")
    places = bits_of(count)[1:]
    owners = count * groups // 2
    rows = (ff + width) // width * (width // owners) + ff // owners
    shape = (groups,) + (2,) * len(places) + (rows, width // 2)
    (out,) = call(
        functools.partial(feed_grads_body, ff),
        [PIN] * 4,
        [(shape, BF16, HBM)],
        [
            pltpu.VMEM(shape, BF16),
            pltpu.SemaphoreType.DMA((groups + (ff + width) // width,)),
        ],
        name="grad_feed",
    )(left, left_got, right, right_got)
    return out


def store_rows(res, lanes, grad):
    rows = res.shape[-2]
    if rows % 16 == 0:
        res[..., lanes] = grad.astype(BF16).reshape(res.shape[:-1] + (grad.shape[1],))
        return
    places = [()]
    for wide in res.shape[:-2]:
        places = [place + (k,) for place in places for k in range(wide)]
    for k, place in enumerate(places):
        res[place + (slice(None), lanes)] = grad[k * rows : (k + 1) * rows].astype(BF16)


def outer_body(plan, cut, bits_ref, left, left_got, rights, rights_got, *rest):
    low_send, low_keep, high_send, high_keep = rest[:4]
    lefts, lefts_got, res, sems = rest[4:]
    height = lefts.shape[1] // len({lane for lane, _, _ in plan})
    waits = []
    for number, (lane, first, wide) in enumerate(plan):
        copies = []
        for far, near, at, size, seen in (
            (left, lefts, lane, height, [other[0] for other in plan[:number]]),
            (left_got, lefts_got, lane, height, [other[0] for other in plan[:number]]),
        ):
            if at not in seen:
                lanes = slice(at, at + size)
                sem = sems.at[sum(map(len, waits)) + len(copies)]
                copies.append(pltpu.make_async_copy(far.at[:, lanes], near.at[:, lanes], sem))
        waits.append(copies)
        for copy in copies:
            copy.start()
    used = sum(map(len, waits))
    low, high = bits_ref[0], bits_ref[1]
    outgoing = []
    whole = slice(None)
    mids = len(res.shape) - 4

    def emit(low_half):
        if low_half:
            place = lambda which: (whole,) * (1 + mids) + (which, whole, slice(0, cut))
            pairs = ((low_send, 1 - low), (low_keep, low))
        else:
            place = lambda which: (whole, which) + (whole,) * (1 + mids) + (slice(cut, res.shape[-1]),)
            pairs = ((high_send, 1 - high), (high_keep, high))
        for out, which in pairs:
            copy = pltpu.make_async_copy(res.at[place(which)], out, sems.at[used + len(outgoing)])
            copy.start()
            outgoing.append(copy)

    lane_at = 0
    for number, (lane, first, wide) in enumerate(plan):
        for copy in waits[number]:
            copy.wait()
        for k in range(0, wide, 512):
            size = min(512, wide - k)
            lanes = slice(first + k, first + k + size)
            grad = dot_tn(lefts[:, lane : lane + height], rights[:, lanes])
            grad = grad + dot_tn(lefts_got[:, lane : lane + height], rights_got[:, lanes])
            lanes = slice(lane_at + k, lane_at + k + size)
            store_rows(res, lanes, grad)
            if lane_at + k + size == cut:
                emit(True)
        lane_at += wide
    emit(False)
    for copy in outgoing:
        copy.wait()


def outer_grads(arrays, plan, cut, height, name):
    count, groups = lax.axis_size("seq"), lax.axis_size("dp")
    places = bits_of(count)[1:]
    rows = 2 * height // (count * groups)
    tokens = arrays[0].shape[0]
    wide = sum(piece[2] for piece in plan)
    lefts = len({piece[0] for piece in plan})
    shape = (groups,) + (2,) * len(places) + (rows,)
    less = (groups,) + (2,) * (len(places) - 1) + (rows,)
    seq = lax.axis_index("seq")
    bits = jnp.stack([(seq // places[0]) % 2, (seq // places[-1]) % 2]).astype(jnp.int32)
    return call(
        functools.partial(outer_body, plan, cut),
        [SMEM, HBM, HBM, PIN, PIN],
        [(less + (cut,), BF16, HBM)] * 2 + [(less + (wide - cut,), BF16, HBM)] * 2,
        [
            pltpu.VMEM((tokens, lefts * height), BF16),
            pltpu.VMEM((tokens, lefts * height), BF16),
            pltpu.VMEM(shape + (wide,), BF16),
            pltpu.SemaphoreType.DMA((4 * len(plan) + 4,)),
        ],
        name=name,
    )(bits, *arrays)


def project_back_body(
    count, seqs, tokens, pairs, size, per_seg,
    me_ref, pre, d_first_in, ptok, near_w,
    *rest,
):
    chunks, rest = rest[:count], rest[count:]
    grad_out, d_perm, payload, vec, keep_out, send_out = rest[:6]
    stage, rights = rest[6:]
    me, core = me_ref[0], me_ref[1]
    width = near_w.shape[1]

    def emit_halves(part):
        wide = width // 2
        for out, which in ((keep_out, core), (send_out, 1 - core)):
            at = pl.ds(pl.multiple_of(part * width + which * wide, LANES), wide)
            out[:, part * wide : (part + 1) * wide] = rights[:, at]

    collect(chunks, stage, me, count)
    targets = [rights.at[:, k * width : (k + 1) * width] for k in range(4)]

    def place(part, row, lane, values):
        at = part * width + lane
        rights[row : row + values.shape[0], at : at + values.shape[1]] = values

    receive_pairs(stage, place, count, seqs, tokens, pairs, size, 3)
    for part in range(3):
        emit_halves(part)
    d_resid = d_first_in[...]
    for k in range(3):
        d_resid = d_resid + dot_nt(targets[k][...], near_w[3 + k])
    grad = d_resid.astype(BF16)
    grad_out[...] = grad
    targets[3][...] = grad
    emit_halves(3)
    vec[0:1] = column_sum(targets[0][...])
    vec[1:2] = column_sum(targets[2][...])
    vec[2:3] = column_sum(grad)
    vec[3:8] = jnp.zeros((5, vec.shape[1]), F32)
    total = seqs * tokens
    half = vec.shape[1] // 2
    row = lax.broadcasted_iota(jnp.int32, (total + 16, total), 0)
    place_at = lax.broadcasted_iota(jnp.int32, (total + 16, total), 1)
    rows = seqs * SEGS
    step, rest_row = row // rows, row % rows
    seq = rest_row // SEGS
    tok = (rest_row % SEGS) * per_seg + step
    extra = row - total
    seq = jnp.where(extra >= 0, extra % seqs, seq)
    tok = jnp.where(extra >= 0, jnp.where(extra < seqs, -1, tokens), tok)
    known = extra < 2 * seqs
    d_char = jnp.zeros((total + 16, 2 * half), F32)
    for k in range(3):
        moved = tok + 1 - k
        pick = (place_at == seq * tokens + moved) & (moved >= 0) & (moved < tokens) & known
        shifted = dot(pick.astype(BF16), grad).astype(BF16)
        d_char = d_char + dot_nt(shifted, near_w[k])
    payload[6 * seqs :] = jnp.zeros((payload.shape[0] - 6 * seqs, half), F32)
    for r in range(2):
        grads = d_char[0:total, r * half : (r + 1) * half].reshape(per_seg, rows, half)
        d_perm[r] = grads
        weighted = jnp.sum(grads * ptok[r], axis=0) * pre[0, r]
        for s in range(seqs):
            row = r * seqs + s
            payload[row : row + 1] = column_sum(weighted[s * SEGS : (s + 1) * SEGS])
        edges = d_char[total : total + 2 * seqs, r * half : (r + 1) * half]
        payload[(2 + r) * seqs : (3 + r) * seqs] = edges[0:seqs]
        payload[(4 + r) * seqs : (5 + r) * seqs] = edges[seqs : 2 * seqs]


def chars_back_body(
    count, seqs, steps, per,
    lang, me_ref, ids, gate_b, enter, pseg, vec1, up_vec, vec2, embedded, ptok, d_perm, gate_w_far, cand_w_far,
    *rest,
):
    groups, back_groups, rest = rest[: count // 2], rest[count // 2 : count], rest[count:]
    (
        keep_out, send_out,
        upd, work, d_all, d_tok, gseg, gin, gate_w, cand_w, held, back, sems, vector, owned,
    ) = rest
    me = me_ref[0]
    wanted = [(gate_w_far, gate_w), (cand_w_far, cand_w)]
    wanted += summaries(groups, held, me) + summaries(back_groups, back, me)
    copies = pull(wanted, sems)
    for copy in copies[:2]:
        copy.wait()

    def gathered(j, k):
        return held[j, k * seqs : (k + 1) * seqs]

    def gathered_back(j, k):
        return back[j, k * seqs : (k + 1) * seqs]

    rows = seqs * SEGS
    half = upd.shape[2]
    gates(embedded[...], gate_w, gate_b[...], cand_w, upd, work)

    def ahead(q, carry):
        h0, h1 = carry
        for j in range(per):
            at = pl.ds(pl.multiple_of((q * per + j) * rows, rows), rows)
            u = upd[0, at, :]
            gap = work[0, at, :] - h0
            work[0, at, :] = gap * (u * (1.0 - u))
            h0 = h0 + u * gap
            at = pl.ds(pl.multiple_of((steps - 1 - q * per - j) * rows, rows), rows)
            u = upd[1, at, :]
            gap = work[1, at, :] - h1
            work[1, at, :] = gap * (u * (1.0 - u))
            h1 = h1 + u * gap
        return h0, h1

    lax.fori_loop(0, steps // per, ahead, (enter[0], enter[1]))

    left = jnp.maximum(me - 1, 0)
    right = jnp.minimum(me + 1, count - 1)
    last = steps // per - 1
    for copy in copies[2:]:
        copy.wait()
    d_tok[...] = d_perm[...]
    for r in range(2):
        from_left = jnp.where(me > 0, gathered_back(left, 4 + r), 0.0)
        from_right = jnp.where(me < count - 1, gathered_back(right, 2 + r), 0.0)
        for s in range(seqs):
            low, high = s * SEGS, s * SEGS + SEGS - 1
            d_tok[r, 0, low : low + 1] += from_left[s : s + 1]
            d_tok[r, last, high : high + 1] += from_right[s : s + 1]
        gseg[r] = jnp.sum(d_tok[r] * ptok[r], axis=0)

    def block_sum(j, r):
        total = gathered_back(j, r)
        near, far = gathered(j, 4 * r + 2), gathered(j, 4 * r)
        if r == 1:
            near, far = far, near
        if j > 0:
            total = total + near * gathered_back(j - 1, 4 + r)
        if j < count - 1:
            total = total + far * gathered_back(j + 1, 2 + r)
        return total

    g0 = jnp.zeros((seqs, half), F32)
    g1 = jnp.zeros((seqs, half), F32)
    for j in range(count):
        i = count - 1 - j
        g0 = jnp.where(i > me, gathered(i, 0) * g0 + block_sum(i, 0), g0)
        g1 = jnp.where(j < me, gathered(j, 4) * g1 + block_sum(j, 1), g1)
    for s in range(seqs):
        flow = g0[s : s + 1]
        for g in range(SEGS - 1, -1, -1):
            row = s * SEGS + g
            gin[0, row : row + 1] = flow
            flow = pseg[0, row : row + 1] * flow + gseg[0, row : row + 1]
        flow = g1[s : s + 1]
        for g in range(SEGS):
            row = s * SEGS + g
            gin[1, row : row + 1] = flow
            flow = pseg[1, row : row + 1] * flow + gseg[1, row : row + 1]

    def astern(q, carry):
        flow0, flow1 = carry
        for j in range(per):
            at = pl.ds(pl.multiple_of((steps - 1 - q * per - j) * rows, rows), rows)
            if j == 0:
                flow0 = flow0 + d_tok[0, steps // per - 1 - q]
            u = upd[0, at, :]
            d_all[at, 0:half] = (flow0 * work[0, at, :]).astype(BF16)
            d_cand = flow0 * u
            d_all[at, half : 2 * half] = d_cand.astype(BF16)
            flow0 = flow0 - d_cand
            at = pl.ds(pl.multiple_of((q * per + j) * rows, rows), rows)
            if j == 0:
                flow1 = flow1 + d_tok[1, q]
            u = upd[1, at, :]
            d_all[at, 2 * half : 3 * half] = (flow1 * work[1, at, :]).astype(BF16)
            d_cand = flow1 * u
            d_all[at, 3 * half : 4 * half] = d_cand.astype(BF16)
            flow1 = flow1 - d_cand
        return flow0, flow1

    lax.fori_loop(0, steps // per, astern, (gin[0], gin[1]))
    grad_w = dot_tn(embedded[...], d_all[...])
    place_owned(owned, grad_w)
    d_emb = jnp.zeros(embedded.shape, F32)
    gate_sums = []
    for r in range(2):
        gate_sums.append(column_sum(d_all[:, 2 * r * half : (2 * r + 1) * half]))
        d_emb = d_emb + dot_nt(d_all[:, 2 * r * half : (2 * r + 1) * half], gate_w[r])
        d_emb = d_emb + dot_nt(d_all[:, (2 * r + 1) * half : (2 * r + 2) * half], cand_w[r])
    partial = dot_tn(one_hot_rows(ids, seqs, steps), d_emb.astype(BF16))
    local = lax.broadcasted_iota(jnp.int32, partial.shape, 0)
    for s in range(seqs):
        tag = lang[s].astype(F32)
        partial = jnp.where(local == s * LANES + LANES - 1, tag, partial)
    core = me_ref[1]
    wide = partial.shape[1] // 2
    low, high = partial[:, :wide].astype(BF16), partial[:, wide:].astype(BF16)
    rows = partial.shape[0]
    keep_out[0:rows] = jnp.where(core == 0, low, high)
    send_out[0:rows] = jnp.where(core == 0, high, low)
    sums = [vec1[k : k + 1] for k in range(6)] + [up_vec[...]]
    sums += [vec2[k : k + 1] for k in range(3)] + gate_sums
    vector[...] = jnp.zeros_like(vector)
    at = 0
    for values in sums:
        for k in range(values.shape[1] // LANES):
            vector[at : at + 1] = values[:, k * LANES : (k + 1) * LANES]
            at += 1
    send_out[rows : rows + vector.shape[0]] = vector[...].astype(BF16)
    keep_out[rows:] = owned[core].astype(BF16)
    send_out[rows + vector.shape[0] :] = owned[1 - core].astype(BF16)


def place_owned(owned, grad):
    count, groups = lax.axis_size("seq"), lax.axis_size("dp")
    rows = grad.shape[0] // (count * groups)
    tiles = grad.shape[1] // LANES
    bits = count.bit_length() - 1
    for d in range(groups):
        for s in range(count):
            mirrored = 0
            for b in range(1, bits):
                mirrored = mirrored * 2 + (s >> b) % 2
            at = (mirrored * groups + d) * rows * tiles
            first = (d * count + s) * rows
            for t in range(tiles):
                value = grad[first : first + rows, t * LANES : (t + 1) * LANES]
                owned[s % 2, at + t * rows : at + (t + 1) * rows] = value


def mix_body(rows, vector_rows, first, last, bits_ref, keep, sent, got, *outs):
    fixed = rows + vector_rows
    table = (keep if first else sent)[0:rows].astype(F32) + got[0:rows].astype(F32)
    vector = sent[rows:fixed].astype(F32) + got[rows:fixed].astype(F32)
    start = rows if first else 0
    size = keep.shape[0] - start
    if last:
        piece = size // len(outs)
        for k, out in enumerate(outs):
            which = jnp.bitwise_xor(bits_ref[0], k) * piece
            at = pl.ds(pl.multiple_of(start + which, 8), piece)
            from_got = pl.ds(pl.multiple_of(fixed + which, 8), piece)
            out[fixed:] = (keep[at].astype(F32) + got[from_got].astype(F32)).astype(BF16)
    else:
        piece = size // 2
        for out, bit in ((outs[0], 1 - bits_ref[0]), (outs[1], bits_ref[0])):
            at = pl.ds(pl.multiple_of(start + bit * piece, 16), piece)
            from_got = pl.ds(pl.multiple_of(fixed + bit * piece, 16), piece)
            total = (keep[at].astype(F32) + got[from_got].astype(F32)).astype(BF16)
            if out is outs[0]:
                out[fixed:] = total
            else:
                out[...] = total
    for out in outs if last else outs[:1]:
        out[0:rows] = table.astype(BF16)
        out[rows:fixed] = vector.astype(BF16)


def table_body(groups, seqs, sub, count, place_ref, *refs):
    own, other, rest = refs[:groups], refs[groups : 2 * groups], refs[2 * groups :]
    table, gate_out, cand_out, *vectors, vector, low, high, vec, held = rest
    dp, core = place_ref[0], place_ref[1]
    vocab, width = table.shape
    half = width // 2
    rows = low.shape[1]
    for k in range(groups):
        at = jnp.bitwise_xor(dp, k)
        mine, their = own[k][0:rows], other[k][0:rows]
        low[at] = jnp.where(core == 0, mine, their)
        high[at] = jnp.where(core == 0, their, mine)
        vec[at] = own[k][rows : rows + vector.shape[0]].astype(F32)
    fixed = rows + vector.shape[0]
    mine = own[0][fixed:].astype(F32)
    for part in own[1:]:
        mine = mine + part[fixed:].astype(F32)
    held[...] = mine
    owned = gate_out.shape[1]
    tiles = held.shape[0] // owned // 4
    for k in range(4):
        home = (gate_out, cand_out)[k % 2]
        for t in range(tiles):
            at = (k * tiles + t) * owned
            home[k // 2, :, t * LANES : (t + 1) * LANES] = held[at : at + owned]
    wide = -(-vocab // 16) * 16
    row = lax.broadcasted_iota(jnp.int32, (wide, LANES), 0)
    local = lax.broadcasted_iota(jnp.int32, (wide, LANES), 1)
    sums = jnp.zeros((wide, width), F32)
    total = jnp.zeros(vector.shape, F32)
    for g in range(groups):
        picks = []
        for s in range(seqs):
            tag = low[g, (s + 1) * LANES - 16 : (s + 1) * LANES, 0:1].astype(F32)[15:16]
            lang = (tag * (1.0 / count) + 0.5).astype(jnp.int32)
            picks.append(jnp.where((row - lang * sub == local) & (local < sub), 1.0, 0.0).astype(BF16))
        both = jnp.concatenate([low[g], high[g]], axis=1)
        sums = sums + dot(jnp.concatenate(picks, axis=1), both)
        total = total + vec[g]
    table[...] = sums[0:vocab]
    vector[...] = total
    at = 0
    for out in vectors:
        for k in range(out.shape[-1] // LANES * (out.shape[0] if len(out.shape) > 1 else 1)):
            if len(out.shape) > 1:
                per_row = out.shape[1] // LANES
                lanes = slice(k % per_row * LANES, (k % per_row + 1) * LANES)
                out[k // per_row : k // per_row + 1, lanes] = vector[at : at + 1]
            else:
                out[k * LANES : (k + 1) * LANES] = vector[at]
            at += 1


def fold_body(bits_ref, *refs):
    ins, outs = refs[:4], refs[4:]
    for k in range(2):
        keep, got, bit = ins[2 * k], ins[2 * k + 1], bits_ref[k]
        for out, which in ((outs[2 * k], 1 - bit), (outs[2 * k + 1], bit)):
            out[...] = (keep[:, which].astype(F32) + got[:, which].astype(F32)).astype(BF16)


def halve_body(sizes, alone, bits_ref, *refs):
    ins, outs = refs[:-4], refs[-4:]
    owners = ins[0].shape[0]
    at = 0
    for k, size in enumerate(sizes):
        rows = slice(at, at + size) if alone else slice(0, size)
        parts = ins if alone else ins[2 * k : 2 * k + 2]
        for out, which in ((outs[2 * k], 1 - bits_ref[k]), (outs[2 * k + 1], bits_ref[k])):
            for i in range(owners // 2):
                place = which * (owners // 2) + i if k == 0 else 2 * i + which
                total = parts[0][place, rows].astype(F32)
                for part in parts[1:]:
                    total = total + part[place, rows].astype(F32)
                out[i] = total.astype(BF16)
        at += size if alone else 0


def part_rows_body(sizes, core_ref, kept, got, kept_on, got_on, send, keep):
    core = core_ref[0]
    total = jnp.concatenate(
        [a[...].astype(F32) + b[...].astype(F32) for a, b in ((kept, got), (kept_on, got_on))], axis=0
    )
    at = 0
    for size in sizes:
        first, second = total[2 * at : 2 * at + size], total[2 * at + size : 2 * at + 2 * size]
        send[at : at + size] = jnp.where(core == 0, second, first)
        keep[at : at + size] = jnp.where(core == 0, first, second)
        at += size


def beside_body(pieces, core_ref, keep, got, up, out, down):
    core = core_ref[0]
    wide = keep.shape[1]
    rows = up.shape[0]
    low = jnp.where(core == 0, keep[...], got[...])
    high = jnp.where(core == 0, got[...], keep[...])
    for k in range(pieces + 1):
        home, lane = (up, k * wide) if k < pieces else (out, 0)
        gap = up.shape[1] // 2 if k < pieces else wide
        home[:, lane : lane + wide] = low[k * rows : (k + 1) * rows]
        home[:, lane + gap : lane + gap + wide] = high[k * rows : (k + 1) * rows]
    down[:, 0:wide] = low[(pieces + 1) * rows :]
    down[:, wide : 2 * wide] = high[(pieces + 1) * rows :]


def part_cores_body(core_ref, low_keep, low_got, high_keep, high_got, send, keep):
    core = core_ref[0]
    rows = keep.shape[1]
    lane = 0
    for mine, got in ((low_keep, low_got), (high_keep, high_got)):
        wide = mine.shape[2]
        total = mine[...].astype(F32) + got[...].astype(F32)
        first, second = total[:, 0:rows], total[:, rows : 2 * rows]
        send[:, :, lane : lane + wide] = jnp.where(core == 0, second, first).astype(BF16)
        keep[:, :, lane : lane + wide] = jnp.where(core == 0, first, second).astype(BF16)
        lane += wide


def both_body(widths, core_ref, keep, got, out):
    core = core_ref[0]
    lane = 0
    for wide in widths:
        a, b = keep[:, :, lane : lane + wide], got[:, :, lane : lane + wide]
        out[:, :, 2 * lane : 2 * lane + wide] = jnp.where(core == 0, a, b)
        out[:, :, 2 * lane + wide : 2 * lane + 2 * wide] = jnp.where(core == 0, b, a)
        lane += wide


def total_body(widths, both, *outs):
    outs = list(outs[:-1]) + [outs[-1].at[k] for k in range(outs[-1].shape[0])]
    lane = 0
    for out, wide in zip(outs, widths):
        out[...] = both[:, lane : lane + 2 * wide].astype(F32)
        lane += 2 * wide


def shift(array, by):
    count = lax.axis_size("seq")
    return lax.ppermute(array, "seq", [(i, (i + by) % count) for i in range(count)])


def swap(array, axis, bit):
    return lax.ppermute(array, axis, [(i, i ^ bit) for i in range(lax.axis_size(axis))])


def exchange(chunks):
    return [chunks[0]] + [shift(chunk, k) for k, chunk in enumerate(chunks) if k > 0]


def bits_of(count):
    return [1 << b for b in range(count.bit_length() - 1)]


def tie(arrays, *after):
    held = lax.optimization_barrier((tuple(arrays), after))
    return list(held[0])


def gather_summaries(rows):
    pair = jnp.stack([rows, swap(rows, "seq", 1)])
    return [pair] + [swap(pair, "seq", 2 * j) for j in range(1, lax.axis_size("seq") // 2)]


class Columns:
    def __init__(self, sends_and_keeps, widths):
        self.places = bits_of(lax.axis_size("seq"))[1:]
        self.seq = lax.axis_index("seq")
        self.widths = widths
        self.done = 0
        low_send, low_keep, high_send, high_keep = sends_and_keeps
        self.sends, self.keeps = (low_send, high_send), (low_keep, high_keep)
        self.hold_swap()

    def hold_swap(self):
        bits = self.places[self.done], self.places[-1 - self.done]
        self.gots = tuple(swap(send, "seq", bit) for send, bit in zip(self.sends, bits))
        self.done += 1

    def fold(self, *after):
        keeps, gots = self.keeps, self.gots
        if after:
            keeps = tie(keeps, *after)
        bits = self.places[self.done], self.places[-1 - self.done]
        chosen = jnp.stack([(self.seq // bit) % 2 for bit in bits]).astype(jnp.int32)
        flat, shapes = [], []
        for k, (keep, got) in enumerate(zip(keeps, gots)):
            dims = keep.shape
            if k == 0:
                flat += [x.reshape((-1, 2) + dims[-2:]) for x in (keep, got)]
                shapes.append(dims[:-3] + dims[-2:])
            else:
                flat += [x.reshape(dims[:2] + (-1, dims[-1])) for x in (keep, got)]
                shapes.append(dims[:1] + dims[2:])
        outs = []
        for k in range(2):
            dims = flat[2 * k].shape
            outs += [((dims[0],) + dims[2:], BF16)] * 2
        got = call(fold_body, [SMEM] + [VMEM] * 4, outs, limit=24, name="fold")(chosen, *flat)
        self.sends = (got[0].reshape(shapes[0]), got[2].reshape(shapes[1]))
        self.keeps = (got[1].reshape(shapes[0]), got[3].reshape(shapes[1]))
        self.hold_swap()

    def part_cores(self, *after):
        while self.done < len(self.places):
            self.fold()
        keeps = self.keeps
        if after:
            keeps = tie(keeps, *after)
        groups, rows, _ = keeps[0].shape
        wide = sum(self.widths)
        core = (self.seq % 2).astype(jnp.int32).reshape(1)
        self.send, self.keep = call(
            part_cores_body,
            [SMEM] + [VMEM] * 4,
            [((groups, rows // 2, wide), BF16)] * 2,
            limit=24,
            name="part_cores",
        )(core, keeps[0], self.gots[0], keeps[1], self.gots[1])
        self.got = swap(self.send, "seq", 1)

    def scatter_groups(self, *after):
        groups, rows, wide = self.keep.shape
        (keep,) = tie([self.keep], *after)
        core = (self.seq % 2).astype(jnp.int32).reshape(1)
        (self.both,) = call(
            functools.partial(both_body, self.widths),
            [SMEM] + [VMEM] * 2,
            [((groups, rows, 2 * wide), BF16)],
            limit=24,
            name="both_cores",
        )(core, keep, self.got)
        both = self.both.reshape(groups * rows, 2 * wide)
        self.own = lax.psum_scatter(both, "dp", scatter_dimension=0, tiled=True)

    def finish(self, last):
        return call(
            functools.partial(total_body, self.widths),
            [VMEM],
            [((self.own.shape[0], 2 * wide), F32) for wide in self.widths[:-last]]
            + [((last, self.own.shape[0], 2 * self.widths[-1]), F32)],
            limit=24,
            name="total",
        )(self.own)


class FeedRows:
    def __init__(self, grad, first):
        self.places = bits_of(lax.axis_size("seq"))[1:]
        self.seq = lax.axis_index("seq")
        self.first = first
        flat = grad.reshape(-1, grad.shape[-1])
        got = lax.psum_scatter(flat, "dp", scatter_dimension=0, tiled=True)
        self.parts = [got.reshape(grad.shape[1:])]
        self.done = 0

    def step(self, *after):
        parts = self.parts
        if after:
            parts = tie(parts, *after)
        bits = self.places[-1 - self.done], self.places[self.done]
        chosen = jnp.stack([(self.seq // bit) % 2 for bit in bits]).astype(jnp.int32)
        if self.done == 0:
            rows, wide = parts[0].shape[-2:]
            sizes = (self.first, rows - self.first)
            ins = [parts[0].reshape((-1, rows, wide))]
        else:
            wide = parts[0].shape[-1]
            sizes = (self.first, parts[2].shape[-2])
            ins = parts
        owners = 2 ** (len(self.places) - self.done - 1)
        outs = [((owners, size, wide), BF16) for size in sizes for _ in range(2)]
        got = call(
            functools.partial(halve_body, sizes, len(ins) == 1),
            [SMEM] + [VMEM] * len(ins),
            outs,
            limit=24,
            name="halve",
        )(chosen, *ins)
        self.sends = (got[0], got[2])
        gots = [swap(send, "seq", bit) for send, bit in zip(self.sends, bits)]
        self.parts = [got[1], gots[0], got[3], gots[1]]
        self.done += 1

    def finish(self, ff, width, *after):
        while self.done < len(self.places):
            self.step()
        parts = tie([part[0] for part in self.parts], *after)
        rows, wide = sum(part.shape[0] for part in parts[::2]), parts[0].shape[1]
        core = (self.seq % 2).astype(jnp.int32).reshape(1)
        pieces = (ff + width) // width
        owned = width // (lax.axis_size("seq") * lax.axis_size("dp"))
        send, keep = call(
            functools.partial(part_rows_body, (owned,) * pieces + (rows // 2 - pieces * owned,)),
            [SMEM] + [VMEM] * 4,
            [((rows // 2, wide), F32)] * 2,
            limit=24,
            name="part_rows",
        )(core, *parts)
        got = swap(send, "seq", 1)
        return call(
            functools.partial(beside_body, pieces - 1),
            [SMEM] + [VMEM] * 2,
            [((owned, ff), F32), ((owned, width), F32), ((rows // 2 - pieces * owned, width), F32)],
            limit=24,
            name="beside",
        )(core, keep, got)


class CharsSums:
    def __init__(self, keep, send, rows, vector_rows):
        self.keep, self.send, self.rows, self.vector_rows = keep, send, rows, vector_rows
        self.seq = lax.axis_index("seq")
        self.bits = bits_of(lax.axis_size("seq"))
        self.first = True

    def step(self, *after):
        bit = self.bits.pop(0)
        groups = lax.axis_size("dp")
        send, keep = self.send, self.keep
        got = swap(send, "seq", bit)
        if after:
            (keep,) = tie([keep], *after)
        last = not self.bits
        start = self.rows if self.first else 0
        size = keep.shape[0] - start
        fixed = self.rows + self.vector_rows
        if last:
            which = lax.axis_index("dp")
            outs = [((fixed + size // groups, LANES), BF16)] * groups
        else:
            which = (self.seq // self.bits[0]) % 2
            outs = [((fixed + size // 2, LANES), BF16), ((size // 2, LANES), BF16)]
        outs = call(
            functools.partial(mix_body, self.rows, self.vector_rows, self.first, last),
            [SMEM] + [VMEM] * 3,
            outs,
            limit=12,
            name="mix",
        )(which.astype(jnp.int32).reshape(1), keep, send, got)
        self.first = False
        if last:
            self.own, self.sends = outs[0], outs[1:]
        else:
            self.send, self.keep = outs

    def across(self, *after):
        self.sends = tie(self.sends, *after)
        self.own = [self.own] + [swap(part, "dp", k + 1) for k, part in enumerate(self.sends)]

    def finish(self, seqs, vocab, sub, gate_shape, sizes, *after):
        own = self.own
        other = tie([swap(part, "seq", 1) for part in own], *after)
        groups = len(own)
        rows, vector_rows = self.rows, self.vector_rows
        place = jnp.stack([lax.axis_index("dp"), self.seq % 2]).astype(jnp.int32)
        return call(
            functools.partial(table_body, groups, seqs, sub, lax.axis_size("seq")),
            [SMEM] + [VMEM] * (2 * groups),
            [((vocab, 2 * LANES), F32)] + [(gate_shape, F32)] * 2 + [(size, F32) for size in sizes],
            [
                pltpu.VMEM((vector_rows, LANES), F32),
                pltpu.VMEM((groups, rows, LANES), BF16),
                pltpu.VMEM((groups, rows, LANES), BF16),
                pltpu.VMEM((groups, vector_rows, LANES), F32),
                pltpu.VMEM((own[0].shape[0] - rows - vector_rows, LANES), F32),
            ],
            limit=24,
            name="table_rows",
        )(place, *own, *other)


def shards(
    inputs, char_ids, lang_ids, lengths, char_table, gate_weight, gate_bias, cand_weight,
    join_weight, join_bias, query_weight, query_bias, key_weight, value_weight, value_bias,
    out_weight, out_bias, norm1_gain, norm1_bias, up_weight, up_bias, down_weight, down_bias,
    norm2_gain, norm2_bias, cotangent,
):
    seqs, tokens, width = inputs.shape
    chars = char_ids.shape[1]
    per = chars // tokens
    steps = chars // SEGS
    per_seg = steps // per
    vocab, embed = char_table.shape
    sub = vocab // GROUPS
    half = width // 2
    size = width // HEADS
    ff = up_weight.shape[1]
    count = lax.axis_size("seq")
    pairs = -(-seqs * HEADS // count)
    while HEADS % pairs:
        pairs += 1
    full = count * tokens
    total = seqs * tokens
    rows = seqs * SEGS
    wide = pairs * size
    seq = lax.axis_index("seq")
    me = jnp.stack([seq, seq % 2]).astype(jnp.int32)
    flat = inputs.reshape(total, width)
    cot = cotangent.reshape(total, width)

    embedded, htok, ptok, pre, pseg, payload = call(
        functools.partial(chars_forward_body, seqs, steps, per, sub),
        [SMEM] + [COPY] * 2 + [HBM] * 3,
        [
            ((seqs * chars, embed), BF16, COPY),
            ((2, per_seg, rows, half), F32, COPY),
            ((2, per_seg, rows, half), F32, COPY),
            ((2, 2, rows, half), F32, COPY),
            ((2, rows, half), F32),
            ((8 * seqs, half), F32),
        ],
        [
            pltpu.VMEM((2, seqs * chars, half), F32),
            pltpu.VMEM((2, seqs * chars, half), F32),
            pltpu.VMEM((2, rows, half), F32),
            pltpu.VMEM((-(-vocab // LANES) * LANES, embed), BF16),
            pltpu.VMEM(gate_weight.shape, BF16),
            pltpu.VMEM(cand_weight.shape, BF16),
            pltpu.SemaphoreType.DMA((3,)),
        ],
        name="chars_forward",
    )(lang_ids, char_ids, gate_bias, char_table, gate_weight, cand_weight)
    groups = gather_summaries(payload)
    projections = (join_weight, query_weight, key_weight, value_weight)
    (near_w,) = ahead_of(projections, groups[0])

    resid, enter, joined, *sent = call(
        functools.partial(join_query_body, count, seqs, tokens, pairs),
        [SMEM] + [COPY] * 6 + [PIN] + [HBM] * (1 + count // 2),
        [
            ((total, width), F32, PIN),
            ((2, rows, half), F32),
            ((total, 4 * width), BF16, HBM),
        ]
        + [((tokens // 2, 6 * wide), BF16, PIN)] * count,
        [
            pltpu.VMEM((count, 8 * seqs, half), F32),
            pltpu.VMEM((total, width), BF16),
            pltpu.SemaphoreType.DMA((count + 1,)),
            pltpu.VMEM((count, tokens // 2, 6 * wide), BF16),
            pltpu.VMEM((total, 4 * width), BF16),
            pltpu.SemaphoreType.DMA((4,)),
        ],
        name="join_query",
    )(
        me, htok, ptok, pre, join_bias, query_bias, value_bias, near_w,
               flat, *groups,
    )
    heads = exchange(sent)

    block = min(1024, full)
    *sent, lse, heads_q, heads_k, heads_v, out_v, up_v = call(
        functools.partial(attend_body, count, seqs, tokens, pairs, size, block),
        [SMEM, SMEM] + [PIN] * count,
        [((tokens // 2, 2 * wide), BF16, PIN)] * count
        + [((8, full), F32)]
        + [((pairs, full, LANES), BF16, HBM)] * 3,
        [pltpu.VMEM((pairs, full, LANES), BF16)] * 3
        + [
            pltpu.VMEM((pairs, size + 16, full), BF16),
            pltpu.VMEM((wide, full), F32),
            pltpu.VMEM((full, wide), BF16),
            pltpu.SemaphoreType.DMA((3,)),
        ],
        name="attend",
        fetch=(out_weight, up_weight),
    )(me, lengths, *heads)
    mixed_chunks = exchange(sent)
    (joined_far,) = tie([joined], *mixed_chunks)
    joined_got = swap(joined_far, "seq", 1)

    ff_block = 768
    output, d_first_in, vec1, up_vec, fed, fed_keep, fed_send, *sent = call(
        functools.partial(feed_body, count, seqs, tokens, pairs, size, ff_block),
        [SMEM] + [VMEM] * 7 + [PIN] * 3 + [HBM] * 2 + [PIN] * count,
        [
            ((total, width), BF16, HBM),
            ((total, width), F32, COPY),
            ((8, width), F32),
            ((1, ff), F32),
            ((total, ff + 2 * width), BF16, PIN),
            ((total, ff // 2 + width), BF16, PIN),
            ((total, ff // 2 + width), BF16),
        ]
        + [((tokens // 2, 2 * wide), BF16, PIN)] * count,
        [
            pltpu.VMEM((count, tokens // 2, 2 * wide), BF16),
            pltpu.VMEM((total, ff), F32),
            pltpu.VMEM((total, width), F32),
            pltpu.VMEM((total, width), BF16),
            pltpu.VMEM((total, width), BF16),
            pltpu.VMEM((total, ff), BF16),
            pltpu.VMEM((total, width), BF16),
            pltpu.VMEM((ff, width), BF16),
            pltpu.SemaphoreType.DMA((2 + ff // ff_block,)),
        ],
        limit=32,
        name="feed_forward",
    )(
        me, out_bias, norm1_gain, norm1_bias, up_bias, down_bias, norm2_gain, norm2_bias, resid,
        out_v, up_v, cot, down_weight, *mixed_chunks,
    )
    d_mixed_chunks = exchange(sent)

    fed_got, fed_keep_got = swap(fed, "seq", 1), swap(fed_send, "seq", 1)
    fed, fed_got, fed_keep, fed_keep_got = tie(
        [fed, fed_got, fed_keep, fed_keep_got], *d_mixed_chunks
    )
    grad_feed = feed_grads(fed, fed_got, fed_keep, fed_keep_got, ff, width)
    feed = FeedRows(grad_feed, (ff + width) * 2 // (count * lax.axis_size("dp")))
    d_mixed_chunks = tie(d_mixed_chunks, grad_feed)

    back_block = min(512, full)
    sent = call(
        functools.partial(attend_back_body, count, seqs, tokens, pairs, size, back_block),
        [SMEM, VMEM] + [HBM] * 3 + [PIN] * count,
        [((tokens // 2, 6 * wide), BF16, PIN)] * count,
        [pltpu.VMEM((pairs, full, LANES), BF16)] * 3
        + [
            pltpu.VMEM((size, full), BF16),
            pltpu.VMEM((pairs, full, size), BF16),
            pltpu.VMEM((wide, full), F32),
            pltpu.VMEM((full, full), BF16),
            pltpu.VMEM((full, full), BF16),
            pltpu.VMEM((full, 3 * wide), BF16),
            pltpu.SemaphoreType.DMA((3,)),
        ],
        name="attend_back",
    )(me, lse, heads_q, heads_k, heads_v, *d_mixed_chunks)
    d_chunks = exchange(sent)
    (near_w,) = ahead_of(projections, sent[0])
    input_grad, d_perm, payload_back, vec2, back_keep, back_send = call(
        functools.partial(project_back_body, count, seqs, tokens, pairs, size, per_seg),
        [SMEM, COPY, COPY, COPY, PIN] + [PIN] * count,
        [
            ((total, width), BF16, COPY),
            ((2, per_seg, rows, half), F32, COPY),
            ((8 * seqs, half), F32),
            ((8, width), F32),
            ((total, 2 * width), BF16, PIN),
            ((total, 2 * width), BF16),
        ],
        [
            pltpu.VMEM((count, tokens // 2, 6 * wide), BF16),
            pltpu.VMEM((total, 4 * width), BF16),
        ],
        name="project_back",
    )(me, pre, d_first_in, ptok, near_w, *d_chunks)
    back_groups = gather_summaries(payload_back)
    vector_rows = -(-(10 * width + ff) // (16 * LANES)) * 16

    back_got = swap(back_send, "seq", 1)
    back_all = tie([joined, joined_got, back_keep, back_got], back_groups[0])
    back_plan = tuple((0, k * half, half) for k in range(3))
    back_plan += tuple(((1 + k) * width, 3 * half, half) for k in range(3))
    back_parts = outer_grads(back_all, back_plan, 3 * half, width, "grad_back")
    back_parts = tie(back_parts, *back_groups)
    back = Columns(back_parts, (half,) * 6)
    back_groups = tie(back_groups, *back_parts)

    own_rows = 4 * half * embed // (2 * LANES)
    table_rows = seqs * LANES
    chars_keep, chars_send = call(
        functools.partial(chars_back_body, count, seqs, steps, per),
        [SMEM, SMEM] + [VMEM] * 7 + [COPY] * 3 + [HBM] * (2 + count),
        [
            ((table_rows + own_rows, LANES), BF16),
            ((table_rows + vector_rows + own_rows, LANES), BF16),
        ],
        [
            pltpu.VMEM((2, seqs * chars, half), F32),
            pltpu.VMEM((2, seqs * chars, half), F32),
            pltpu.VMEM((seqs * chars, 4 * half), BF16),
            pltpu.VMEM((2, per_seg, rows, half), F32),
            pltpu.VMEM((2, rows, half), F32),
            pltpu.VMEM((2, rows, half), F32),
            pltpu.VMEM(gate_weight.shape, BF16),
            pltpu.VMEM(cand_weight.shape, BF16),
            pltpu.VMEM((count, 8 * seqs, half), F32),
            pltpu.VMEM((count, 8 * seqs, half), F32),
            pltpu.SemaphoreType.DMA((2 + 2 * count,)),
            pltpu.VMEM((vector_rows, LANES), F32),
            pltpu.VMEM((2, own_rows, LANES), F32),
        ],
        name="chars_back",
    )(
        lang_ids, me, char_ids, gate_bias, enter, pseg, vec1, up_vec, vec2, embedded, ptok, d_perm,
        gate_weight, cand_weight, *groups, *back_groups,
    )
    chars_sums = CharsSums(chars_keep, chars_send, table_rows, vector_rows)
    chars_sums.step()
    back.fold(chars_sums.send)
    chars_sums.step()
    back.part_cores()
    back.scatter_groups(chars_sums.send)
    while chars_sums.bits:
        chars_sums.step()
    chars_sums.across()
    feed.step(back.both, *chars_sums.sends)
    feed.step(*chars_sums.own[1:3])
    grad_up, grad_out, grad_down = feed.finish(ff, width, *chars_sums.own)
    grad_query, grad_key, grad_value, grad_join = back.finish(3)
    gate_shape = (2, embed // (count * lax.axis_size("dp")), half)
    sizes = [(width,)] * 6 + [(ff,)] + [(width,)] * 3 + [(2, half)]
    grad_table, grad_gate, grad_cand, *sums = chars_sums.finish(
        seqs, vocab, sub, gate_shape, sizes, grad_up, grad_query
    )

    return (
        output.reshape(inputs.shape),
        input_grad.reshape(inputs.shape),
        grad_table,
        grad_gate,
        sums[10],
        grad_cand,
        grad_join,
        sums[9],
        grad_query,
        sums[7],
        grad_key,
        grad_value,
        sums[8],
        grad_out,
        sums[5],
        sums[3],
        sums[4],
        grad_up,
        sums[6],
        grad_down,
        sums[2],
        sums[0],
        sums[1],
    )


def solution(mesh):
    spread_rows = P("dp", "seq", None)
    placed = (
        (spread_rows, P("dp", "seq"), P("dp"), P("dp")) + (P(),) * 21 + (spread_rows,)
    )
    owned = P(("dp", "seq"), None)
    owned_mid = P(None, ("dp", "seq"), None)
    return jax.shard_map(
        shards,
        mesh=mesh,
        in_specs=placed,
        out_specs=(
            spread_rows, spread_rows, P(), owned_mid, P(), owned_mid, owned_mid, P(),
            owned, P(), owned, owned, P(), owned, P(), P(), P(), owned, P(), owned, P(), P(), P(),
        ),
        check_vma=False,
    )
```

```python
import functools

import jax
import jax.numpy as jnp
from jax import lax
from jax.experimental import pallas as pl
from jax.experimental.pallas import tpu as pltpu
from jax.sharding import PartitionSpec as P

HEADS = 12
GROUPS = 8
SEGS = 8
LANES = 128
NORM_EPS = 1e-05
MASKED = (-998244352.0, -1753088.0, -2560.0)
MIB = 1 << 20
F32 = jnp.float32
BF16 = jnp.bfloat16


def dot(left, right):
    return jnp.dot(left, right, preferred_element_type=F32)


def dot_nt(left, right):
    return lax.dot_general(left, right, (((1,), (1,)), ((), ())), preferred_element_type=F32)


def dot_tn(left, right):
    return lax.dot_general(left, right, (((0,), (0,)), ((), ())), preferred_element_type=F32)


def column_sum(values):
    return jnp.sum(values.astype(F32), axis=0, keepdims=True)


VMEM = pl.BlockSpec(memory_space=pltpu.VMEM)
SMEM = pl.BlockSpec(memory_space=pltpu.SMEM)
HBM, PIN, COPY = "hbm", "pin", "copy"


def call(body, ins, outs, scratch=(), limit=40, name=None, fetch=()):
    spaces = {PIN: pltpu.VMEM, HBM: pltpu.HBM, COPY: pltpu.HBM}
    specs = {PIN: VMEM, HBM: pl.BlockSpec(memory_space=pltpu.HBM), COPY: VMEM}
    space_of = lambda spec: spaces[spec] if isinstance(spec, str) else None
    spec_of = lambda spec: specs[spec] if isinstance(spec, str) else spec
    all_ins = list(ins) + [HBM] * len(fetch)
    all_outs = [out if len(out) > 2 else out + (VMEM,) for out in outs]
    homes = {}
    for array in fetch:
        homes.setdefault(array.shape[-2:], []).append(array)
    homes = list(homes.items())
    fetch = [array for _, arrays in homes for array in arrays]
    for shape, arrays in homes:
        count = sum(array.size for array in arrays) // (shape[0] * shape[1])
        all_outs.append(((count,) + shape, arrays[0].dtype, PIN))
    scratch = list(scratch)
    inner = body
    if fetch:
        parts = 4
        scratch.append(pltpu.SemaphoreType.DMA((len(fetch) * parts,)))

        def inner(*refs):
            sems, n_in = refs[-1], len(ins)
            far, rest = refs[n_in : n_in + len(fetch)], refs[n_in + len(fetch) :]
            near, last = rest[len(outs) : len(outs) + len(homes)], len(outs) + len(homes)
            rest = rest[: len(outs)] + rest[last:-1]
            far = list(far)
            copies = []
            for b, (shape, arrays) in zip(near, homes):
                at = 0
                for _ in arrays:
                    a = far.pop(0)
                    wide = a.shape[0] if len(a.shape) > 2 else 1
                    rows = shape[0] // parts
                    for k in range(parts):
                        piece = slice(k * rows, (k + 1) * rows)
                        if len(a.shape) > 2:
                            pair = a.at[:, piece], b.at[slice(at, at + wide), piece]
                        else:
                            pair = a.at[piece], b.at[at, piece]
                        copies.append(pltpu.make_async_copy(*pair, sems.at[len(copies)]))
                    at += wide

            def begin():
                for copy in copies:
                    copy.start()

            body(begin, *refs[:n_in], *rest)
            for copy in copies:
                copy.wait()

    kernel = pl.pallas_call(
        inner,
        in_specs=[spec_of(spec) for spec in all_ins],
        out_specs=[spec_of(out[2]) for out in all_outs],
        out_shape=[
            space_of(out[2])(out[0], out[1]) if space_of(out[2]) else jax.ShapeDtypeStruct(out[0], out[1])
            for out in all_outs
        ],
        scratch_shapes=scratch,
        compiler_params=pltpu.CompilerParams(vmem_limit_bytes=limit * MIB),
        cost_estimate=pl.CostEstimate(flops=1, bytes_accessed=1, transcendentals=0),
        name=name,
    )

    def run(*args):
        args = list(args) + list(fetch)
        held = [
            pltpu.with_memory_space_constraint(arg, space_of(spec)) if space_of(spec) else arg
            for arg, spec in zip(args, all_ins)
        ]
        return kernel(*held)

    return run


def ahead_of(arrays, *after):
    def body(begin, *refs):
        begin()

    arrays = tie(arrays, *after)
    return call(body, [], [], fetch=tuple(arrays), limit=8, name="weights")()


def pull(pairs, sems):
    copies = [pltpu.make_async_copy(far, near, sems.at[k]) for k, (far, near) in enumerate(pairs)]
    for copy in copies:
        copy.start()
    return copies


def collect(chunks, stage, me, count):
    for k, chunk in enumerate(chunks):
        stage[lax.rem(me + count - k, count)] = chunk[...]


def summaries(groups, gathered, me):
    pairs = []
    for j, group in enumerate(groups):
        for i in range(2):
            pairs.append((group.at[i], gathered.at[jnp.bitwise_xor(me, 2 * j + i)]))
    return pairs


def gates(embedded, gate_w, gate_b, cand_w, upd, cand):
    for r in range(2):
        upd[r] = jax.nn.sigmoid(dot(embedded, gate_w[r]) + gate_b[r : r + 1])
        cand[r] = dot(embedded, cand_w[r])


def one_hot_rows(ids, seqs, steps):
    rows = []
    for s in range(seqs):
        for g in range(SEGS):
            rows.append(ids[s : s + 1, g * steps : (g + 1) * steps] + s * LANES)
    held = jnp.concatenate(rows, axis=0)
    place = lax.broadcasted_iota(jnp.int32, (seqs * SEGS, seqs * LANES), 1)
    return jnp.concatenate(
        [(place == held[:, t : t + 1]).astype(F32).astype(BF16) for t in range(steps)], axis=0
    )


def chars_forward_body(
    seqs, steps, per, sub,
    lang, ids, gate_b, table, gate_w_far, cand_w_far,
    embedded_out, htok, ptok, pre, pseg, payload,
    upd, cand, hseg, padded_table, gate_w, cand_w, sems,
):
    rows = seqs * SEGS
    vocab = table.shape[0]
    wide = padded_table.shape[0]
    copies = pull(
        [(table, padded_table.at[0:vocab]), (gate_w_far, gate_w), (cand_w_far, cand_w)], sems
    )
    padded_table[vocab:wide] = jnp.zeros((wide - vocab, padded_table.shape[1]), BF16)
    copies[0].wait()
    local = lax.broadcasted_iota(jnp.int32, (LANES, wide), 0)
    place = lax.broadcasted_iota(jnp.int32, (LANES, wide), 1)
    mine = []
    for s in range(seqs):
        pick = (place == lang[s] * sub + local) & (local < sub)
        mine.append(dot(pick.astype(BF16), padded_table[...]).astype(BF16))
    own_table = jnp.concatenate(mine, axis=0)
    embedded = dot(one_hot_rows(ids, seqs, steps), own_table).astype(BF16)
    embedded_out[...] = embedded
    copies[1].wait()
    copies[2].wait()
    gates(embedded, gate_w, gate_b[...], cand_w, upd, cand)

    def token(q, carry):
        h0, p0, h1, p1 = carry
        for j in range(per):
            at = pl.ds(pl.multiple_of((q * per + j) * rows, rows), rows)
            u = upd[0, at, :]
            h0 = h0 + u * (cand[0, at, :] - h0)
            p0 = p0 * (1.0 - u)
            at = pl.ds(pl.multiple_of((steps - 1 - q * per - j) * rows, rows), rows)
            u = upd[1, at, :]
            h1 = h1 + u * (cand[1, at, :] - h1)
            p1 = p1 * (1.0 - u)
        htok[0, q] = h0
        ptok[0, q] = p0
        back = steps // per - 1 - q
        htok[1, back] = h1
        ptok[1, back] = p1
        return h0, p0, h1, p1

    zero = jnp.zeros((rows, upd.shape[2]), F32)
    h0, p0, h1, p1 = lax.fori_loop(0, steps // per, token, (zero, zero + 1.0, zero, zero + 1.0))
    pseg[0], pseg[1], hseg[0], hseg[1] = p0, p1, h0, h1
    last = steps // per - 1
    for s in range(seqs):
        for r in range(2):
            total_a = jnp.ones((1, upd.shape[2]), F32)
            total_b = jnp.zeros((1, upd.shape[2]), F32)
            order = range(SEGS) if r == 0 else range(SEGS - 1, -1, -1)
            for g in order:
                row = s * SEGS + g
                pre[0, r, row : row + 1] = total_a
                pre[1, r, row : row + 1] = total_b
                p_row = pseg[r, row : row + 1]
                total_b = p_row * total_b + hseg[r, row : row + 1]
                total_a = p_row * total_a
            edge = s * SEGS if r == 0 else s * SEGS + SEGS - 1
            q = 0 if r == 0 else last
            near_a, near_b = ptok[r, q, edge : edge + 1], htok[r, q, edge : edge + 1]
            for k, value in enumerate((total_a, total_b, near_a, near_b)):
                row = (4 * r + k) * seqs + s
                payload[row : row + 1] = value


def spread(values, seqs):
    wide = values.shape[1]
    return jnp.concatenate(
        [jnp.broadcast_to(values[s : s + 1], (SEGS, wide)) for s in range(seqs)], axis=0
    )


def token_row(token, tokens, per_seg, seqs):
    s = token // tokens
    t = token % tokens
    return (t % per_seg) * (seqs * SEGS) + s * SEGS + t // per_seg


def join_query_body(
    count, seqs, tokens, pairs,
    me_ref, htok, ptok, pre, join_b, query_b, value_b, near_w, inputs_far,
    *rest,
):
    groups, rest = rest[: count // 2], rest[count // 2 :]
    resid_out, enter, left_out = rest[:3]
    chunks = rest[3 : 3 + count]
    held, inputs, sems, stage, lefts, left_sems = rest[3 + count :]
    me = me_ref[0]
    width = near_w.shape[1]
    outgoing = []

    def emit(k, values):
        lanes = slice(k * width, (k + 1) * width)
        lefts[:, lanes] = values
        copy = pltpu.make_async_copy(lefts.at[:, lanes], left_out.at[:, lanes], left_sems.at[k])
        copy.start()
        outgoing.append(copy)

    copies = pull(summaries(groups, held, me) + [(inputs_far, inputs)], sems)
    for copy in copies[:count]:
        copy.wait()
    copies = copies[count:]
    half = htok.shape[3]

    def gathered(j, k):
        return held[j, k * seqs : (k + 1) * seqs]

    per_seg = htok.shape[1]
    total = seqs * tokens
    x0 = jnp.zeros((seqs, half), F32)
    x1 = jnp.zeros((seqs, half), F32)
    for j in range(count):
        x0 = jnp.where(j < me, gathered(j, 0) * x0 + gathered(j, 1), x0)
        i = count - 1 - j
        x1 = jnp.where(i > me, gathered(i, 4) * x1 + gathered(i, 5), x1)
    carry0 = pre[0, 0] * spread(x0, seqs) + pre[1, 0]
    carry1 = pre[0, 1] * spread(x1, seqs) + pre[1, 1]
    enter[0] = carry0
    enter[1] = carry1
    forward = htok[0] + ptok[0] * carry0[None]
    backward = htok[1] + ptok[1] * carry1[None]
    rows = seqs * SEGS
    last = per_seg - 1
    f_last = jnp.concatenate(
        [forward[last, s * SEGS + SEGS - 1 : s * SEGS + SEGS] for s in range(seqs)], axis=0
    )
    b_first = jnp.concatenate(
        [backward[0, s * SEGS : s * SEGS + 1] for s in range(seqs)], axis=0
    )
    left = jnp.maximum(me - 1, 0)
    right = jnp.minimum(me + 1, count - 1)
    left_b = gathered(left, 6) * b_first + gathered(left, 7)
    right_f = gathered(right, 2) * f_last + gathered(right, 3)
    left_row = jnp.where(me > 0, jnp.concatenate([x0, left_b], axis=1), 0.0)
    right_row = jnp.where(me < count - 1, jnp.concatenate([right_f, x1], axis=1), 0.0)
    rim = jnp.concatenate(
        [left_row, right_row, jnp.zeros((16 - 2 * seqs, 2 * half), F32)], axis=0
    ).astype(BF16)
    tokens_perm = jnp.concatenate(
        [forward.reshape(total, half), backward.reshape(total, half)], axis=1
    ).astype(BF16)
    source = jnp.concatenate([tokens_perm, rim], axis=0)
    token = lax.broadcasted_iota(jnp.int32, (total, total + 16), 0)
    place = lax.broadcasted_iota(jnp.int32, (total, total + 16), 1)
    joining = jnp.broadcast_to(join_b[...][None], (total, 2 * half))
    for k in range(3):
        moved = token + (k - 1)
        want = token_row(moved, tokens, per_seg, seqs)
        if k == 0:
            want = jnp.where(token % tokens == 0, total + token // tokens, want)
        if k == 2:
            want = jnp.where(token % tokens == tokens - 1, total + seqs + token // tokens, want)
        tap = dot((place == want).astype(BF16), source).astype(BF16)
        emit(1 + k, tap)
        joining = joining + dot(tap, near_w[k])
    copies[0].wait()
    resid = inputs[...].astype(F32) + joining
    resid_out[...] = resid
    low = resid.astype(BF16)
    emit(0, low)
    size = 2 * half // HEADS
    wide = pairs * size
    query = (dot(low, near_w[3]) + query_b[...][None]).astype(BF16)
    key = dot(low, near_w[4]).astype(BF16)
    value = (dot(low, near_w[5]) + value_b[...][None]).astype(BF16)
    send_pairs((query, key, value), stage, chunks, me, count, seqs, tokens, pairs, size, wide)
    for copy in outgoing:
        copy.wait()


def send_pairs(arrays, stage, chunks, me, count, seqs, tokens, pairs, size, wide):
    half = tokens // 2
    for d in range(count):
        for a, array in enumerate(arrays):
            first = d * pairs
            for part in range(2):
                lane = (part * len(arrays) + a) * wide
                if first >= seqs * HEADS:
                    stage[d, :, lane : lane + wide] = jnp.zeros((half, wide), BF16)
                    continue
                s, head = first // HEADS, first % HEADS
                row = s * tokens + part * half
                stage[d, :, lane : lane + wide] = array[row : row + half, head * size : head * size + wide]
    for k in range(count):
        chunks[k][...] = stage[lax.rem(me + k, count)]


def split_tokens(source, me, chunks, tokens):
    half, wide = tokens // 2, source.shape[1]
    for k, chunk in enumerate(chunks):
        start = lax.rem(me + k, len(chunks)) * tokens
        for part in range(2):
            at = pl.ds(pl.multiple_of(start + part * half, half), half)
            chunk[:, part * wide : (part + 1) * wide] = source[at, :]


def receive_pairs(stage, place, count, seqs, tokens, pairs, size, parts):
    wide = pairs * size
    for d in range(count):
        first = d * pairs
        if first >= seqs * HEADS:
            continue
        s, head = first // HEADS, first % HEADS
        for part in range(2):
            for a in range(parts):
                lane = (part * parts + a) * wide
                row = s * tokens + part * (tokens // 2)
                place(a, row, head * size, stage[d, :, lane : lane + wide])


def load_heads(chunks, me, count, tokens, pairs, size, parts, part, target, scale=None):
    wide, half = pairs * size, tokens // 2
    for k in range(count):
        start = lax.rem(me + count - k, count) * tokens
        for second in range(2):
            at = pl.ds(pl.multiple_of(start + second * half, half), half)
            for h in range(pairs):
                lane = (second * parts + part) * wide + h * size
                block = chunks[k][:, lane : lane + size]
                target[h, at, 0:size] = block if scale is None else block * scale


def pair_length(lengths, me, pairs, h, seqs):
    return lengths[jnp.minimum((me * pairs + h) // HEADS, seqs - 1)]


def transposed(values):
    return jnp.transpose(values.astype(F32))


def mask_lanes(q, k, full, valid, size):
    shape = (full, k.shape[2] - size)
    lane = lax.broadcasted_iota(jnp.int32, shape, 1)
    padded = lax.broadcasted_iota(jnp.int32, shape, 0) >= valid
    ones = jnp.where(lane < 3, 1.0, 0.0).astype(BF16)
    parts = jnp.where(lane == 0, MASKED[0], jnp.where(lane == 1, MASKED[1], MASKED[2]))
    mask = jnp.where((lane < 3) & padded, parts, 0.0).astype(BF16)
    keep = (lax.broadcasted_iota(jnp.int32, (full, size), 0) < valid).astype(F32).astype(BF16)
    for h in range(k.shape[0]):
        q[h, :, size:] = ones
        k[h, :, size:] = mask
        k[h, :, 0:size] = k[h, :, 0:size] * keep


def attend_body(count, seqs, tokens, pairs, size, block, begin, me_ref, lengths, *rest):
    chunks, rest = rest[:count], rest[count:]
    outs, lse, far = rest[:count], rest[count], rest[count + 1 : count + 4]
    q, k, v, vt, mixed_t, mixed, sems = rest[count + 4 :]
    me = me_ref[0]
    full = count * tokens
    begin()
    load_heads(chunks, me, count, tokens, pairs, size, 3, 0, q, jnp.asarray(0.125, BF16))
    load_heads(chunks, me, count, tokens, pairs, size, 3, 1, k)
    load_heads(chunks, me, count, tokens, pairs, size, 3, 2, v)
    lse[...] = jnp.zeros_like(lse)
    mask_lanes(q, k, full, pair_length(lengths, me, pairs, 0, seqs), size)
    copies = pull(list(zip((q, k, v), far)), sems)
    for h in range(pairs):
        vt[h, 0:size] = transposed(v[h, :, 0:size]).astype(BF16)
        row = lax.broadcasted_iota(jnp.int32, (vt.shape[1] - size, full), 0)
        vt[h, size:] = jnp.where(row == 0, 1.0, 0.0).astype(BF16)

        def rows(i, _, h=h):
            at = pl.ds(pl.multiple_of(i * block, block), block)
            scores = dot_nt(k[h], q[h, at, :])
            top = jnp.max(scores, axis=0, keepdims=True)
            sums = dot(vt[h], jnp.exp(scores - top).astype(BF16))
            total = sums[size : size + 1]
            lse[h : h + 1, at] = top + jnp.log(total)
            mixed_t[h * size : (h + 1) * size, at] = sums[0:size] / total
            return 0

        lax.fori_loop(0, full // block, rows, 0, unroll=2)
    mixed[...] = transposed(mixed_t[...]).astype(BF16)
    split_tokens(mixed, me, outs, tokens)
    for copy in copies:
        copy.wait()


def attend_back_body(count, seqs, tokens, pairs, size, block, me_ref, lse, *rest):
    far, d_chunks, rest = rest[:3], rest[3 : 3 + count], rest[3 + count :]
    outs = rest[:count]
    q, k, v, kt, d_o, dq_t, probs_all, d_scores_all, stage, sems = rest[count:]
    me = me_ref[0]
    full = count * tokens
    wide = pairs * size
    copies = pull(list(zip(far, (q, k, v))), sems)
    load_heads(d_chunks, me, count, tokens, pairs, size, 1, 0, d_o)
    for copy in copies:
        copy.wait()
    for h in range(pairs):
        kt[...] = transposed(k[h, :, 0:size]).astype(BF16)

        def rows(i, _, h=h):
            at = pl.ds(pl.multiple_of(i * block, block), block)
            probs = jnp.exp(dot_nt(k[h], q[h, at, :]) - lse[h : h + 1, at])
            d_probs = dot_nt(v[h, :, 0:size], d_o[h, at, :])
            probs_all[:, at] = probs.astype(BF16)
            row_dot = jnp.sum(probs * d_probs, axis=0, keepdims=True)
            d_scores_all[:, at] = (probs * (d_probs - row_dot)).astype(BF16)
            return 0

        lax.fori_loop(0, full // block, rows, 0, unroll=2)
        dq_t[h * size : (h + 1) * size, :] = dot(kt[...], d_scores_all[...]) * 0.125
        for part, grad in (
            (1, dot(d_scores_all[...], q[h])), (2, dot(probs_all[...], d_o[h])),
        ):
            lane = part * wide + h * size
            stage[:, lane : lane + size] = grad[:, 0:size].astype(BF16)
    stage[:, 0:wide] = transposed(dq_t[...]).astype(BF16)
    split_tokens(stage, me, outs, tokens)


def normed(values):
    center = values - jnp.mean(values, axis=-1, keepdims=True)
    scale = lax.rsqrt(jnp.mean(center * center, axis=-1, keepdims=True) + NORM_EPS)
    return center * scale, scale


def norm_back(cotangent, unit, scale, gain):
    d_unit = cotangent * gain
    mean = jnp.mean(d_unit, axis=-1, keepdims=True)
    lean = jnp.mean(d_unit * unit, axis=-1, keepdims=True)
    return scale * (d_unit - mean - unit * lean)


GELU_A = 0.7978845608028654
GELU_B = 0.044715


def feed_body(
    count, seqs, tokens, pairs, size, block,
    me_ref, out_b, gain1, shift1, up_b, down_b, gain2, shift2,
    resid, out_v, up_v, cotangent_far, down_far,
    *rest,
):
    chunks, rest = rest[:count], rest[count:]
    output_far, d_first_in_out, vec, up_vec, lefts, keep_out, send_out = rest[:7]
    outs = rest[7 : 7 + count]
    out_v, up_v = out_v.at[0], up_v.at[0]
    stage, slope, acc, cotangent, output, d_hidden_v, d_second_v, down_v, sems = rest[7 + count :]
    me, core = me_ref[0], me_ref[1]
    width = out_v.shape[0]
    ff = up_v.shape[1]
    parts = ff // block
    mixed = lefts.at[:, ff + width : ff + 2 * width]
    first_low_v = lefts.at[:, ff : ff + width]

    def emit_halves(source, lane, wide):
        for out, part in ((keep_out, core), (send_out, 1 - core)):
            at = pl.ds(pl.multiple_of(part * wide, LANES), wide)
            out[:, lane : lane + wide] = source[:, at]

    pieces = [slice(j * block, (j + 1) * block) for j in range(parts)]
    first_copies = pull(
        [(cotangent_far, cotangent)]
        + [(down_far.at[piece], down_v.at[piece]) for piece in pieces],
        sems,
    )
    collect(chunks, stage, me, count)

    def lanes(j):
        return pl.ds(pl.multiple_of(j * block, block), block)

    def place(part, row, lane, values):
        mixed[row : row + values.shape[0], lane : lane + values.shape[1]] = values

    receive_pairs(stage, place, count, seqs, tokens, pairs, size, 1)
    first_in = resid[...] + dot(mixed[...], out_v[...]) + out_b[...][None]
    unit1, scale1 = normed(first_in)
    first = unit1 * gain1[...][None] + shift1[...][None]
    first_low = first.astype(BF16)
    first_low_v[...] = first_low
    acc[...] = first + down_b[...][None]

    def ahead(j, _):
        hidden = dot(first_low_v[...], up_v[:, lanes(j)]) + up_b[lanes(j)][None]
        square = hidden * hidden
        bend = jnp.tanh(GELU_A * (hidden + GELU_B * (square * hidden)))
        act = (0.5 * hidden * (1.0 + bend)).astype(BF16)
        lefts[:, lanes(j)] = act
        slope[:, lanes(j)] = 0.5 * (1.0 + bend) + 0.5 * hidden * (1.0 - bend * bend) * (
            GELU_A * (1.0 + 3.0 * GELU_B * square)
        )
        first_copies[1 + j].wait()
        acc[...] += dot(act, down_v[lanes(j), :])

    for j in range(parts):
        ahead(j, 0)
    unit2, scale2 = normed(acc[...])
    first_copies[0].wait()
    output[...] = (unit2 * gain2[...][None] + shift2[...][None]).astype(BF16)
    done = pltpu.make_async_copy(output, output_far, sems.at[1 + parts])
    done.start()
    cot = cotangent[...].astype(F32)
    vec[0:1] = column_sum(cot * unit2)
    vec[1:2] = column_sum(cot)
    d_second_in = norm_back(cot, unit2, scale2, gain2[...][None])
    d_second = d_second_in.astype(BF16)
    d_second_v[...] = d_second
    emit_halves(d_second_v, ff // 2, width // 2)
    vec[2:3] = column_sum(d_second)
    acc[...] = d_second_in

    def astern(j, _):
        d_act = dot_nt(d_second_v[...], down_v[lanes(j), :])
        d_hidden = (d_act * slope[:, lanes(j)]).astype(BF16)
        d_hidden_v[:, lanes(j)] = d_hidden
        up_vec[:, lanes(j)] = column_sum(d_hidden)
        acc[...] += dot_nt(d_hidden, up_v[:, lanes(j)])
        return 0

    lax.fori_loop(0, parts, astern, 0, unroll=True)
    emit_halves(d_hidden_v, 0, ff // 2)
    d_first = acc[...]
    vec[3:4] = column_sum(d_first * unit1)
    vec[4:5] = column_sum(d_first)
    d_first_in = norm_back(d_first, unit1, scale1, gain1[...][None])
    d_first_in_out[...] = d_first_in
    d_attn = d_first_in.astype(BF16)
    d_second_v[...] = d_attn
    emit_halves(d_second_v, ff // 2 + width // 2, width // 2)
    vec[5:6] = column_sum(d_attn)
    vec[6:8] = jnp.zeros((2, vec.shape[1]), F32)
    d_mixed = dot_nt(d_attn, out_v[...]).astype(BF16)
    send_pairs((d_mixed,), stage, outs, me, count, seqs, tokens, pairs, size, pairs * size)
    done.wait()


def fetch_columns(arrays, lanes, sems, at):
    copies = []
    for far, near in arrays:
        copy = pltpu.make_async_copy(far.at[:, lanes], near.at[:, lanes], sems.at[at + len(copies)])
        copy.start()
        copies.append(copy)
    return copies


def feed_grads_body(ff, lefts, lefts_got, rights, rights_got, out, res, sems):
    half = out.shape[-1]
    width = 2 * half
    blocks = out.shape[0]
    step = ff // blocks
    first = ff // 2
    outgoing = []

    def emit(place):
        at = sems.at[len(outgoing)]
        copy = pltpu.make_async_copy(res.at[place], out.at[place], at)
        copy.start()
        outgoing.append(copy)

    def grad(at, size, begin):
        rows, lanes = slice(at, at + size), slice(begin, begin + half)
        return dot_tn(lefts[:, rows], rights[:, lanes]) + dot_tn(lefts_got[:, rows], rights_got[:, lanes])

    whole = slice(None)
    owners = 1
    for size in out.shape[:-2]:
        owners *= size
    pieces = (ff + width) // width
    up_rows = width // owners
    down_rows = ff // owners
    start = pieces * up_rows
    mids = (whole,) * (len(out.shape) - 3)
    by_piece = up_rows % 16 == 0 and down_rows % 16 == 0
    for j in range(blocks):
        part = grad(j * step, step, first)
        spread_rows(res, (j,), slice(start, start + down_rows), part)
        if by_piece:
            emit((j,) + mids + (slice(start, start + down_rows), whole))
    for k in range(pieces):
        if k == pieces - 1:
            part = grad(ff + width, width, first + half)
        else:
            part = grad(ff, width, k * half)
        rows = slice(k * up_rows, (k + 1) * up_rows)
        spread_rows(res, (), rows, part)
        if by_piece:
            emit((whole,) + mids + (rows, whole))
    if not by_piece:
        emit((whole,) * len(out.shape))
    for copy in outgoing:
        copy.wait()


def spread_rows(res, head, rows, grad):
    size = rows.stop - rows.start
    wide = res.shape[len(head) : -2]
    if size % 16 == 0:
        at = head + (slice(None),) * len(wide) + (rows, slice(None))
        res[at] = grad.astype(BF16).reshape(wide + (size, grad.shape[1]))
        return
    places = [()]
    for count in wide:
        places = [place + (k,) for place in places for k in range(count)]
    for k, place in enumerate(places):
        res[head + place + (rows, slice(None))] = grad[k * size : (k + 1) * size].astype(BF16)


def feed_grads(left, left_got, right, right_got, ff, width):
    count, groups = lax.axis_size("seq"), lax.axis_size("dp")
    places = bits_of(count)[1:]
    owners = count * groups // 2
    rows = (ff + width) // width * (width // owners) + ff // owners
    shape = (groups,) + (2,) * len(places) + (rows, width // 2)
    (out,) = call(
        functools.partial(feed_grads_body, ff),
        [PIN] * 4,
        [(shape, BF16, HBM)],
        [
            pltpu.VMEM(shape, BF16),
            pltpu.SemaphoreType.DMA((groups + (ff + width) // width,)),
        ],
        name="grad_feed",
    )(left, left_got, right, right_got)
    return out


def store_rows(res, lanes, grad):
    rows = res.shape[-2]
    if rows % 16 == 0:
        res[..., lanes] = grad.astype(BF16).reshape(res.shape[:-1] + (grad.shape[1],))
        return
    places = [()]
    for wide in res.shape[:-2]:
        places = [place + (k,) for place in places for k in range(wide)]
    for k, place in enumerate(places):
        res[place + (slice(None), lanes)] = grad[k * rows : (k + 1) * rows].astype(BF16)


def outer_body(plan, cut, bits_ref, left, left_got, rights, rights_got, *rest):
    low_send, low_keep, high_send, high_keep = rest[:4]
    lefts, lefts_got, res, sems = rest[4:]
    height = lefts.shape[1] // len({lane for lane, _, _ in plan})
    waits = []
    for number, (lane, first, wide) in enumerate(plan):
        copies = []
        for far, near, at, size, seen in (
            (left, lefts, lane, height, [other[0] for other in plan[:number]]),
            (left_got, lefts_got, lane, height, [other[0] for other in plan[:number]]),
        ):
            if at not in seen:
                lanes = slice(at, at + size)
                sem = sems.at[sum(map(len, waits)) + len(copies)]
                copies.append(pltpu.make_async_copy(far.at[:, lanes], near.at[:, lanes], sem))
        waits.append(copies)
        for copy in copies:
            copy.start()
    used = sum(map(len, waits))
    low, high = bits_ref[0], bits_ref[1]
    outgoing = []
    whole = slice(None)
    mids = len(res.shape) - 4

    def emit(low_half):
        if low_half:
            place = lambda which: (whole,) * (1 + mids) + (which, whole, slice(0, cut))
            pairs = ((low_send, 1 - low), (low_keep, low))
        else:
            place = lambda which: (whole, which) + (whole,) * (1 + mids) + (slice(cut, res.shape[-1]),)
            pairs = ((high_send, 1 - high), (high_keep, high))
        for out, which in pairs:
            copy = pltpu.make_async_copy(res.at[place(which)], out, sems.at[used + len(outgoing)])
            copy.start()
            outgoing.append(copy)

    lane_at = 0
    for number, (lane, first, wide) in enumerate(plan):
        for copy in waits[number]:
            copy.wait()
        for k in range(0, wide, 512):
            size = min(512, wide - k)
            lanes = slice(first + k, first + k + size)
            grad = dot_tn(lefts[:, lane : lane + height], rights[:, lanes])
            grad = grad + dot_tn(lefts_got[:, lane : lane + height], rights_got[:, lanes])
            lanes = slice(lane_at + k, lane_at + k + size)
            store_rows(res, lanes, grad)
            if lane_at + k + size == cut:
                emit(True)
        lane_at += wide
    emit(False)
    for copy in outgoing:
        copy.wait()


def outer_grads(arrays, plan, cut, height, name):
    count, groups = lax.axis_size("seq"), lax.axis_size("dp")
    places = bits_of(count)[1:]
    rows = 2 * height // (count * groups)
    tokens = arrays[0].shape[0]
    wide = sum(piece[2] for piece in plan)
    lefts = len({piece[0] for piece in plan})
    shape = (groups,) + (2,) * len(places) + (rows,)
    less = (groups,) + (2,) * (len(places) - 1) + (rows,)
    seq = lax.axis_index("seq")
    bits = jnp.stack([(seq // places[0]) % 2, (seq // places[-1]) % 2]).astype(jnp.int32)
    return call(
        functools.partial(outer_body, plan, cut),
        [SMEM, HBM, HBM, PIN, PIN],
        [(less + (cut,), BF16, HBM)] * 2 + [(less + (wide - cut,), BF16, HBM)] * 2,
        [
            pltpu.VMEM((tokens, lefts * height), BF16),
            pltpu.VMEM((tokens, lefts * height), BF16),
            pltpu.VMEM(shape + (wide,), BF16),
            pltpu.SemaphoreType.DMA((4 * len(plan) + 4,)),
        ],
        name=name,
    )(bits, *arrays)


def project_back_body(
    count, seqs, tokens, pairs, size, per_seg,
    me_ref, pre, d_first_in, ptok, near_w,
    *rest,
):
    chunks, rest = rest[:count], rest[count:]
    grad_out, d_perm, payload, vec, keep_out, send_out = rest[:6]
    stage, rights = rest[6:]
    me, core = me_ref[0], me_ref[1]
    width = near_w.shape[1]

    def emit_halves(part):
        wide = width // 2
        for out, which in ((keep_out, core), (send_out, 1 - core)):
            at = pl.ds(pl.multiple_of(part * width + which * wide, LANES), wide)
            out[:, part * wide : (part + 1) * wide] = rights[:, at]

    collect(chunks, stage, me, count)
    targets = [rights.at[:, k * width : (k + 1) * width] for k in range(4)]

    def place(part, row, lane, values):
        at = part * width + lane
        rights[row : row + values.shape[0], at : at + values.shape[1]] = values

    receive_pairs(stage, place, count, seqs, tokens, pairs, size, 3)
    for part in range(3):
        emit_halves(part)
    d_resid = d_first_in[...]
    for k in range(3):
        d_resid = d_resid + dot_nt(targets[k][...], near_w[3 + k])
    grad = d_resid.astype(BF16)
    grad_out[...] = grad
    targets[3][...] = grad
    emit_halves(3)
    vec[0:1] = column_sum(targets[0][...])
    vec[1:2] = column_sum(targets[2][...])
    vec[2:3] = column_sum(grad)
    vec[3:8] = jnp.zeros((5, vec.shape[1]), F32)
    total = seqs * tokens
    half = vec.shape[1] // 2
    row = lax.broadcasted_iota(jnp.int32, (total + 16, total), 0)
    place_at = lax.broadcasted_iota(jnp.int32, (total + 16, total), 1)
    rows = seqs * SEGS
    step, rest_row = row // rows, row % rows
    seq = rest_row // SEGS
    tok = (rest_row % SEGS) * per_seg + step
    extra = row - total
    seq = jnp.where(extra >= 0, extra % seqs, seq)
    tok = jnp.where(extra >= 0, jnp.where(extra < seqs, -1, tokens), tok)
    known = extra < 2 * seqs
    d_char = jnp.zeros((total + 16, 2 * half), F32)
    for k in range(3):
        moved = tok + 1 - k
        pick = (place_at == seq * tokens + moved) & (moved >= 0) & (moved < tokens) & known
        shifted = dot(pick.astype(BF16), grad).astype(BF16)
        d_char = d_char + dot_nt(shifted, near_w[k])
    payload[6 * seqs :] = jnp.zeros((payload.shape[0] - 6 * seqs, half), F32)
    for r in range(2):
        grads = d_char[0:total, r * half : (r + 1) * half].reshape(per_seg, rows, half)
        d_perm[r] = grads
        weighted = jnp.sum(grads * ptok[r], axis=0) * pre[0, r]
        for s in range(seqs):
            row = r * seqs + s
            payload[row : row + 1] = column_sum(weighted[s * SEGS : (s + 1) * SEGS])
        edges = d_char[total : total + 2 * seqs, r * half : (r + 1) * half]
        payload[(2 + r) * seqs : (3 + r) * seqs] = edges[0:seqs]
        payload[(4 + r) * seqs : (5 + r) * seqs] = edges[seqs : 2 * seqs]


def chars_back_body(
    count, seqs, steps, per,
    lang, me_ref, ids, gate_b, enter, pseg, vec1, up_vec, vec2, embedded, ptok, d_perm, gate_w_far, cand_w_far,
    *rest,
):
    groups, back_groups, rest = rest[: count // 2], rest[count // 2 : count], rest[count:]
    (
        keep_out, send_out,
        upd, work, d_all, d_tok, gseg, gin, gate_w, cand_w, held, back, sems, vector, owned,
    ) = rest
    me = me_ref[0]
    wanted = [(gate_w_far, gate_w), (cand_w_far, cand_w)]
    wanted += summaries(groups, held, me) + summaries(back_groups, back, me)
    copies = pull(wanted, sems)
    for copy in copies[:2]:
        copy.wait()

    def gathered(j, k):
        return held[j, k * seqs : (k + 1) * seqs]

    def gathered_back(j, k):
        return back[j, k * seqs : (k + 1) * seqs]

    rows = seqs * SEGS
    half = upd.shape[2]
    gates(embedded[...], gate_w, gate_b[...], cand_w, upd, work)

    def ahead(q, carry):
        h0, h1 = carry
        for j in range(per):
            at = pl.ds(pl.multiple_of((q * per + j) * rows, rows), rows)
            u = upd[0, at, :]
            gap = work[0, at, :] - h0
            work[0, at, :] = gap * (u * (1.0 - u))
            h0 = h0 + u * gap
            at = pl.ds(pl.multiple_of((steps - 1 - q * per - j) * rows, rows), rows)
            u = upd[1, at, :]
            gap = work[1, at, :] - h1
            work[1, at, :] = gap * (u * (1.0 - u))
            h1 = h1 + u * gap
        return h0, h1

    lax.fori_loop(0, steps // per, ahead, (enter[0], enter[1]))

    left = jnp.maximum(me - 1, 0)
    right = jnp.minimum(me + 1, count - 1)
    last = steps // per - 1
    for copy in copies[2:]:
        copy.wait()
    d_tok[...] = d_perm[...]
    for r in range(2):
        from_left = jnp.where(me > 0, gathered_back(left, 4 + r), 0.0)
        from_right = jnp.where(me < count - 1, gathered_back(right, 2 + r), 0.0)
        for s in range(seqs):
            low, high = s * SEGS, s * SEGS + SEGS - 1
            d_tok[r, 0, low : low + 1] += from_left[s : s + 1]
            d_tok[r, last, high : high + 1] += from_right[s : s + 1]
        gseg[r] = jnp.sum(d_tok[r] * ptok[r], axis=0)

    def block_sum(j, r):
        total = gathered_back(j, r)
        near, far = gathered(j, 4 * r + 2), gathered(j, 4 * r)
        if r == 1:
            near, far = far, near
        if j > 0:
            total = total + near * gathered_back(j - 1, 4 + r)
        if j < count - 1:
            total = total + far * gathered_back(j + 1, 2 + r)
        return total

    g0 = jnp.zeros((seqs, half), F32)
    g1 = jnp.zeros((seqs, half), F32)
    for j in range(count):
        i = count - 1 - j
        g0 = jnp.where(i > me, gathered(i, 0) * g0 + block_sum(i, 0), g0)
        g1 = jnp.where(j < me, gathered(j, 4) * g1 + block_sum(j, 1), g1)
    for s in range(seqs):
        flow = g0[s : s + 1]
        for g in range(SEGS - 1, -1, -1):
            row = s * SEGS + g
            gin[0, row : row + 1] = flow
            flow = pseg[0, row : row + 1] * flow + gseg[0, row : row + 1]
        flow = g1[s : s + 1]
        for g in range(SEGS):
            row = s * SEGS + g
            gin[1, row : row + 1] = flow
            flow = pseg[1, row : row + 1] * flow + gseg[1, row : row + 1]

    def astern(q, carry):
        flow0, flow1 = carry
        for j in range(per):
            at = pl.ds(pl.multiple_of((steps - 1 - q * per - j) * rows, rows), rows)
            if j == 0:
                flow0 = flow0 + d_tok[0, steps // per - 1 - q]
            u = upd[0, at, :]
            d_all[at, 0:half] = (flow0 * work[0, at, :]).astype(BF16)
            d_cand = flow0 * u
            d_all[at, half : 2 * half] = d_cand.astype(BF16)
            flow0 = flow0 - d_cand
            at = pl.ds(pl.multiple_of((q * per + j) * rows, rows), rows)
            if j == 0:
                flow1 = flow1 + d_tok[1, q]
            u = upd[1, at, :]
            d_all[at, 2 * half : 3 * half] = (flow1 * work[1, at, :]).astype(BF16)
            d_cand = flow1 * u
            d_all[at, 3 * half : 4 * half] = d_cand.astype(BF16)
            flow1 = flow1 - d_cand
        return flow0, flow1

    lax.fori_loop(0, steps // per, astern, (gin[0], gin[1]))
    grad_w = dot_tn(embedded[...], d_all[...])
    place_owned(owned, grad_w)
    d_emb = jnp.zeros(embedded.shape, F32)
    gate_sums = []
    for r in range(2):
        gate_sums.append(column_sum(d_all[:, 2 * r * half : (2 * r + 1) * half]))
        d_emb = d_emb + dot_nt(d_all[:, 2 * r * half : (2 * r + 1) * half], gate_w[r])
        d_emb = d_emb + dot_nt(d_all[:, (2 * r + 1) * half : (2 * r + 2) * half], cand_w[r])
    partial = dot_tn(one_hot_rows(ids, seqs, steps), d_emb.astype(BF16))
    local = lax.broadcasted_iota(jnp.int32, partial.shape, 0)
    for s in range(seqs):
        tag = lang[s].astype(F32)
        partial = jnp.where(local == s * LANES + LANES - 1, tag, partial)
    core = me_ref[1]
    wide = partial.shape[1] // 2
    low, high = partial[:, :wide].astype(BF16), partial[:, wide:].astype(BF16)
    rows = partial.shape[0]
    keep_out[0:rows] = jnp.where(core == 0, low, high)
    send_out[0:rows] = jnp.where(core == 0, high, low)
    sums = [vec1[k : k + 1] for k in range(6)] + [up_vec[...]]
    sums += [vec2[k : k + 1] for k in range(3)] + gate_sums
    vector[...] = jnp.zeros_like(vector)
    at = 0
    for values in sums:
        for k in range(values.shape[1] // LANES):
            vector[at : at + 1] = values[:, k * LANES : (k + 1) * LANES]
            at += 1
    send_out[rows : rows + vector.shape[0]] = vector[...].astype(BF16)
    keep_out[rows:] = owned[core].astype(BF16)
    send_out[rows + vector.shape[0] :] = owned[1 - core].astype(BF16)


def place_owned(owned, grad):
    count, groups = lax.axis_size("seq"), lax.axis_size("dp")
    rows = grad.shape[0] // (count * groups)
    tiles = grad.shape[1] // LANES
    bits = count.bit_length() - 1
    for d in range(groups):
        for s in range(count):
            mirrored = 0
            for b in range(1, bits):
                mirrored = mirrored * 2 + (s >> b) % 2
            at = (mirrored * groups + d) * rows * tiles
            first = (d * count + s) * rows
            for t in range(tiles):
                value = grad[first : first + rows, t * LANES : (t + 1) * LANES]
                owned[s % 2, at + t * rows : at + (t + 1) * rows] = value


def mix_body(rows, vector_rows, first, last, bits_ref, keep, sent, got, *outs):
    fixed = rows + vector_rows
    table = (keep if first else sent)[0:rows].astype(F32) + got[0:rows].astype(F32)
    vector = sent[rows:fixed].astype(F32) + got[rows:fixed].astype(F32)
    start = rows if first else 0
    size = keep.shape[0] - start
    if last:
        piece = size // len(outs)
        for k, out in enumerate(outs):
            which = jnp.bitwise_xor(bits_ref[0], k) * piece
            at = pl.ds(pl.multiple_of(start + which, 8), piece)
            from_got = pl.ds(pl.multiple_of(fixed + which, 8), piece)
            out[fixed:] = (keep[at].astype(F32) + got[from_got].astype(F32)).astype(BF16)
    else:
        piece = size // 2
        for out, bit in ((outs[0], 1 - bits_ref[0]), (outs[1], bits_ref[0])):
            at = pl.ds(pl.multiple_of(start + bit * piece, 16), piece)
            from_got = pl.ds(pl.multiple_of(fixed + bit * piece, 16), piece)
            total = (keep[at].astype(F32) + got[from_got].astype(F32)).astype(BF16)
            if out is outs[0]:
                out[fixed:] = total
            else:
                out[...] = total
    for out in outs if last else outs[:1]:
        out[0:rows] = table.astype(BF16)
        out[rows:fixed] = vector.astype(BF16)


def table_body(groups, seqs, sub, count, place_ref, *refs):
    own, other, rest = refs[:groups], refs[groups : 2 * groups], refs[2 * groups :]
    table, gate_out, cand_out, *vectors, vector, low, high, vec, held = rest
    dp, core = place_ref[0], place_ref[1]
    vocab, width = table.shape
    half = width // 2
    rows = low.shape[1]
    for k in range(groups):
        at = jnp.bitwise_xor(dp, k)
        mine, their = own[k][0:rows], other[k][0:rows]
        low[at] = jnp.where(core == 0, mine, their)
        high[at] = jnp.where(core == 0, their, mine)
        vec[at] = own[k][rows : rows + vector.shape[0]].astype(F32)
    fixed = rows + vector.shape[0]
    mine = own[0][fixed:].astype(F32)
    for part in own[1:]:
        mine = mine + part[fixed:].astype(F32)
    held[...] = mine
    owned = gate_out.shape[1]
    tiles = held.shape[0] // owned // 4
    for k in range(4):
        home = (gate_out, cand_out)[k % 2]
        for t in range(tiles):
            at = (k * tiles + t) * owned
            home[k // 2, :, t * LANES : (t + 1) * LANES] = held[at : at + owned]
    wide = -(-vocab // 16) * 16
    row = lax.broadcasted_iota(jnp.int32, (wide, LANES), 0)
    local = lax.broadcasted_iota(jnp.int32, (wide, LANES), 1)
    sums = jnp.zeros((wide, width), F32)
    total = jnp.zeros(vector.shape, F32)
    for g in range(groups):
        picks = []
        for s in range(seqs):
            tag = low[g, (s + 1) * LANES - 16 : (s + 1) * LANES, 0:1].astype(F32)[15:16]
            lang = (tag * (1.0 / count) + 0.5).astype(jnp.int32)
            picks.append(jnp.where((row - lang * sub == local) & (local < sub), 1.0, 0.0).astype(BF16))
        both = jnp.concatenate([low[g], high[g]], axis=1)
        sums = sums + dot(jnp.concatenate(picks, axis=1), both)
        total = total + vec[g]
    table[...] = sums[0:vocab]
    vector[...] = total
    at = 0
    for out in vectors:
        for k in range(out.shape[-1] // LANES * (out.shape[0] if len(out.shape) > 1 else 1)):
            if len(out.shape) > 1:
                per_row = out.shape[1] // LANES
                lanes = slice(k % per_row * LANES, (k % per_row + 1) * LANES)
                out[k // per_row : k // per_row + 1, lanes] = vector[at : at + 1]
            else:
                out[k * LANES : (k + 1) * LANES] = vector[at]
            at += 1


def fold_body(bits_ref, *refs):
    ins, outs = refs[:4], refs[4:]
    for k in range(2):
        keep, got, bit = ins[2 * k], ins[2 * k + 1], bits_ref[k]
        for out, which in ((outs[2 * k], 1 - bit), (outs[2 * k + 1], bit)):
            out[...] = (keep[:, which].astype(F32) + got[:, which].astype(F32)).astype(BF16)


def halve_body(sizes, alone, bits_ref, *refs):
    ins, outs = refs[:-4], refs[-4:]
    owners = ins[0].shape[0]
    at = 0
    for k, size in enumerate(sizes):
        rows = slice(at, at + size) if alone else slice(0, size)
        parts = ins if alone else ins[2 * k : 2 * k + 2]
        for out, which in ((outs[2 * k], 1 - bits_ref[k]), (outs[2 * k + 1], bits_ref[k])):
            for i in range(owners // 2):
                place = which * (owners // 2) + i if k == 0 else 2 * i + which
                total = parts[0][place, rows].astype(F32)
                for part in parts[1:]:
                    total = total + part[place, rows].astype(F32)
                out[i] = total.astype(BF16)
        at += size if alone else 0


def part_rows_body(sizes, core_ref, kept, got, kept_on, got_on, send, keep):
    core = core_ref[0]
    total = jnp.concatenate(
        [a[...].astype(F32) + b[...].astype(F32) for a, b in ((kept, got), (kept_on, got_on))], axis=0
    )
    at = 0
    for size in sizes:
        first, second = total[2 * at : 2 * at + size], total[2 * at + size : 2 * at + 2 * size]
        send[at : at + size] = jnp.where(core == 0, second, first)
        keep[at : at + size] = jnp.where(core == 0, first, second)
        at += size


def beside_body(pieces, core_ref, keep, got, up, out, down):
    core = core_ref[0]
    wide = keep.shape[1]
    rows = up.shape[0]
    low = jnp.where(core == 0, keep[...], got[...])
    high = jnp.where(core == 0, got[...], keep[...])
    for k in range(pieces + 1):
        home, lane = (up, k * wide) if k < pieces else (out, 0)
        gap = up.shape[1] // 2 if k < pieces else wide
        home[:, lane : lane + wide] = low[k * rows : (k + 1) * rows]
        home[:, lane + gap : lane + gap + wide] = high[k * rows : (k + 1) * rows]
    down[:, 0:wide] = low[(pieces + 1) * rows :]
    down[:, wide : 2 * wide] = high[(pieces + 1) * rows :]


def part_cores_body(core_ref, low_keep, low_got, high_keep, high_got, send, keep):
    core = core_ref[0]
    rows = keep.shape[1]
    lane = 0
    for mine, got in ((low_keep, low_got), (high_keep, high_got)):
        wide = mine.shape[2]
        total = mine[...].astype(F32) + got[...].astype(F32)
        first, second = total[:, 0:rows], total[:, rows : 2 * rows]
        send[:, :, lane : lane + wide] = jnp.where(core == 0, second, first).astype(BF16)
        keep[:, :, lane : lane + wide] = jnp.where(core == 0, first, second).astype(BF16)
        lane += wide


def both_body(widths, core_ref, keep, got, out):
    core = core_ref[0]
    lane = 0
    for wide in widths:
        a, b = keep[:, :, lane : lane + wide], got[:, :, lane : lane + wide]
        out[:, :, 2 * lane : 2 * lane + wide] = jnp.where(core == 0, a, b)
        out[:, :, 2 * lane + wide : 2 * lane + 2 * wide] = jnp.where(core == 0, b, a)
        lane += wide


def total_body(widths, both, *outs):
    outs = list(outs[:-1]) + [outs[-1].at[k] for k in range(outs[-1].shape[0])]
    lane = 0
    for out, wide in zip(outs, widths):
        out[...] = both[:, lane : lane + 2 * wide].astype(F32)
        lane += 2 * wide


def shift(array, by):
    count = lax.axis_size("seq")
    return lax.ppermute(array, "seq", [(i, (i + by) % count) for i in range(count)])


def swap(array, axis, bit):
    return lax.ppermute(array, axis, [(i, i ^ bit) for i in range(lax.axis_size(axis))])


def exchange(chunks):
    return [chunks[0]] + [shift(chunk, k) for k, chunk in enumerate(chunks) if k > 0]


def bits_of(count):
    return [1 << b for b in range(count.bit_length() - 1)]


def tie(arrays, *after):
    held = lax.optimization_barrier((tuple(arrays), after))
    return list(held[0])


def gather_summaries(rows):
    pair = jnp.stack([rows, swap(rows, "seq", 1)])
    return [pair] + [swap(pair, "seq", 2 * j) for j in range(1, lax.axis_size("seq") // 2)]


class Columns:
    def __init__(self, sends_and_keeps, widths):
        self.places = bits_of(lax.axis_size("seq"))[1:]
        self.seq = lax.axis_index("seq")
        self.widths = widths
        self.done = 0
        low_send, low_keep, high_send, high_keep = sends_and_keeps
        self.sends, self.keeps = (low_send, high_send), (low_keep, high_keep)
        self.hold_swap()

    def hold_swap(self):
        bits = self.places[self.done], self.places[-1 - self.done]
        self.gots = tuple(swap(send, "seq", bit) for send, bit in zip(self.sends, bits))
        self.done += 1

    def fold(self, *after):
        keeps, gots = self.keeps, self.gots
        if after:
            keeps = tie(keeps, *after)
        bits = self.places[self.done], self.places[-1 - self.done]
        chosen = jnp.stack([(self.seq // bit) % 2 for bit in bits]).astype(jnp.int32)
        flat, shapes = [], []
        for k, (keep, got) in enumerate(zip(keeps, gots)):
            dims = keep.shape
            if k == 0:
                flat += [x.reshape((-1, 2) + dims[-2:]) for x in (keep, got)]
                shapes.append(dims[:-3] + dims[-2:])
            else:
                flat += [x.reshape(dims[:2] + (-1, dims[-1])) for x in (keep, got)]
                shapes.append(dims[:1] + dims[2:])
        outs = []
        for k in range(2):
            dims = flat[2 * k].shape
            outs += [((dims[0],) + dims[2:], BF16)] * 2
        got = call(fold_body, [SMEM] + [VMEM] * 4, outs, limit=24, name="fold")(chosen, *flat)
        self.sends = (got[0].reshape(shapes[0]), got[2].reshape(shapes[1]))
        self.keeps = (got[1].reshape(shapes[0]), got[3].reshape(shapes[1]))
        self.hold_swap()

    def part_cores(self, *after):
        while self.done < len(self.places):
            self.fold()
        keeps = self.keeps
        if after:
            keeps = tie(keeps, *after)
        groups, rows, _ = keeps[0].shape
        wide = sum(self.widths)
        core = (self.seq % 2).astype(jnp.int32).reshape(1)
        self.send, self.keep = call(
            part_cores_body,
            [SMEM] + [VMEM] * 4,
            [((groups, rows // 2, wide), BF16)] * 2,
            limit=24,
            name="part_cores",
        )(core, keeps[0], self.gots[0], keeps[1], self.gots[1])
        self.got = swap(self.send, "seq", 1)

    def scatter_groups(self, *after):
        groups, rows, wide = self.keep.shape
        (keep,) = tie([self.keep], *after)
        core = (self.seq % 2).astype(jnp.int32).reshape(1)
        (self.both,) = call(
            functools.partial(both_body, self.widths),
            [SMEM] + [VMEM] * 2,
            [((groups, rows, 2 * wide), BF16)],
            limit=24,
            name="both_cores",
        )(core, keep, self.got)
        both = self.both.reshape(groups * rows, 2 * wide)
        self.own = lax.psum_scatter(both, "dp", scatter_dimension=0, tiled=True)

    def finish(self, last, *after):
        (own,) = tie([self.own], *after)
        return call(
            functools.partial(total_body, self.widths),
            [VMEM],
            [((self.own.shape[0], 2 * wide), F32) for wide in self.widths[:-last]]
            + [((last, self.own.shape[0], 2 * self.widths[-1]), F32)],
            limit=24,
            name="total",
        )(own)


class FeedRows:
    def __init__(self, grad, first):
        self.places = bits_of(lax.axis_size("seq"))[1:]
        self.seq = lax.axis_index("seq")
        self.first = first
        flat = grad.reshape(-1, grad.shape[-1])
        got = lax.psum_scatter(flat, "dp", scatter_dimension=0, tiled=True)
        self.parts = [got.reshape(grad.shape[1:])]
        self.done = 0

    def step(self, *after):
        parts = self.parts
        if after:
            parts = tie(parts, *after)
        bits = self.places[-1 - self.done], self.places[self.done]
        chosen = jnp.stack([(self.seq // bit) % 2 for bit in bits]).astype(jnp.int32)
        if self.done == 0:
            rows, wide = parts[0].shape[-2:]
            sizes = (self.first, rows - self.first)
            ins = [parts[0].reshape((-1, rows, wide))]
        else:
            wide = parts[0].shape[-1]
            sizes = (self.first, parts[2].shape[-2])
            ins = parts
        owners = 2 ** (len(self.places) - self.done - 1)
        outs = [((owners, size, wide), BF16) for size in sizes for _ in range(2)]
        got = call(
            functools.partial(halve_body, sizes, len(ins) == 1),
            [SMEM] + [VMEM] * len(ins),
            outs,
            limit=24,
            name="halve",
        )(chosen, *ins)
        self.sends = (got[0], got[2])
        gots = [swap(send, "seq", bit) for send, bit in zip(self.sends, bits)]
        self.parts = [got[1], gots[0], got[3], gots[1]]
        self.done += 1

    def finish(self, ff, width, *after):
        while self.done < len(self.places):
            self.step()
        parts = tie([part[0] for part in self.parts], *after)
        rows, wide = sum(part.shape[0] for part in parts[::2]), parts[0].shape[1]
        core = (self.seq % 2).astype(jnp.int32).reshape(1)
        pieces = (ff + width) // width
        owned = width // (lax.axis_size("seq") * lax.axis_size("dp"))
        send, keep = call(
            functools.partial(part_rows_body, (owned,) * pieces + (rows // 2 - pieces * owned,)),
            [SMEM] + [VMEM] * 4,
            [((rows // 2, wide), F32)] * 2,
            limit=24,
            name="part_rows",
        )(core, *parts)
        got = swap(send, "seq", 1)
        return call(
            functools.partial(beside_body, pieces - 1),
            [SMEM] + [VMEM] * 2,
            [((owned, ff), F32), ((owned, width), F32), ((rows // 2 - pieces * owned, width), F32)],
            limit=24,
            name="beside",
        )(core, keep, got)


class CharsSums:
    def __init__(self, keep, send, rows, vector_rows):
        self.keep, self.send, self.rows, self.vector_rows = keep, send, rows, vector_rows
        self.seq = lax.axis_index("seq")
        self.bits = bits_of(lax.axis_size("seq"))
        self.first = True

    def step(self, *after):
        bit = self.bits.pop(0)
        groups = lax.axis_size("dp")
        send, keep = self.send, self.keep
        got = swap(send, "seq", bit)
        if after:
            (keep,) = tie([keep], *after)
        last = not self.bits
        start = self.rows if self.first else 0
        size = keep.shape[0] - start
        fixed = self.rows + self.vector_rows
        if last:
            which = lax.axis_index("dp")
            outs = [((fixed + size // groups, LANES), BF16)] * groups
        else:
            which = (self.seq // self.bits[0]) % 2
            outs = [((fixed + size // 2, LANES), BF16), ((size // 2, LANES), BF16)]
        outs = call(
            functools.partial(mix_body, self.rows, self.vector_rows, self.first, last),
            [SMEM] + [VMEM] * 3,
            outs,
            limit=12,
            name="mix",
        )(which.astype(jnp.int32).reshape(1), keep, send, got)
        self.first = False
        if last:
            self.own, self.sends = outs[0], outs[1:]
        else:
            self.send, self.keep = outs

    def across(self, *after):
        self.sends = tie(self.sends, *after)
        self.own = [self.own] + [swap(part, "dp", k + 1) for k, part in enumerate(self.sends)]

    def finish(self, seqs, vocab, sub, gate_shape, sizes):
        own = self.own
        other = [swap(part, "seq", 1) for part in own]
        groups = len(own)
        rows, vector_rows = self.rows, self.vector_rows
        place = jnp.stack([lax.axis_index("dp"), self.seq % 2]).astype(jnp.int32)
        return call(
            functools.partial(table_body, groups, seqs, sub, lax.axis_size("seq")),
            [SMEM] + [VMEM] * (2 * groups),
            [((vocab, 2 * LANES), F32)] + [(gate_shape, F32)] * 2 + [(size, F32) for size in sizes],
            [
                pltpu.VMEM((vector_rows, LANES), F32),
                pltpu.VMEM((groups, rows, LANES), BF16),
                pltpu.VMEM((groups, rows, LANES), BF16),
                pltpu.VMEM((groups, vector_rows, LANES), F32),
                pltpu.VMEM((own[0].shape[0] - rows - vector_rows, LANES), F32),
            ],
            limit=24,
            name="table_rows",
        )(place, *own, *other)


def shards(
    inputs, char_ids, lang_ids, lengths, char_table, gate_weight, gate_bias, cand_weight,
    join_weight, join_bias, query_weight, query_bias, key_weight, value_weight, value_bias,
    out_weight, out_bias, norm1_gain, norm1_bias, up_weight, up_bias, down_weight, down_bias,
    norm2_gain, norm2_bias, cotangent,
):
    seqs, tokens, width = inputs.shape
    chars = char_ids.shape[1]
    per = chars // tokens
    steps = chars // SEGS
    per_seg = steps // per
    vocab, embed = char_table.shape
    sub = vocab // GROUPS
    half = width // 2
    size = width // HEADS
    ff = up_weight.shape[1]
    count = lax.axis_size("seq")
    pairs = -(-seqs * HEADS // count)
    while HEADS % pairs:
        pairs += 1
    full = count * tokens
    total = seqs * tokens
    rows = seqs * SEGS
    wide = pairs * size
    seq = lax.axis_index("seq")
    me = jnp.stack([seq, seq % 2]).astype(jnp.int32)
    flat = inputs.reshape(total, width)
    cot = cotangent.reshape(total, width)

    embedded, htok, ptok, pre, pseg, payload = call(
        functools.partial(chars_forward_body, seqs, steps, per, sub),
        [SMEM] + [COPY] * 2 + [HBM] * 3,
        [
            ((seqs * chars, embed), BF16, COPY),
            ((2, per_seg, rows, half), F32, COPY),
            ((2, per_seg, rows, half), F32, COPY),
            ((2, 2, rows, half), F32, COPY),
            ((2, rows, half), F32),
            ((8 * seqs, half), F32),
        ],
        [
            pltpu.VMEM((2, seqs * chars, half), F32),
            pltpu.VMEM((2, seqs * chars, half), F32),
            pltpu.VMEM((2, rows, half), F32),
            pltpu.VMEM((-(-vocab // LANES) * LANES, embed), BF16),
            pltpu.VMEM(gate_weight.shape, BF16),
            pltpu.VMEM(cand_weight.shape, BF16),
            pltpu.SemaphoreType.DMA((3,)),
        ],
        name="chars_forward",
    )(lang_ids, char_ids, gate_bias, char_table, gate_weight, cand_weight)
    groups = gather_summaries(payload)
    projections = (join_weight, query_weight, key_weight, value_weight)
    (near_w,) = ahead_of(projections, groups[0])

    resid, enter, joined, *sent = call(
        functools.partial(join_query_body, count, seqs, tokens, pairs),
        [SMEM] + [COPY] * 6 + [PIN] + [HBM] * (1 + count // 2),
        [
            ((total, width), F32, PIN),
            ((2, rows, half), F32),
            ((total, 4 * width), BF16, HBM),
        ]
        + [((tokens // 2, 6 * wide), BF16, PIN)] * count,
        [
            pltpu.VMEM((count, 8 * seqs, half), F32),
            pltpu.VMEM((total, width), BF16),
            pltpu.SemaphoreType.DMA((count + 1,)),
            pltpu.VMEM((count, tokens // 2, 6 * wide), BF16),
            pltpu.VMEM((total, 4 * width), BF16),
            pltpu.SemaphoreType.DMA((4,)),
        ],
        name="join_query",
    )(
        me, htok, ptok, pre, join_bias, query_bias, value_bias, near_w,
               flat, *groups,
    )
    heads = exchange(sent)

    block = min(1024, full)
    *sent, lse, heads_q, heads_k, heads_v, out_v, up_v = call(
        functools.partial(attend_body, count, seqs, tokens, pairs, size, block),
        [SMEM, SMEM] + [PIN] * count,
        [((tokens // 2, 2 * wide), BF16, PIN)] * count
        + [((8, full), F32)]
        + [((pairs, full, LANES), BF16, HBM)] * 3,
        [pltpu.VMEM((pairs, full, LANES), BF16)] * 3
        + [
            pltpu.VMEM((pairs, size + 16, full), BF16),
            pltpu.VMEM((wide, full), F32),
            pltpu.VMEM((full, wide), BF16),
            pltpu.SemaphoreType.DMA((3,)),
        ],
        name="attend",
        fetch=(out_weight, up_weight),
    )(me, lengths, *heads)
    mixed_chunks = exchange(sent)
    (joined_far,) = tie([joined], *mixed_chunks)
    joined_got = swap(joined_far, "seq", 1)

    ff_block = 768
    output, d_first_in, vec1, up_vec, fed, fed_keep, fed_send, *sent = call(
        functools.partial(feed_body, count, seqs, tokens, pairs, size, ff_block),
        [SMEM] + [VMEM] * 7 + [PIN] * 3 + [HBM] * 2 + [PIN] * count,
        [
            ((total, width), BF16, HBM),
            ((total, width), F32, COPY),
            ((8, width), F32),
            ((1, ff), F32),
            ((total, ff + 2 * width), BF16, PIN),
            ((total, ff // 2 + width), BF16, PIN),
            ((total, ff // 2 + width), BF16),
        ]
        + [((tokens // 2, 2 * wide), BF16, PIN)] * count,
        [
            pltpu.VMEM((count, tokens // 2, 2 * wide), BF16),
            pltpu.VMEM((total, ff), F32),
            pltpu.VMEM((total, width), F32),
            pltpu.VMEM((total, width), BF16),
            pltpu.VMEM((total, width), BF16),
            pltpu.VMEM((total, ff), BF16),
            pltpu.VMEM((total, width), BF16),
            pltpu.VMEM((ff, width), BF16),
            pltpu.SemaphoreType.DMA((2 + ff // ff_block,)),
        ],
        limit=32,
        name="feed_forward",
    )(
        me, out_bias, norm1_gain, norm1_bias, up_bias, down_bias, norm2_gain, norm2_bias, resid,
        out_v, up_v, cot, down_weight, *mixed_chunks,
    )
    d_mixed_chunks = exchange(sent)

    fed_got, fed_keep_got = swap(fed, "seq", 1), swap(fed_send, "seq", 1)
    fed, fed_got, fed_keep, fed_keep_got = tie(
        [fed, fed_got, fed_keep, fed_keep_got], *d_mixed_chunks
    )
    grad_feed = feed_grads(fed, fed_got, fed_keep, fed_keep_got, ff, width)
    feed = FeedRows(grad_feed, (ff + width) * 2 // (count * lax.axis_size("dp")))
    d_mixed_chunks = tie(d_mixed_chunks, grad_feed)

    back_block = min(512, full)
    sent = call(
        functools.partial(attend_back_body, count, seqs, tokens, pairs, size, back_block),
        [SMEM, VMEM] + [HBM] * 3 + [PIN] * count,
        [((tokens // 2, 6 * wide), BF16, PIN)] * count,
        [pltpu.VMEM((pairs, full, LANES), BF16)] * 3
        + [
            pltpu.VMEM((size, full), BF16),
            pltpu.VMEM((pairs, full, size), BF16),
            pltpu.VMEM((wide, full), F32),
            pltpu.VMEM((full, full), BF16),
            pltpu.VMEM((full, full), BF16),
            pltpu.VMEM((full, 3 * wide), BF16),
            pltpu.SemaphoreType.DMA((3,)),
        ],
        name="attend_back",
    )(me, lse, heads_q, heads_k, heads_v, *d_mixed_chunks)
    d_chunks = exchange(sent)
    (near_w,) = ahead_of(projections, sent[0])
    input_grad, d_perm, payload_back, vec2, back_keep, back_send = call(
        functools.partial(project_back_body, count, seqs, tokens, pairs, size, per_seg),
        [SMEM, COPY, COPY, COPY, PIN] + [PIN] * count,
        [
            ((total, width), BF16, COPY),
            ((2, per_seg, rows, half), F32, COPY),
            ((8 * seqs, half), F32),
            ((8, width), F32),
            ((total, 2 * width), BF16, PIN),
            ((total, 2 * width), BF16),
        ],
        [
            pltpu.VMEM((count, tokens // 2, 6 * wide), BF16),
            pltpu.VMEM((total, 4 * width), BF16),
        ],
        name="project_back",
    )(me, pre, d_first_in, ptok, near_w, *d_chunks)
    back_groups = gather_summaries(payload_back)
    vector_rows = -(-(10 * width + ff) // (16 * LANES)) * 16

    back_got = swap(back_send, "seq", 1)
    back_all = tie([joined, joined_got, back_keep, back_got], back_groups[0])
    back_plan = tuple((0, k * half, half) for k in range(3))
    back_plan += tuple(((1 + k) * width, 3 * half, half) for k in range(3))
    back_parts = outer_grads(back_all, back_plan, 3 * half, width, "grad_back")
    back_parts = tie(back_parts, *back_groups)
    back = Columns(back_parts, (half,) * 6)
    back_groups = tie(back_groups, *back_parts)

    own_rows = 4 * half * embed // (2 * LANES)
    table_rows = seqs * LANES
    chars_keep, chars_send = call(
        functools.partial(chars_back_body, count, seqs, steps, per),
        [SMEM, SMEM] + [VMEM] * 7 + [COPY] * 3 + [HBM] * (2 + count),
        [
            ((table_rows + own_rows, LANES), BF16),
            ((table_rows + vector_rows + own_rows, LANES), BF16),
        ],
        [
            pltpu.VMEM((2, seqs * chars, half), F32),
            pltpu.VMEM((2, seqs * chars, half), F32),
            pltpu.VMEM((seqs * chars, 4 * half), BF16),
            pltpu.VMEM((2, per_seg, rows, half), F32),
            pltpu.VMEM((2, rows, half), F32),
            pltpu.VMEM((2, rows, half), F32),
            pltpu.VMEM(gate_weight.shape, BF16),
            pltpu.VMEM(cand_weight.shape, BF16),
            pltpu.VMEM((count, 8 * seqs, half), F32),
            pltpu.VMEM((count, 8 * seqs, half), F32),
            pltpu.SemaphoreType.DMA((2 + 2 * count,)),
            pltpu.VMEM((vector_rows, LANES), F32),
            pltpu.VMEM((2, own_rows, LANES), F32),
        ],
        name="chars_back",
    )(
        lang_ids, me, char_ids, gate_bias, enter, pseg, vec1, up_vec, vec2, embedded, ptok, d_perm,
        gate_weight, cand_weight, *groups, *back_groups,
    )
    chars_sums = CharsSums(chars_keep, chars_send, table_rows, vector_rows)
    chars_sums.step()
    chars_sums.step()
    back.fold(chars_sums.send)
    while chars_sums.bits:
        chars_sums.step()
    back.part_cores(*chars_sums.sends)
    back.scatter_groups()
    chars_sums.across()
    feed.step(back.both)
    feed.step(*chars_sums.own[1:3])
    gate_shape = (2, embed // (count * lax.axis_size("dp")), half)
    sizes = [(width,)] * 6 + [(ff,)] + [(width,)] * 3 + [(2, half)]
    grad_table, grad_gate, grad_cand, *sums = chars_sums.finish(seqs, vocab, sub, gate_shape, sizes)
    grad_up, grad_out, grad_down = feed.finish(ff, width, *chars_sums.own)
    grad_query, grad_key, grad_value, grad_join = back.finish(3, grad_table, grad_up)

    return (
        output.reshape(inputs.shape),
        input_grad.reshape(inputs.shape),
        grad_table,
        grad_gate,
        sums[10],
        grad_cand,
        grad_join,
        sums[9],
        grad_query,
        sums[7],
        grad_key,
        grad_value,
        sums[8],
        grad_out,
        sums[5],
        sums[3],
        sums[4],
        grad_up,
        sums[6],
        grad_down,
        sums[2],
        sums[0],
        sums[1],
    )


def solution(mesh):
    spread_rows = P("dp", "seq", None)
    placed = (
        (spread_rows, P("dp", "seq"), P("dp"), P("dp")) + (P(),) * 21 + (spread_rows,)
    )
    owned = P(("dp", "seq"), None)
    owned_mid = P(None, ("dp", "seq"), None)
    return jax.shard_map(
        shards,
        mesh=mesh,
        in_specs=placed,
        out_specs=(
            spread_rows, spread_rows, P(), owned_mid, P(), owned_mid, owned_mid, P(),
            owned, P(), owned, owned, P(), owned, P(), P(), P(), owned, P(), owned, P(), P(), P(),
        ),
        check_vma=False,
    )
```
